32 devices in a mesh: tm: 8 (over z, core), sta: 4 (over y, x).
Axes of the slice: x: 2, y: 2, z: 4, core: 2. Of those that a mesh axis runs over, the one named last changes fastest.
Arguments:
- waveforms: bfloat16 [120, 4096], P('sta', 'tm'), may hold values from -6 to 6
- templates: bfloat16 [16, 64, 120, 100], P('tm', None, 'sta'), may hold values from -6 to 6
- available: int32 [16, 64, 120], P('tm', None, 'sta'), may hold values 0 or 1
- moveout: int32 [16, 64, 120], P('tm', None, 'sta'), may hold values from 0 to 63
- bank_blocks: int32 [2], replicated, may hold values from 0 to 15
Outputs:
- detect_sum: float32 [128, 4096], P('sta', 'tm')
The draws below stay inside these ranges and needn't reach their ends.
Inputs may be any that keep to these rules, and one draw needn't show every extreme that they name: `bank_blocks`: block b is stored at index b // 2 of tm.
All inputs are finite; a program needn't handle non-finite values. No bound on the sum of `available` on one device may be relied on, other than what follows from the above.
Results may differ from the reference program's by a relative error of at most 0.0029.
Values may be sent and summed in bfloat16 or wider, within the bound.
No kernel may reach another device: no remote copies, remote signals or barrier semaphores. Data moves between devices by JAX's collectives and lax.ppermute only.
A program may use at most 128 MiB of HBM per device.

```python
import jax
import jax.numpy as jnp
from jax import lax

EVENTS = 64
TLEN = 100
MOVE = 64
CHANNELS = 120
TIME = 4096
BLOCKS = 16
TEMPLATES = 128


def set_ends(values, stream_key, smallest, largest):
    dims = values.shape
    spot = [jax.random.randint(jax.random.fold_in(stream_key, axis), (), 0, dims[axis]) for axis in range(len(dims))]
    values = values.at[tuple(spot)].set(smallest)
    longest = dims.index(max(dims))
    spot[longest] = (spot[longest] + 1) % dims[longest]
    return values.at[tuple(spot)].set(largest)


def shard_levels(key, dims, cuts, smallest, high):
    def one(position, parts):
        heights = jax.random.uniform(jax.random.fold_in(jax.random.fold_in(key, 6), position), (parts,), jnp.float32, smallest / len(cuts), high / len(cuts))
        return jnp.repeat(jnp.exp(heights), dims[position] // parts).reshape((-1,) + (1,) * (len(dims) - position - 1))

    factor_of = one(*cuts[0])
    for cut in cuts[1:]:
        factor_of = factor_of * one(*cut)
    return factor_of


def gaussian(own_key, extent, width, reach, shards=(), kind=jnp.bfloat16):
    drawn = width * jax.random.normal(own_key, extent, jnp.float32)
    if shards:
        drawn = drawn * shard_levels(own_key, extent, shards, -0.22, 0.18)
    return jnp.clip(drawn, -reach, reach).astype(kind)


def setup_inputs(seed: int = 0) -> dict:
    keys = jax.random.split(jax.random.key(seed), 6)
    return {
        "waveforms": gaussian(keys[0], (CHANNELS, TIME), 1.0, 6.0, ((0, 4), (1, 8))),
        "templates": gaussian(keys[1], (BLOCKS, EVENTS, CHANNELS, TLEN), 1.0, 6.0, ((0, 8), (2, 4))),
        "available": set_ends((jax.random.randint(keys[2], (BLOCKS, EVENTS, CHANNELS), 0, 4) < 3).astype(jnp.int32), jax.random.fold_in(keys[2], 1), 0, 1),
        "moveout": set_ends(jax.random.randint(keys[3], (BLOCKS, EVENTS, CHANNELS), 0, MOVE), jax.random.fold_in(keys[3], 1), 0, MOVE - 1).astype(jnp.int32),
        "bank_blocks": jax.random.randint(keys[4], (2,), 0, BLOCKS).astype(jnp.int32),
    }


epsilon = 1e-06
block_span = 512

def normalize_bank(bank):
    values = bank.astype(jnp.float32)
    center = lax.optimization_barrier(jnp.mean(values, axis=-1, keepdims=True))
    deviate = values - center
    spread = jnp.sqrt(lax.optimization_barrier(jnp.mean(deviate * deviate, axis=-1, keepdims=True)) + epsilon)
    return (deviate / (spread * bank.shape[-1])).astype(jnp.bfloat16)

def window_sigma(padded, length, tlen):
    first_sum = jnp.zeros((padded.shape[0], length), jnp.float32)
    second_sum = jnp.zeros((padded.shape[0], length), jnp.float32)
    for lag in range(tlen):
        piece = padded[:, lag:lag + length].astype(jnp.float32)
        first_sum = first_sum + piece
        second_sum = second_sum + piece * piece
    mean_value = first_sum / tlen
    return jnp.sqrt(second_sum / tlen - mean_value * mean_value + epsilon)

def reference(waveforms, templates, available, moveout, bank_blocks):
    tlen = templates.shape[3]
    total_len = waveforms.shape[1]
    chosen = templates[bank_blocks].reshape(TEMPLATES, CHANNELS, tlen)
    unit_norm_templates = normalize_bank(chosen).astype(jnp.float32)
    weights = available[bank_blocks].reshape(TEMPLATES, CHANNELS).astype(jnp.float32)
    shifts = moveout[bank_blocks].reshape(TEMPLATES, CHANNELS).astype(jnp.int32)
    padded = jnp.pad(waveforms, ((0, 0), (0, MOVE + tlen - 1)))
    sigma = window_sigma(padded, total_len + MOVE, tlen)

    def one_window(block):
        reference_sample = block * block_span
        segment = lax.dynamic_slice_in_dim(padded, reference_sample, block_span + MOVE + tlen - 1, 1)
        stacked_correlation = jnp.stack([segment[:, lag:lag + block_span + MOVE] for lag in range(tlen)], axis=1).astype(jnp.float32)
        correlation_values = jnp.einsum('ofn,fnw->ofw', unit_norm_templates, stacked_correlation)
        scaled_traces = correlation_values / lax.dynamic_slice_in_dim(sigma, reference_sample, block_span + MOVE, 1)[None]
        index_grid = jnp.arange(block_span, dtype=jnp.int32)[None, None, :] + shifts[:, :, None]
        picked = jnp.take_along_axis(scaled_traces, index_grid, axis=2)
        return lax.optimization_barrier(jnp.sum(picked * weights[:, :, None], axis=1))
    result = lax.map(one_window, jnp.arange(total_len // block_span, dtype=jnp.int32))
    return jnp.transpose(result, (1, 0, 2)).reshape(TEMPLATES, total_len)
```

```python
import functools

import jax
import jax.numpy as jnp
from jax import lax
from jax.experimental import pallas as pl
from jax.experimental.pallas import tpu as pltpu
from jax.sharding import PartitionSpec as P

MOVE = 64
EPSILON = 1e-06
LANES = 128
OFFSETS = 16
CODE = 100
VMEM_LIMIT = 40 * 1024 * 1024


def pack_kernel(chips, group, scalars, templates, available, moveout, mine, theirs, raw, packed, sems):
    blocks, events = templates.shape[:2]
    channels, tlen = templates.shape[2:]
    fetch = [
        pltpu.make_async_copy(templates.at[scalars[which]], raw.at[which], sems.at[which])
        for which in range(2)
    ]
    for copy in fetch:
        copy.start()
    packed[...] = jnp.zeros_like(packed)
    flags = jnp.where(available[...] > 0, moveout[...] + 1, 0).astype(jnp.float32)
    for which in range(2):
        code = flags[:, 0, :]
        for block in range(1, blocks):
            code = jnp.where(scalars[which] == block, flags[:, block, :], code)
        code = code.astype(jnp.bfloat16)
        fetch[which].wait()
        for event in range(events):
            row = which * events + event
            dest, item = divmod(row, group)
            chip, core = divmod(dest, 2)
            packed[core, chip, item, 0:channels, 0:tlen] = raw[which, event]
            packed[core, chip, item, 0:channels, CODE : CODE + 1] = code[:, event : event + 1]
    me = scalars[2]
    send = [
        pltpu.make_async_copy(packed.at[me], mine, sems.at[0]),
        pltpu.make_async_copy(packed.at[1 - me], theirs, sems.at[1]),
    ]
    for copy in send:
        copy.start()
    for copy in send:
        copy.wait()


def pack(chips, group, scalars, templates, available, moveout):
    _, events, channels, tlen = templates.shape
    shape = (chips, group, 32, LANES)
    return pl.pallas_call(
        functools.partial(pack_kernel, chips, group),
        out_shape=[jax.ShapeDtypeStruct(shape, jnp.bfloat16)] * 2,
        in_specs=[
            pl.BlockSpec(memory_space=pltpu.SMEM),
            pl.BlockSpec(memory_space=pl.ANY),
            pl.BlockSpec(memory_space=pltpu.VMEM),
            pl.BlockSpec(memory_space=pltpu.VMEM),
        ],
        out_specs=[pl.BlockSpec(memory_space=pl.ANY)] * 2,
        scratch_shapes=[
            pltpu.VMEM((2, events, channels, tlen), jnp.bfloat16),
            pltpu.VMEM((2,) + shape, jnp.bfloat16),
            pltpu.SemaphoreType.DMA((2,)),
        ],
        compiler_params=pltpu.CompilerParams(vmem_limit_bytes=VMEM_LIMIT),
        name="pack",
    )(scalars, templates, available, moveout)


def merge_kernel(chips, scalars, mine, other, *rest):
    outs, sems = rest[:-1], rest[-1]
    chip, core = scalars[0], scalars[1]
    for step in range(chips):
        dest = jnp.bitwise_xor(chip, step)
        owner = jnp.where(dest < chips // 2, scalars[2], scalars[3])
        here = owner % 2 == core

        @pl.when(here)
        def _():
            pltpu.make_async_copy(mine.at[dest], outs[step], sems.at[step]).start()

        @pl.when(jnp.logical_not(here))
        def _():
            pltpu.make_async_copy(other.at[dest], outs[step], sems.at[step]).start()

    for step in range(chips):
        pltpu.make_async_copy(mine.at[0], outs[step], sems.at[step]).wait()


def merge(chips, scalars, mine, other):
    return pl.pallas_call(
        functools.partial(merge_kernel, chips),
        out_shape=[jax.ShapeDtypeStruct(mine.shape[1:], mine.dtype)] * chips,
        in_specs=[pl.BlockSpec(memory_space=pltpu.SMEM)] + [pl.BlockSpec(memory_space=pl.ANY)] * 2,
        out_specs=[pl.BlockSpec(memory_space=pl.ANY)] * chips,
        scratch_shapes=[pltpu.SemaphoreType.DMA((chips,))],
        compiler_params=pltpu.CompilerParams(vmem_limit_bytes=VMEM_LIMIT),
        name="merge",
    )(scalars, mine, other)


def left(values, count):
    return pltpu.roll(values, values.shape[1] - count, 1)


def window_sums(values):
    sums = {1: values}
    width = 1
    while width < 64:
        sums[2 * width] = sums[width] + left(sums[width], width)
        width *= 2
    return sums[64] + left(sums[32], 64) + left(sums[4], 96)


def stacked(row, span):
    copies = jnp.broadcast_to(row, (8, row.shape[1]))
    return pltpu.roll(copies, row.shape[1] - 112, 1, stride=16, stride_axis=0)


def tiles(values, first, count):
    return jnp.concatenate(
        [values[:, LANES * m : LANES * (m + 1)] for m in range(first, first + count)], axis=0
    )


def main_kernel(sources, channels, tlen, group, scalars, waves, *rest):
    pieces = rest[:sources]
    outs = rest[sources:-8]
    padded, inverse, piece, bank, weight_a, weight_r, total, sem = rest[-8:]
    length = waves.shape[1]
    span = padded.shape[1]
    per_tile = LANES // group
    tile_count = OFFSETS // per_tile
    row_tiles = length // LANES

    source = scalars[0]
    for index in range(sources):

        @pl.when(source == index)
        def _():
            pltpu.make_async_copy(pieces[index], piece, sem).start()

    padded[...] = jnp.zeros_like(padded)
    padded[0:channels, 0:length] = waves[...].astype(jnp.float32)

    @pl.loop(0, 4)
    def _(part):
        rows = pl.ds(pl.multiple_of(part * 8, 8), 8)
        values = padded[rows, :]
        first_sum = window_sums(values)
        second_sum = window_sums(values * values)
        mean = first_sum / tlen
        inverse[rows, :] = lax.rsqrt(second_sum / tlen - mean * mean + EPSILON)

    pltpu.make_async_copy(pieces[0], piece, sem).wait()

    lag = lax.broadcasted_iota(jnp.int32, (LANES, 8 * group), 0)
    for part in range(4):
        half = piece[:, 16 * (part // 2) : 16 * (part // 2) + 16, :].astype(jnp.float32)
        values = half[:, 8 * (part % 2) : 8 * (part % 2) + 8, :].reshape(8 * group, LANES).T
        used = lag < tlen
        center = jnp.sum(jnp.where(used, values, 0.0), axis=0, keepdims=True) / tlen
        deviate = jnp.where(used, values - center, 0.0)
        spread = jnp.sqrt(jnp.sum(deviate * deviate, axis=0, keepdims=True) / tlen + EPSILON)
        unit = jnp.where(lag == CODE, values, deviate / (spread * tlen))
        bank[part] = unit.astype(jnp.bfloat16)

    @pl.loop(0, channels)
    def _(channel):
        part, item = channel // 8, channel % 8
        source_lane = lax.broadcasted_iota(jnp.int32, (8 * group, LANES), 0)
        target_lane = lax.broadcasted_iota(jnp.int32, (8 * group, LANES), 1)
        expand = (source_lane == (target_lane % group) * 8 + item).astype(jnp.float32)
        spreaded = jnp.dot(
            bank[part], expand.astype(jnp.bfloat16), preferred_element_type=jnp.float32
        )
        code = spreaded[CODE : CODE + 1, :].astype(jnp.int32)
        usable = code > 0
        shift = code - 1 + lax.broadcasted_iota(jnp.int32, (1, LANES), 1) // group
        rows = lax.broadcasted_iota(jnp.int32, (112, LANES), 0)
        taps = jnp.where(jnp.logical_and(rows < tlen, usable), spreaded[0:112, :], 0.0)
        for bit in (1, 2, 4):
            taps = jnp.where(jnp.bitwise_and(shift, bit) > 0, pltpu.roll(taps, bit, 0), taps)
        for bit in (8, 16, 32, 64):
            gap = jnp.zeros((bit, LANES), jnp.float32)
            taps = jnp.where(
                jnp.bitwise_and(shift, bit) > 0,
                jnp.concatenate([gap, taps], axis=0),
                jnp.concatenate([taps, gap], axis=0),
            )[0:184]
        offset_rows = lax.broadcasted_iota(jnp.int32, (LANES, LANES), 0)
        for index in range(tile_count):
            ahead = index * per_tile
            column = [taps, jnp.zeros((256 - 184 - ahead, LANES), jnp.float32)]
            if ahead:
                column = [jnp.zeros((ahead, LANES), jnp.float32)] + column
            lanes = slice(LANES * index, LANES * (index + 1))
            weight_a[channel, :, lanes] = jnp.concatenate(column, axis=0).astype(jnp.bfloat16)
            pick = jnp.logical_and(offset_rows == shift + ahead, usable)
            pick = jnp.where(pick, 1.0, 0.0).astype(jnp.bfloat16)
            weight_r[channel, 0:LANES, lanes] = pick
            weight_r[channel, LANES : 2 * LANES, lanes] = pick

    total[...] = jnp.zeros_like(total)

    @pl.loop(0, channels)
    def _(channel):
        samples = stacked(padded[pl.ds(channel, 1), :], span)
        left_a = jnp.concatenate(
            [tiles(samples, 0, row_tiles), tiles(samples, 1, row_tiles)], axis=1
        ).astype(jnp.bfloat16)
        scale = tiles(stacked(inverse[pl.ds(channel, 1), :], span), 0, row_tiles)
        high = scale.astype(jnp.bfloat16)
        low = (scale - high.astype(jnp.float32)).astype(jnp.bfloat16)
        left_r = jnp.concatenate([high, low], axis=1)
        corr = jnp.dot(left_a, weight_a[channel], preferred_element_type=jnp.float32)
        factor = jnp.dot(left_r, weight_r[channel], preferred_element_type=jnp.float32)
        total[...] += corr * factor

    rows_out = outs[0].shape[0]
    for step, out in enumerate(outs):
        segment = jnp.bitwise_xor(scalars[1], step)
        out[...] = total[pl.ds(pl.multiple_of(segment * rows_out, rows_out), rows_out), :].astype(
            jnp.bfloat16
        )


def correlate(channels, tlen, group, samples, scalars, waves, pieces):
    length = waves.shape[1]
    segments = length // samples
    span = length + 2 * LANES
    rows = length // OFFSETS
    width = OFFSETS * group
    out = jax.ShapeDtypeStruct((samples // OFFSETS, width), jnp.bfloat16)
    return pl.pallas_call(
        functools.partial(main_kernel, len(pieces), channels, tlen, group),
        out_shape=[out] * segments,
        in_specs=[
            pl.BlockSpec(memory_space=pltpu.SMEM),
            pl.BlockSpec(memory_space=pltpu.VMEM),
        ]
        + [pl.BlockSpec(memory_space=pl.ANY)] * len(pieces),
        out_specs=[pl.BlockSpec(memory_space=pltpu.VMEM)] * segments,
        scratch_shapes=[
            pltpu.VMEM((32, span), jnp.float32),
            pltpu.VMEM((32, span), jnp.float32),
            pltpu.VMEM((group, 32, LANES), jnp.bfloat16),
            pltpu.VMEM((4, LANES, 8 * group), jnp.bfloat16),
            pltpu.VMEM((channels, 256, width), jnp.bfloat16),
            pltpu.VMEM((channels, 256, width), jnp.bfloat16),
            pltpu.VMEM((rows, width), jnp.float32),
            pltpu.SemaphoreType.DMA(()),
        ],
        compiler_params=pltpu.CompilerParams(vmem_limit_bytes=VMEM_LIMIT),
        name="correlate",
    )(scalars, waves, *pieces)


def finish_kernel(group, scalars, *rest):
    parts, out = rest[:-1], rest[-1]
    rows, width = parts[0].shape
    samples = out.shape[1]
    sums = []
    for parity in range(2):
        value = parts[parity][...].astype(jnp.float32)
        for part in parts[parity + 2 :: 2]:
            value = value + part[...].astype(jnp.float32)
        sums.append(value)
    swapped = scalars[0] == 1
    halves = [jnp.where(swapped, sums[1], sums[0]), jnp.where(swapped, sums[0], sums[1])]
    row = lax.broadcasted_iota(jnp.int32, (rows, samples), 0)
    lane = lax.broadcasted_iota(jnp.int32, (rows, samples), 1)
    place = (lane // OFFSETS == 8 * (row // 8) + 7 - row % 8).astype(jnp.float32)
    lane = lax.broadcasted_iota(jnp.int32, (group, samples), 1) % OFFSETS
    for index, half in enumerate(halves):
        wide = jnp.dot(
            half.T, place, precision=lax.Precision.HIGHEST, preferred_element_type=jnp.float32
        )
        value = jnp.zeros((group, samples), jnp.float32)
        for offset in range(OFFSETS):
            value = jnp.where(lane == offset, wide[offset * group : (offset + 1) * group], value)
        out[index * group : (index + 1) * group, :] = value


def finish(group, samples, scalars, parts):
    return pl.pallas_call(
        functools.partial(finish_kernel, group),
        out_shape=jax.ShapeDtypeStruct((2 * group, samples), jnp.float32),
        in_specs=[pl.BlockSpec(memory_space=pltpu.SMEM)]
        + [pl.BlockSpec(memory_space=pltpu.VMEM)] * len(parts),
        out_specs=pl.BlockSpec(memory_space=pltpu.VMEM),
        compiler_params=pltpu.CompilerParams(vmem_limit_bytes=VMEM_LIMIT),
        name="finish",
    )(scalars, *parts)


def shards(waveforms, templates, available, moveout, bank_blocks):
    channels, samples = waveforms.shape
    blocks, events, _, tlen = templates.shape
    count_tm = lax.axis_size("tm")
    count_sta = lax.axis_size("sta")
    chips = count_tm // 2
    group = 2 * events // count_tm
    me = lax.axis_index("tm").astype(jnp.int32)
    station = lax.axis_index("sta").astype(jnp.int32)
    chip, core = me // 2, me % 2

    owners = bank_blocks // blocks
    slots = bank_blocks % blocks
    waves = lax.all_gather(waveforms, "tm", axis=1, tiled=True)

    mine, theirs = pack(
        chips,
        group,
        jnp.stack([slots[0], slots[1], core]),
        templates,
        jnp.transpose(available, (2, 0, 1)),
        jnp.transpose(moveout, (2, 0, 1)),
    )
    other = lax.ppermute(theirs, "tm", [(i, i ^ 1) for i in range(count_tm)])
    merged = merge(chips, jnp.stack([chip, core, owners[0], owners[1]]), mine, other)
    pieces = [merged[0]]
    for step in range(1, chips):
        pieces.append(
            lax.ppermute(merged[step], "tm", [(i, i ^ (2 * step)) for i in range(count_tm)])
        )
    owner = jnp.where(chip < chips // 2, owners[0], owners[1])
    slot = 2 * station + core
    parts = correlate(
        channels, tlen, group, samples, jnp.stack([(owner // 2) ^ chip, slot]), waves, pieces
    )
    gathered = []
    for step in range(count_tm):
        route = [
            (d * count_sta + s, ((2 * s + d % 2) ^ step) * count_sta + d // 2)
            for d in range(count_tm)
            for s in range(count_sta)
        ]
        gathered.append(lax.ppermute(parts[step], ("tm", "sta"), route))
    return finish(group, samples, core[None], gathered)


def solution(mesh):
    in_specs = (
        P("sta", "tm"),
        P("tm", None, "sta", None),
        P("tm", None, "sta"),
        P("tm", None, "sta"),
        P(),
    )
    out_specs = P("sta", "tm")
    return jax.shard_map(shards, mesh=mesh, in_specs=in_specs, out_specs=out_specs, check_vma=False)
```

```python
import functools

import jax
import jax.numpy as jnp
from jax import lax
from jax.experimental import pallas as pl
from jax.experimental.pallas import tpu as pltpu
from jax.sharding import PartitionSpec as P

MOVE = 64
EPSILON = 1e-06
LANES = 128
OFFSETS = 8
STRIDE = 64
DEPTH = 256
VMEM_LIMIT = 28 * 1024 * 1024

SMEM = pl.BlockSpec(memory_space=pltpu.SMEM)
VMEM = pl.BlockSpec(memory_space=pltpu.VMEM)
ANY = pl.BlockSpec(memory_space=pl.ANY)


def params():
    return pltpu.CompilerParams(vmem_limit_bytes=VMEM_LIMIT)


def cost(micros):
    return pl.CostEstimate(
        flops=int(micros * 1e9), bytes_accessed=int(micros * 1e6), transcendentals=0
    )


def pack_kernel(scalars, templates, available, moveout, mine, theirs, square, sems):
    blocks, channels, events, tlen = templates.shape
    chips, _, group, _ = mine.shape
    half = channels // 2
    me = scalars[2]
    copies = []
    for chip in range(chips):
        which, part = divmod(chip * group, events)
        for side, out in enumerate((mine, theirs)):
            first = half * jnp.where(me == side, 0, 1)
            copy = pltpu.make_async_copy(
                templates.at[scalars[which], pl.ds(first, half), pl.ds(part, group), :],
                out.at[chip, pl.ds(0, half)],
                sems.at[chip, side],
            )
            copy.start()
            copies.append(copy)
    flags = jnp.where(available[...] > 0, moveout[...] + 1, 0).astype(jnp.float32)
    for which in range(2):
        code = flags[:, 0, :]
        for block in range(1, blocks):
            code = jnp.where(scalars[which] == block, flags[:, block, :], code)
        square[...] = jnp.zeros_like(square)
        square[0:channels, 0:events] = code
        turned = square[...].T
        other = pltpu.roll(turned, LANES - half, 1)
        here = jnp.where(me == 0, turned, other)[:, 0:tlen].astype(jnp.bfloat16)
        there = jnp.where(me == 0, other, turned)[:, 0:tlen].astype(jnp.bfloat16)
        for index in range(events // group):
            chip = which * (events // group) + index
            rows = slice(index * group, (index + 1) * group)
            mine[chip, half] = here[rows]
            theirs[chip, half] = there[rows]
    for copy in copies:
        copy.wait()


def pack(chips, group, scalars, templates, available, moveout):
    channels, tlen = templates.shape[1], templates.shape[3]
    shape = (chips, channels // 2 + 1, group, tlen)
    return pl.pallas_call(
        pack_kernel,
        out_shape=[jax.ShapeDtypeStruct(shape, jnp.bfloat16)] * 2,
        in_specs=[SMEM, ANY, VMEM, VMEM],
        out_specs=[VMEM] * 2,
        scratch_shapes=[
            pltpu.VMEM((LANES, LANES), jnp.float32),
            pltpu.SemaphoreType.DMA((chips, 2)),
        ],
        compiler_params=params(),
        cost_estimate=cost(1.5),
        name="pack",
    )(scalars, templates, available, moveout)


def merge_kernel(chips, scalars, mine, other, *rest):
    outs, sems = rest[:-1], rest[-1]
    chip, core = scalars[0], scalars[1]
    for step in range(chips):
        dest = jnp.bitwise_xor(chip, step)
        owner = jnp.where(dest < chips // 2, scalars[2], scalars[3])
        here = owner % 2 == core

        @pl.when(here)
        def _():
            pltpu.make_async_copy(mine.at[dest], outs[step], sems.at[step]).start()

        @pl.when(jnp.logical_not(here))
        def _():
            pltpu.make_async_copy(other.at[dest], outs[step], sems.at[step]).start()

    for step in range(chips):
        pltpu.make_async_copy(mine.at[0], outs[step], sems.at[step]).wait()


def merge(chips, scalars, mine, other):
    return pl.pallas_call(
        functools.partial(merge_kernel, chips),
        out_shape=[jax.ShapeDtypeStruct(mine.shape[1:], mine.dtype)] * chips,
        in_specs=[SMEM, ANY, ANY],
        out_specs=[ANY] * chips,
        scratch_shapes=[pltpu.SemaphoreType.DMA((chips,))],
        compiler_params=params(),
        cost_estimate=cost(1),
        name="merge",
    )(scalars, mine, other)


def left(values, count):
    return pltpu.roll(values, values.shape[1] - count, 1)


def window_sums(values):
    sums = {1: values}
    width = 1
    while width < 64:
        sums[2 * width] = sums[width] + left(sums[width], width)
        width *= 2
    return sums[64] + left(sums[32], 64) + left(sums[4], 96)


def lagged(row, ahead):
    copies = jnp.broadcast_to(row, (8, row.shape[1]))
    return pltpu.roll(copies, row.shape[1] - 7 - ahead, 1, stride=1, stride_axis=0)


def waves_kernel(channels, samples, tlen, *rest):
    waves = rest[:-4]
    left_a, left_r, padded, inverse = rest[-4:]
    span = waves[0].shape[1]
    steps = samples // STRIDE
    padded[...] = jnp.zeros_like(padded)
    for index, wave in enumerate(waves):
        padded[0:channels, span * index : span * (index + 1)] = wave[...].astype(jnp.float32)

    @pl.loop(0, 4)
    def _(part):
        rows = pl.ds(pl.multiple_of(part * 8, 8), 8)
        values = padded[rows, :]
        first_sum = window_sums(values)
        second_sum = window_sums(values * values)
        mean = first_sum / tlen
        inverse[rows, :] = lax.rsqrt(second_sum / tlen - mean * mean + EPSILON)

    @pl.loop(0, channels)
    def _(channel):
        row = padded[pl.ds(channel, 1), :]
        scale = inverse[pl.ds(channel, 1), :]
        even, odd = lagged(row, 0), lagged(row, STRIDE)
        even_scale, odd_scale = lagged(scale, 0), lagged(scale, STRIDE)
        columns = ([], [], [])
        for index in range(len(waves)):
            for step in range(steps):
                start = span * index + STRIDE * (step - step % 2)
                values = odd if step % 2 else even
                columns[0].append(values[:, start : start + LANES])
                columns[1].append(values[:, start + LANES : start + 2 * LANES])
                values = odd_scale if step % 2 else even_scale
                columns[2].append(values[:, start : start + LANES])
        left_a[channel, :, 0:LANES] = jnp.concatenate(columns[0], axis=0).astype(jnp.bfloat16)
        left_a[channel, :, LANES:] = jnp.concatenate(columns[1], axis=0).astype(jnp.bfloat16)
        value = jnp.concatenate(columns[2], axis=0)
        high = value.astype(jnp.bfloat16)
        left_r[channel, :, 0:LANES] = high
        left_r[channel, :, LANES:] = (value - high.astype(jnp.float32)).astype(jnp.bfloat16)


def prepare_waves(samples, tlen, waves):
    channels, span = waves[0].shape
    rows = len(waves) * samples // OFFSETS
    out = jax.ShapeDtypeStruct((channels, rows, DEPTH), jnp.bfloat16)
    return pl.pallas_call(
        functools.partial(waves_kernel, channels, samples, tlen),
        out_shape=[out, out],
        in_specs=[VMEM] * len(waves),
        out_specs=[VMEM, VMEM],
        scratch_shapes=[
            pltpu.VMEM((32, span * len(waves)), jnp.float32),
            pltpu.VMEM((32, span * len(waves)), jnp.float32),
        ],
        compiler_params=params(),
        cost_estimate=cost(5),
        name="prepare_waves",
    )(*waves)


def main_kernel(channels, tlen, group, scalars, first, second, left_a, left_r, *rest):
    outs = rest[:-4]
    bank, weight_a, weight_r, total = rest[-4:]
    half = channels // 2
    slots = LANES // group
    banks = (half + 1) // slots
    offset_count = LANES // group
    tile_count = OFFSETS // offset_count
    code_lane = (half % slots) * group
    top = 112 + 8 * (7 + offset_count - 1)

    lag = lax.broadcasted_iota(jnp.int32, (LANES, LANES), 0)
    lane = lax.broadcasted_iota(jnp.int32, (1, LANES), 1)
    used = lag < tlen
    for side, piece in enumerate((first, second)):
        turned = []
        for index in range(banks):
            values = piece[slots * index : slots * (index + 1)].astype(jnp.float32)
            values = values.reshape(LANES, tlen)
            values = jnp.concatenate([values, jnp.zeros((LANES, LANES - tlen), jnp.float32)], axis=1)
            turned.append(values.T)
        codes = turned[-1]
        for index, values in enumerate(turned):
            code = jnp.zeros((1, LANES), jnp.float32)
            for slot in range(slots):
                item = slots * index + slot
                if item < half:
                    moved = pltpu.roll(
                        codes[item : item + 1, :], (group * slot - code_lane) % LANES, 1
                    )
                    code = jnp.where(lane // group == slot, moved, code)
            center = jnp.sum(jnp.where(used, values, 0.0), axis=0, keepdims=True) / tlen
            deviate = jnp.where(used, values - center, 0.0)
            spread = jnp.sqrt(jnp.sum(deviate * deviate, axis=0, keepdims=True) / tlen + EPSILON)
            unit = (deviate / (spread * tlen)).astype(jnp.bfloat16).astype(jnp.float32)
            unit = jnp.where(code > 0, unit, 0.0)
            shift = code.astype(jnp.int32) - 1
            for bit in (1, 2, 4):
                unit = jnp.where(jnp.bitwise_and(shift, bit) > 0, pltpu.roll(unit, bit, 0), unit)
            unit = jnp.where(lag == 112, code, unit)
            bank[side * banks + index] = unit.astype(jnp.bfloat16)

    source_lane = lax.broadcasted_iota(jnp.int32, (LANES, LANES), 0)
    target_lane = lax.broadcasted_iota(jnp.int32, (LANES, LANES), 1)
    ahead = lane // group
    for side in range(2):
        base = half * jnp.where(scalars[1] == side, 0, 1)

        @pl.loop(0, half)
        def _(item):
            slot = item % slots
            expand = (source_lane == target_lane % group + slot * group).astype(jnp.float32)
            spreaded = jnp.dot(
                bank[side * banks + item // slots],
                expand.astype(jnp.bfloat16),
                preferred_element_type=jnp.float32,
            )
            code = spreaded[112:113, :].astype(jnp.int32)
            usable = code > 0
            shift = code - 1
            moves = shift // 8 + ahead
            taps = spreaded[0:112, :]
            for bit in (1, 2, 4, 8):
                gap = jnp.zeros((8 * bit, LANES), jnp.float32)
                taps = jnp.where(
                    jnp.bitwise_and(moves, bit) > 0,
                    jnp.concatenate([gap, taps], axis=0),
                    jnp.concatenate([taps, gap], axis=0),
                )[0:top]
            channel = base + item
            reach = shift + 8 * ahead
            for index in range(tile_count):
                skip = 8 * offset_count * index
                column = [taps, jnp.zeros((DEPTH - top - skip, LANES), jnp.float32)]
                if skip:
                    column = [jnp.zeros((skip, LANES), jnp.float32)] + column
                lanes = slice(LANES * index, LANES * (index + 1))
                weight_a[channel, :, lanes] = jnp.concatenate(column, axis=0).astype(jnp.bfloat16)
                pick = jnp.logical_and(source_lane == reach + skip, usable)
                pick = jnp.where(pick, 1.0, 0.0).astype(jnp.bfloat16)
                weight_r[channel, 0:LANES, lanes] = pick
                weight_r[channel, LANES : 2 * LANES, lanes] = pick

    total[...] = jnp.zeros_like(total)

    @pl.loop(0, channels // 2)
    def _(pair):
        for channel in (2 * pair, 2 * pair + 1):
            corr = jnp.dot(left_a[channel], weight_a[channel], preferred_element_type=jnp.float32)
            factor = jnp.dot(left_r[channel], weight_r[channel], preferred_element_type=jnp.float32)
            total[...] += corr * factor

    rows_out = outs[0].shape[0]
    for step, out in enumerate(outs):
        segment = jnp.bitwise_xor(scalars[0], step)
        out[...] = total[pl.ds(pl.multiple_of(segment * rows_out, rows_out), rows_out), :].astype(
            jnp.bfloat16
        )


def correlate(channels, tlen, group, samples, scalars, first, second, left_a, left_r):
    rows = left_a.shape[1]
    width = OFFSETS * group
    rows_out = samples // OFFSETS
    out = jax.ShapeDtypeStruct((rows_out, width), jnp.bfloat16)
    banks = 2 * (channels // 2 + 1) * group // LANES
    return pl.pallas_call(
        functools.partial(main_kernel, channels, tlen, group),
        out_shape=[out] * (rows // rows_out),
        in_specs=[SMEM, VMEM, VMEM, VMEM, VMEM],
        out_specs=[VMEM] * (rows // rows_out),
        scratch_shapes=[
            pltpu.VMEM((banks, LANES, LANES), jnp.bfloat16),
            pltpu.VMEM((channels, DEPTH, width), jnp.bfloat16),
            pltpu.VMEM((channels, DEPTH, width), jnp.bfloat16),
            pltpu.VMEM((rows, width), jnp.float32),
        ],
        compiler_params=params(),
        cost_estimate=cost(9),
        name="correlate",
    )(scalars, first, second, left_a, left_r)


def finish_kernel(group, *rest):
    parts, out = rest[:-1], rest[-1]
    samples = out.shape[1]
    rows = parts[0].shape[0]
    value = parts[0][...].astype(jnp.float32)
    for part in parts[1:]:
        value = value + part[...].astype(jnp.float32)
    high = value.astype(jnp.bfloat16).astype(jnp.float32)
    both = jnp.concatenate([high, value - high], axis=0).T.astype(jnp.bfloat16)
    row = lax.broadcasted_iota(jnp.int32, (2 * rows, samples), 0) % rows
    lane = lax.broadcasted_iota(jnp.int32, (2 * rows, samples), 1)
    place = jnp.logical_and(lane // STRIDE == row // 8, lane % 8 == 7 - row % 8)
    place = jnp.where(place, 1.0, 0.0).astype(jnp.bfloat16)
    wide = jnp.dot(both, place, preferred_element_type=jnp.float32)
    lane = lax.broadcasted_iota(jnp.int32, (group, samples), 1) // 8 % OFFSETS
    result = jnp.zeros((group, samples), jnp.float32)
    for offset in range(OFFSETS):
        result = jnp.where(lane == offset, wide[offset * group : (offset + 1) * group], result)
    out[...] = result


def finish(group, samples, parts):
    return pl.pallas_call(
        functools.partial(finish_kernel, group),
        out_shape=jax.ShapeDtypeStruct((group, samples), jnp.float32),
        in_specs=[VMEM] * len(parts),
        out_specs=VMEM,
        compiler_params=params(),
        cost_estimate=cost(1),
        name="finish",
    )(*parts)


def shards(waveforms, templates, available, moveout, bank_blocks):
    channels, samples = waveforms.shape
    blocks, events, _, tlen = templates.shape
    count_tm = lax.axis_size("tm")
    count_sta = lax.axis_size("sta")
    chips = count_tm // 2
    group = 2 * events // chips
    rim = MOVE + tlen - 1
    me = lax.axis_index("tm").astype(jnp.int32)
    station = lax.axis_index("sta").astype(jnp.int32)
    chip, core = me // 2, me % 2
    swap = [(i, i ^ 1) for i in range(count_tm)]

    def across(array, step):
        return lax.ppermute(array, "tm", [(i, i ^ (2 * step)) for i in range(count_tm)])

    owners = bank_blocks // blocks
    slots = bank_blocks % blocks

    next_rim = lax.ppermute(
        waveforms[:, :rim], "tm", [(i, i - 1) for i in range(1, count_tm)]
    )
    tail = jnp.zeros((channels, 2 * LANES - rim), waveforms.dtype)
    segment = jnp.concatenate([waveforms, next_rim, tail], axis=1)
    segments = [segment] + [across(segment, step) for step in range(1, chips)]

    mine, theirs = pack(
        chips,
        group,
        jnp.stack([slots[0], slots[1], core]),
        jnp.transpose(templates, (0, 2, 1, 3)),
        jnp.transpose(available, (2, 0, 1)),
        jnp.transpose(moveout, (2, 0, 1)),
    )
    other = lax.ppermute(theirs, "tm", swap)
    merged = merge(chips, jnp.stack([chip, core, owners[0], owners[1]]), mine, other)
    pieces = [merged[0]] + [across(merged[step], step) for step in range(1, chips)]
    left_a, left_r = prepare_waves(samples, tlen, segments)

    source = (jnp.where(chip < chips // 2, owners[0], owners[1]) // 2) ^ chip
    first = pieces[0]
    for step in range(1, chips):
        first = jnp.where(source == step, pieces[step], first)
    second = lax.ppermute(first, "tm", swap)
    parts = correlate(
        channels, tlen, group, samples, jnp.stack([chip ^ station, core]), first, second, left_a, left_r
    )
    gathered = []
    for step in range(chips):
        route = [
            (d * count_sta + s, (2 * (s ^ step) + d % 2) * count_sta + d // 2)
            for d in range(count_tm)
            for s in range(count_sta)
        ]
        gathered.append(lax.ppermute(parts[step], ("tm", "sta"), route))
    return finish(group, samples, gathered)


def solution(mesh):
    in_specs = (
        P("sta", "tm"),
        P("tm", None, "sta", None),
        P("tm", None, "sta"),
        P("tm", None, "sta"),
        P(),
    )
    out_specs = P("sta", "tm")
    return jax.shard_map(shards, mesh=mesh, in_specs=in_specs, out_specs=out_specs, check_vma=False)
```

```python
import functools

import jax
import jax.numpy as jnp
from jax import lax
from jax.experimental import pallas as pl
from jax.experimental.pallas import tpu as pltpu
from jax.sharding import PartitionSpec as P

EPSILON = 1e-06
LANES = 128
OFFSETS = 8
STRIDE = 64
DEPTH = 256
VMEM_LIMIT = 28 * 1024 * 1024

SMEM = pl.BlockSpec(memory_space=pltpu.SMEM)
VMEM = pl.BlockSpec(memory_space=pltpu.VMEM)
ANY = pl.BlockSpec(memory_space=pl.ANY)
HBM = pl.BlockSpec(memory_space=pltpu.HBM)


def params():
    return pltpu.CompilerParams(vmem_limit_bytes=VMEM_LIMIT)


def cost(micros):
    return pl.CostEstimate(
        flops=int(micros * 1e9), bytes_accessed=int(micros * 1e6), transcendentals=0
    )


def pack_kernel(scalars, templates, available, moveout, mine, theirs, usable, shifts, square, sems, fetched):
    blocks, channels, events, tlen = templates.shape
    chips, _, group, _ = mine.shape
    half = channels // 2
    me = scalars[2]
    flag_copies = [
        pltpu.make_async_copy(available, usable, fetched.at[0]),
        pltpu.make_async_copy(moveout, shifts, fetched.at[1]),
    ]
    for copy in flag_copies:
        copy.start()
    copies = []
    for chip in range(chips):
        which, part = divmod(chip * group, events)
        for side, out in enumerate((mine, theirs)):
            first = half * jnp.where(me == side, 0, 1)
            copy = pltpu.make_async_copy(
                templates.at[scalars[which], pl.ds(first, half), pl.ds(part, group), :],
                out.at[chip, pl.ds(0, half)],
                sems.at[chip, side],
            )
            copy.start()
            copies.append(copy)
    for copy in flag_copies:
        copy.wait()
    flags = jnp.where(usable[...] > 0, shifts[...] + 1, 0).astype(jnp.float32)
    for which in range(2):
        code = flags[:, 0, :]
        for block in range(1, blocks):
            code = jnp.where(scalars[which] == block, flags[:, block, :], code)
        square[...] = jnp.zeros_like(square)
        square[0:channels, 0:events] = code
        turned = square[...].T
        other = pltpu.roll(turned, LANES - half, 1)
        here = jnp.where(me == 0, turned, other)[:, 0:tlen].astype(jnp.bfloat16)
        there = jnp.where(me == 0, other, turned)[:, 0:tlen].astype(jnp.bfloat16)
        for index in range(events // group):
            chip = which * (events // group) + index
            rows = slice(index * group, (index + 1) * group)
            mine[chip, half] = here[rows]
            theirs[chip, half] = there[rows]
    for copy in copies:
        copy.wait()


def pack(chips, group, scalars, templates, available, moveout):
    channels, tlen = templates.shape[1], templates.shape[3]
    shape = (chips, channels // 2 + 1, group, tlen)
    return pl.pallas_call(
        pack_kernel,
        out_shape=[jax.ShapeDtypeStruct(shape, jnp.bfloat16)] * 2,
        in_specs=[SMEM, HBM, HBM, HBM],
        out_specs=[VMEM] * 2,
        scratch_shapes=[
            pltpu.VMEM(available.shape, jnp.int32),
            pltpu.VMEM(moveout.shape, jnp.int32),
            pltpu.VMEM((LANES, LANES), jnp.float32),
            pltpu.SemaphoreType.DMA((chips, 2)),
            pltpu.SemaphoreType.DMA((2,)),
        ],
        compiler_params=params(),
        cost_estimate=cost(1.5),
        name="pack",
    )(scalars, templates, available, moveout)


def merge_kernel(chips, scalars, mine, other, out, sems):
    core = scalars[0]
    for chip in range(chips):
        owner = scalars[1] if chip < chips // 2 else scalars[2]
        here = owner % 2 == core

        @pl.when(here)
        def _():
            pltpu.make_async_copy(mine.at[chip], out.at[chip], sems.at[chip]).start()

        @pl.when(jnp.logical_not(here))
        def _():
            pltpu.make_async_copy(other.at[chip], out.at[chip], sems.at[chip]).start()

    for chip in range(chips):
        pltpu.make_async_copy(mine.at[chip], out.at[chip], sems.at[chip]).wait()


def merge(chips, scalars, mine, other):
    return pl.pallas_call(
        functools.partial(merge_kernel, chips),
        out_shape=jax.ShapeDtypeStruct(mine.shape, mine.dtype),
        in_specs=[SMEM, ANY, ANY],
        out_specs=ANY,
        scratch_shapes=[pltpu.SemaphoreType.DMA((chips,))],
        compiler_params=params(),
        cost_estimate=cost(1),
        name="merge",
    )(scalars, mine, other)


def left(values, count):
    return pltpu.roll(values, values.shape[1] - count, 1)


def window_sums(values):
    sums = {1: values}
    width = 1
    while width < 64:
        sums[2 * width] = sums[width] + left(sums[width], width)
        width *= 2
    return sums[64] + left(sums[32], 64) + left(sums[4], 96)


def lagged(row, ahead):
    copies = jnp.broadcast_to(row, (8, row.shape[1]))
    return pltpu.roll(copies, row.shape[1] - 7 - ahead, 1, stride=1, stride_axis=0)


def waves_kernel(channels, samples, tlen, scalars, rims, *rest):
    waves = rest[:-4]
    left_a, left_r, padded, inverse = rest[-4:]
    chips = len(waves)
    span = padded.shape[1] // chips
    steps = samples // STRIDE
    chip, core = scalars[0], scalars[1]
    padded[...] = jnp.zeros_like(padded)
    for index, wave in enumerate(waves):
        start = span * index
        padded[0:channels, start : start + samples] = wave[...].astype(jnp.float32)
        following = jnp.bitwise_xor(chip, index) + core
        inside = following < chips
        rim = rims[jnp.bitwise_xor(chip, jnp.where(inside, following, chips - 1))]
        rim = jnp.where(inside, rim.astype(jnp.float32), 0.0)
        padded[0:channels, start + samples : start + span] = rim

    @pl.loop(0, 4)
    def _(part):
        rows = pl.ds(pl.multiple_of(part * 8, 8), 8)
        values = padded[rows, :]
        first_sum = window_sums(values)
        second_sum = window_sums(values * values)
        mean = first_sum / tlen
        inverse[rows, :] = lax.rsqrt(second_sum / tlen - mean * mean + EPSILON)

    @pl.loop(0, channels)
    def _(channel):
        row = padded[pl.ds(channel, 1), :]
        scale = inverse[pl.ds(channel, 1), :]
        even, odd = lagged(row, 0), lagged(row, STRIDE)
        even_scale, odd_scale = lagged(scale, 0), lagged(scale, STRIDE)
        columns = ([], [], [])
        for index in range(chips):
            for step in range(steps):
                start = span * index + STRIDE * (step - step % 2)
                values = odd if step % 2 else even
                columns[0].append(values[:, start : start + LANES])
                columns[1].append(values[:, start + LANES : start + 2 * LANES])
                values = odd_scale if step % 2 else even_scale
                columns[2].append(values[:, start : start + LANES])
        left_a[channel, :, 0:LANES] = jnp.concatenate(columns[0], axis=0).astype(jnp.bfloat16)
        left_a[channel, :, LANES:] = jnp.concatenate(columns[1], axis=0).astype(jnp.bfloat16)
        value = jnp.concatenate(columns[2], axis=0)
        high = value.astype(jnp.bfloat16)
        left_r[channel, :, 0:LANES] = high
        left_r[channel, :, LANES:] = (value - high.astype(jnp.float32)).astype(jnp.bfloat16)


def prepare_waves(tlen, scalars, rims, waves):
    channels, samples = waves[0].shape
    span = samples + rims.shape[2]
    rows = len(waves) * samples // OFFSETS
    out = jax.ShapeDtypeStruct((channels, rows, DEPTH), jnp.bfloat16)
    return pl.pallas_call(
        functools.partial(waves_kernel, channels, samples, tlen),
        out_shape=[out, out],
        in_specs=[SMEM, VMEM] + [VMEM] * len(waves),
        out_specs=[VMEM, VMEM],
        scratch_shapes=[
            pltpu.VMEM((32, span * len(waves)), jnp.float32),
            pltpu.VMEM((32, span * len(waves)), jnp.float32),
        ],
        compiler_params=params(),
        cost_estimate=cost(5),
        name="prepare_waves",
    )(scalars, rims, *waves)


def main_kernel(channels, tlen, group, scalars, first, second, left_a, left_r, out, *scratch):
    bank, expand, weight_a, weight_r, total = scratch
    half = channels // 2
    slots = LANES // group
    banks = (half + 1) // slots
    offset_count = LANES // group
    tile_count = OFFSETS // offset_count
    code_lane = (half % slots) * group
    top = 112 + 8 * (7 + offset_count - 1)
    top = top + top % 16

    lag = lax.broadcasted_iota(jnp.int32, (LANES, LANES), 0)
    target = lax.broadcasted_iota(jnp.int32, (LANES, LANES), 1)
    lane = lax.broadcasted_iota(jnp.int32, (1, LANES), 1)
    used = lag < tlen
    for slot in range(slots):
        chosen = jnp.where(lag == target % group + slot * group, 1.0, 0.0)
        expand[:, slot * LANES : (slot + 1) * LANES] = chosen.astype(jnp.bfloat16)
    for side, piece in enumerate((first, second)):
        turned = []
        for index in range(banks):
            values = piece[slots * index : slots * (index + 1)].astype(jnp.float32)
            values = values.reshape(LANES, tlen)
            values = jnp.concatenate([values, jnp.zeros((LANES, LANES - tlen), jnp.float32)], axis=1)
            turned.append(values.T)
        codes = turned[-1]
        for index, values in enumerate(turned):
            code = jnp.zeros((1, LANES), jnp.float32)
            for slot in range(slots):
                item = slots * index + slot
                if item < half:
                    moved = pltpu.roll(
                        codes[item : item + 1, :], (group * slot - code_lane) % LANES, 1
                    )
                    code = jnp.where(lane // group == slot, moved, code)
            center = jnp.sum(jnp.where(used, values, 0.0), axis=0, keepdims=True) / tlen
            deviate = jnp.where(used, values - center, 0.0)
            spread = jnp.sqrt(jnp.sum(deviate * deviate, axis=0, keepdims=True) / tlen + EPSILON)
            unit = (deviate / (spread * tlen)).astype(jnp.bfloat16).astype(jnp.float32)
            unit = jnp.where(code > 0, unit, 0.0)
            shift = code.astype(jnp.int32) - 1
            for bit in (1, 2, 4):
                unit = jnp.where(jnp.bitwise_and(shift, bit) > 0, pltpu.roll(unit, bit, 0), unit)
            unit = jnp.where(lag == 112, code, unit)
            bank[side * banks + index] = unit.astype(jnp.bfloat16)

    ahead = lane // group

    def channel_of(number, slot):
        side = number // banks
        item = (number % banks) * slots + slot
        base = half * jnp.where(scalars[1] == side, 0, 1)
        return jnp.where(item < half, base + item, channels + side)

    def build(number):
        wide = jnp.dot(bank[number], expand[...], preferred_element_type=jnp.float32)
        for slot in range(slots):
            spreaded = wide[:, slot * LANES : (slot + 1) * LANES]
            code = spreaded[112:113, :].astype(jnp.int32)
            usable = code > 0
            shift = code - 1
            moves = shift // 8 + ahead
            taps = spreaded[0:112, :]
            for bit in (1, 2, 4, 8):
                gap = jnp.zeros((8 * bit, LANES), jnp.float32)
                taps = jnp.where(
                    jnp.bitwise_and(moves, bit) > 0,
                    jnp.concatenate([gap, taps], axis=0),
                    jnp.concatenate([taps, gap], axis=0),
                )[0:top]
            taps = taps.astype(jnp.bfloat16)
            channel = channel_of(number, slot)
            pick = jnp.logical_and(lag == shift + 8 * ahead, usable)
            pick = jnp.where(pick, 1.0, 0.0).astype(jnp.bfloat16)
            for index in range(tile_count):
                skip = 8 * offset_count * index
                lanes = slice(LANES * index, LANES * (index + 1))
                if skip:
                    weight_a[channel, 0:skip, lanes] = jnp.zeros((skip, LANES), jnp.bfloat16)
                    pick = jnp.concatenate(
                        [jnp.zeros((skip, LANES), jnp.bfloat16), pick[0 : LANES - skip]], axis=0
                    )
                weight_a[channel, skip : skip + top, lanes] = taps
                rest = DEPTH - top - skip
                if rest:
                    weight_a[channel, skip + top :, lanes] = jnp.zeros((rest, LANES), jnp.bfloat16)
                weight_r[channel, 0:LANES, lanes] = pick
                weight_r[channel, LANES : 2 * LANES, lanes] = pick

    def apply(number):
        for slot in range(slots):
            channel = channel_of(number, slot)
            samples = jnp.minimum(channel, channels - 1)
            corr = jnp.dot(left_a[samples], weight_a[channel], preferred_element_type=jnp.float32)
            factor = jnp.dot(left_r[samples], weight_r[channel], preferred_element_type=jnp.float32)
            total[...] += corr * factor

    total[...] = jnp.zeros_like(total)
    build(0)

    @pl.loop(1, 2 * banks)
    def _(number):
        apply(number - 1)
        build(number)

    apply(2 * banks - 1)

    rows_out = out.shape[1]
    for chip in range(out.shape[0]):
        segment = jnp.bitwise_xor(scalars[0], chip)
        out[chip] = total[pl.ds(pl.multiple_of(segment * rows_out, rows_out), rows_out), :].astype(
            jnp.bfloat16
        )


def correlate(channels, tlen, group, samples, scalars, first, second, left_a, left_r):
    rows = left_a.shape[1]
    width = OFFSETS * group
    rows_out = samples // OFFSETS
    banks = 2 * (channels // 2 + 1) * group // LANES
    return pl.pallas_call(
        functools.partial(main_kernel, channels, tlen, group),
        out_shape=jax.ShapeDtypeStruct((rows // rows_out, rows_out, width), jnp.bfloat16),
        in_specs=[SMEM, VMEM, VMEM, VMEM, VMEM],
        out_specs=VMEM,
        scratch_shapes=[
            pltpu.VMEM((banks, LANES, LANES), jnp.bfloat16),
            pltpu.VMEM((LANES, LANES // group * LANES), jnp.bfloat16),
            pltpu.VMEM((channels + 2, DEPTH, width), jnp.bfloat16),
            pltpu.VMEM((channels + 2, DEPTH, width), jnp.bfloat16),
            pltpu.VMEM((rows, width), jnp.float32),
        ],
        compiler_params=params(),
        cost_estimate=cost(9),
        name="correlate",
    )(scalars, first, second, left_a, left_r)


def finish_kernel(group, parts, out):
    samples = out.shape[1]
    count, rows, _ = parts.shape
    value = parts[0].astype(jnp.float32)
    for index in range(1, count):
        value = value + parts[index].astype(jnp.float32)
    high = value.astype(jnp.bfloat16).astype(jnp.float32)
    both = jnp.concatenate([high, value - high], axis=0).T.astype(jnp.bfloat16)
    row = lax.broadcasted_iota(jnp.int32, (2 * rows, samples), 0) % rows
    lane = lax.broadcasted_iota(jnp.int32, (2 * rows, samples), 1)
    place = jnp.logical_and(lane // STRIDE == row // 8, lane % 8 == 7 - row % 8)
    place = jnp.where(place, 1.0, 0.0).astype(jnp.bfloat16)
    wide = jnp.dot(both, place, preferred_element_type=jnp.float32)
    lane = lax.broadcasted_iota(jnp.int32, (group, samples), 1) // 8 % OFFSETS
    result = jnp.zeros((group, samples), jnp.float32)
    for offset in range(OFFSETS):
        result = jnp.where(lane == offset, wide[offset * group : (offset + 1) * group], result)
    out[...] = result


def finish(group, samples, parts):
    return pl.pallas_call(
        functools.partial(finish_kernel, group),
        out_shape=jax.ShapeDtypeStruct((group, samples), jnp.float32),
        in_specs=[VMEM],
        out_specs=VMEM,
        compiler_params=params(),
        cost_estimate=cost(1),
        name="finish",
    )(parts)


def shards(waveforms, templates, available, moveout, bank_blocks):
    channels, samples = waveforms.shape
    blocks, events, _, tlen = templates.shape
    count_tm = lax.axis_size("tm")
    chips = count_tm // 2
    group = 2 * events // chips
    me = lax.axis_index("tm").astype(jnp.int32)
    chip, core = me // 2, me % 2
    swap = [(i, i ^ 1) for i in range(count_tm)]

    def across(array, step):
        return lax.ppermute(array, "tm", [(i, i ^ (2 * step)) for i in range(count_tm)])

    owners = bank_blocks // blocks
    slots = bank_blocks % blocks

    segments = [waveforms] + [across(waveforms, step) for step in range(1, chips)]
    mine, theirs = pack(
        chips,
        group,
        jnp.stack([slots[0], slots[1], core]),
        jnp.transpose(templates, (0, 2, 1, 3)),
        jnp.transpose(available, (2, 0, 1)),
        jnp.transpose(moveout, (2, 0, 1)),
    )
    other = lax.ppermute(theirs, "tm", swap)
    rims = lax.ppermute(jnp.stack([s[:, : 2 * LANES] for s in segments]), "tm", swap)
    other, rims, *segments = lax.optimization_barrier((other, rims, *segments))
    merged = merge(chips, jnp.stack([core, owners[0], owners[1]]), mine, other)
    lines = [[2 * z + c for z in range(chips)] for c in range(2)]
    pieces = lax.all_to_all(merged, "tm", 0, 0, axis_index_groups=lines, tiled=True)
    left_a, left_r = prepare_waves(tlen, jnp.stack([chip, core]), rims, segments)

    source = jnp.where(chip < chips // 2, owners[0], owners[1]) // 2
    first = lax.dynamic_index_in_dim(pieces, source, 0, keepdims=False)
    second = lax.ppermute(first, "tm", swap)
    parts = correlate(
        channels, tlen, group, samples, jnp.stack([chip, core]), first, second, left_a, left_r
    )
    parts = lax.all_to_all(parts, "tm", 0, 0, axis_index_groups=lines, tiled=True)
    parts = lax.all_to_all(parts, "sta", 0, 0, tiled=True)
    return finish(group, samples, parts)


def solution(mesh):
    in_specs = (
        P("sta", "tm"),
        P("tm", None, "sta", None),
        P("tm", None, "sta"),
        P("tm", None, "sta"),
        P(),
    )
    out_specs = P("sta", "tm")
    return jax.shard_map(shards, mesh=mesh, in_specs=in_specs, out_specs=out_specs, check_vma=False)
```

```python
import functools

import jax
import jax.numpy as jnp
from jax import lax
from jax.experimental import pallas as pl
from jax.experimental.pallas import tpu as pltpu
from jax.sharding import PartitionSpec as P

EPSILON = 1e-06
LANES = 128
OFFSETS = 8
STRIDE = 64
DEPTH = 256
VMEM_LIMIT = 28 * 1024 * 1024

SMEM = pl.BlockSpec(memory_space=pltpu.SMEM)
VMEM = pl.BlockSpec(memory_space=pltpu.VMEM)
ANY = pl.BlockSpec(memory_space=pl.ANY)


def params():
    return pltpu.CompilerParams(vmem_limit_bytes=VMEM_LIMIT)


def cost(micros):
    return pl.CostEstimate(
        flops=int(micros * 1e9), bytes_accessed=int(micros * 1e6), transcendentals=0
    )


def pack_kernel(bank_blocks, templates, available, moveout, mine, theirs, usable, shifts, square, codes, sems, fetched):
    blocks, channels, events, tlen = templates.shape
    chips, _, group, _ = mine.shape
    half = channels // 2
    me = lax.axis_index("tm") % 2
    slots = [bank_blocks[which] % blocks for which in range(2)]
    flag_copies = [
        pltpu.make_async_copy(available, usable, fetched.at[0]),
        pltpu.make_async_copy(moveout, shifts, fetched.at[1]),
    ]
    for copy in flag_copies:
        copy.start()
    copies = []
    for chip in range(chips):
        which, part = divmod(chip * group, events)
        for side, out in enumerate((theirs, mine)):
            first = half * jnp.where(me == 1 - side, 0, 1)
            copy = pltpu.make_async_copy(
                templates.at[slots[which], pl.ds(first, half), pl.ds(part, group), :],
                out.at[chip, pl.ds(0, half)],
                sems.at[chip, side],
            )
            copy.start()
            copies.append(copy)
    for copy in flag_copies:
        copy.wait()
    flags = jnp.where(usable[...] > 0, shifts[...] + 1, 0).astype(jnp.float32)
    for which in range(2):
        code = flags[:, 0, :]
        for block in range(1, blocks):
            code = jnp.where(slots[which] == block, flags[:, block, :], code)
        square[...] = jnp.zeros_like(square)
        square[0:channels, 0:events] = code
        turned = square[...].T
        other = pltpu.roll(turned, LANES - half, 1)
        here = jnp.where(me == 0, turned, other)[:, 0:tlen].astype(jnp.bfloat16)
        there = jnp.where(me == 0, other, turned)[:, 0:tlen].astype(jnp.bfloat16)
        for index in range(events // group):
            chip = which * (events // group) + index
            rows = slice(index * group, (index + 1) * group)
            codes[0, chip, 0] = there[rows]
            codes[1, chip, 0] = here[rows]
    for side, out in enumerate((theirs, mine)):
        copy = pltpu.make_async_copy(
            codes.at[side], out.at[pl.ds(0, chips), pl.ds(half, 1)], fetched.at[side]
        )
        copy.start()
        copies.append(copy)
    for copy in copies:
        copy.wait()


def pack(chips, group, bank_blocks, templates, available, moveout):
    channels, tlen = templates.shape[1], templates.shape[3]
    shape = (chips, channels // 2 + 1, group, tlen)
    return pl.pallas_call(
        pack_kernel,
        out_shape=[jax.ShapeDtypeStruct(shape, jnp.bfloat16)] * 2,
        in_specs=[SMEM, ANY, ANY, ANY],
        out_specs=[ANY] * 2,
        scratch_shapes=[
            pltpu.VMEM(available.shape, jnp.int32),
            pltpu.VMEM(moveout.shape, jnp.int32),
            pltpu.VMEM((LANES, LANES), jnp.float32),
            pltpu.VMEM((2, chips, 1, group, tlen), jnp.bfloat16),
            pltpu.SemaphoreType.DMA((chips, 2)),
            pltpu.SemaphoreType.DMA((2,)),
        ],
        cost_estimate=cost(1.5),
        name="pack",
    )(bank_blocks, templates, available, moveout)


def merge_kernel(blocks, bank_blocks, mine, other, *outs):
    chips = len(outs)
    me = lax.axis_index("tm")
    for step, out in enumerate(outs):
        dest = jnp.bitwise_xor(me // 2, step)
        owner = jnp.where(dest < chips // 2, bank_blocks[0], bank_blocks[1]) // blocks
        here = owner % 2 == me % 2

        @pl.when(here)
        def _():
            out[...] = mine[dest]

        @pl.when(jnp.logical_not(here))
        def _():
            out[...] = other[dest]


def merge(blocks, bank_blocks, mine, other):
    chips = mine.shape[0]
    return pl.pallas_call(
        functools.partial(merge_kernel, blocks),
        out_shape=[jax.ShapeDtypeStruct(mine.shape[1:], mine.dtype)] * chips,
        in_specs=[SMEM, VMEM, VMEM],
        out_specs=[VMEM] * chips,
        compiler_params=params(),
        cost_estimate=cost(1),
        name="merge",
    )(bank_blocks, mine, other)


def left(values, count):
    return pltpu.roll(values, values.shape[1] - count, 1)


def window_sums(values):
    sums = {1: values}
    width = 1
    while width < 64:
        sums[2 * width] = sums[width] + left(sums[width], width)
        width *= 2
    return sums[64] + left(sums[32], 64) + left(sums[4], 96)


def lagged(row, ahead):
    copies = jnp.broadcast_to(row, (8, row.shape[1]))
    return pltpu.roll(copies, row.shape[1] - 7 - ahead, 1, stride=1, stride_axis=0)


def waves_kernel(channels, tlen, swapped, local, left_a, left_r, padded, inverse):
    chips, _, samples = local.shape
    near = chips // 2
    steps = 2 * near * samples // STRIDE
    me = lax.axis_index("tm")
    chip, core = me // 2, me % 2
    padded[...] = jnp.zeros_like(padded)
    for index in range(2 * near):
        source = jnp.bitwise_xor(chip, near * core + index // 2)
        wave = jnp.where(core == index % 2, local[source], swapped[index // 2])
        padded[0:channels, samples * index : samples * (index + 1)] = wave.astype(jnp.float32)
    rim = local[jnp.bitwise_xor(chip, near)][:, 0 : padded.shape[1] - 2 * near * samples]
    rim = jnp.where(core == 0, rim.astype(jnp.float32), 0.0)
    padded[0:channels, 2 * near * samples :] = rim

    @pl.loop(0, 4)
    def _(part):
        rows = pl.ds(pl.multiple_of(part * 8, 8), 8)
        values = padded[rows, :]
        first_sum = window_sums(values)
        second_sum = window_sums(values * values)
        mean = first_sum / tlen
        inverse[rows, :] = lax.rsqrt(second_sum / tlen - mean * mean + EPSILON)

    @pl.loop(0, channels)
    def _(channel):
        row = padded[pl.ds(channel, 1), :]
        scale = inverse[pl.ds(channel, 1), :]
        even, odd = lagged(row, 0), lagged(row, STRIDE)
        even_scale, odd_scale = lagged(scale, 0), lagged(scale, STRIDE)
        columns = ([], [], [])
        for step in range(steps):
            start = STRIDE * (step - step % 2)
            values = odd if step % 2 else even
            columns[0].append(values[:, start : start + LANES])
            columns[1].append(values[:, start + LANES : start + 2 * LANES])
            values = odd_scale if step % 2 else even_scale
            columns[2].append(values[:, start : start + LANES])
        left_a[channel, :, 0:LANES] = jnp.concatenate(columns[0], axis=0).astype(jnp.bfloat16)
        left_a[channel, :, LANES:] = jnp.concatenate(columns[1], axis=0).astype(jnp.bfloat16)
        value = jnp.concatenate(columns[2], axis=0)
        high = value.astype(jnp.bfloat16)
        left_r[channel, :, 0:LANES] = high
        left_r[channel, :, LANES:] = (value - high.astype(jnp.float32)).astype(jnp.bfloat16)


def prepare_waves(tlen, swapped, local):
    chips, channels, samples = local.shape
    length = chips * samples
    out = jax.ShapeDtypeStruct((channels, length // OFFSETS, DEPTH), jnp.bfloat16)
    return pl.pallas_call(
        functools.partial(waves_kernel, channels, tlen),
        out_shape=[out, out],
        in_specs=[VMEM, VMEM],
        out_specs=[VMEM, VMEM],
        scratch_shapes=[
            pltpu.VMEM((32, length + 2 * LANES), jnp.float32),
            pltpu.VMEM((32, length + 2 * LANES), jnp.float32),
        ],
        compiler_params=params(),
        cost_estimate=cost(7),
        name="prepare_waves",
    )(swapped, local)


def main_kernel(channels, tlen, group, first, second, left_a, left_r, *rest):
    outs = rest[:-5]
    bank, expand, weight_a, weight_r, total = rest[-5:]
    core = lax.axis_index("tm") % 2
    half = channels // 2
    slots = LANES // group
    banks = (half + 1) // slots
    offset_count = LANES // group
    tile_count = OFFSETS // offset_count
    code_lane = (half % slots) * group
    top = 112 + 8 * (7 + offset_count - 1)
    top = top + top % 16

    lag = lax.broadcasted_iota(jnp.int32, (LANES, LANES), 0)
    target = lax.broadcasted_iota(jnp.int32, (LANES, LANES), 1)
    lane = lax.broadcasted_iota(jnp.int32, (1, LANES), 1)
    used = lag < tlen
    for slot in range(slots):
        chosen = jnp.where(lag == target % group + slot * group, 1.0, 0.0)
        expand[:, slot * LANES : (slot + 1) * LANES] = chosen.astype(jnp.bfloat16)
    for side, piece in enumerate((first, second)):
        turned = []
        for index in range(banks):
            values = piece[slots * index : slots * (index + 1)].astype(jnp.float32)
            values = values.reshape(LANES, tlen)
            values = jnp.concatenate([values, jnp.zeros((LANES, LANES - tlen), jnp.float32)], axis=1)
            turned.append(values.T)
        codes = turned[-1]
        for index, values in enumerate(turned):
            code = jnp.zeros((1, LANES), jnp.float32)
            for slot in range(slots):
                item = slots * index + slot
                if item < half:
                    moved = pltpu.roll(
                        codes[item : item + 1, :], (group * slot - code_lane) % LANES, 1
                    )
                    code = jnp.where(lane // group == slot, moved, code)
            center = jnp.sum(jnp.where(used, values, 0.0), axis=0, keepdims=True) / tlen
            deviate = jnp.where(used, values - center, 0.0)
            spread = jnp.sqrt(jnp.sum(deviate * deviate, axis=0, keepdims=True) / tlen + EPSILON)
            unit = (deviate / (spread * tlen)).astype(jnp.bfloat16).astype(jnp.float32)
            unit = jnp.where(code > 0, unit, 0.0)
            shift = code.astype(jnp.int32) - 1
            for bit in (1, 2, 4):
                unit = jnp.where(jnp.bitwise_and(shift, bit) > 0, pltpu.roll(unit, bit, 0), unit)
            unit = jnp.where(lag == 112, code, unit)
            bank[side * banks + index] = unit.astype(jnp.bfloat16)

    ahead = lane // group

    def channel_of(number, slot):
        side = number // banks
        item = (number % banks) * slots + slot
        base = half * jnp.where(core == side, 0, 1)
        return jnp.where(item < half, base + item, channels + side)

    def build(number):
        wide = jnp.dot(bank[number], expand[...], preferred_element_type=jnp.float32)
        for slot in range(slots):
            spreaded = wide[:, slot * LANES : (slot + 1) * LANES]
            code = spreaded[112:113, :].astype(jnp.int32)
            usable = code > 0
            shift = code - 1
            moves = shift // 8 + ahead
            taps = spreaded[0:112, :]
            for bit in (1, 2, 4, 8):
                gap = jnp.zeros((8 * bit, LANES), jnp.float32)
                taps = jnp.where(
                    jnp.bitwise_and(moves, bit) > 0,
                    jnp.concatenate([gap, taps], axis=0),
                    jnp.concatenate([taps, gap], axis=0),
                )[0:top]
            taps = taps.astype(jnp.bfloat16)
            channel = channel_of(number, slot)
            pick = jnp.logical_and(lag == shift + 8 * ahead, usable)
            pick = jnp.where(pick, 1.0, 0.0).astype(jnp.bfloat16)
            for index in range(tile_count):
                skip = 8 * offset_count * index
                lanes = slice(LANES * index, LANES * (index + 1))
                if skip:
                    weight_a[channel, 0:skip, lanes] = jnp.zeros((skip, LANES), jnp.bfloat16)
                    pick = jnp.concatenate(
                        [jnp.zeros((skip, LANES), jnp.bfloat16), pick[0 : LANES - skip]], axis=0
                    )
                weight_a[channel, skip : skip + top, lanes] = taps
                rest = DEPTH - top - skip
                if rest:
                    weight_a[channel, skip + top :, lanes] = jnp.zeros((rest, LANES), jnp.bfloat16)
                weight_r[channel, 0:LANES, lanes] = pick
                weight_r[channel, LANES : 2 * LANES, lanes] = pick

    def apply(number):
        for slot in range(slots):
            channel = channel_of(number, slot)
            samples = jnp.minimum(channel, channels - 1)
            corr = jnp.dot(left_a[samples], weight_a[channel], preferred_element_type=jnp.float32)
            factor = jnp.dot(left_r[samples], weight_r[channel], preferred_element_type=jnp.float32)
            total[...] += corr * factor

    total[...] = jnp.zeros_like(total)
    build(0)

    @pl.loop(1, 2 * banks)
    def _(number):
        apply(number - 1)
        build(number)

    apply(2 * banks - 1)

    rows_out = outs[0].shape[0]
    station = lax.axis_index("sta") % len(outs)
    for step, out in enumerate(outs):
        part = jnp.bitwise_xor(station, step)
        out[...] = total[pl.ds(pl.multiple_of(part * rows_out, rows_out), rows_out), :].astype(
            jnp.bfloat16
        )


def correlate(channels, tlen, group, count, first, second, left_a, left_r):
    rows = left_a.shape[1]
    width = OFFSETS * group
    banks = 2 * (channels // 2 + 1) * group // LANES
    return pl.pallas_call(
        functools.partial(main_kernel, channels, tlen, group),
        out_shape=[jax.ShapeDtypeStruct((rows // count, width), jnp.bfloat16)] * count,
        in_specs=[VMEM, VMEM, VMEM, VMEM],
        out_specs=[VMEM] * count,
        scratch_shapes=[
            pltpu.VMEM((banks, LANES, LANES), jnp.bfloat16),
            pltpu.VMEM((LANES, LANES // group * LANES), jnp.bfloat16),
            pltpu.VMEM((channels + 2, DEPTH, width), jnp.bfloat16),
            pltpu.VMEM((channels + 2, DEPTH, width), jnp.bfloat16),
            pltpu.VMEM((rows, width), jnp.float32),
        ],
        compiler_params=params(),
        cost_estimate=cost(6),
        name="correlate",
    )(first, second, left_a, left_r)


def add_kernel(*refs):
    parts, keep, send = refs[:-2], refs[-2], refs[-1]
    rows = keep.shape[0]
    core = lax.axis_index("tm") % 2
    for out, which in ((keep, core), (send, 1 - core)):
        place = pl.ds(pl.multiple_of(which * rows, rows), rows)
        value = parts[0][place, :].astype(jnp.float32)
        for part in parts[1:]:
            value = value + part[place, :].astype(jnp.float32)
        out[...] = value


def add(parts):
    rows, width = parts[0].shape
    out = jax.ShapeDtypeStruct((rows // 2, width), jnp.float32)
    return pl.pallas_call(
        add_kernel,
        out_shape=[out, out],
        in_specs=[VMEM] * len(parts),
        out_specs=[VMEM, VMEM],
        compiler_params=params(),
        cost_estimate=cost(0.5),
        name="add",
    )(*parts)


def finish_kernel(group, ours, received, out):
    samples = out.shape[1]
    rows = ours.shape[0]
    value = ours[...] + received[...]
    high = value.astype(jnp.bfloat16).astype(jnp.float32)
    both = jnp.concatenate([high, value - high], axis=0).T.astype(jnp.bfloat16)
    row = lax.broadcasted_iota(jnp.int32, (2 * rows, samples), 0) % rows
    lane = lax.broadcasted_iota(jnp.int32, (2 * rows, samples), 1)
    place = jnp.logical_and(lane // STRIDE == row // 8, lane % 8 == 7 - row % 8)
    place = jnp.where(place, 1.0, 0.0).astype(jnp.bfloat16)
    wide = jnp.dot(both, place, preferred_element_type=jnp.float32)
    lane = lax.broadcasted_iota(jnp.int32, (group, samples), 1) // 8 % OFFSETS
    result = jnp.zeros((group, samples), jnp.float32)
    for offset in range(OFFSETS):
        result = jnp.where(lane == offset, wide[offset * group : (offset + 1) * group], result)
    out[...] = result


def finish(group, samples, ours, received):
    return pl.pallas_call(
        functools.partial(finish_kernel, group),
        out_shape=jax.ShapeDtypeStruct((group, samples), jnp.float32),
        in_specs=[VMEM, VMEM],
        out_specs=VMEM,
        compiler_params=params(),
        cost_estimate=cost(1),
        name="finish",
    )(ours, received)


def shards(waveforms, templates, available, moveout, bank_blocks):
    channels, samples = waveforms.shape
    blocks, events, _, tlen = templates.shape
    count_tm = lax.axis_size("tm")
    count_sta = lax.axis_size("sta")
    chips = count_tm // 2
    near = chips // 2
    group = 2 * events // chips
    me = lax.axis_index("tm").astype(jnp.int32)
    chip, core = me // 2, me % 2

    def swap(array):
        return lax.ppermute(array, "tm", [(i, i ^ 1) for i in range(count_tm)])

    def across(array, step):
        return lax.ppermute(array, "tm", [(i, i ^ (2 * step)) for i in range(count_tm)])

    mine, theirs = pack(
        chips,
        group,
        bank_blocks,
        jnp.transpose(templates, (0, 2, 1, 3)),
        jnp.transpose(available, (2, 0, 1)),
        jnp.transpose(moveout, (2, 0, 1)),
    )
    other = swap(theirs)
    waveforms, mine = lax.optimization_barrier((waveforms, mine))
    local = jnp.stack([waveforms] + [across(waveforms, step) for step in range(1, chips)])
    other, local = lax.optimization_barrier((other, local))
    merged = merge(blocks, bank_blocks, mine, other)
    pieces = [merged[0]] + [across(merged[step], step) for step in range(1, chips)]

    wanted = [
        lax.dynamic_index_in_dim(local, chip ^ (near * (1 - core) + step), 0, keepdims=False)
        for step in range(near)
    ]
    swapped = swap(jnp.stack(wanted))
    left_a, left_r = prepare_waves(tlen, swapped, local)

    left_a, left_r, *pieces = lax.optimization_barrier((left_a, left_r, *pieces))
    owner = jnp.where(chip < near, bank_blocks[0], bank_blocks[1]) // blocks
    source = (owner // 2) ^ chip
    first = pieces[0]
    for step in range(1, chips):
        first = jnp.where(source == step, pieces[step], first)
    second = swap(first)
    parts = correlate(channels, tlen, group, near, first, second, left_a, left_r)
    gathered = []
    for step in range(near):
        route = []
        for d in range(count_tm):
            for s in range(count_sta):
                dest = near * (d % 2) + (s % near ^ step)
                route.append((d * count_sta + s, (2 * dest + s // near) * count_sta + d // 2))
        gathered.append(lax.ppermute(parts[step], ("tm", "sta"), route))
    ours, send = add(gathered)
    return finish(group, samples, ours, swap(send))


def solution(mesh):
    in_specs = (
        P("sta", "tm"),
        P("tm", None, "sta", None),
        P("tm", None, "sta"),
        P("tm", None, "sta"),
        P(),
    )
    out_specs = P("sta", "tm")
    return jax.shard_map(shards, mesh=mesh, in_specs=in_specs, out_specs=out_specs, check_vma=False)
```

```python
import functools

import jax
import jax.numpy as jnp
from jax import lax
from jax.experimental import pallas as pl
from jax.experimental.pallas import tpu as pltpu
from jax.sharding import PartitionSpec as P

EPSILON = 1e-06
LANES = 128
OFFSETS = 8
STRIDE = 64
DEPTH = 256
VMEM_LIMIT = 28 * 1024 * 1024

SMEM = pl.BlockSpec(memory_space=pltpu.SMEM)
VMEM = pl.BlockSpec(memory_space=pltpu.VMEM)
ANY = pl.BlockSpec(memory_space=pl.ANY)


def params():
    return pltpu.CompilerParams(vmem_limit_bytes=VMEM_LIMIT)


def cost(micros):
    return pl.CostEstimate(
        flops=int(micros * 1e9), bytes_accessed=int(micros * 1e6), transcendentals=0
    )


def pack_kernel(bank_blocks, templates, available, moveout, mine, theirs, usable, shifts, square, sems, fetched):
    blocks, channels, events, tlen = templates.shape
    chips, _, group, _ = mine.shape
    half = channels // 2
    me = lax.axis_index("tm") % 2
    station = lax.axis_index("sta")
    slots = [bank_blocks[which] % blocks for which in range(2)]
    flag_copies = [
        pltpu.make_async_copy(available, usable, fetched.at[0]),
        pltpu.make_async_copy(moveout, shifts, fetched.at[1]),
    ]
    for copy in flag_copies:
        copy.start()
    copies = []
    for index in range(chips):
        which, part = divmod(index * group, events)
        chip = jnp.bitwise_xor(station, index)
        for side, out in enumerate((theirs, mine)):
            first = half * jnp.where(me == 1 - side, 0, 1)
            copy = pltpu.make_async_copy(
                templates.at[slots[which], pl.ds(first, half), pl.ds(part, group), :],
                out.at[chip, pl.ds(0, half)],
                sems.at[index, side],
            )
            copy.start()
            copies.append(copy)
    for copy in flag_copies:
        copy.wait()
    flags = jnp.where(usable[...] > 0, shifts[...] + 1, 0).astype(jnp.float32)
    for which in range(2):
        code = flags[:, 0, :]
        for block in range(1, blocks):
            code = jnp.where(slots[which] == block, flags[:, block, :], code)
        square[...] = jnp.zeros_like(square)
        square[0:channels, 0:events] = code
        turned = square[...].T
        other = pltpu.roll(turned, LANES - half, 1)
        here = jnp.where(me == 0, turned, other)[:, 0:tlen].astype(jnp.bfloat16)
        there = jnp.where(me == 0, other, turned)[:, 0:tlen].astype(jnp.bfloat16)
        for index in range(events // group):
            chip = jnp.bitwise_xor(station, which * (events // group) + index)
            rows = slice(index * group, (index + 1) * group)
            mine[chip, half] = here[rows]
            theirs[chip, half] = there[rows]
    for copy in copies:
        copy.wait()


def pack(chips, group, bank_blocks, templates, available, moveout):
    channels, tlen = templates.shape[1], templates.shape[3]
    shape = (chips, channels // 2 + 1, group, tlen)
    held = [
        pltpu.with_memory_space_constraint(array, pltpu.HBM)
        for array in (templates, available, moveout)
    ]
    return pl.pallas_call(
        pack_kernel,
        out_shape=[jax.ShapeDtypeStruct(shape, jnp.bfloat16)] * 2,
        in_specs=[SMEM, ANY, ANY, ANY],
        out_specs=[VMEM] * 2,
        scratch_shapes=[
            pltpu.VMEM(available.shape, jnp.int32),
            pltpu.VMEM(moveout.shape, jnp.int32),
            pltpu.VMEM((LANES, LANES), jnp.float32),
            pltpu.SemaphoreType.DMA((chips, 2)),
            pltpu.SemaphoreType.DMA((2,)),
        ],
        compiler_params=params(),
        cost_estimate=cost(1.5),
        name="pack",
    )(bank_blocks, *held)


def merge_kernel(blocks, bank_blocks, mine, other, *outs):
    chips = len(outs)
    me = lax.axis_index("tm")
    station = lax.axis_index("sta")
    for step, out in enumerate(outs):
        dest = jnp.bitwise_xor(me // 2, step)
        first = jnp.bitwise_xor(dest, station) < chips // 2
        owner = jnp.where(first, bank_blocks[0], bank_blocks[1]) // blocks
        here = owner % 2 == me % 2

        @pl.when(here)
        def _():
            out[...] = mine[dest]

        @pl.when(jnp.logical_not(here))
        def _():
            out[...] = other[dest]


def merge(blocks, bank_blocks, mine, other):
    chips = mine.shape[0]
    return pl.pallas_call(
        functools.partial(merge_kernel, blocks),
        out_shape=[jax.ShapeDtypeStruct(mine.shape[1:], mine.dtype)] * chips,
        in_specs=[SMEM, VMEM, VMEM],
        out_specs=[VMEM] * chips,
        compiler_params=params(),
        cost_estimate=cost(1),
        name="merge",
    )(bank_blocks, mine, other)


def left(values, count):
    return pltpu.roll(values, values.shape[1] - count, 1)


def window_sums(values):
    sums = {1: values}
    width = 1
    while width < 64:
        sums[2 * width] = sums[width] + left(sums[width], width)
        width *= 2
    return sums[64] + left(sums[32], 64) + left(sums[4], 96)


def lagged(row, ahead):
    copies = jnp.broadcast_to(row, (8, row.shape[1]))
    return pltpu.roll(copies, row.shape[1] - 7 - ahead, 1, stride=1, stride_axis=0)


def waves_kernel(channels, tlen, rim, local, left_a, left_r, padded, inverse):
    chips, _, _, samples = local.shape
    near = chips // 2
    length = chips * samples
    steps = length // STRIDE
    me = lax.axis_index("tm")
    chip, core = me // 2, me % 2
    padded[...] = jnp.zeros_like(padded)
    for index in range(chips):
        source = jnp.bitwise_xor(chip, near * core + index // 2)
        wave = local[source, index % 2].astype(jnp.float32)
        padded[0:channels, samples * index : samples * (index + 1)] = wave
    padded[0:channels, length:] = rim[...].astype(jnp.float32)

    @pl.loop(0, 4)
    def _(part):
        rows = pl.ds(pl.multiple_of(part * 8, 8), 8)
        values = padded[rows, :]
        first_sum = window_sums(values)
        second_sum = window_sums(values * values)
        mean = first_sum / tlen
        inverse[rows, :] = lax.rsqrt(second_sum / tlen - mean * mean + EPSILON)

    @pl.loop(0, channels)
    def _(channel):
        row = padded[pl.ds(channel, 1), :]
        scale = inverse[pl.ds(channel, 1), :]
        even, odd = lagged(row, 0), lagged(row, STRIDE)
        even_scale, odd_scale = lagged(scale, 0), lagged(scale, STRIDE)
        columns = ([], [], [])
        for step in range(steps):
            start = STRIDE * (step - step % 2)
            values = odd if step % 2 else even
            columns[0].append(values[:, start : start + LANES])
            columns[1].append(values[:, start + LANES : start + 2 * LANES])
            values = odd_scale if step % 2 else even_scale
            columns[2].append(values[:, start : start + LANES])
        left_a[channel, :, 0:LANES] = jnp.concatenate(columns[0], axis=0).astype(jnp.bfloat16)
        left_a[channel, :, LANES:] = jnp.concatenate(columns[1], axis=0).astype(jnp.bfloat16)
        value = jnp.concatenate(columns[2], axis=0)
        high = value.astype(jnp.bfloat16)
        left_r[channel, :, 0:LANES] = high
        left_r[channel, :, LANES:] = (value - high.astype(jnp.float32)).astype(jnp.bfloat16)


def prepare_waves(tlen, rim, local):
    chips, _, channels, samples = local.shape
    length = chips * samples
    out = jax.ShapeDtypeStruct((channels, length // OFFSETS, DEPTH), jnp.bfloat16)
    return pl.pallas_call(
        functools.partial(waves_kernel, channels, tlen),
        out_shape=[out, out],
        in_specs=[VMEM, VMEM],
        out_specs=[VMEM, VMEM],
        scratch_shapes=[
            pltpu.VMEM((32, length + 2 * LANES), jnp.float32),
            pltpu.VMEM((32, length + 2 * LANES), jnp.float32),
        ],
        compiler_params=params(),
        cost_estimate=cost(7),
        name="prepare_waves",
    )(rim, local)


def main_kernel(side, tlen, group, piece, left_a, left_r, *rest):
    outs = rest[:-5]
    if side:
        before, outs = outs[0], outs[1:]
    bank, expand, weight_a, weight_r, total = rest[-5:]
    core = lax.axis_index("tm") % 2
    channels = left_a.shape[0]
    half = channels // 2
    base = half * jnp.where(core == side, 0, 1)
    slots = LANES // group
    banks = (half + 1) // slots
    offset_count = LANES // group
    tile_count = OFFSETS // offset_count
    code_lane = (half % slots) * group
    top = 112 + 8 * (7 + offset_count - 1)
    top = top + top % 16

    lag = lax.broadcasted_iota(jnp.int32, (LANES, LANES), 0)
    target = lax.broadcasted_iota(jnp.int32, (LANES, LANES), 1)
    lane = lax.broadcasted_iota(jnp.int32, (1, LANES), 1)
    used = lag < tlen
    ahead = lane // group
    for slot in range(slots):
        chosen = jnp.where(lag == target % group + slot * group, 1.0, 0.0)
        expand[:, slot * LANES : (slot + 1) * LANES] = chosen.astype(jnp.bfloat16)
    turned = []
    for index in range(banks):
        values = piece[slots * index : slots * (index + 1)].astype(jnp.float32)
        values = values.reshape(LANES, tlen)
        values = jnp.concatenate([values, jnp.zeros((LANES, LANES - tlen), jnp.float32)], axis=1)
        turned.append(values.T)
    codes = turned[-1]
    for index, values in enumerate(turned):
        code = jnp.zeros((1, LANES), jnp.float32)
        for slot in range(slots):
            item = slots * index + slot
            if item < half:
                moved = pltpu.roll(codes[item : item + 1, :], (group * slot - code_lane) % LANES, 1)
                code = jnp.where(ahead == slot, moved, code)
        center = jnp.sum(jnp.where(used, values, 0.0), axis=0, keepdims=True) / tlen
        deviate = jnp.where(used, values - center, 0.0)
        spread = jnp.sqrt(jnp.sum(deviate * deviate, axis=0, keepdims=True) / tlen + EPSILON)
        unit = (deviate / (spread * tlen)).astype(jnp.bfloat16).astype(jnp.float32)
        unit = jnp.where(code > 0, unit, 0.0)
        shift = code.astype(jnp.int32) - 1
        for bit in (1, 2, 4):
            unit = jnp.where(jnp.bitwise_and(shift, bit) > 0, pltpu.roll(unit, bit, 0), unit)
        unit = jnp.where(lag == 112, code, unit)
        bank[index] = unit.astype(jnp.bfloat16)

    def build(number):
        wide = jnp.dot(bank[number], expand[...], preferred_element_type=jnp.float32)
        for slot in range(slots):
            spreaded = wide[:, slot * LANES : (slot + 1) * LANES]
            code = spreaded[112:113, :].astype(jnp.int32)
            usable = code > 0
            shift = code - 1
            moves = shift // 8 + ahead
            taps = spreaded[0:112, :]
            for bit in (1, 2, 4, 8):
                gap = jnp.zeros((8 * bit, LANES), jnp.float32)
                taps = jnp.where(
                    jnp.bitwise_and(moves, bit) > 0,
                    jnp.concatenate([gap, taps], axis=0),
                    jnp.concatenate([taps, gap], axis=0),
                )[0:top]
            taps = taps.astype(jnp.bfloat16)
            item = number * slots + slot
            pick = jnp.logical_and(lag == shift + 8 * ahead, usable)
            pick = jnp.where(pick, 1.0, 0.0).astype(jnp.bfloat16)
            for index in range(tile_count):
                skip = 8 * offset_count * index
                lanes = slice(LANES * index, LANES * (index + 1))
                if skip:
                    weight_a[item, 0:skip, lanes] = jnp.zeros((skip, LANES), jnp.bfloat16)
                    pick = jnp.concatenate(
                        [jnp.zeros((skip, LANES), jnp.bfloat16), pick[0 : LANES - skip]], axis=0
                    )
                weight_a[item, skip : skip + top, lanes] = taps
                rest = DEPTH - top - skip
                if rest:
                    weight_a[item, skip + top :, lanes] = jnp.zeros((rest, LANES), jnp.bfloat16)
                weight_r[item, 0:LANES, lanes] = pick
                weight_r[item, LANES : 2 * LANES, lanes] = pick

    def apply(number, count):
        for slot in range(count):
            item = number * slots + slot
            corr = jnp.dot(left_a[base + item], weight_a[item], preferred_element_type=jnp.float32)
            factor = jnp.dot(
                left_r[base + item], weight_r[item], preferred_element_type=jnp.float32
            )
            total[...] += corr * factor

    total[...] = before[...] if side else jnp.zeros_like(total)
    build(0)

    @pl.loop(1, banks)
    def _(number):
        apply(number - 1, slots)
        build(number)

    apply(banks - 1, half - slots * (banks - 1))

    if not side:
        outs[0][...] = total[...]
        return
    rows_out = outs[0].shape[0]
    station = lax.axis_index("sta") % len(outs)
    for step, out in enumerate(outs):
        part = jnp.bitwise_xor(station, step)
        out[...] = total[pl.ds(pl.multiple_of(part * rows_out, rows_out), rows_out), :].astype(
            jnp.bfloat16
        )


def correlate(side, group, count, piece, left_a, left_r, *before):
    channels, rows, _ = left_a.shape
    width = OFFSETS * group
    half = channels // 2
    if side:
        out = [jax.ShapeDtypeStruct((rows // count, width), jnp.bfloat16)] * count
    else:
        out = [jax.ShapeDtypeStruct((rows, width), jnp.float32)]
    return pl.pallas_call(
        functools.partial(main_kernel, side, piece.shape[2], group),
        out_shape=out,
        in_specs=[VMEM] * (3 + len(before)),
        out_specs=[VMEM] * len(out),
        scratch_shapes=[
            pltpu.VMEM(((half + 1) * group // LANES, LANES, LANES), jnp.bfloat16),
            pltpu.VMEM((LANES, LANES // group * LANES), jnp.bfloat16),
            pltpu.VMEM((half + 1, DEPTH, width), jnp.bfloat16),
            pltpu.VMEM((half + 1, DEPTH, width), jnp.bfloat16),
            pltpu.VMEM((rows, width), jnp.float32),
        ],
        compiler_params=params(),
        cost_estimate=cost(3),
        name="correlate_" + ("second" if side else "first"),
    )(piece, left_a, left_r, *before)


def add_kernel(*refs):
    parts, keep, send = refs[:-2], refs[-2], refs[-1]
    rows = keep.shape[0]
    core = lax.axis_index("tm") % 2
    for out, which in ((keep, core), (send, 1 - core)):
        place = pl.ds(pl.multiple_of(which * rows, rows), rows)
        value = parts[0][place, :].astype(jnp.float32)
        for part in parts[1:]:
            value = value + part[place, :].astype(jnp.float32)
        out[...] = value


def add(parts):
    rows, width = parts[0].shape
    out = jax.ShapeDtypeStruct((rows // 2, width), jnp.float32)
    return pl.pallas_call(
        add_kernel,
        out_shape=[out, out],
        in_specs=[VMEM] * len(parts),
        out_specs=[VMEM, VMEM],
        compiler_params=params(),
        cost_estimate=cost(0.5),
        name="add",
    )(*parts)


def finish_kernel(group, ours, received, out):
    samples = out.shape[1]
    rows = ours.shape[0]
    value = ours[...] + received[...]
    high = value.astype(jnp.bfloat16).astype(jnp.float32)
    both = jnp.concatenate([high, value - high], axis=0).T.astype(jnp.bfloat16)
    row = lax.broadcasted_iota(jnp.int32, (2 * rows, samples), 0) % rows
    lane = lax.broadcasted_iota(jnp.int32, (2 * rows, samples), 1)
    place = jnp.logical_and(lane // STRIDE == row // 8, lane % 8 == 7 - row % 8)
    place = jnp.where(place, 1.0, 0.0).astype(jnp.bfloat16)
    wide = jnp.dot(both, place, preferred_element_type=jnp.float32)
    lane = lax.broadcasted_iota(jnp.int32, (group, samples), 1) // 8 % OFFSETS
    result = jnp.zeros((group, samples), jnp.float32)
    for offset in range(OFFSETS):
        result = jnp.where(lane == offset, wide[offset * group : (offset + 1) * group], result)
    out[...] = result


def finish(group, samples, ours, received):
    return pl.pallas_call(
        functools.partial(finish_kernel, group),
        out_shape=jax.ShapeDtypeStruct((group, samples), jnp.float32),
        in_specs=[VMEM, VMEM],
        out_specs=VMEM,
        compiler_params=params(),
        cost_estimate=cost(1),
        name="finish",
    )(ours, received)


def shards(waveforms, templates, available, moveout, bank_blocks):
    channels, samples = waveforms.shape
    blocks, events, _, tlen = templates.shape
    count_tm = lax.axis_size("tm")
    count_sta = lax.axis_size("sta")
    chips = count_tm // 2
    near = chips // 2
    group = 2 * events // chips
    me = lax.axis_index("tm").astype(jnp.int32)
    station = lax.axis_index("sta").astype(jnp.int32)
    chip, core = me // 2, me % 2

    def swap(array):
        return lax.ppermute(array, "tm", [(i, i ^ 1) for i in range(count_tm)])

    def across(array, step):
        return lax.ppermute(array, "tm", [(i, i ^ (2 * step)) for i in range(count_tm)])

    def spread(array, step):
        route = [(2 * z + z // near, 2 * (z ^ step) + z // near) for z in range(chips)]
        return lax.ppermute(array, "tm", route)

    mine, theirs = pack(
        chips,
        group,
        bank_blocks,
        jnp.transpose(templates, (0, 2, 1, 3)),
        jnp.transpose(available, (2, 0, 1)),
        jnp.transpose(moveout, (2, 0, 1)),
    )
    waveforms, theirs = lax.optimization_barrier((waveforms, theirs))
    paired = swap(waveforms)
    other = swap(theirs)
    both = jnp.where(
        core == 0, jnp.stack([waveforms, paired]), jnp.stack([paired, waveforms])
    )
    far = [spread(both, step) for step in range(near, chips)]
    local = jnp.stack([both] + [spread(both, step) for step in range(1, near)] + far)
    other, local = lax.optimization_barrier((other, local))
    merged = merge(blocks, bank_blocks, mine, other)
    pieces = [merged[0]] + [across(merged[step], step) for step in range(1, chips)]

    rim = lax.dynamic_index_in_dim(local, chip ^ near, 0, keepdims=False)[0, :, : 2 * LANES]
    rim = lax.ppermute(rim, "tm", [(2 * z + 1, 2 * z) for z in range(chips)])
    left_a, left_r = prepare_waves(tlen, rim, local)

    left_a, left_r, *pieces = lax.optimization_barrier((left_a, left_r, *pieces))
    owner = jnp.where(chip ^ station < near, bank_blocks[0], bank_blocks[1]) // blocks
    source = (owner // 2) ^ chip
    first = pieces[0]
    for step in range(1, chips):
        first = jnp.where(source == step, pieces[step], first)
    second = swap(first)
    total = correlate(0, group, near, first, left_a, left_r)
    parts = correlate(1, group, near, second, left_a, left_r, *total)
    gathered = []
    for step in range(near):
        route = []
        for d in range(count_tm):
            for s in range(count_sta):
                dest = near * (d % 2) + (s % near ^ step)
                sta = d // 2 ^ s
                route.append((d * count_sta + s, (2 * dest + s // near) * count_sta + sta))
        gathered.append(lax.ppermute(parts[step], ("tm", "sta"), route))
    ours, send = add(gathered)
    return finish(group, samples, ours, swap(send))


def solution(mesh):
    in_specs = (
        P("sta", "tm"),
        P("tm", None, "sta", None),
        P("tm", None, "sta"),
        P("tm", None, "sta"),
        P(),
    )
    out_specs = P("sta", "tm")
    return jax.shard_map(shards, mesh=mesh, in_specs=in_specs, out_specs=out_specs, check_vma=False)
```

```python
import functools

import jax
import jax.numpy as jnp
from jax import lax
from jax.experimental import pallas as pl
from jax.experimental.pallas import tpu as pltpu
from jax.sharding import PartitionSpec as P

EPSILON = 1e-06
LANES = 128
OFFSETS = 8
TILES = 12
QUARTER = 25
STRIDE = 64
DEPTH = 256
VMEM_LIMIT = 28 * 1024 * 1024

SMEM = pl.BlockSpec(memory_space=pltpu.SMEM)
VMEM = pl.BlockSpec(memory_space=pltpu.VMEM)
ANY = pl.BlockSpec(memory_space=pl.ANY)


def params():
    return pltpu.CompilerParams(vmem_limit_bytes=VMEM_LIMIT)


def cost(micros):
    return pl.CostEstimate(
        flops=int(micros * 1e9), bytes_accessed=int(micros * 1e6), transcendentals=0
    )


def pack_kernel(bank_blocks, templates, available, moveout, mine, theirs, chosen, raw, usable, shifts, square, packed, sems):
    blocks, channels, events, tlen = templates.shape
    chips, _, group, _ = mine.shape
    half = channels // 2
    me = lax.axis_index("tm") % 2
    fetch = [
        pltpu.make_async_copy(source, target, sems.at[index])
        for index, (source, target) in enumerate(
            ((bank_blocks, chosen), (available, usable), (moveout, shifts), (templates, raw))
        )
    ]
    for copy in fetch:
        copy.start()
    packed[...] = jnp.zeros_like(packed)
    square[...] = jnp.zeros_like(square)
    for copy in fetch[:3]:
        copy.wait()
    slots = [chosen[which] % blocks for which in range(2)]
    flags = jnp.where(usable[...] > 0, shifts[...] + 1, 0).astype(jnp.float32)
    turned = []
    for which in range(2):
        code = flags[:, 0, :]
        for block in range(1, blocks):
            code = jnp.where(slots[which] == block, flags[:, block, :], code)
        square[0:channels, 0:events] = code
        turned.append(square[...].T.astype(jnp.bfloat16))
    fetch[3].wait()
    for which in range(2):
        for core in range(2):
            for tile in range(TILES):
                channel = half * core + tile
                extra = half * core + TILES + tile // 4
                start = QUARTER * (tile % 4)
                for index in range(events // group):
                    chip = which * (events // group) + index
                    rows = slice(index * group, (index + 1) * group)
                    packed[core, chip, tile, :, 0:tlen] = raw[slots[which], channel, rows, :]
                    packed[core, chip, tile, :, tlen : tlen + QUARTER] = raw[
                        slots[which], extra, rows, start : start + QUARTER
                    ]
                    packed[core, chip, tile, :, 125:126] = turned[which][rows, channel : channel + 1]
                    if tile < half - TILES:
                        beyond = channel + TILES
                        packed[core, chip, tile, :, 126:127] = turned[which][rows, beyond : beyond + 1]
    mine[...] = packed[me]
    theirs[...] = packed[1 - me]


def pack(chips, group, bank_blocks, templates, available, moveout):
    shape = (chips, TILES, group, LANES)
    held = [
        pltpu.with_memory_space_constraint(array, pltpu.HBM)
        for array in (bank_blocks, templates, available, moveout)
    ]
    return pl.pallas_call(
        pack_kernel,
        out_shape=[jax.ShapeDtypeStruct(shape, jnp.bfloat16)] * 2,
        in_specs=[ANY] * 4,
        out_specs=[VMEM] * 2,
        scratch_shapes=[
            pltpu.SMEM(bank_blocks.shape, jnp.int32),
            pltpu.VMEM(templates.shape, jnp.bfloat16),
            pltpu.VMEM(available.shape, jnp.int32),
            pltpu.VMEM(moveout.shape, jnp.int32),
            pltpu.VMEM((LANES, LANES), jnp.float32),
            pltpu.VMEM((2,) + shape, jnp.bfloat16),
            pltpu.SemaphoreType.DMA((4,)),
        ],
        compiler_params=params(),
        cost_estimate=cost(2),
        name="pack",
    )(*held)


def merge_kernel(blocks, bank_blocks, mine, other, *outs):
    chips = len(outs)
    me = lax.axis_index("tm")
    for step, out in enumerate(outs):
        dest = jnp.bitwise_xor(me // 2, step)
        owner = jnp.where(dest < chips // 2, bank_blocks[0], bank_blocks[1]) // blocks
        here = owner % 2 == me % 2

        @pl.when(here)
        def _():
            out[...] = mine[dest]

        @pl.when(jnp.logical_not(here))
        def _():
            out[...] = other[dest]


def merge(blocks, bank_blocks, mine, other):
    chips = mine.shape[0]
    return pl.pallas_call(
        functools.partial(merge_kernel, blocks),
        out_shape=[jax.ShapeDtypeStruct(mine.shape[1:], mine.dtype)] * chips,
        in_specs=[SMEM, VMEM, VMEM],
        out_specs=[VMEM] * chips,
        compiler_params=params(),
        cost_estimate=cost(1),
        name="merge",
    )(bank_blocks, mine, other)


def left(values, count):
    return pltpu.roll(values, values.shape[1] - count, 1)


def window_sums(values):
    sums = {1: values}
    width = 1
    while width < 64:
        sums[2 * width] = sums[width] + left(sums[width], width)
        width *= 2
    return sums[64] + left(sums[32], 64) + left(sums[4], 96)


def lagged(row, ahead):
    copies = jnp.broadcast_to(row, (8, row.shape[1]))
    return pltpu.roll(copies, row.shape[1] - 7 - ahead, 1, stride=1, stride_axis=0)


def waves_kernel(channels, tlen, swapped, local, left_a, left_r, padded, inverse):
    chips, _, samples = local.shape
    near = chips // 2
    length = chips * samples
    steps = length // STRIDE
    me = lax.axis_index("tm")
    chip, core = me // 2, me % 2
    padded[...] = jnp.zeros_like(padded)
    for index in range(chips):
        source = jnp.bitwise_xor(chip, near * core + index // 2)
        wave = jnp.where(core == index % 2, local[source], swapped[index // 2])
        padded[0:channels, samples * index : samples * (index + 1)] = wave.astype(jnp.float32)
    rim = local[jnp.bitwise_xor(chip, near)][:, 0 : padded.shape[1] - length]
    padded[0:channels, length:] = jnp.where(core == 0, rim.astype(jnp.float32), 0.0)

    @pl.loop(0, 4)
    def _(part):
        rows = pl.ds(pl.multiple_of(part * 8, 8), 8)
        values = padded[rows, :]
        first_sum = window_sums(values)
        second_sum = window_sums(values * values)
        mean = first_sum / tlen
        inverse[rows, :] = lax.rsqrt(second_sum / tlen - mean * mean + EPSILON)

    @pl.loop(0, channels)
    def _(channel):
        row = padded[pl.ds(channel, 1), :]
        scale = inverse[pl.ds(channel, 1), :]
        even, odd = lagged(row, 0), lagged(row, STRIDE)
        even_scale, odd_scale = lagged(scale, 0), lagged(scale, STRIDE)
        columns = ([], [], [])
        for step in range(steps):
            start = STRIDE * (step - step % 2)
            values = odd if step % 2 else even
            columns[0].append(values[:, start : start + LANES])
            columns[1].append(values[:, start + LANES : start + 2 * LANES])
            values = odd_scale if step % 2 else even_scale
            columns[2].append(values[:, start : start + LANES])
        left_a[channel, :, 0:LANES] = jnp.concatenate(columns[0], axis=0).astype(jnp.bfloat16)
        left_a[channel, :, LANES:] = jnp.concatenate(columns[1], axis=0).astype(jnp.bfloat16)
        value = jnp.concatenate(columns[2], axis=0)
        high = value.astype(jnp.bfloat16)
        left_r[channel, :, 0:LANES] = high
        left_r[channel, :, LANES:] = (value - high.astype(jnp.float32)).astype(jnp.bfloat16)


def prepare_waves(tlen, swapped, local):
    chips, channels, samples = local.shape
    length = chips * samples
    out = jax.ShapeDtypeStruct((channels, length // OFFSETS, DEPTH), jnp.bfloat16)
    return pl.pallas_call(
        functools.partial(waves_kernel, channels, tlen),
        out_shape=[out, out],
        in_specs=[VMEM, VMEM],
        out_specs=[VMEM, VMEM],
        scratch_shapes=[
            pltpu.VMEM((32, length + 2 * LANES), jnp.float32),
            pltpu.VMEM((32, length + 2 * LANES), jnp.float32),
        ],
        compiler_params=params(),
        cost_estimate=cost(7),
        name="prepare_waves",
    )(swapped, local)


def main_kernel(side, tlen, group, piece, left_a, left_r, *rest):
    outs = rest[:-5]
    if side:
        before, outs = outs[0], outs[1:]
    bank, expand, weight_a, weight_r, total = rest[-5:]
    core = lax.axis_index("tm") % 2
    channels = left_a.shape[0]
    half = channels // 2
    base = half * jnp.where(core == side, 0, 1)
    slots = LANES // group
    banks = (half + 1) // slots
    offset_count = LANES // group
    tile_count = OFFSETS // offset_count
    top = 112 + 8 * (7 + offset_count - 1)
    top = top + top % 16

    lag = lax.broadcasted_iota(jnp.int32, (LANES, LANES), 0)
    target = lax.broadcasted_iota(jnp.int32, (LANES, LANES), 1)
    lane = lax.broadcasted_iota(jnp.int32, (1, LANES), 1)
    used = lag < tlen
    ahead = lane // group
    for slot in range(slots):
        chosen = jnp.where(lag == target % group + slot * group, 1.0, 0.0)
        expand[:, slot * LANES : (slot + 1) * LANES] = chosen.astype(jnp.bfloat16)
    turned = []
    for index in range(banks):
        count = min(slots, max(TILES - slots * index, 0))
        values = jnp.zeros((LANES, LANES), jnp.float32)
        if count:
            values = piece[slots * index : slots * index + count].astype(jnp.float32)
            values = values.reshape(count * group, LANES)
            if count < slots:
                gap = jnp.zeros((LANES - count * group, LANES), jnp.float32)
                values = jnp.concatenate([values, gap], axis=0)
            values = values.T
        turned.append(values)
    codes = [values[125:126, :] for values in turned]
    heads = [jnp.where(used, values, 0.0) for values in turned]
    for extra in range(half - TILES):
        place, slot = divmod(TILES + extra, slots)
        mask = ahead == slot
        code = pltpu.roll(turned[0][126:127, :], (slot - extra) * group % LANES, 1)
        codes[place] = jnp.where(mask, code, codes[place])
        for quarter in range(4):
            source, lanes = divmod(4 * extra + quarter, slots)
            values = turned[source][96:128]
            rows = lag[96:128]
            inside = jnp.logical_and(rows >= tlen, rows < tlen + QUARTER)
            values = jnp.where(inside, values, 0.0)
            values = pltpu.roll(values, (slot - lanes) * group % LANES, 1)
            start = QUARTER * quarter - (tlen - 96)
            values = jnp.concatenate([values, jnp.zeros((8, LANES), jnp.float32)], axis=0)
            values = pltpu.roll(values, start % 8, 0)
            start -= start % 8
            if start < 0:
                values, start = values[8:], 0
            below = LANES - start - values.shape[0]
            if start:
                values = jnp.concatenate([jnp.zeros((start, LANES), jnp.float32), values], axis=0)
            if below > 0:
                values = jnp.concatenate([values, jnp.zeros((below, LANES), jnp.float32)], axis=0)
            heads[place] = heads[place] + jnp.where(mask, values[0:LANES], 0.0)
    for index, (values, code) in enumerate(zip(heads, codes)):
        code = jnp.where(slots * index + ahead < half, code, 0.0)
        center = jnp.sum(values, axis=0, keepdims=True) / tlen
        deviate = jnp.where(used, values - center, 0.0)
        spread = jnp.sqrt(jnp.sum(deviate * deviate, axis=0, keepdims=True) / tlen + EPSILON)
        unit = (deviate / (spread * tlen)).astype(jnp.bfloat16).astype(jnp.float32)
        unit = jnp.where(code > 0, unit, 0.0)
        shift = code.astype(jnp.int32) - 1
        for bit in (1, 2, 4):
            unit = jnp.where(jnp.bitwise_and(shift, bit) > 0, pltpu.roll(unit, bit, 0), unit)
        unit = jnp.where(lag == 112, code, unit)
        bank[index] = unit.astype(jnp.bfloat16)

    def build(number):
        wide = jnp.dot(bank[number], expand[...], preferred_element_type=jnp.float32)
        for slot in range(slots):
            spreaded = wide[:, slot * LANES : (slot + 1) * LANES]
            code = spreaded[112:113, :].astype(jnp.int32)
            usable = code > 0
            shift = code - 1
            moves = shift // 8 + ahead
            taps = spreaded[0:112, :]
            for bit in (1, 2, 4, 8):
                gap = jnp.zeros((8 * bit, LANES), jnp.float32)
                taps = jnp.where(
                    jnp.bitwise_and(moves, bit) > 0,
                    jnp.concatenate([gap, taps], axis=0),
                    jnp.concatenate([taps, gap], axis=0),
                )[0:top]
            taps = taps.astype(jnp.bfloat16)
            item = number * slots + slot
            pick = jnp.logical_and(lag == shift + 8 * ahead, usable)
            pick = jnp.where(pick, 1.0, 0.0).astype(jnp.bfloat16)
            for index in range(tile_count):
                skip = 8 * offset_count * index
                lanes = slice(LANES * index, LANES * (index + 1))
                if skip:
                    weight_a[item, 0:skip, lanes] = jnp.zeros((skip, LANES), jnp.bfloat16)
                    pick = jnp.concatenate(
                        [jnp.zeros((skip, LANES), jnp.bfloat16), pick[0 : LANES - skip]], axis=0
                    )
                weight_a[item, skip : skip + top, lanes] = taps
                rest = DEPTH - top - skip
                if rest:
                    weight_a[item, skip + top :, lanes] = jnp.zeros((rest, LANES), jnp.bfloat16)
                weight_r[item, 0:LANES, lanes] = pick
                weight_r[item, LANES : 2 * LANES, lanes] = pick

    def apply(number, count):
        for slot in range(count):
            item = number * slots + slot
            corr = jnp.dot(left_a[base + item], weight_a[item], preferred_element_type=jnp.float32)
            factor = jnp.dot(
                left_r[base + item], weight_r[item], preferred_element_type=jnp.float32
            )
            total[...] += corr * factor

    total[...] = before[...] if side else jnp.zeros_like(total)
    build(0)

    @pl.loop(1, banks)
    def _(number):
        apply(number - 1, slots)
        build(number)

    apply(banks - 1, half - slots * (banks - 1))

    if not side:
        outs[0][...] = total[...]
        return
    rows_out = outs[0].shape[0]
    station = lax.axis_index("sta") % len(outs)
    for step, out in enumerate(outs):
        part = jnp.bitwise_xor(station, step)
        out[...] = total[pl.ds(pl.multiple_of(part * rows_out, rows_out), rows_out), :].astype(
            jnp.bfloat16
        )


def correlate(side, tlen, group, count, piece, left_a, left_r, *before):
    channels, rows, _ = left_a.shape
    width = OFFSETS * group
    half = channels // 2
    if side:
        out = [jax.ShapeDtypeStruct((rows // count, width), jnp.bfloat16)] * count
    else:
        out = [jax.ShapeDtypeStruct((rows, width), jnp.float32)]
    return pl.pallas_call(
        functools.partial(main_kernel, side, tlen, group),
        out_shape=out,
        in_specs=[VMEM] * (3 + len(before)),
        out_specs=[VMEM] * len(out),
        scratch_shapes=[
            pltpu.VMEM(((half + 1) * group // LANES, LANES, LANES), jnp.bfloat16),
            pltpu.VMEM((LANES, LANES // group * LANES), jnp.bfloat16),
            pltpu.VMEM((half + 1, DEPTH, width), jnp.bfloat16),
            pltpu.VMEM((half + 1, DEPTH, width), jnp.bfloat16),
            pltpu.VMEM((rows, width), jnp.float32),
        ],
        compiler_params=params(),
        cost_estimate=cost(3),
        name="correlate_" + ("second" if side else "first"),
    )(piece, left_a, left_r, *before)


def add_kernel(*refs):
    parts, keep, send = refs[:-2], refs[-2], refs[-1]
    rows = keep.shape[0]
    core = lax.axis_index("tm") % 2
    for out, which in ((keep, core), (send, 1 - core)):
        place = pl.ds(pl.multiple_of(which * rows, rows), rows)
        value = parts[0][place, :].astype(jnp.float32)
        for part in parts[1:]:
            value = value + part[place, :].astype(jnp.float32)
        out[...] = value


def add(parts):
    rows, width = parts[0].shape
    out = jax.ShapeDtypeStruct((rows // 2, width), jnp.float32)
    return pl.pallas_call(
        add_kernel,
        out_shape=[out, out],
        in_specs=[VMEM] * len(parts),
        out_specs=[VMEM, VMEM],
        compiler_params=params(),
        cost_estimate=cost(0.5),
        name="add",
    )(*parts)


def finish_kernel(group, ours, received, out):
    samples = out.shape[1]
    rows = ours.shape[0]
    value = ours[...] + received[...]
    high = value.astype(jnp.bfloat16).astype(jnp.float32)
    both = jnp.concatenate([high, value - high], axis=0).T.astype(jnp.bfloat16)
    row = lax.broadcasted_iota(jnp.int32, (2 * rows, samples), 0) % rows
    lane = lax.broadcasted_iota(jnp.int32, (2 * rows, samples), 1)
    place = jnp.logical_and(lane // STRIDE == row // 8, lane % 8 == 7 - row % 8)
    place = jnp.where(place, 1.0, 0.0).astype(jnp.bfloat16)
    wide = jnp.dot(both, place, preferred_element_type=jnp.float32)
    lane = lax.broadcasted_iota(jnp.int32, (group, samples), 1) // 8 % OFFSETS
    result = jnp.zeros((group, samples), jnp.float32)
    for offset in range(OFFSETS):
        result = jnp.where(lane == offset, wide[offset * group : (offset + 1) * group], result)
    out[...] = result


def finish(group, samples, ours, received):
    return pl.pallas_call(
        functools.partial(finish_kernel, group),
        out_shape=jax.ShapeDtypeStruct((group, samples), jnp.float32),
        in_specs=[VMEM, VMEM],
        out_specs=VMEM,
        compiler_params=params(),
        cost_estimate=cost(1),
        name="finish",
    )(ours, received)


def shards(waveforms, templates, available, moveout, bank_blocks):
    channels, samples = waveforms.shape
    blocks, events, _, tlen = templates.shape
    count_tm = lax.axis_size("tm")
    count_sta = lax.axis_size("sta")
    chips = count_tm // 2
    near = chips // 2
    group = 2 * events // chips
    me = lax.axis_index("tm").astype(jnp.int32)
    chip, core = me // 2, me % 2

    def swap(array):
        return lax.ppermute(array, "tm", [(i, i ^ 1) for i in range(count_tm)])

    def across(array, step):
        return lax.ppermute(array, "tm", [(i, i ^ (2 * step)) for i in range(count_tm)])

    local = jnp.stack([waveforms] + [across(waveforms, step) for step in range(1, chips)])
    mine, theirs = pack(
        chips,
        group,
        bank_blocks,
        jnp.transpose(templates, (0, 2, 1, 3)),
        jnp.transpose(available, (2, 0, 1)),
        jnp.transpose(moveout, (2, 0, 1)),
    )
    other = swap(theirs)
    other, local = lax.optimization_barrier((other, local))
    merged = merge(blocks, bank_blocks, mine, other)
    pieces = [merged[0]] + [across(merged[step], step) for step in range(1, chips)]

    wanted = [
        lax.dynamic_index_in_dim(local, chip ^ (near * (1 - core) + step), 0, keepdims=False)
        for step in range(near)
    ]
    swapped = swap(jnp.stack(wanted))
    left_a, left_r = prepare_waves(tlen, swapped, local)

    left_a, left_r, *pieces = lax.optimization_barrier((left_a, left_r, *pieces))
    owner = jnp.where(chip < near, bank_blocks[0], bank_blocks[1]) // blocks
    source = (owner // 2) ^ chip
    first = pieces[0]
    for step in range(1, chips):
        first = jnp.where(source == step, pieces[step], first)
    second = swap(first)
    total = correlate(0, tlen, group, near, first, left_a, left_r)
    parts = correlate(1, tlen, group, near, second, left_a, left_r, *total)
    gathered = []
    for step in range(near):
        route = []
        for d in range(count_tm):
            for s in range(count_sta):
                dest = near * (d % 2) + (s % near ^ step)
                route.append((d * count_sta + s, (2 * dest + s // near) * count_sta + d // 2))
        gathered.append(lax.ppermute(parts[step], ("tm", "sta"), route))
    ours, send = add(gathered)
    return finish(group, samples, ours, swap(send))


def solution(mesh):
    in_specs = (
        P("sta", "tm"),
        P("tm", None, "sta", None),
        P("tm", None, "sta"),
        P("tm", None, "sta"),
        P(),
    )
    out_specs = P("sta", "tm")
    return jax.shard_map(shards, mesh=mesh, in_specs=in_specs, out_specs=out_specs, check_vma=False)
```

```python
import functools

import jax
import jax.numpy as jnp
from jax import lax
from jax.experimental import pallas as pl
from jax.experimental.pallas import tpu as pltpu
from jax.sharding import PartitionSpec as P

EPSILON = 1e-06
LANES = 128
OFFSETS = 8
TILES = 12
QUARTER = 25
STRIDE = 64
DEPTH = 256
VMEM_LIMIT = 28 * 1024 * 1024

SMEM = pl.BlockSpec(memory_space=pltpu.SMEM)
VMEM = pl.BlockSpec(memory_space=pltpu.VMEM)
ANY = pl.BlockSpec(memory_space=pl.ANY)


def params():
    return pltpu.CompilerParams(vmem_limit_bytes=VMEM_LIMIT)


def cost(micros):
    return pl.CostEstimate(
        flops=int(micros * 1e9), bytes_accessed=int(micros * 1e6), transcendentals=0
    )


def pack_kernel(bank_blocks, templates, available, moveout, mine, theirs, chosen, raw, usable, shifts, square, packed, sems):
    blocks, channels, events, tlen = templates.shape
    chips, _, group, _ = mine.shape
    half = channels // 2
    me = lax.axis_index("tm") % 2
    fetch = [
        pltpu.make_async_copy(source, target, sems.at[index])
        for index, (source, target) in enumerate(
            ((bank_blocks, chosen), (available, usable), (moveout, shifts), (templates, raw))
        )
    ]
    for copy in fetch:
        copy.start()
    packed[...] = jnp.zeros_like(packed)
    square[...] = jnp.zeros_like(square)
    for copy in fetch[:3]:
        copy.wait()
    slots = [chosen[which] % blocks for which in range(2)]
    flags = jnp.where(usable[...] > 0, shifts[...] + 1, 0).astype(jnp.float32)
    turned = []
    for which in range(2):
        code = flags[:, 0, :]
        for block in range(1, blocks):
            code = jnp.where(slots[which] == block, flags[:, block, :], code)
        square[0:channels, 0:events] = code
        turned.append(square[...].T.astype(jnp.bfloat16))
    fetch[3].wait()
    for which in range(2):
        for core in range(2):
            for tile in range(TILES):
                channel = half * core + tile
                extra = half * core + TILES + tile // 4
                start = QUARTER * (tile % 4)
                for index in range(events // group):
                    chip = which * (events // group) + index
                    rows = slice(index * group, (index + 1) * group)
                    packed[core, chip, tile, :, 0:tlen] = raw[slots[which], channel, rows, :]
                    packed[core, chip, tile, :, tlen : tlen + QUARTER] = raw[
                        slots[which], extra, rows, start : start + QUARTER
                    ]
                    packed[core, chip, tile, :, 125:126] = turned[which][rows, channel : channel + 1]
                    if tile < half - TILES:
                        beyond = channel + TILES
                        packed[core, chip, tile, :, 126:127] = turned[which][rows, beyond : beyond + 1]
    mine[...] = packed[me]
    theirs[...] = packed[1 - me]


def pack(chips, group, bank_blocks, templates, available, moveout):
    shape = (chips, TILES, group, LANES)
    held = [
        pltpu.with_memory_space_constraint(array, pltpu.HBM)
        for array in (bank_blocks, templates, available, moveout)
    ]
    return pl.pallas_call(
        pack_kernel,
        out_shape=[jax.ShapeDtypeStruct(shape, jnp.bfloat16)] * 2,
        in_specs=[ANY] * 4,
        out_specs=[VMEM] * 2,
        scratch_shapes=[
            pltpu.SMEM(bank_blocks.shape, jnp.int32),
            pltpu.VMEM(templates.shape, jnp.bfloat16),
            pltpu.VMEM(available.shape, jnp.int32),
            pltpu.VMEM(moveout.shape, jnp.int32),
            pltpu.VMEM((LANES, LANES), jnp.float32),
            pltpu.VMEM((2,) + shape, jnp.bfloat16),
            pltpu.SemaphoreType.DMA((4,)),
        ],
        compiler_params=params(),
        cost_estimate=cost(2),
        name="pack",
    )(*held)


def merge_kernel(blocks, bank_blocks, mine, other, *outs):
    chips = len(outs)
    me = lax.axis_index("tm")
    for step, out in enumerate(outs):
        dest = jnp.bitwise_xor(me // 2, step)
        owner = jnp.where(dest < chips // 2, bank_blocks[0], bank_blocks[1]) // blocks
        here = owner % 2 == me % 2

        @pl.when(here)
        def _():
            out[...] = mine[dest]

        @pl.when(jnp.logical_not(here))
        def _():
            out[...] = other[dest]


def merge(blocks, bank_blocks, mine, other):
    chips = mine.shape[0]
    return pl.pallas_call(
        functools.partial(merge_kernel, blocks),
        out_shape=[jax.ShapeDtypeStruct(mine.shape[1:], mine.dtype)] * chips,
        in_specs=[SMEM, VMEM, VMEM],
        out_specs=[VMEM] * chips,
        compiler_params=params(),
        cost_estimate=cost(1),
        name="merge",
    )(bank_blocks, mine, other)


def left(values, count):
    return pltpu.roll(values, values.shape[1] - count, 1)


def window_sums(values):
    sums = {1: values}
    width = 1
    while width < 64:
        sums[2 * width] = sums[width] + left(sums[width], width)
        width *= 2
    return sums[64] + left(sums[32], 64) + left(sums[4], 96)


def lagged(row, ahead):
    copies = jnp.broadcast_to(row, (8, row.shape[1]))
    return pltpu.roll(copies, row.shape[1] - 7 - ahead, 1, stride=1, stride_axis=0)


def pick(arrays, index):
    value = arrays[0][...]
    for number, array in enumerate(arrays[1:], 1):
        value = jnp.where(index == number, array[...], value)
    return value


def choose_kernel(near, *refs):
    waves, out = refs[:-1], refs[-1]
    me = lax.axis_index("tm")
    for step in range(near):
        out[step] = pick(waves, jnp.bitwise_xor(me // 2, near * (1 - me % 2) + step))


def choose_waves(waves):
    near = len(waves) // 2
    return pl.pallas_call(
        functools.partial(choose_kernel, near),
        out_shape=jax.ShapeDtypeStruct((near,) + waves[0].shape, waves[0].dtype),
        in_specs=[VMEM] * len(waves),
        out_specs=VMEM,
        compiler_params=params(),
        cost_estimate=cost(0.3),
        name="choose_waves",
    )(*waves)


def own_kernel(blocks, bank_blocks, *refs):
    pieces, out = refs[:-1], refs[-1]
    chip = lax.axis_index("tm") // 2
    first = chip < len(pieces) // 2
    owner = jnp.where(first, bank_blocks[0], bank_blocks[1]) // blocks
    out[...] = pick(pieces, jnp.bitwise_xor(owner // 2, chip))


def choose_piece(blocks, bank_blocks, pieces):
    return pl.pallas_call(
        functools.partial(own_kernel, blocks),
        out_shape=jax.ShapeDtypeStruct(pieces[0].shape, pieces[0].dtype),
        in_specs=[SMEM] + [VMEM] * len(pieces),
        out_specs=VMEM,
        compiler_params=params(),
        cost_estimate=cost(0.3),
        name="choose_piece",
    )(bank_blocks, *pieces)


def waves_kernel(channels, tlen, swapped, *rest):
    local = rest[:-4]
    left_a, left_r, padded, inverse = rest[-4:]
    chips = len(local)
    samples = local[0].shape[1]
    near = chips // 2
    length = chips * samples
    steps = length // STRIDE
    me = lax.axis_index("tm")
    chip, core = me // 2, me % 2
    padded[...] = jnp.zeros_like(padded)
    for index in range(chips):
        wave = pick(local, jnp.bitwise_xor(chip, near * core + index // 2))
        wave = jnp.where(core == index % 2, wave, swapped[index // 2])
        padded[0:channels, samples * index : samples * (index + 1)] = wave.astype(jnp.float32)
    rim = pick(local, jnp.bitwise_xor(chip, near))[:, 0 : padded.shape[1] - length]
    padded[0:channels, length:] = jnp.where(core == 0, rim.astype(jnp.float32), 0.0)

    @pl.loop(0, 4)
    def _(part):
        rows = pl.ds(pl.multiple_of(part * 8, 8), 8)
        values = padded[rows, :]
        first_sum = window_sums(values)
        second_sum = window_sums(values * values)
        mean = first_sum / tlen
        inverse[rows, :] = lax.rsqrt(second_sum / tlen - mean * mean + EPSILON)

    @pl.loop(0, channels)
    def _(channel):
        row = padded[pl.ds(channel, 1), :]
        scale = inverse[pl.ds(channel, 1), :]
        even, odd = lagged(row, 0), lagged(row, STRIDE)
        even_scale, odd_scale = lagged(scale, 0), lagged(scale, STRIDE)
        columns = ([], [], [])
        for step in range(steps):
            start = STRIDE * (step - step % 2)
            values = odd if step % 2 else even
            columns[0].append(values[:, start : start + LANES])
            columns[1].append(values[:, start + LANES : start + 2 * LANES])
            values = odd_scale if step % 2 else even_scale
            columns[2].append(values[:, start : start + LANES])
        left_a[channel, :, 0:LANES] = jnp.concatenate(columns[0], axis=0).astype(jnp.bfloat16)
        left_a[channel, :, LANES:] = jnp.concatenate(columns[1], axis=0).astype(jnp.bfloat16)
        value = jnp.concatenate(columns[2], axis=0)
        high = value.astype(jnp.bfloat16)
        left_r[channel, :, 0:LANES] = high
        left_r[channel, :, LANES:] = (value - high.astype(jnp.float32)).astype(jnp.bfloat16)


def prepare_waves(tlen, swapped, local):
    channels, samples = local[0].shape
    length = len(local) * samples
    out = jax.ShapeDtypeStruct((channels, length // OFFSETS, DEPTH), jnp.bfloat16)
    return pl.pallas_call(
        functools.partial(waves_kernel, channels, tlen),
        out_shape=[out, out],
        in_specs=[VMEM] * (1 + len(local)),
        out_specs=[VMEM, VMEM],
        scratch_shapes=[
            pltpu.VMEM((32, length + 2 * LANES), jnp.float32),
            pltpu.VMEM((32, length + 2 * LANES), jnp.float32),
        ],
        compiler_params=params(),
        cost_estimate=cost(0.05),
        name="prepare_waves",
    )(swapped, *local)


def main_kernel(side, tlen, group, piece, left_a, left_r, *rest):
    outs = rest[:-5]
    if side:
        before, outs = outs[0], outs[1:]
    bank, expand, weight_a, weight_r, total = rest[-5:]
    core = lax.axis_index("tm") % 2
    channels = left_a.shape[0]
    half = channels // 2
    base = half * jnp.where(core == side, 0, 1)
    slots = LANES // group
    banks = (half + 1) // slots
    offset_count = LANES // group
    tile_count = OFFSETS // offset_count
    top = 112 + 8 * (7 + offset_count - 1)
    top = top + top % 16

    lag = lax.broadcasted_iota(jnp.int32, (LANES, LANES), 0)
    target = lax.broadcasted_iota(jnp.int32, (LANES, LANES), 1)
    lane = lax.broadcasted_iota(jnp.int32, (1, LANES), 1)
    used = lag < tlen
    ahead = lane // group
    for slot in range(slots):
        chosen = jnp.where(lag == target % group + slot * group, 1.0, 0.0)
        expand[:, slot * LANES : (slot + 1) * LANES] = chosen.astype(jnp.bfloat16)
    turned = []
    for index in range(banks):
        count = min(slots, max(TILES - slots * index, 0))
        values = jnp.zeros((LANES, LANES), jnp.float32)
        if count:
            values = piece[slots * index : slots * index + count].astype(jnp.float32)
            values = values.reshape(count * group, LANES)
            if count < slots:
                gap = jnp.zeros((LANES - count * group, LANES), jnp.float32)
                values = jnp.concatenate([values, gap], axis=0)
            values = values.T
        turned.append(values)
    codes = [values[125:126, :] for values in turned]
    heads = [jnp.where(used, values, 0.0) for values in turned]
    for extra in range(half - TILES):
        place, slot = divmod(TILES + extra, slots)
        mask = ahead == slot
        code = pltpu.roll(turned[0][126:127, :], (slot - extra) * group % LANES, 1)
        codes[place] = jnp.where(mask, code, codes[place])
        for quarter in range(4):
            source, lanes = divmod(4 * extra + quarter, slots)
            values = turned[source][96:128]
            rows = lag[96:128]
            inside = jnp.logical_and(rows >= tlen, rows < tlen + QUARTER)
            values = jnp.where(inside, values, 0.0)
            values = pltpu.roll(values, (slot - lanes) * group % LANES, 1)
            start = QUARTER * quarter - (tlen - 96)
            values = jnp.concatenate([values, jnp.zeros((8, LANES), jnp.float32)], axis=0)
            values = pltpu.roll(values, start % 8, 0)
            start -= start % 8
            if start < 0:
                values, start = values[8:], 0
            below = LANES - start - values.shape[0]
            if start:
                values = jnp.concatenate([jnp.zeros((start, LANES), jnp.float32), values], axis=0)
            if below > 0:
                values = jnp.concatenate([values, jnp.zeros((below, LANES), jnp.float32)], axis=0)
            heads[place] = heads[place] + jnp.where(mask, values[0:LANES], 0.0)
    for index, (values, code) in enumerate(zip(heads, codes)):
        code = jnp.where(slots * index + ahead < half, code, 0.0)
        center = jnp.sum(values, axis=0, keepdims=True) / tlen
        deviate = jnp.where(used, values - center, 0.0)
        spread = jnp.sqrt(jnp.sum(deviate * deviate, axis=0, keepdims=True) / tlen + EPSILON)
        unit = (deviate / (spread * tlen)).astype(jnp.bfloat16).astype(jnp.float32)
        unit = jnp.where(code > 0, unit, 0.0)
        shift = code.astype(jnp.int32) - 1
        for bit in (1, 2, 4):
            unit = jnp.where(jnp.bitwise_and(shift, bit) > 0, pltpu.roll(unit, bit, 0), unit)
        unit = jnp.where(lag == 112, code, unit)
        bank[index] = unit.astype(jnp.bfloat16)

    def build(number):
        wide = jnp.dot(bank[number], expand[...], preferred_element_type=jnp.float32)
        for slot in range(slots):
            spreaded = wide[:, slot * LANES : (slot + 1) * LANES]
            code = spreaded[112:113, :].astype(jnp.int32)
            usable = code > 0
            shift = code - 1
            moves = shift // 8 + ahead
            taps = spreaded[0:112, :]
            for bit in (1, 2, 4, 8):
                gap = jnp.zeros((8 * bit, LANES), jnp.float32)
                taps = jnp.where(
                    jnp.bitwise_and(moves, bit) > 0,
                    jnp.concatenate([gap, taps], axis=0),
                    jnp.concatenate([taps, gap], axis=0),
                )[0:top]
            taps = taps.astype(jnp.bfloat16)
            item = number * slots + slot
            pick = jnp.logical_and(lag == shift + 8 * ahead, usable)
            pick = jnp.where(pick, 1.0, 0.0).astype(jnp.bfloat16)
            for index in range(tile_count):
                skip = 8 * offset_count * index
                lanes = slice(LANES * index, LANES * (index + 1))
                if skip:
                    weight_a[item, 0:skip, lanes] = jnp.zeros((skip, LANES), jnp.bfloat16)
                    pick = jnp.concatenate(
                        [jnp.zeros((skip, LANES), jnp.bfloat16), pick[0 : LANES - skip]], axis=0
                    )
                weight_a[item, skip : skip + top, lanes] = taps
                rest = DEPTH - top - skip
                if rest:
                    weight_a[item, skip + top :, lanes] = jnp.zeros((rest, LANES), jnp.bfloat16)
                weight_r[item, 0:LANES, lanes] = pick
                weight_r[item, LANES : 2 * LANES, lanes] = pick

    def apply(number, count):
        for slot in range(count):
            item = number * slots + slot
            corr = jnp.dot(left_a[base + item], weight_a[item], preferred_element_type=jnp.float32)
            factor = jnp.dot(
                left_r[base + item], weight_r[item], preferred_element_type=jnp.float32
            )
            total[...] += corr * factor

    total[...] = before[...] if side else jnp.zeros_like(total)
    build(0)

    @pl.loop(1, banks)
    def _(number):
        apply(number - 1, slots)
        build(number)

    apply(banks - 1, half - slots * (banks - 1))

    if not side:
        outs[0][...] = total[...]
        return
    rows_out = outs[0].shape[0]
    station = lax.axis_index("sta") % len(outs)
    for step, out in enumerate(outs):
        part = jnp.bitwise_xor(station, step)
        out[...] = total[pl.ds(pl.multiple_of(part * rows_out, rows_out), rows_out), :].astype(
            jnp.bfloat16
        )


def correlate(side, tlen, group, count, piece, left_a, left_r, *before):
    channels, rows, _ = left_a.shape
    width = OFFSETS * group
    half = channels // 2
    if side:
        out = [jax.ShapeDtypeStruct((rows // count, width), jnp.bfloat16)] * count
    else:
        out = [jax.ShapeDtypeStruct((rows, width), jnp.float32)]
    return pl.pallas_call(
        functools.partial(main_kernel, side, tlen, group),
        out_shape=out,
        in_specs=[VMEM] * (3 + len(before)),
        out_specs=[VMEM] * len(out),
        scratch_shapes=[
            pltpu.VMEM(((half + 1) * group // LANES, LANES, LANES), jnp.bfloat16),
            pltpu.VMEM((LANES, LANES // group * LANES), jnp.bfloat16),
            pltpu.VMEM((half + 1, DEPTH, width), jnp.bfloat16),
            pltpu.VMEM((half + 1, DEPTH, width), jnp.bfloat16),
            pltpu.VMEM((rows, width), jnp.float32),
        ],
        compiler_params=params(),
        cost_estimate=cost(3),
        name="correlate_" + ("second" if side else "first"),
    )(piece, left_a, left_r, *before)


def add_kernel(*refs):
    parts, keep, send = refs[:-2], refs[-2], refs[-1]
    rows = keep.shape[0]
    core = lax.axis_index("tm") % 2
    for out, which in ((keep, core), (send, 1 - core)):
        place = pl.ds(pl.multiple_of(which * rows, rows), rows)
        value = parts[0][place, :].astype(jnp.float32)
        for part in parts[1:]:
            value = value + part[place, :].astype(jnp.float32)
        out[...] = value


def add(parts):
    rows, width = parts[0].shape
    out = jax.ShapeDtypeStruct((rows // 2, width), jnp.float32)
    return pl.pallas_call(
        add_kernel,
        out_shape=[out, out],
        in_specs=[VMEM] * len(parts),
        out_specs=[VMEM, VMEM],
        compiler_params=params(),
        cost_estimate=cost(0.5),
        name="add",
    )(*parts)


def finish_kernel(group, ours, received, out):
    samples = out.shape[1]
    rows = ours.shape[0]
    value = ours[...] + received[...]
    high = value.astype(jnp.bfloat16).astype(jnp.float32)
    both = jnp.concatenate([high, value - high], axis=0).T.astype(jnp.bfloat16)
    row = lax.broadcasted_iota(jnp.int32, (2 * rows, samples), 0) % rows
    lane = lax.broadcasted_iota(jnp.int32, (2 * rows, samples), 1)
    place = jnp.logical_and(lane // STRIDE == row // 8, lane % 8 == 7 - row % 8)
    place = jnp.where(place, 1.0, 0.0).astype(jnp.bfloat16)
    wide = jnp.dot(both, place, preferred_element_type=jnp.float32)
    lane = lax.broadcasted_iota(jnp.int32, (group, samples), 1) // 8 % OFFSETS
    result = jnp.zeros((group, samples), jnp.float32)
    for offset in range(OFFSETS):
        result = jnp.where(lane == offset, wide[offset * group : (offset + 1) * group], result)
    out[...] = result


def finish(group, samples, ours, received):
    return pl.pallas_call(
        functools.partial(finish_kernel, group),
        out_shape=jax.ShapeDtypeStruct((group, samples), jnp.float32),
        in_specs=[VMEM, VMEM],
        out_specs=VMEM,
        compiler_params=params(),
        cost_estimate=cost(1),
        name="finish",
    )(ours, received)


def shards(waveforms, templates, available, moveout, bank_blocks):
    channels, samples = waveforms.shape
    blocks, events, _, tlen = templates.shape
    count_tm = lax.axis_size("tm")
    count_sta = lax.axis_size("sta")
    chips = count_tm // 2
    near = chips // 2
    group = 2 * events // chips

    def swap(array):
        return lax.ppermute(array, "tm", [(i, i ^ 1) for i in range(count_tm)])

    def across(array, step):
        return lax.ppermute(array, "tm", [(i, i ^ (2 * step)) for i in range(count_tm)])

    local = [waveforms] + [across(waveforms, step) for step in range(1, chips)]
    mine, theirs = pack(
        chips,
        group,
        bank_blocks,
        jnp.transpose(templates, (0, 2, 1, 3)),
        jnp.transpose(available, (2, 0, 1)),
        jnp.transpose(moveout, (2, 0, 1)),
    )
    other = swap(theirs)
    merged = merge(blocks, bank_blocks, mine, other)
    pieces = [across(merged[step], step) for step in reversed(range(1, chips))]
    pieces = [merged[0]] + pieces[::-1]
    left_a, left_r = prepare_waves(tlen, swap(choose_waves(local)), local)

    left_a, left_r, *pieces = lax.optimization_barrier((left_a, left_r, *pieces[::-1]))
    pieces = pieces[::-1]
    first = choose_piece(blocks, bank_blocks, pieces)
    second = swap(first)
    total = correlate(0, tlen, group, near, first, left_a, left_r)
    parts = correlate(1, tlen, group, near, second, left_a, left_r, *total)
    gathered = []
    for step in range(near):
        route = []
        for d in range(count_tm):
            for s in range(count_sta):
                dest = near * (d % 2) + (s % near ^ step)
                route.append((d * count_sta + s, (2 * dest + s // near) * count_sta + d // 2))
        gathered.append(lax.ppermute(parts[step], ("tm", "sta"), route))
    ours, send = add(gathered)
    return finish(group, samples, ours, swap(send))


def solution(mesh):
    in_specs = (
        P("sta", "tm"),
        P("tm", None, "sta", None),
        P("tm", None, "sta"),
        P("tm", None, "sta"),
        P(),
    )
    out_specs = P("sta", "tm")
    return jax.shard_map(shards, mesh=mesh, in_specs=in_specs, out_specs=out_specs, check_vma=False)
```

```python
import functools

import jax
import jax.numpy as jnp
from jax import lax
from jax.experimental import pallas as pl
from jax.experimental.pallas import tpu as pltpu
from jax.sharding import PartitionSpec as P

EPSILON = 1e-06
LANES = 128
OFFSETS = 8
TILES = 12
QUARTER = 25
STRIDE = 64
DEPTH = 256
VMEM_LIMIT = 28 * 1024 * 1024

VMEM = pl.BlockSpec(memory_space=pltpu.VMEM)
ANY = pl.BlockSpec(memory_space=pl.ANY)


def params():
    return pltpu.CompilerParams(vmem_limit_bytes=VMEM_LIMIT)


def cost(micros):
    return pl.CostEstimate(
        flops=int(micros * 1e9), bytes_accessed=int(micros * 1e6), transcendentals=0
    )


def pack_kernel(bank_blocks, templates, available, moveout, mine, theirs, owners, chosen, raw, usable, shifts, square, packed, sems):
    blocks, channels, events, tlen = templates.shape
    chips, _, group, _ = mine.shape
    half = channels // 2
    me = lax.axis_index("tm") % 2
    fetch = [
        pltpu.make_async_copy(source, target, sems.at[index])
        for index, (source, target) in enumerate(
            ((bank_blocks, chosen), (available, usable), (moveout, shifts), (templates, raw))
        )
    ]
    for copy in fetch:
        copy.start()
    packed[...] = jnp.zeros_like(packed)
    square[...] = jnp.zeros_like(square)
    for copy in fetch[:3]:
        copy.wait()
    slots = [chosen[which] % blocks for which in range(2)]
    row = lax.broadcasted_iota(jnp.int32, owners.shape, 0)
    owners[...] = jnp.where(row == 0, chosen[0] // blocks, chosen[1] // blocks)
    flags = jnp.where(usable[...] > 0, shifts[...] + 1, 0).astype(jnp.float32)
    turned = []
    for which in range(2):
        code = flags[:, 0, :]
        for block in range(1, blocks):
            code = jnp.where(slots[which] == block, flags[:, block, :], code)
        square[0:channels, 0:events] = code
        turned.append(square[...].T.astype(jnp.bfloat16))
    fetch[3].wait()
    for which in range(2):
        for core in range(2):
            for tile in range(TILES):
                channel = half * core + tile
                extra = half * core + TILES + tile // 4
                start = QUARTER * (tile % 4)
                for index in range(events // group):
                    chip = which * (events // group) + index
                    rows = slice(index * group, (index + 1) * group)
                    packed[core, chip, tile, :, 0:tlen] = raw[slots[which], channel, rows, :]
                    packed[core, chip, tile, :, tlen : tlen + QUARTER] = raw[
                        slots[which], extra, rows, start : start + QUARTER
                    ]
                    packed[core, chip, tile, :, 125:126] = turned[which][rows, channel : channel + 1]
                    if tile < half - TILES:
                        beyond = channel + TILES
                        packed[core, chip, tile, :, 126:127] = turned[which][rows, beyond : beyond + 1]
    mine[...] = packed[me]
    theirs[...] = packed[1 - me]


def pack(chips, group, bank_blocks, templates, available, moveout):
    shape = (chips, TILES, group, LANES)
    held = [
        pltpu.with_memory_space_constraint(array, pltpu.HBM)
        for array in (bank_blocks, templates, available, moveout)
    ]
    return pl.pallas_call(
        pack_kernel,
        out_shape=[jax.ShapeDtypeStruct(shape, jnp.bfloat16)] * 2
        + [jax.ShapeDtypeStruct((8, LANES), jnp.int32)],
        in_specs=[ANY] * 4,
        out_specs=[VMEM] * 3,
        scratch_shapes=[
            pltpu.SMEM(bank_blocks.shape, jnp.int32),
            pltpu.VMEM(templates.shape, jnp.bfloat16),
            pltpu.VMEM(available.shape, jnp.int32),
            pltpu.VMEM(moveout.shape, jnp.int32),
            pltpu.VMEM((LANES, LANES), jnp.float32),
            pltpu.VMEM((2,) + shape, jnp.bfloat16),
            pltpu.SemaphoreType.DMA((4,)),
        ],
        compiler_params=params(),
        cost_estimate=cost(2),
        name="pack",
    )(*held)


def merge_kernel(owners, mine, other, *outs):
    chips = len(outs)
    me = lax.axis_index("tm")
    for step, out in enumerate(outs):
        dest = jnp.bitwise_xor(me // 2, step)
        owner = jnp.where(dest < chips // 2, owners[0, 0], owners[1, 0])
        here = owner % 2 == me % 2

        @pl.when(here)
        def _():
            out[...] = mine[dest]

        @pl.when(jnp.logical_not(here))
        def _():
            out[...] = other[dest]


def merge(owners, mine, other):
    chips = mine.shape[0]
    return pl.pallas_call(
        merge_kernel,
        out_shape=[jax.ShapeDtypeStruct(mine.shape[1:], mine.dtype)] * chips,
        in_specs=[VMEM] * 3,
        out_specs=[VMEM] * chips,
        compiler_params=params(),
        cost_estimate=cost(0.3),
        name="merge",
    )(owners, mine, other)


def lagged(row, ahead):
    copies = jnp.broadcast_to(row, (8, row.shape[1]))
    return pltpu.roll(copies, row.shape[1] - 7 - ahead, 1, stride=1, stride_axis=0)


def pick(arrays, index):
    entries = [array.at[place] for array in arrays for place in range(array.shape[0])]
    value = entries[0][...]
    for number, entry in enumerate(entries[1:], 1):
        value = jnp.where(index == number, entry[...], value)
    return value


def choose_kernel(*refs):
    waves, out = refs[:-1], refs[-1]
    near = out.shape[0]
    me = lax.axis_index("tm")
    for step in range(near):
        out[step] = pick(waves, jnp.bitwise_xor(me // 2, near * (1 - me % 2) + step))


def choose_waves(near, waves):
    return pl.pallas_call(
        choose_kernel,
        out_shape=jax.ShapeDtypeStruct((near,) + waves[0].shape[1:], waves[0].dtype),
        in_specs=[VMEM] * len(waves),
        out_specs=VMEM,
        compiler_params=params(),
        cost_estimate=cost(0.05),
        name="choose_waves",
    )(*waves)


def own_kernel(owners, *refs):
    pieces, out = refs[:-1], refs[-1]
    chip = lax.axis_index("tm") // 2
    owner = jnp.where(chip < len(pieces) // 2, owners[0, 0], owners[1, 0])
    source = jnp.bitwise_xor(owner // 2, chip)
    value = pieces[0][...]
    for number, piece in enumerate(pieces[1:], 1):
        value = jnp.where(source == number, piece[...], value)
    out[...] = value


def choose_piece(owners, pieces):
    return pl.pallas_call(
        own_kernel,
        out_shape=jax.ShapeDtypeStruct(pieces[0].shape, pieces[0].dtype),
        in_specs=[VMEM] * (1 + len(pieces)),
        out_specs=VMEM,
        compiler_params=params(),
        cost_estimate=cost(0.3),
        name="choose_piece",
    )(owners, *pieces)


def waves_kernel(channels, tlen, unroll, swapped, *rest):
    local = rest[:-4]
    left_a, left_r, padded, inverse = rest[-4:]
    near, _, samples = swapped.shape
    chips = 2 * near
    length = chips * samples
    count = padded.shape[1] // LANES
    me = lax.axis_index("tm")
    chip, core = me // 2, me % 2
    padded[...] = jnp.zeros_like(padded)
    for index in range(chips):
        wave = pick(local, jnp.bitwise_xor(chip, near * core + index // 2))
        wave = jnp.where(core == index % 2, wave, swapped[index // 2])
        padded[0:channels, samples * index : samples * (index + 1)] = wave.astype(jnp.float32)
    rim = pick(local, jnp.bitwise_xor(chip, near))[:, 0 : padded.shape[1] - length]
    padded[0:channels, length:] = jnp.where(core == 0, rim.astype(jnp.float32), 0.0)

    rows = 32 * count
    values = [padded[:, LANES * tile : LANES * (tile + 1)] for tile in range(count)]
    values = jnp.concatenate(values + [jnp.zeros((32, LANES), jnp.float32)], axis=0)
    square = values * values
    high = square.astype(jnp.bfloat16)
    low = (square - high.astype(jnp.float32)).astype(jnp.bfloat16)
    values = values.astype(jnp.bfloat16)
    lag = lax.broadcasted_iota(jnp.int32, (2 * LANES, LANES), 0)
    lag = lag - lax.broadcasted_iota(jnp.int32, (2 * LANES, LANES), 1)
    band = jnp.where(jnp.logical_and(lag >= 0, lag < tlen), 1.0, 0.0).astype(jnp.bfloat16)

    def windows(array):
        both = jnp.concatenate([array[0:rows], array[32 : rows + 32]], axis=1)
        return jnp.dot(both, band, preferred_element_type=jnp.float32)

    mean = windows(values) / tlen
    scale = lax.rsqrt((windows(high) + windows(low)) / tlen - mean * mean + EPSILON)
    for tile in range(count):
        inverse[:, LANES * tile : LANES * (tile + 1)] = scale[32 * tile : 32 * (tile + 1)]

    def interleaved(row, tiles):
        even, odd = lagged(row, 0), lagged(row, STRIDE)
        parts = []
        for tile in range(tiles):
            lanes = slice(LANES * tile, LANES * (tile + 1))
            parts += [even[:, lanes], odd[:, lanes]]
        return jnp.concatenate(parts, axis=0)

    @pl.loop(0, channels // unroll)
    def _(step):
        for item in range(unroll):
            channel = step * unroll + item
            value = interleaved(padded[pl.ds(channel, 1), :], length // LANES + 1)
            left_a[channel] = value.astype(jnp.bfloat16)
            value = interleaved(inverse[pl.ds(channel, 1), :], length // LANES)
            high = value.astype(jnp.bfloat16)
            left_r[channel, :, 0:LANES] = high
            left_r[channel, :, LANES:] = (value - high.astype(jnp.float32)).astype(jnp.bfloat16)


def prepare_waves(tlen, swapped, local):
    near, channels, samples = swapped.shape
    length = 2 * near * samples
    rows = length // OFFSETS
    unroll = max(step for step in (1, 2, 3) if channels % step == 0)
    return pl.pallas_call(
        functools.partial(waves_kernel, channels, tlen, unroll),
        out_shape=[
            jax.ShapeDtypeStruct((channels, rows + 16, LANES), jnp.bfloat16),
            jax.ShapeDtypeStruct((channels, rows, 2 * LANES), jnp.bfloat16),
        ],
        in_specs=[VMEM] * (1 + len(local)),
        out_specs=[VMEM, VMEM],
        scratch_shapes=[
            pltpu.VMEM((32, length + 2 * LANES), jnp.float32),
            pltpu.VMEM((32, length + 2 * LANES), jnp.float32),
        ],
        compiler_params=params(),
        cost_estimate=cost(0.05),
        name="prepare_waves",
    )(swapped, *local)


def main_kernel(side, tlen, group, piece, left_a, left_r, *rest):
    outs = rest[:-5]
    if side:
        before, outs = outs[0], outs[1:]
    bank, expand, weight_a, weight_r, total = rest[-5:]
    core = lax.axis_index("tm") % 2
    channels, rows, _ = left_r.shape
    half = channels // 2
    base = half * jnp.where(core == side, 0, 1)
    slots = LANES // group
    banks = (half + 1) // slots
    offset_count = LANES // group
    tile_count = OFFSETS // offset_count
    top = 112 + 8 * (7 + offset_count - 1)
    top = top + top % 16

    lag = lax.broadcasted_iota(jnp.int32, (LANES, LANES), 0)
    target = lax.broadcasted_iota(jnp.int32, (LANES, LANES), 1)
    lane = lax.broadcasted_iota(jnp.int32, (1, LANES), 1)
    used = lag < tlen
    ahead = lane // group
    for slot in range(slots):
        chosen = jnp.where(lag == target % group + slot * group, 1.0, 0.0)
        expand[:, slot * LANES : (slot + 1) * LANES] = chosen.astype(jnp.bfloat16)
    turned = []
    for index in range(banks):
        count = min(slots, max(TILES - slots * index, 0))
        values = jnp.zeros((LANES, LANES), jnp.float32)
        if count:
            values = piece[slots * index : slots * index + count].astype(jnp.float32)
            values = values.reshape(count * group, LANES)
            if count < slots:
                gap = jnp.zeros((LANES - count * group, LANES), jnp.float32)
                values = jnp.concatenate([values, gap], axis=0)
            values = values.T
        turned.append(values)
    codes = [values[125:126, :] for values in turned]
    heads = [jnp.where(used, values, 0.0) for values in turned]
    for extra in range(half - TILES):
        place, slot = divmod(TILES + extra, slots)
        mask = ahead == slot
        code = pltpu.roll(turned[0][126:127, :], (slot - extra) * group % LANES, 1)
        codes[place] = jnp.where(mask, code, codes[place])
        for quarter in range(4):
            source, lanes = divmod(4 * extra + quarter, slots)
            values = turned[source][96:128]
            sample = lag[96:128]
            inside = jnp.logical_and(sample >= tlen, sample < tlen + QUARTER)
            values = jnp.where(inside, values, 0.0)
            values = pltpu.roll(values, (slot - lanes) * group % LANES, 1)
            start = QUARTER * quarter - (tlen - 96)
            values = jnp.concatenate([values, jnp.zeros((8, LANES), jnp.float32)], axis=0)
            values = pltpu.roll(values, start % 8, 0)
            start -= start % 8
            if start < 0:
                values, start = values[8:], 0
            below = LANES - start - values.shape[0]
            if start:
                values = jnp.concatenate([jnp.zeros((start, LANES), jnp.float32), values], axis=0)
            if below > 0:
                values = jnp.concatenate([values, jnp.zeros((below, LANES), jnp.float32)], axis=0)
            heads[place] = heads[place] + jnp.where(mask, values[0:LANES], 0.0)
    for index, (values, code) in enumerate(zip(heads, codes)):
        code = jnp.where(slots * index + ahead < half, code, 0.0)
        center = jnp.sum(values, axis=0, keepdims=True) / tlen
        deviate = jnp.where(used, values - center, 0.0)
        spread = jnp.sqrt(jnp.sum(deviate * deviate, axis=0, keepdims=True) / tlen + EPSILON)
        unit = (deviate / (spread * tlen)).astype(jnp.bfloat16).astype(jnp.float32)
        unit = jnp.where(code > 0, unit, 0.0)
        shift = code.astype(jnp.int32) - 1
        for bit in (1, 2, 4):
            unit = jnp.where(jnp.bitwise_and(shift, bit) > 0, pltpu.roll(unit, bit, 0), unit)
        unit = jnp.where(lag == 112, code, unit)
        bank[index] = unit.astype(jnp.bfloat16)

    def build(number):
        wide = jnp.dot(bank[number], expand[...], preferred_element_type=jnp.float32)
        for slot in range(slots):
            spreaded = wide[:, slot * LANES : (slot + 1) * LANES]
            code = spreaded[112:113, :].astype(jnp.int32)
            usable = code > 0
            shift = code - 1
            moves = shift // 8 + ahead
            taps = spreaded[0:112, :]
            for bit in (1, 2, 4, 8):
                gap = jnp.zeros((8 * bit, LANES), jnp.float32)
                taps = jnp.where(
                    jnp.bitwise_and(moves, bit) > 0,
                    jnp.concatenate([gap, taps], axis=0),
                    jnp.concatenate([taps, gap], axis=0),
                )[0:top]
            taps = taps.astype(jnp.bfloat16)
            item = number * slots + slot
            pick = jnp.logical_and(lag == shift + 8 * ahead, usable)
            pick = jnp.where(pick, 1.0, 0.0).astype(jnp.bfloat16)
            for index in range(tile_count):
                skip = 8 * offset_count * index
                lanes = slice(LANES * index, LANES * (index + 1))
                if skip:
                    weight_a[item, 0:skip, lanes] = jnp.zeros((skip, LANES), jnp.bfloat16)
                    pick = jnp.concatenate(
                        [jnp.zeros((skip, LANES), jnp.bfloat16), pick[0 : LANES - skip]], axis=0
                    )
                weight_a[item, skip : skip + top, lanes] = taps
                rest = DEPTH - top - skip
                if rest:
                    weight_a[item, skip + top :, lanes] = jnp.zeros((rest, LANES), jnp.bfloat16)
                weight_r[item, 0:LANES, lanes] = pick
                weight_r[item, LANES : 2 * LANES, lanes] = pick

    def apply(number, count):
        for slot in range(count):
            item = number * slots + slot
            both = [left_a[base + item, 0:rows, :], left_a[base + item, 16 : rows + 16, :]]
            corr = jnp.dot(
                jnp.concatenate(both, axis=1), weight_a[item], preferred_element_type=jnp.float32
            )
            factor = jnp.dot(
                left_r[base + item], weight_r[item], preferred_element_type=jnp.float32
            )
            total[...] += corr * factor

    total[...] = before[...] if side else jnp.zeros_like(total)
    build(0)

    @pl.loop(1, banks)
    def _(number):
        apply(number - 1, slots)
        build(number)

    apply(banks - 1, half - slots * (banks - 1))

    if not side:
        outs[0][...] = total[...]
        return
    rows_out = outs[0].shape[0]
    station = lax.axis_index("sta") % len(outs)
    for step, out in enumerate(outs):
        part = jnp.bitwise_xor(station, step)
        out[...] = total[pl.ds(pl.multiple_of(part * rows_out, rows_out), rows_out), :].astype(
            jnp.bfloat16
        )


def correlate(side, tlen, group, count, piece, left_a, left_r, *before):
    channels, rows, _ = left_r.shape
    width = OFFSETS * group
    half = channels // 2
    if side:
        out = [jax.ShapeDtypeStruct((rows // count, width), jnp.bfloat16)] * count
    else:
        out = [jax.ShapeDtypeStruct((rows, width), jnp.float32)]
    return pl.pallas_call(
        functools.partial(main_kernel, side, tlen, group),
        out_shape=out,
        in_specs=[VMEM] * (3 + len(before)),
        out_specs=[VMEM] * len(out),
        scratch_shapes=[
            pltpu.VMEM(((half + 1) * group // LANES, LANES, LANES), jnp.bfloat16),
            pltpu.VMEM((LANES, LANES // group * LANES), jnp.bfloat16),
            pltpu.VMEM((half + 1, DEPTH, width), jnp.bfloat16),
            pltpu.VMEM((half + 1, DEPTH, width), jnp.bfloat16),
            pltpu.VMEM((rows, width), jnp.float32),
        ],
        compiler_params=params(),
        cost_estimate=cost(3),
        name="correlate_" + ("second" if side else "first"),
    )(piece, left_a, left_r, *before)


def add_kernel(*refs):
    parts, keep, send = refs[:-2], refs[-2], refs[-1]
    rows = keep.shape[0]
    core = lax.axis_index("tm") % 2
    for out, which in ((keep, core), (send, 1 - core)):
        place = pl.ds(pl.multiple_of(which * rows, rows), rows)
        value = parts[0][place, :].astype(jnp.float32)
        for part in parts[1:]:
            value = value + part[place, :].astype(jnp.float32)
        out[...] = value


def add(parts):
    rows, width = parts[0].shape
    out = jax.ShapeDtypeStruct((rows // 2, width), jnp.float32)
    return pl.pallas_call(
        add_kernel,
        out_shape=[out, out],
        in_specs=[VMEM] * len(parts),
        out_specs=[VMEM, VMEM],
        compiler_params=params(),
        cost_estimate=cost(0.5),
        name="add",
    )(*parts)


def finish_kernel(group, ours, received, out):
    samples = out.shape[1]
    rows = ours.shape[0]
    value = ours[...] + received[...]
    high = value.astype(jnp.bfloat16).astype(jnp.float32)
    both = jnp.concatenate([high, value - high], axis=0).T.astype(jnp.bfloat16)
    row = lax.broadcasted_iota(jnp.int32, (2 * rows, samples), 0) % rows
    lane = lax.broadcasted_iota(jnp.int32, (2 * rows, samples), 1)
    place = jnp.logical_and(lane // STRIDE == row // 8, lane % 8 == 7 - row % 8)
    place = jnp.where(place, 1.0, 0.0).astype(jnp.bfloat16)
    wide = jnp.dot(both, place, preferred_element_type=jnp.float32)
    lane = lax.broadcasted_iota(jnp.int32, (group, samples), 1) // 8 % OFFSETS
    result = jnp.zeros((group, samples), jnp.float32)
    for offset in range(OFFSETS):
        result = jnp.where(lane == offset, wide[offset * group : (offset + 1) * group], result)
    out[...] = result


def finish(group, samples, ours, received):
    return pl.pallas_call(
        functools.partial(finish_kernel, group),
        out_shape=jax.ShapeDtypeStruct((group, samples), jnp.float32),
        in_specs=[VMEM, VMEM],
        out_specs=VMEM,
        compiler_params=params(),
        cost_estimate=cost(1),
        name="finish",
    )(ours, received)


def shards(waveforms, templates, available, moveout, bank_blocks):
    channels, samples = waveforms.shape
    blocks, events, _, tlen = templates.shape
    count_tm = lax.axis_size("tm")
    count_sta = lax.axis_size("sta")
    chips = count_tm // 2
    near = chips // 2
    group = 2 * events // chips

    def swap(array):
        return lax.ppermute(array, "tm", [(i, i ^ 1) for i in range(count_tm)])

    def across(array, step):
        return lax.ppermute(array, "tm", [(i, i ^ (2 * step)) for i in range(count_tm)])

    local = [waveforms[None]]
    for bit in range(chips.bit_length() - 1):
        local.append(across(jnp.concatenate(local), 1 << bit))
    mine, theirs, owners = pack(
        chips,
        group,
        bank_blocks,
        jnp.transpose(templates, (0, 2, 1, 3)),
        jnp.transpose(available, (2, 0, 1)),
        jnp.transpose(moveout, (2, 0, 1)),
    )
    other = swap(theirs)
    merged = merge(owners, mine, other)
    pieces = [across(merged[step], step) for step in reversed(range(1, chips))]
    pieces = [merged[0]] + pieces[::-1]
    left_a, left_r = prepare_waves(tlen, swap(choose_waves(near, local)), local)

    left_a, left_r, *pieces = lax.optimization_barrier((left_a, left_r, *pieces[::-1]))
    pieces = pieces[::-1]
    first = choose_piece(owners, pieces)
    second = swap(first)
    total = correlate(0, tlen, group, near, first, left_a, left_r)
    parts = correlate(1, tlen, group, near, second, left_a, left_r, *total)
    gathered = []
    for step in range(near):
        route = []
        for d in range(count_tm):
            for s in range(count_sta):
                dest = near * (d % 2) + (s % near ^ step)
                route.append((d * count_sta + s, (2 * dest + s // near) * count_sta + d // 2))
        gathered.append(lax.ppermute(parts[step], ("tm", "sta"), route))
    ours, send = add(gathered)
    return finish(group, samples, ours, swap(send))


def solution(mesh):
    in_specs = (
        P("sta", "tm"),
        P("tm", None, "sta", None),
        P("tm", None, "sta"),
        P("tm", None, "sta"),
        P(),
    )
    out_specs = P("sta", "tm")
    return jax.shard_map(shards, mesh=mesh, in_specs=in_specs, out_specs=out_specs, check_vma=False)
```

```python
import functools

import jax
import jax.numpy as jnp
from jax import lax
from jax.experimental import pallas as pl
from jax.experimental.pallas import tpu as pltpu
from jax.sharding import PartitionSpec as P

EPSILON = 1e-06
LANES = 128
OFFSETS = 8
TILES = 12
QUARTER = 25
STRIDE = 64
DEPTH = 256
VMEM_LIMIT = 28 * 1024 * 1024

VMEM = pl.BlockSpec(memory_space=pltpu.VMEM)
ANY = pl.BlockSpec(memory_space=pl.ANY)


def params():
    return pltpu.CompilerParams(vmem_limit_bytes=VMEM_LIMIT)


def cost(micros):
    return pl.CostEstimate(
        flops=int(micros * 1e9), bytes_accessed=int(micros * 1e6), transcendentals=0
    )


def pack_kernel(bank_blocks, templates, available, moveout, mine, theirs, owners, chosen, raw, usable, shifts, square, packed, sems):
    blocks, channels, events, tlen = templates.shape
    chips, _, group, _ = mine.shape
    half = channels // 2
    me = lax.axis_index("tm") % 2
    fetch = [
        pltpu.make_async_copy(source, target, sems.at[index])
        for index, (source, target) in enumerate(
            ((bank_blocks, chosen), (available, usable), (moveout, shifts), (templates, raw))
        )
    ]
    for copy in fetch:
        copy.start()
    packed[...] = jnp.zeros_like(packed)
    square[...] = jnp.zeros_like(square)
    for copy in fetch[:3]:
        copy.wait()
    slots = [chosen[which] % blocks for which in range(2)]
    row = lax.broadcasted_iota(jnp.int32, owners.shape, 0)
    owners[...] = jnp.where(row == 0, chosen[0] // blocks, chosen[1] // blocks)
    flags = jnp.where(usable[...] > 0, shifts[...] + 1, 0).astype(jnp.float32)
    turned = []
    for which in range(2):
        code = flags[:, 0, :]
        for block in range(1, blocks):
            code = jnp.where(slots[which] == block, flags[:, block, :], code)
        square[0:channels, 0:events] = code
        turned.append(square[...].T.astype(jnp.bfloat16))
    fetch[3].wait()
    for which in range(2):
        for core in range(2):
            for tile in range(TILES):
                channel = half * core + tile
                extra = half * core + TILES + tile // 4
                start = QUARTER * (tile % 4)
                for index in range(events // group):
                    chip = which * (events // group) + index
                    rows = slice(index * group, (index + 1) * group)
                    packed[core, chip, tile, :, 0:tlen] = raw[slots[which], channel, rows, :]
                    packed[core, chip, tile, :, tlen : tlen + QUARTER] = raw[
                        slots[which], extra, rows, start : start + QUARTER
                    ]
                    packed[core, chip, tile, :, 125:126] = turned[which][rows, channel : channel + 1]
                    if tile < half - TILES:
                        beyond = channel + TILES
                        packed[core, chip, tile, :, 126:127] = turned[which][rows, beyond : beyond + 1]
    mine[...] = packed[me]
    theirs[...] = packed[1 - me]


def pack(chips, group, bank_blocks, templates, available, moveout):
    shape = (chips, TILES, group, LANES)
    held = [
        pltpu.with_memory_space_constraint(array, pltpu.HBM)
        for array in (bank_blocks, templates, available, moveout)
    ]
    return pl.pallas_call(
        pack_kernel,
        out_shape=[jax.ShapeDtypeStruct(shape, jnp.bfloat16)] * 2
        + [jax.ShapeDtypeStruct((8, LANES), jnp.int32)],
        in_specs=[ANY] * 4,
        out_specs=[VMEM] * 3,
        scratch_shapes=[
            pltpu.SMEM(bank_blocks.shape, jnp.int32),
            pltpu.VMEM(templates.shape, jnp.bfloat16),
            pltpu.VMEM(available.shape, jnp.int32),
            pltpu.VMEM(moveout.shape, jnp.int32),
            pltpu.VMEM((LANES, LANES), jnp.float32),
            pltpu.VMEM((2,) + shape, jnp.bfloat16),
            pltpu.SemaphoreType.DMA((4,)),
        ],
        compiler_params=params(),
        cost_estimate=cost(2),
        name="pack",
    )(*held)


def merge_kernel(owners, mine, other, *outs):
    chips = len(outs)
    me = lax.axis_index("tm")
    for step, out in enumerate(outs):
        dest = jnp.bitwise_xor(me // 2, step)
        owner = jnp.where(dest < chips // 2, owners[0, 0], owners[1, 0])
        here = owner % 2 == me % 2

        @pl.when(here)
        def _():
            out[...] = mine[dest]

        @pl.when(jnp.logical_not(here))
        def _():
            out[...] = other[dest]


def merge(owners, mine, other):
    chips = mine.shape[0]
    return pl.pallas_call(
        merge_kernel,
        out_shape=[jax.ShapeDtypeStruct(mine.shape[1:], mine.dtype)] * chips,
        in_specs=[VMEM] * 3,
        out_specs=[VMEM] * chips,
        compiler_params=params(),
        cost_estimate=cost(0.3),
        name="merge",
    )(owners, mine, other)


def lagged(row, ahead):
    copies = jnp.broadcast_to(row, (8, row.shape[1]))
    return pltpu.roll(copies, row.shape[1] - 7 - ahead, 1, stride=1, stride_axis=0)


def pick(arrays, index):
    entries = [array.at[place] for array in arrays for place in range(array.shape[0])]
    value = entries[0][...]
    for number, entry in enumerate(entries[1:], 1):
        value = jnp.where(index == number, entry[...], value)
    return value


def choose_kernel(*refs):
    waves, out = refs[:-1], refs[-1]
    near = out.shape[0]
    me = lax.axis_index("tm")
    for step in range(near):
        out[step] = pick(waves, jnp.bitwise_xor(me // 2, near * (1 - me % 2) + step))


def choose_waves(near, waves):
    return pl.pallas_call(
        choose_kernel,
        out_shape=jax.ShapeDtypeStruct((near,) + waves[0].shape[1:], waves[0].dtype),
        in_specs=[VMEM] * len(waves),
        out_specs=VMEM,
        compiler_params=params(),
        cost_estimate=cost(0.05),
        name="choose_waves",
    )(*waves)


def own_kernel(owners, *refs):
    pieces, out = refs[:-1], refs[-1]
    chip = lax.axis_index("tm") // 2
    owner = jnp.where(chip < len(pieces) // 2, owners[0, 0], owners[1, 0])
    source = jnp.bitwise_xor(owner // 2, chip)
    value = pieces[0][...]
    for number, piece in enumerate(pieces[1:], 1):
        value = jnp.where(source == number, piece[...], value)
    out[...] = value


def choose_piece(owners, pieces):
    return pl.pallas_call(
        own_kernel,
        out_shape=jax.ShapeDtypeStruct(pieces[0].shape, pieces[0].dtype),
        in_specs=[VMEM] * (1 + len(pieces)),
        out_specs=VMEM,
        compiler_params=params(),
        cost_estimate=cost(0.3),
        name="choose_piece",
    )(owners, *pieces)


def waves_kernel(channels, tlen, unroll, swapped, *rest):
    local = rest[:-4]
    left_a, left_r, padded, inverse = rest[-4:]
    near, _, samples = swapped.shape
    chips = 2 * near
    length = chips * samples
    count = padded.shape[1] // LANES
    me = lax.axis_index("tm")
    chip, core = me // 2, me % 2
    padded[...] = jnp.zeros_like(padded)
    for index in range(chips):
        wave = pick(local, jnp.bitwise_xor(chip, near * core + index // 2))
        wave = jnp.where(core == index % 2, wave, swapped[index // 2])
        padded[0:channels, samples * index : samples * (index + 1)] = wave.astype(jnp.float32)
    rim = pick(local, jnp.bitwise_xor(chip, near))[:, 0 : padded.shape[1] - length]
    padded[0:channels, length:] = jnp.where(core == 0, rim.astype(jnp.float32), 0.0)

    rows = 32 * count
    values = [padded[:, LANES * tile : LANES * (tile + 1)] for tile in range(count)]
    values = jnp.concatenate(values + [jnp.zeros((32, LANES), jnp.float32)], axis=0)
    square = values * values
    high = square.astype(jnp.bfloat16)
    low = (square - high.astype(jnp.float32)).astype(jnp.bfloat16)
    values = values.astype(jnp.bfloat16)
    lag = lax.broadcasted_iota(jnp.int32, (2 * LANES, LANES), 0)
    lag = lag - lax.broadcasted_iota(jnp.int32, (2 * LANES, LANES), 1)
    band = jnp.where(jnp.logical_and(lag >= 0, lag < tlen), 1.0, 0.0).astype(jnp.bfloat16)

    def windows(array):
        both = jnp.concatenate([array[0:rows], array[32 : rows + 32]], axis=1)
        return jnp.dot(both, band, preferred_element_type=jnp.float32)

    mean = windows(values) / tlen
    scale = lax.rsqrt((windows(high) + windows(low)) / tlen - mean * mean + EPSILON)
    for tile in range(count):
        inverse[:, LANES * tile : LANES * (tile + 1)] = scale[32 * tile : 32 * (tile + 1)]

    def interleaved(row, tiles):
        even, odd = lagged(row, 0), lagged(row, STRIDE)
        parts = []
        for tile in range(tiles):
            lanes = slice(LANES * tile, LANES * (tile + 1))
            parts += [even[:, lanes], odd[:, lanes]]
        return jnp.concatenate(parts, axis=0)

    @pl.loop(0, channels // unroll)
    def _(step):
        for item in range(unroll):
            channel = step * unroll + item
            value = interleaved(padded[pl.ds(channel, 1), :], length // LANES + 1)
            left_a[channel] = value.astype(jnp.bfloat16)
            value = interleaved(inverse[pl.ds(channel, 1), :], length // LANES)
            high = value.astype(jnp.bfloat16)
            left_r[channel, :, 0:LANES] = high
            left_r[channel, :, LANES:] = (value - high.astype(jnp.float32)).astype(jnp.bfloat16)


def prepare_waves(tlen, swapped, local):
    near, channels, samples = swapped.shape
    length = 2 * near * samples
    rows = length // OFFSETS
    unroll = max(step for step in (1, 2, 3) if channels % step == 0)
    return pl.pallas_call(
        functools.partial(waves_kernel, channels, tlen, unroll),
        out_shape=[
            jax.ShapeDtypeStruct((channels, rows + 16, LANES), jnp.bfloat16),
            jax.ShapeDtypeStruct((channels, rows, 2 * LANES), jnp.bfloat16),
        ],
        in_specs=[VMEM] * (1 + len(local)),
        out_specs=[VMEM, VMEM],
        scratch_shapes=[
            pltpu.VMEM((32, length + 2 * LANES), jnp.float32),
            pltpu.VMEM((32, length + 2 * LANES), jnp.float32),
        ],
        compiler_params=params(),
        cost_estimate=cost(0.05),
        name="prepare_waves",
    )(swapped, *local)


def main_kernel(side, tlen, group, piece, left_a, left_r, *rest):
    outs = rest[:-5]
    if side:
        before, outs = outs[0], outs[1:]
    bank, expand, weight_a, weight_r, total = rest[-5:]
    core = lax.axis_index("tm") % 2
    channels, rows, _ = left_r.shape
    half = channels // 2
    base = half * jnp.where(core == side, 0, 1)
    slots = LANES // group
    banks = (half + 1) // slots
    offset_count = LANES // group
    tile_count = OFFSETS // offset_count
    top = 112 + 8 * (7 + offset_count - 1)
    top = top + top % 16

    lag = lax.broadcasted_iota(jnp.int32, (LANES, LANES), 0)
    target = lax.broadcasted_iota(jnp.int32, (LANES, LANES), 1)
    lane = lax.broadcasted_iota(jnp.int32, (1, LANES), 1)
    used = lag < tlen
    ahead = lane // group
    for slot in range(slots):
        chosen = jnp.where(lag == target % group + slot * group, 1.0, 0.0)
        expand[:, slot * LANES : (slot + 1) * LANES] = chosen.astype(jnp.bfloat16)
    turned = []
    for index in range(banks):
        count = min(slots, max(TILES - slots * index, 0))
        values = jnp.zeros((LANES, LANES), jnp.float32)
        if count:
            values = piece[slots * index : slots * index + count].astype(jnp.float32)
            values = values.reshape(count * group, LANES)
            if count < slots:
                gap = jnp.zeros((LANES - count * group, LANES), jnp.float32)
                values = jnp.concatenate([values, gap], axis=0)
            values = values.T
        turned.append(values)
    codes = [values[125:126, :] for values in turned]
    heads = [jnp.where(used, values, 0.0) for values in turned]
    for extra in range(half - TILES):
        place, slot = divmod(TILES + extra, slots)
        mask = ahead == slot
        code = pltpu.roll(turned[0][126:127, :], (slot - extra) * group % LANES, 1)
        codes[place] = jnp.where(mask, code, codes[place])
        for quarter in range(4):
            source, lanes = divmod(4 * extra + quarter, slots)
            values = turned[source][96:128]
            sample = lag[96:128]
            inside = jnp.logical_and(sample >= tlen, sample < tlen + QUARTER)
            values = jnp.where(inside, values, 0.0)
            values = pltpu.roll(values, (slot - lanes) * group % LANES, 1)
            start = QUARTER * quarter - (tlen - 96)
            values = jnp.concatenate([values, jnp.zeros((8, LANES), jnp.float32)], axis=0)
            values = pltpu.roll(values, start % 8, 0)
            start -= start % 8
            if start < 0:
                values, start = values[8:], 0
            below = LANES - start - values.shape[0]
            if start:
                values = jnp.concatenate([jnp.zeros((start, LANES), jnp.float32), values], axis=0)
            if below > 0:
                values = jnp.concatenate([values, jnp.zeros((below, LANES), jnp.float32)], axis=0)
            heads[place] = heads[place] + jnp.where(mask, values[0:LANES], 0.0)
    for index, (values, code) in enumerate(zip(heads, codes)):
        code = jnp.where(slots * index + ahead < half, code, 0.0)
        center = jnp.sum(values, axis=0, keepdims=True) / tlen
        deviate = jnp.where(used, values - center, 0.0)
        spread = jnp.sqrt(jnp.sum(deviate * deviate, axis=0, keepdims=True) / tlen + EPSILON)
        unit = (deviate / (spread * tlen)).astype(jnp.bfloat16).astype(jnp.float32)
        unit = jnp.where(code > 0, unit, 0.0)
        shift = code.astype(jnp.int32) - 1
        for bit in (1, 2, 4):
            unit = jnp.where(jnp.bitwise_and(shift, bit) > 0, pltpu.roll(unit, bit, 0), unit)
        unit = jnp.where(lag == 112, code, unit)
        bank[index] = unit.astype(jnp.bfloat16)

    def build(number):
        wide = jnp.dot(bank[number], expand[...], preferred_element_type=jnp.float32)
        for slot in range(slots):
            spreaded = wide[:, slot * LANES : (slot + 1) * LANES]
            code = spreaded[112:113, :].astype(jnp.int32)
            usable = code > 0
            shift = code - 1
            moves = shift // 8 + ahead
            taps = spreaded[0:112, :]
            for bit in (1, 2, 4, 8):
                gap = jnp.zeros((8 * bit, LANES), jnp.float32)
                taps = jnp.where(
                    jnp.bitwise_and(moves, bit) > 0,
                    jnp.concatenate([gap, taps], axis=0),
                    jnp.concatenate([taps, gap], axis=0),
                )[0:top]
            taps = taps.astype(jnp.bfloat16)
            item = number * slots + slot
            pick = jnp.logical_and(lag == shift + 8 * ahead, usable)
            pick = jnp.where(pick, 1.0, 0.0).astype(jnp.bfloat16)
            for index in range(tile_count):
                skip = 8 * offset_count * index
                lanes = slice(LANES * index, LANES * (index + 1))
                if skip:
                    weight_a[item, 0:skip, lanes] = jnp.zeros((skip, LANES), jnp.bfloat16)
                    pick = jnp.concatenate(
                        [jnp.zeros((skip, LANES), jnp.bfloat16), pick[0 : LANES - skip]], axis=0
                    )
                weight_a[item, skip : skip + top, lanes] = taps
                rest = DEPTH - top - skip
                if rest:
                    weight_a[item, skip + top :, lanes] = jnp.zeros((rest, LANES), jnp.bfloat16)
                weight_r[item, 0:LANES, lanes] = pick
                weight_r[item, LANES : 2 * LANES, lanes] = pick

    def apply(number, count):
        for slot in range(count):
            item = number * slots + slot
            both = [left_a[base + item, 0:rows, :], left_a[base + item, 16 : rows + 16, :]]
            corr = jnp.dot(
                jnp.concatenate(both, axis=1), weight_a[item], preferred_element_type=jnp.float32
            )
            factor = jnp.dot(
                left_r[base + item], weight_r[item], preferred_element_type=jnp.float32
            )
            total[...] += corr * factor

    total[...] = before[...] if side else jnp.zeros_like(total)
    build(0)

    for number in range(1, banks):
        apply(number - 1, slots)
        build(number)

    apply(banks - 1, half - slots * (banks - 1))

    if not side:
        outs[0][...] = total[...]
        return
    rows_out = outs[0].shape[0]
    station = lax.axis_index("sta") % len(outs)
    for step, out in enumerate(outs):
        part = jnp.bitwise_xor(station, step)
        out[...] = total[pl.ds(pl.multiple_of(part * rows_out, rows_out), rows_out), :].astype(
            jnp.bfloat16
        )


def correlate(side, tlen, group, count, piece, left_a, left_r, *before):
    channels, rows, _ = left_r.shape
    width = OFFSETS * group
    half = channels // 2
    if side:
        out = [jax.ShapeDtypeStruct((rows // count, width), jnp.bfloat16)] * count
    else:
        out = [jax.ShapeDtypeStruct((rows, width), jnp.float32)]
    return pl.pallas_call(
        functools.partial(main_kernel, side, tlen, group),
        out_shape=out,
        in_specs=[VMEM] * (3 + len(before)),
        out_specs=[VMEM] * len(out),
        scratch_shapes=[
            pltpu.VMEM(((half + 1) * group // LANES, LANES, LANES), jnp.bfloat16),
            pltpu.VMEM((LANES, LANES // group * LANES), jnp.bfloat16),
            pltpu.VMEM((half + 1, DEPTH, width), jnp.bfloat16),
            pltpu.VMEM((half + 1, DEPTH, width), jnp.bfloat16),
            pltpu.VMEM((rows, width), jnp.float32),
        ],
        compiler_params=params(),
        cost_estimate=cost(3),
        name="correlate_" + ("second" if side else "first"),
    )(piece, left_a, left_r, *before)


def add_kernel(*refs):
    parts, keep, send = refs[:-2], refs[-2], refs[-1]
    rows = keep.shape[0]
    core = lax.axis_index("tm") % 2
    for out, which in ((keep, core), (send, 1 - core)):
        place = pl.ds(pl.multiple_of(which * rows, rows), rows)
        value = parts[0][place, :].astype(jnp.float32)
        for part in parts[1:]:
            value = value + part[place, :].astype(jnp.float32)
        out[...] = value


def add(parts):
    rows, width = parts[0].shape
    out = jax.ShapeDtypeStruct((rows // 2, width), jnp.float32)
    return pl.pallas_call(
        add_kernel,
        out_shape=[out, out],
        in_specs=[VMEM] * len(parts),
        out_specs=[VMEM, VMEM],
        compiler_params=params(),
        cost_estimate=cost(0.5),
        name="add",
    )(*parts)


def finish_kernel(group, ours, received, out):
    samples = out.shape[1]
    rows = ours.shape[0]
    value = ours[...] + received[...]
    high = value.astype(jnp.bfloat16).astype(jnp.float32)
    both = jnp.concatenate([high, value - high], axis=0).T.astype(jnp.bfloat16)
    row = lax.broadcasted_iota(jnp.int32, (2 * rows, samples), 0) % rows
    lane = lax.broadcasted_iota(jnp.int32, (2 * rows, samples), 1)
    place = jnp.logical_and(lane // STRIDE == row // 8, lane % 8 == 7 - row % 8)
    place = jnp.where(place, 1.0, 0.0).astype(jnp.bfloat16)
    wide = jnp.dot(both, place, preferred_element_type=jnp.float32)
    lane = lax.broadcasted_iota(jnp.int32, (group, samples), 1) // 8 % OFFSETS
    result = jnp.zeros((group, samples), jnp.float32)
    for offset in range(OFFSETS):
        result = jnp.where(lane == offset, wide[offset * group : (offset + 1) * group], result)
    out[...] = result


def finish(group, samples, ours, received):
    return pl.pallas_call(
        functools.partial(finish_kernel, group),
        out_shape=jax.ShapeDtypeStruct((group, samples), jnp.float32),
        in_specs=[VMEM, VMEM],
        out_specs=VMEM,
        compiler_params=params(),
        cost_estimate=cost(1),
        name="finish",
    )(ours, received)


def shards(waveforms, templates, available, moveout, bank_blocks):
    channels, samples = waveforms.shape
    blocks, events, _, tlen = templates.shape
    count_tm = lax.axis_size("tm")
    count_sta = lax.axis_size("sta")
    chips = count_tm // 2
    near = chips // 2
    group = 2 * events // chips

    def swap(array):
        return lax.ppermute(array, "tm", [(i, i ^ 1) for i in range(count_tm)])

    def across(array, step):
        return lax.ppermute(array, "tm", [(i, i ^ (2 * step)) for i in range(count_tm)])

    local = [waveforms[None]]
    local += [across(local[0], step) for step in range(1, chips)]
    mine, theirs, owners = pack(
        chips,
        group,
        bank_blocks,
        jnp.transpose(templates, (0, 2, 1, 3)),
        jnp.transpose(available, (2, 0, 1)),
        jnp.transpose(moveout, (2, 0, 1)),
    )
    other = swap(theirs)
    merged = merge(owners, mine, other)
    pieces = [across(merged[step], step) for step in reversed(range(1, chips))]
    pieces = [merged[0]] + pieces[::-1]
    left_a, left_r = prepare_waves(tlen, swap(choose_waves(near, local)), local)

    left_a, left_r, *pieces = lax.optimization_barrier((left_a, left_r, *pieces[::-1]))
    pieces = pieces[::-1]
    first = choose_piece(owners, pieces)
    second = swap(first)
    total = correlate(0, tlen, group, near, first, left_a, left_r)
    parts = correlate(1, tlen, group, near, second, left_a, left_r, *total)
    gathered = []
    for step in range(near):
        route = []
        for d in range(count_tm):
            for s in range(count_sta):
                dest = near * (d % 2) + (s % near ^ step)
                route.append((d * count_sta + s, (2 * dest + s // near) * count_sta + d // 2))
        gathered.append(lax.ppermute(parts[step], ("tm", "sta"), route))
    ours, send = add(gathered)
    return finish(group, samples, ours, swap(send))


def solution(mesh):
    in_specs = (
        P("sta", "tm"),
        P("tm", None, "sta", None),
        P("tm", None, "sta"),
        P("tm", None, "sta"),
        P(),
    )
    out_specs = P("sta", "tm")
    return jax.shard_map(shards, mesh=mesh, in_specs=in_specs, out_specs=out_specs, check_vma=False)
```

```python
import functools

import jax
import jax.numpy as jnp
from jax import lax
from jax.experimental import pallas as pl
from jax.experimental.pallas import tpu as pltpu
from jax.sharding import PartitionSpec as P

EPSILON = 1e-06
LANES = 128
OFFSETS = 8
TILES = 12
QUARTER = 25
STRIDE = 64
DEPTH = 256
VMEM_LIMIT = 28 * 1024 * 1024

VMEM = pl.BlockSpec(memory_space=pltpu.VMEM)
ANY = pl.BlockSpec(memory_space=pl.ANY)


def params():
    return pltpu.CompilerParams(vmem_limit_bytes=VMEM_LIMIT)


def cost(micros):
    return pl.CostEstimate(
        flops=int(micros * 1e9), bytes_accessed=int(micros * 1e6), transcendentals=0
    )


def pack_kernel(bank_blocks, templates, available, moveout, mine, theirs, owners, chosen, raw, usable, shifts, square, sems):
    blocks, channels, events, tlen = templates.shape
    chips, _, group, _ = mine.shape
    half = channels // 2
    me = lax.axis_index("tm") % 2
    fetch = [
        pltpu.make_async_copy(source, target, sems.at[index])
        for index, (source, target) in enumerate(
            ((bank_blocks, chosen), (available, usable), (moveout, shifts), (templates, raw))
        )
    ]
    for copy in fetch:
        copy.start()
    mine[...] = jnp.zeros_like(mine)
    theirs[...] = jnp.zeros_like(theirs)
    square[...] = jnp.zeros_like(square)
    for copy in fetch[:3]:
        copy.wait()
    slots = [chosen[which] % blocks for which in range(2)]
    row = lax.broadcasted_iota(jnp.int32, owners.shape, 0)
    owners[...] = jnp.where(row == 0, chosen[0] // blocks, chosen[1] // blocks)
    flags = jnp.where(usable[...] > 0, shifts[...] + 1, 0).astype(jnp.float32)
    codes = []
    for which in range(2):
        code = flags[:, 0, :]
        for block in range(1, blocks):
            code = jnp.where(slots[which] == block, flags[:, block, :], code)
        square[0:channels, 0:events] = code
        turned = square[...].T
        later = pltpu.roll(turned, LANES - half, 1)
        codes.append([jnp.where(me == core, turned, later) for core in range(2)])
    fetch[3].wait()
    for which in range(2):
        for side, out in enumerate((mine, theirs)):
            first = half * jnp.where(me == side, 0, 1)
            code = codes[which][side].astype(jnp.bfloat16)
            for tile in range(TILES):
                extra = TILES + tile // 4
                start = QUARTER * (tile % 4)
                for index in range(events // group):
                    chip = which * (events // group) + index
                    rows = slice(index * group, (index + 1) * group)
                    out[chip, tile, :, 0:tlen] = raw[slots[which], first + tile, rows, :]
                    out[chip, tile, :, tlen : tlen + QUARTER] = raw[
                        slots[which], first + extra, rows, start : start + QUARTER
                    ]
                    out[chip, tile, :, 125:126] = code[rows, tile : tile + 1]
                    if tile < half - TILES:
                        beyond = TILES + tile
                        out[chip, tile, :, 126:127] = code[rows, beyond : beyond + 1]


def pack(chips, group, bank_blocks, templates, available, moveout):
    shape = (chips, TILES, group, LANES)
    held = [
        pltpu.with_memory_space_constraint(array, pltpu.HBM)
        for array in (bank_blocks, templates, available, moveout)
    ]
    return pl.pallas_call(
        pack_kernel,
        out_shape=[jax.ShapeDtypeStruct(shape, jnp.bfloat16)] * 2
        + [jax.ShapeDtypeStruct((8, LANES), jnp.int32)],
        in_specs=[ANY] * 4,
        out_specs=[VMEM] * 3,
        scratch_shapes=[
            pltpu.SMEM(bank_blocks.shape, jnp.int32),
            pltpu.VMEM(templates.shape, jnp.bfloat16),
            pltpu.VMEM(available.shape, jnp.int32),
            pltpu.VMEM(moveout.shape, jnp.int32),
            pltpu.VMEM((LANES, LANES), jnp.float32),
            pltpu.SemaphoreType.DMA((4,)),
        ],
        compiler_params=params(),
        cost_estimate=cost(2),
        name="pack",
    )(*held)


def merge_kernel(owners, mine, other, *outs):
    chips = len(outs)
    me = lax.axis_index("tm")
    for step, out in enumerate(outs):
        dest = jnp.bitwise_xor(me // 2, step)
        owner = jnp.where(dest < chips // 2, owners[0, 0], owners[1, 0])
        here = owner % 2 == me % 2

        @pl.when(here)
        def _():
            out[...] = mine[dest]

        @pl.when(jnp.logical_not(here))
        def _():
            out[...] = other[dest]


def merge(owners, mine, other):
    chips = mine.shape[0]
    return pl.pallas_call(
        merge_kernel,
        out_shape=[jax.ShapeDtypeStruct(mine.shape[1:], mine.dtype)] * chips,
        in_specs=[VMEM] * 3,
        out_specs=[VMEM] * chips,
        compiler_params=params(),
        cost_estimate=cost(0.3),
        name="merge",
    )(owners, mine, other)


def lagged(row, ahead):
    copies = jnp.broadcast_to(row, (8, row.shape[1]))
    return pltpu.roll(copies, row.shape[1] - 7 - ahead, 1, stride=1, stride_axis=0)


def pick(arrays, index):
    entries = [array.at[place] for array in arrays for place in range(array.shape[0])]
    value = entries[0][...]
    for number, entry in enumerate(entries[1:], 1):
        value = jnp.where(index == number, entry[...], value)
    return value


def choose_kernel(*refs):
    waves, out = refs[:-1], refs[-1]
    near = out.shape[0]
    me = lax.axis_index("tm")
    for step in range(near):
        out[step] = pick(waves, jnp.bitwise_xor(me // 2, near * (1 - me % 2) + step))


def choose_waves(near, waves):
    return pl.pallas_call(
        choose_kernel,
        out_shape=jax.ShapeDtypeStruct((near,) + waves[0].shape[1:], waves[0].dtype),
        in_specs=[VMEM] * len(waves),
        out_specs=VMEM,
        compiler_params=params(),
        cost_estimate=cost(0.05),
        name="choose_waves",
    )(*waves)


def own_kernel(owners, *refs):
    pieces, out = refs[:-1], refs[-1]
    chip = lax.axis_index("tm") // 2
    owner = jnp.where(chip < len(pieces) // 2, owners[0, 0], owners[1, 0])
    source = jnp.bitwise_xor(owner // 2, chip)
    value = pieces[0][...]
    for number, piece in enumerate(pieces[1:], 1):
        value = jnp.where(source == number, piece[...], value)
    out[...] = value


def choose_piece(owners, pieces):
    return pl.pallas_call(
        own_kernel,
        out_shape=jax.ShapeDtypeStruct(pieces[0].shape, pieces[0].dtype),
        in_specs=[VMEM] * (1 + len(pieces)),
        out_specs=VMEM,
        compiler_params=params(),
        cost_estimate=cost(0.3),
        name="choose_piece",
    )(owners, *pieces)


def waves_kernel(channels, tlen, unroll, swapped, *rest):
    local = rest[:-4]
    left_a, left_r, padded, inverse = rest[-4:]
    near, _, samples = swapped.shape
    chips = 2 * near
    length = chips * samples
    count = padded.shape[1] // LANES
    me = lax.axis_index("tm")
    chip, core = me // 2, me % 2
    padded[...] = jnp.zeros_like(padded)
    for index in range(chips):
        wave = pick(local, jnp.bitwise_xor(chip, near * core + index // 2))
        wave = jnp.where(core == index % 2, wave, swapped[index // 2])
        padded[0:channels, samples * index : samples * (index + 1)] = wave.astype(jnp.float32)
    rim = pick(local, jnp.bitwise_xor(chip, near))[:, 0 : padded.shape[1] - length]
    padded[0:channels, length:] = jnp.where(core == 0, rim.astype(jnp.float32), 0.0)

    rows = 32 * count
    values = [padded[:, LANES * tile : LANES * (tile + 1)] for tile in range(count)]
    values = jnp.concatenate(values + [jnp.zeros((32, LANES), jnp.float32)], axis=0)
    square = values * values
    high = square.astype(jnp.bfloat16)
    low = (square - high.astype(jnp.float32)).astype(jnp.bfloat16)
    values = values.astype(jnp.bfloat16)
    lag = lax.broadcasted_iota(jnp.int32, (2 * LANES, LANES), 0)
    lag = lag - lax.broadcasted_iota(jnp.int32, (2 * LANES, LANES), 1)
    band = jnp.where(jnp.logical_and(lag >= 0, lag < tlen), 1.0, 0.0).astype(jnp.bfloat16)

    def windows(array):
        both = jnp.concatenate([array[0:rows], array[32 : rows + 32]], axis=1)
        return jnp.dot(both, band, preferred_element_type=jnp.float32)

    mean = windows(values) / tlen
    scale = lax.rsqrt((windows(high) + windows(low)) / tlen - mean * mean + EPSILON)
    for tile in range(count):
        inverse[:, LANES * tile : LANES * (tile + 1)] = scale[32 * tile : 32 * (tile + 1)]

    def interleaved(row, tiles):
        even, odd = lagged(row, 0), lagged(row, STRIDE)
        parts = []
        for tile in range(tiles):
            lanes = slice(LANES * tile, LANES * (tile + 1))
            parts += [even[:, lanes], odd[:, lanes]]
        return jnp.concatenate(parts, axis=0)

    @pl.loop(0, channels // unroll)
    def _(step):
        for item in range(unroll):
            channel = step * unroll + item
            value = interleaved(padded[pl.ds(channel, 1), :], length // LANES + 1)
            left_a[channel] = value.astype(jnp.bfloat16)
            value = interleaved(inverse[pl.ds(channel, 1), :], length // LANES)
            high = value.astype(jnp.bfloat16)
            left_r[channel, :, 0:LANES] = high
            left_r[channel, :, LANES:] = (value - high.astype(jnp.float32)).astype(jnp.bfloat16)


def prepare_waves(tlen, swapped, local):
    near, channels, samples = swapped.shape
    length = 2 * near * samples
    rows = length // OFFSETS
    unroll = max(step for step in (1, 2, 3) if channels % step == 0)
    return pl.pallas_call(
        functools.partial(waves_kernel, channels, tlen, unroll),
        out_shape=[
            jax.ShapeDtypeStruct((channels, rows + 16, LANES), jnp.bfloat16),
            jax.ShapeDtypeStruct((channels, rows, 2 * LANES), jnp.bfloat16),
        ],
        in_specs=[VMEM] * (1 + len(local)),
        out_specs=[VMEM, VMEM],
        scratch_shapes=[
            pltpu.VMEM((32, length + 2 * LANES), jnp.float32),
            pltpu.VMEM((32, length + 2 * LANES), jnp.float32),
        ],
        compiler_params=params(),
        cost_estimate=cost(0.05),
        name="prepare_waves",
    )(swapped, *local)


def main_kernel(side, tlen, group, piece, left_a, left_r, *rest):
    outs = rest[:-5]
    if side:
        before, outs = outs[0], outs[1:]
    bank, expand, weight_a, weight_r, total = rest[-5:]
    core = lax.axis_index("tm") % 2
    channels, rows, _ = left_r.shape
    half = channels // 2
    base = half * jnp.where(core == side, 0, 1)
    slots = LANES // group
    banks = (half + 1) // slots
    offset_count = LANES // group
    tile_count = OFFSETS // offset_count
    top = 112 + 8 * (7 + offset_count - 1)
    top = top + top % 16

    lag = lax.broadcasted_iota(jnp.int32, (LANES, LANES), 0)
    target = lax.broadcasted_iota(jnp.int32, (LANES, LANES), 1)
    lane = lax.broadcasted_iota(jnp.int32, (1, LANES), 1)
    used = lag < tlen
    ahead = lane // group
    for slot in range(slots):
        chosen = jnp.where(lag == target % group + slot * group, 1.0, 0.0)
        expand[:, slot * LANES : (slot + 1) * LANES] = chosen.astype(jnp.bfloat16)
    turned = []
    for index in range(banks):
        count = min(slots, max(TILES - slots * index, 0))
        values = jnp.zeros((LANES, LANES), jnp.float32)
        if count:
            values = piece[slots * index : slots * index + count].astype(jnp.float32)
            values = values.reshape(count * group, LANES)
            if count < slots:
                gap = jnp.zeros((LANES - count * group, LANES), jnp.float32)
                values = jnp.concatenate([values, gap], axis=0)
            values = values.T
        turned.append(values)
    codes = [values[125:126, :] for values in turned]
    heads = [jnp.where(used, values, 0.0) for values in turned]
    for extra in range(half - TILES):
        place, slot = divmod(TILES + extra, slots)
        mask = ahead == slot
        code = pltpu.roll(turned[0][126:127, :], (slot - extra) * group % LANES, 1)
        codes[place] = jnp.where(mask, code, codes[place])
        for quarter in range(4):
            source, lanes = divmod(4 * extra + quarter, slots)
            values = turned[source][96:128]
            sample = lag[96:128]
            inside = jnp.logical_and(sample >= tlen, sample < tlen + QUARTER)
            values = jnp.where(inside, values, 0.0)
            values = pltpu.roll(values, (slot - lanes) * group % LANES, 1)
            start = QUARTER * quarter - (tlen - 96)
            values = jnp.concatenate([values, jnp.zeros((8, LANES), jnp.float32)], axis=0)
            values = pltpu.roll(values, start % 8, 0)
            start -= start % 8
            if start < 0:
                values, start = values[8:], 0
            below = LANES - start - values.shape[0]
            if start:
                values = jnp.concatenate([jnp.zeros((start, LANES), jnp.float32), values], axis=0)
            if below > 0:
                values = jnp.concatenate([values, jnp.zeros((below, LANES), jnp.float32)], axis=0)
            heads[place] = heads[place] + jnp.where(mask, values[0:LANES], 0.0)
    for index, (values, code) in enumerate(zip(heads, codes)):
        code = jnp.where(slots * index + ahead < half, code, 0.0)
        center = jnp.sum(values, axis=0, keepdims=True) / tlen
        deviate = jnp.where(used, values - center, 0.0)
        spread = jnp.sqrt(jnp.sum(deviate * deviate, axis=0, keepdims=True) / tlen + EPSILON)
        unit = (deviate / (spread * tlen)).astype(jnp.bfloat16).astype(jnp.float32)
        unit = jnp.where(code > 0, unit, 0.0)
        shift = code.astype(jnp.int32) - 1
        for bit in (1, 2, 4):
            unit = jnp.where(jnp.bitwise_and(shift, bit) > 0, pltpu.roll(unit, bit, 0), unit)
        unit = jnp.where(lag == 112, code, unit)
        bank[index] = unit.astype(jnp.bfloat16)

    def build(number):
        wide = jnp.dot(bank[number], expand[...], preferred_element_type=jnp.float32)
        for slot in range(slots):
            spreaded = wide[:, slot * LANES : (slot + 1) * LANES]
            code = spreaded[112:113, :].astype(jnp.int32)
            usable = code > 0
            shift = code - 1
            moves = shift // 8 + ahead
            taps = spreaded[0:112, :]
            for bit in (1, 2, 4, 8):
                gap = jnp.zeros((8 * bit, LANES), jnp.float32)
                taps = jnp.where(
                    jnp.bitwise_and(moves, bit) > 0,
                    jnp.concatenate([gap, taps], axis=0),
                    jnp.concatenate([taps, gap], axis=0),
                )[0:top]
            taps = taps.astype(jnp.bfloat16)
            item = number * slots + slot
            pick = jnp.logical_and(lag == shift + 8 * ahead, usable)
            pick = jnp.where(pick, 1.0, 0.0).astype(jnp.bfloat16)
            for index in range(tile_count):
                skip = 8 * offset_count * index
                lanes = slice(LANES * index, LANES * (index + 1))
                if skip:
                    weight_a[item, 0:skip, lanes] = jnp.zeros((skip, LANES), jnp.bfloat16)
                    pick = jnp.concatenate(
                        [jnp.zeros((skip, LANES), jnp.bfloat16), pick[0 : LANES - skip]], axis=0
                    )
                weight_a[item, skip : skip + top, lanes] = taps
                rest = DEPTH - top - skip
                if rest:
                    weight_a[item, skip + top :, lanes] = jnp.zeros((rest, LANES), jnp.bfloat16)
                weight_r[item, 0:LANES, lanes] = pick
                weight_r[item, LANES : 2 * LANES, lanes] = pick

    def apply(number, count):
        for slot in range(count):
            item = number * slots + slot
            both = [left_a[base + item, 0:rows, :], left_a[base + item, 16 : rows + 16, :]]
            corr = jnp.dot(
                jnp.concatenate(both, axis=1), weight_a[item], preferred_element_type=jnp.float32
            )
            factor = jnp.dot(
                left_r[base + item], weight_r[item], preferred_element_type=jnp.float32
            )
            total[...] += corr * factor

    total[...] = before[...] if side else jnp.zeros_like(total)
    build(0)

    for number in range(1, banks):
        apply(number - 1, slots)
        build(number)

    apply(banks - 1, half - slots * (banks - 1))

    if not side:
        outs[0][...] = total[...]
        return
    rows_out = outs[0].shape[0]
    station = lax.axis_index("sta") % len(outs)
    for step, out in enumerate(outs):
        part = jnp.bitwise_xor(station, step)
        out[...] = total[pl.ds(pl.multiple_of(part * rows_out, rows_out), rows_out), :].astype(
            jnp.bfloat16
        )


def correlate(side, tlen, group, count, piece, left_a, left_r, *before):
    channels, rows, _ = left_r.shape
    width = OFFSETS * group
    half = channels // 2
    if side:
        out = [jax.ShapeDtypeStruct((rows // count, width), jnp.bfloat16)] * count
    else:
        out = [jax.ShapeDtypeStruct((rows, width), jnp.float32)]
    return pl.pallas_call(
        functools.partial(main_kernel, side, tlen, group),
        out_shape=out,
        in_specs=[VMEM] * (3 + len(before)),
        out_specs=[VMEM] * len(out),
        scratch_shapes=[
            pltpu.VMEM(((half + 1) * group // LANES, LANES, LANES), jnp.bfloat16),
            pltpu.VMEM((LANES, LANES // group * LANES), jnp.bfloat16),
            pltpu.VMEM((half + 1, DEPTH, width), jnp.bfloat16),
            pltpu.VMEM((half + 1, DEPTH, width), jnp.bfloat16),
            pltpu.VMEM((rows, width), jnp.float32),
        ],
        compiler_params=params(),
        cost_estimate=cost(3),
        name="correlate_" + ("second" if side else "first"),
    )(piece, left_a, left_r, *before)


def add_kernel(*refs):
    parts, keep, send = refs[:-2], refs[-2], refs[-1]
    rows = keep.shape[0]
    core = lax.axis_index("tm") % 2
    for out, which in ((keep, core), (send, 1 - core)):
        place = pl.ds(pl.multiple_of(which * rows, rows), rows)
        value = parts[0][place, :].astype(jnp.float32)
        for part in parts[1:]:
            value = value + part[place, :].astype(jnp.float32)
        out[...] = value


def add(parts):
    rows, width = parts[0].shape
    out = jax.ShapeDtypeStruct((rows // 2, width), jnp.float32)
    return pl.pallas_call(
        add_kernel,
        out_shape=[out, out],
        in_specs=[VMEM] * len(parts),
        out_specs=[VMEM, VMEM],
        compiler_params=params(),
        cost_estimate=cost(0.5),
        name="add",
    )(*parts)


def finish_kernel(group, ours, received, out):
    samples = out.shape[1]
    rows = ours.shape[0]
    value = ours[...] + received[...]
    high = value.astype(jnp.bfloat16).astype(jnp.float32)
    both = jnp.concatenate([high, value - high], axis=0).T.astype(jnp.bfloat16)
    row = lax.broadcasted_iota(jnp.int32, (2 * rows, samples), 0) % rows
    lane = lax.broadcasted_iota(jnp.int32, (2 * rows, samples), 1)
    place = jnp.logical_and(lane // STRIDE == row // 8, lane % 8 == 7 - row % 8)
    place = jnp.where(place, 1.0, 0.0).astype(jnp.bfloat16)
    wide = jnp.dot(both, place, preferred_element_type=jnp.float32)
    lane = lax.broadcasted_iota(jnp.int32, (group, samples), 1) // 8 % OFFSETS
    result = jnp.zeros((group, samples), jnp.float32)
    for offset in range(OFFSETS):
        result = jnp.where(lane == offset, wide[offset * group : (offset + 1) * group], result)
    out[...] = result


def finish(group, samples, ours, received):
    return pl.pallas_call(
        functools.partial(finish_kernel, group),
        out_shape=jax.ShapeDtypeStruct((group, samples), jnp.float32),
        in_specs=[VMEM, VMEM],
        out_specs=VMEM,
        compiler_params=params(),
        cost_estimate=cost(1),
        name="finish",
    )(ours, received)


def shards(waveforms, templates, available, moveout, bank_blocks):
    channels, samples = waveforms.shape
    blocks, events, _, tlen = templates.shape
    count_tm = lax.axis_size("tm")
    count_sta = lax.axis_size("sta")
    chips = count_tm // 2
    near = chips // 2
    group = 2 * events // chips

    def swap(array):
        return lax.ppermute(array, "tm", [(i, i ^ 1) for i in range(count_tm)])

    def across(array, step):
        return lax.ppermute(array, "tm", [(i, i ^ (2 * step)) for i in range(count_tm)])

    local = [waveforms[None]]
    local += [across(local[0], step) for step in range(1, chips)]
    mine, theirs, owners = pack(
        chips,
        group,
        bank_blocks,
        jnp.transpose(templates, (0, 2, 1, 3)),
        jnp.transpose(available, (2, 0, 1)),
        jnp.transpose(moveout, (2, 0, 1)),
    )
    other = swap(theirs)
    merged = merge(owners, mine, other)
    pieces = [across(merged[step], step) for step in reversed(range(1, chips))]
    pieces = [merged[0]] + pieces[::-1]
    left_a, left_r = prepare_waves(tlen, swap(choose_waves(near, local)), local)

    left_a, left_r, *pieces = lax.optimization_barrier((left_a, left_r, *pieces[::-1]))
    pieces = pieces[::-1]
    first = choose_piece(owners, pieces)
    second = swap(first)
    total = correlate(0, tlen, group, near, first, left_a, left_r)
    parts = correlate(1, tlen, group, near, second, left_a, left_r, *total)
    gathered = []
    for step in range(near):
        route = []
        for d in range(count_tm):
            for s in range(count_sta):
                dest = near * (d % 2) + (s % near ^ step)
                route.append((d * count_sta + s, (2 * dest + s // near) * count_sta + d // 2))
        gathered.append(lax.ppermute(parts[step], ("tm", "sta"), route))
    ours, send = add(gathered)
    return finish(group, samples, ours, swap(send))


def solution(mesh):
    in_specs = (
        P("sta", "tm"),
        P("tm", None, "sta", None),
        P("tm", None, "sta"),
        P("tm", None, "sta"),
        P(),
    )
    out_specs = P("sta", "tm")
    return jax.shard_map(shards, mesh=mesh, in_specs=in_specs, out_specs=out_specs, check_vma=False)
```

```python
import functools

import jax
import jax.numpy as jnp
from jax import lax
from jax.experimental import pallas as pl
from jax.experimental.pallas import tpu as pltpu
from jax.sharding import PartitionSpec as P

EPSILON = 1e-06
LANES = 128
OFFSETS = 8
TILES = 12
QUARTER = 25
STRIDE = 64
DEPTH = 256
VMEM_LIMIT = 28 * 1024 * 1024

VMEM = pl.BlockSpec(memory_space=pltpu.VMEM)
ANY = pl.BlockSpec(memory_space=pl.ANY)


def params():
    return pltpu.CompilerParams(vmem_limit_bytes=VMEM_LIMIT)


def cost(micros):
    return pl.CostEstimate(
        flops=int(micros * 1e9), bytes_accessed=int(micros * 1e6), transcendentals=0
    )


def pack_kernel(bank_blocks, templates, available, moveout, mine, theirs, owners, chosen, raw, usable, shifts, square, sems):
    blocks, channels, events, tlen = templates.shape
    chips, _, group, _ = mine.shape
    half = channels // 2
    me = lax.axis_index("tm") % 2
    fetch = [
        pltpu.make_async_copy(source, target, sems.at[index])
        for index, (source, target) in enumerate(
            ((bank_blocks, chosen), (available, usable), (moveout, shifts), (templates, raw))
        )
    ]
    for copy in fetch:
        copy.start()
    mine[...] = jnp.zeros_like(mine)
    theirs[...] = jnp.zeros_like(theirs)
    square[...] = jnp.zeros_like(square)
    for copy in fetch[:3]:
        copy.wait()
    slots = [chosen[which] % blocks for which in range(2)]
    row = lax.broadcasted_iota(jnp.int32, owners.shape, 0)
    owners[...] = jnp.where(row == 0, chosen[0] // blocks, chosen[1] // blocks)
    flags = jnp.where(usable[...] > 0, shifts[...] + 1, 0).astype(jnp.float32)
    codes = []
    for which in range(2):
        code = flags[:, 0, :]
        for block in range(1, blocks):
            code = jnp.where(slots[which] == block, flags[:, block, :], code)
        square[0:channels, 0:events] = code
        turned = square[...].T
        later = pltpu.roll(turned, LANES - half, 1)
        codes.append([jnp.where(me == core, turned, later) for core in range(2)])
    fetch[3].wait()
    for which in range(2):
        for side, out in enumerate((mine, theirs)):
            first = half * jnp.where(me == side, 0, 1)
            code = codes[which][side].astype(jnp.bfloat16)
            for tile in range(TILES):
                extra = TILES + tile // 4
                start = QUARTER * (tile % 4)
                for index in range(events // group):
                    chip = which * (events // group) + index
                    rows = slice(index * group, (index + 1) * group)
                    out[chip, tile, :, 0:tlen] = raw[slots[which], first + tile, rows, :]
                    out[chip, tile, :, tlen : tlen + QUARTER] = raw[
                        slots[which], first + extra, rows, start : start + QUARTER
                    ]
                    out[chip, tile, :, 125:126] = code[rows, tile : tile + 1]
                    if tile < half - TILES:
                        beyond = TILES + tile
                        out[chip, tile, :, 126:127] = code[rows, beyond : beyond + 1]


def pack(chips, group, bank_blocks, templates, available, moveout):
    shape = (chips, TILES, group, LANES)
    held = [
        pltpu.with_memory_space_constraint(array, pltpu.HBM)
        for array in (bank_blocks, templates, available, moveout)
    ]
    return pl.pallas_call(
        pack_kernel,
        out_shape=[jax.ShapeDtypeStruct(shape, jnp.bfloat16)] * 2
        + [jax.ShapeDtypeStruct((8, LANES), jnp.int32)],
        in_specs=[ANY] * 4,
        out_specs=[VMEM] * 3,
        scratch_shapes=[
            pltpu.SMEM(bank_blocks.shape, jnp.int32),
            pltpu.VMEM(templates.shape, jnp.bfloat16),
            pltpu.VMEM(available.shape, jnp.int32),
            pltpu.VMEM(moveout.shape, jnp.int32),
            pltpu.VMEM((LANES, LANES), jnp.float32),
            pltpu.SemaphoreType.DMA((4,)),
        ],
        compiler_params=params(),
        cost_estimate=cost(2),
        name="pack",
    )(*held)


def merge_kernel(owners, mine, other, *outs):
    chips = len(outs)
    me = lax.axis_index("tm")
    for step, out in enumerate(outs):
        dest = jnp.bitwise_xor(me // 2, step)
        owner = jnp.where(dest < chips // 2, owners[0, 0], owners[1, 0])
        here = owner % 2 == me % 2

        @pl.when(here)
        def _():
            out[...] = mine[dest]

        @pl.when(jnp.logical_not(here))
        def _():
            out[...] = other[dest]


def merge(owners, mine, other):
    chips = mine.shape[0]
    return pl.pallas_call(
        merge_kernel,
        out_shape=[jax.ShapeDtypeStruct(mine.shape[1:], mine.dtype)] * chips,
        in_specs=[VMEM] * 3,
        out_specs=[VMEM] * chips,
        compiler_params=params(),
        cost_estimate=cost(0.3),
        name="merge",
    )(owners, mine, other)


def lagged(row, ahead):
    copies = jnp.broadcast_to(row, (8, row.shape[1]))
    return pltpu.roll(copies, row.shape[1] - 7 - ahead, 1, stride=1, stride_axis=0)


def segment(me, other, parity, pair, beside, far, default):
    chip, core = me // 2, me % 2
    chips = 2 * len(far) + 2
    step = jnp.bitwise_xor(chip, other)
    value = default[...]
    value = jnp.where(jnp.logical_and(step == 1, core == parity), beside[...], value)
    value = jnp.where(step == 0, pair[parity], value)
    for number, array in enumerate(far):
        value = jnp.where(step == chips - 1 - 2 * number - core, array[parity], value)
    return value


def pair_kernel(own, partner, out):
    core = lax.axis_index("tm") % 2
    out[core] = own[...]
    out[1 - core] = partner[...]


def pair_waves(own, partner):
    return pl.pallas_call(
        pair_kernel,
        out_shape=jax.ShapeDtypeStruct((2,) + own.shape, own.dtype),
        in_specs=[VMEM] * 2,
        out_specs=VMEM,
        compiler_params=params(),
        cost_estimate=cost(0.05),
        name="pair_waves",
    )(own, partner)


def choose_kernel(pair, beside, *rest):
    far, out = rest[:-1], rest[-1]
    near = out.shape[0] - 1
    me = lax.axis_index("tm")
    chip, core = me // 2, me % 2
    for entry in range(near):
        number, parity = divmod(entry, 2)
        step = jnp.bitwise_xor(chip, near * (1 - core) + 2 * number) // 2
        value = beside[...]
        for place, array in enumerate(far):
            value = jnp.where(step == near - 1 - place, array[parity], value)
        out[entry] = value
    out[near] = segment(me, near, 0, pair, beside, far, beside)


def choose_waves(pair, beside, far):
    return pl.pallas_call(
        choose_kernel,
        out_shape=jax.ShapeDtypeStruct((len(far) + 2,) + beside.shape, beside.dtype),
        in_specs=[VMEM] * (2 + len(far)),
        out_specs=VMEM,
        compiler_params=params(),
        cost_estimate=cost(0.05),
        name="choose_waves",
    )(pair, beside, *far)


def own_kernel(owners, *refs):
    pieces, out = refs[:-1], refs[-1]
    chip = lax.axis_index("tm") // 2
    owner = jnp.where(chip < len(pieces) // 2, owners[0, 0], owners[1, 0])
    source = jnp.bitwise_xor(owner // 2, chip)
    value = pieces[0][...]
    for number, piece in enumerate(pieces[1:], 1):
        value = jnp.where(source == number, piece[...], value)
    out[...] = value


def choose_piece(owners, pieces):
    return pl.pallas_call(
        own_kernel,
        out_shape=jax.ShapeDtypeStruct(pieces[0].shape, pieces[0].dtype),
        in_specs=[VMEM] * (1 + len(pieces)),
        out_specs=VMEM,
        compiler_params=params(),
        cost_estimate=cost(0.3),
        name="choose_piece",
    )(owners, *pieces)


def waves_kernel(channels, tlen, unroll, swapped, pair, beside, *rest):
    far = rest[:-4]
    left_a, left_r, padded, inverse = rest[-4:]
    samples = beside.shape[1]
    near = swapped.shape[0] - 1
    length = 2 * near * samples
    count = padded.shape[1] // LANES
    me = lax.axis_index("tm")
    core = me % 2
    padded[...] = jnp.zeros_like(padded)
    for index in range(2 * near):
        entry, parity = divmod(index, 2)
        given = swapped.at[2 * (entry // 2) + parity]
        wave = segment(me, near * core + entry, parity, pair, beside, far, given)
        padded[0:channels, samples * index : samples * (index + 1)] = wave.astype(jnp.float32)
    rim = segment(me, near * core + near, 0, pair, beside, far, swapped.at[near])
    rim = rim[:, 0 : padded.shape[1] - length].astype(jnp.float32)
    padded[0:channels, length:] = jnp.where(core == 0, rim, 0.0)

    rows = 32 * count
    values = [padded[:, LANES * tile : LANES * (tile + 1)] for tile in range(count)]
    values = jnp.concatenate(values + [jnp.zeros((32, LANES), jnp.float32)], axis=0)
    square = values * values
    high = square.astype(jnp.bfloat16)
    low = (square - high.astype(jnp.float32)).astype(jnp.bfloat16)
    values = values.astype(jnp.bfloat16)
    lag = lax.broadcasted_iota(jnp.int32, (2 * LANES, LANES), 0)
    lag = lag - lax.broadcasted_iota(jnp.int32, (2 * LANES, LANES), 1)
    band = jnp.where(jnp.logical_and(lag >= 0, lag < tlen), 1.0, 0.0).astype(jnp.bfloat16)

    def windows(array):
        both = jnp.concatenate([array[0:rows], array[32 : rows + 32]], axis=1)
        return jnp.dot(both, band, preferred_element_type=jnp.float32)

    mean = windows(values) / tlen
    scale = lax.rsqrt((windows(high) + windows(low)) / tlen - mean * mean + EPSILON)
    for tile in range(count):
        inverse[:, LANES * tile : LANES * (tile + 1)] = scale[32 * tile : 32 * (tile + 1)]

    def interleaved(row, tiles):
        even, odd = lagged(row, 0), lagged(row, STRIDE)
        parts = []
        for tile in range(tiles):
            lanes = slice(LANES * tile, LANES * (tile + 1))
            parts += [even[:, lanes], odd[:, lanes]]
        return jnp.concatenate(parts, axis=0)

    @pl.loop(0, channels // unroll)
    def _(step):
        for item in range(unroll):
            channel = step * unroll + item
            value = interleaved(padded[pl.ds(channel, 1), :], length // LANES + 1)
            left_a[channel] = value.astype(jnp.bfloat16)
            value = interleaved(inverse[pl.ds(channel, 1), :], length // LANES)
            high = value.astype(jnp.bfloat16)
            left_r[channel, :, 0:LANES] = high
            left_r[channel, :, LANES:] = (value - high.astype(jnp.float32)).astype(jnp.bfloat16)


def prepare_waves(tlen, swapped, pair, beside, far):
    channels, samples = beside.shape
    length = 2 * (swapped.shape[0] - 1) * samples
    rows = length // OFFSETS
    unroll = max(step for step in (1, 2, 3) if channels % step == 0)
    return pl.pallas_call(
        functools.partial(waves_kernel, channels, tlen, unroll),
        out_shape=[
            jax.ShapeDtypeStruct((channels, rows + 16, LANES), jnp.bfloat16),
            jax.ShapeDtypeStruct((channels, rows, 2 * LANES), jnp.bfloat16),
        ],
        in_specs=[VMEM] * (3 + len(far)),
        out_specs=[VMEM, VMEM],
        scratch_shapes=[
            pltpu.VMEM((32, length + 2 * LANES), jnp.float32),
            pltpu.VMEM((32, length + 2 * LANES), jnp.float32),
        ],
        compiler_params=params(),
        cost_estimate=cost(0.05),
        name="prepare_waves",
    )(swapped, pair, beside, *far)


def main_kernel(side, tlen, group, piece, left_a, left_r, *rest):
    outs = rest[:-5]
    if side:
        before, outs = outs[0], outs[1:]
    bank, expand, weight_a, weight_r, total = rest[-5:]
    core = lax.axis_index("tm") % 2
    channels, rows, _ = left_r.shape
    half = channels // 2
    base = half * jnp.where(core == side, 0, 1)
    slots = LANES // group
    banks = (half + 1) // slots
    offset_count = LANES // group
    tile_count = OFFSETS // offset_count
    top = 112 + 8 * (7 + offset_count - 1)
    top = top + top % 16

    lag = lax.broadcasted_iota(jnp.int32, (LANES, LANES), 0)
    target = lax.broadcasted_iota(jnp.int32, (LANES, LANES), 1)
    lane = lax.broadcasted_iota(jnp.int32, (1, LANES), 1)
    used = lag < tlen
    ahead = lane // group
    for slot in range(slots):
        chosen = jnp.where(lag == target % group + slot * group, 1.0, 0.0)
        expand[:, slot * LANES : (slot + 1) * LANES] = chosen.astype(jnp.bfloat16)
    turned = []
    for index in range(banks):
        count = min(slots, max(TILES - slots * index, 0))
        values = jnp.zeros((LANES, LANES), jnp.float32)
        if count:
            values = piece[slots * index : slots * index + count].astype(jnp.float32)
            values = values.reshape(count * group, LANES)
            if count < slots:
                gap = jnp.zeros((LANES - count * group, LANES), jnp.float32)
                values = jnp.concatenate([values, gap], axis=0)
            values = values.T
        turned.append(values)
    codes = [values[125:126, :] for values in turned]
    heads = [jnp.where(used, values, 0.0) for values in turned]
    for extra in range(half - TILES):
        place, slot = divmod(TILES + extra, slots)
        mask = ahead == slot
        code = pltpu.roll(turned[0][126:127, :], (slot - extra) * group % LANES, 1)
        codes[place] = jnp.where(mask, code, codes[place])
        for quarter in range(4):
            source, lanes = divmod(4 * extra + quarter, slots)
            values = turned[source][96:128]
            sample = lag[96:128]
            inside = jnp.logical_and(sample >= tlen, sample < tlen + QUARTER)
            values = jnp.where(inside, values, 0.0)
            values = pltpu.roll(values, (slot - lanes) * group % LANES, 1)
            start = QUARTER * quarter - (tlen - 96)
            values = jnp.concatenate([values, jnp.zeros((8, LANES), jnp.float32)], axis=0)
            values = pltpu.roll(values, start % 8, 0)
            start -= start % 8
            if start < 0:
                values, start = values[8:], 0
            below = LANES - start - values.shape[0]
            if start:
                values = jnp.concatenate([jnp.zeros((start, LANES), jnp.float32), values], axis=0)
            if below > 0:
                values = jnp.concatenate([values, jnp.zeros((below, LANES), jnp.float32)], axis=0)
            heads[place] = heads[place] + jnp.where(mask, values[0:LANES], 0.0)
    for index, (values, code) in enumerate(zip(heads, codes)):
        code = jnp.where(slots * index + ahead < half, code, 0.0)
        center = jnp.sum(values, axis=0, keepdims=True) / tlen
        deviate = jnp.where(used, values - center, 0.0)
        spread = jnp.sqrt(jnp.sum(deviate * deviate, axis=0, keepdims=True) / tlen + EPSILON)
        unit = (deviate / (spread * tlen)).astype(jnp.bfloat16).astype(jnp.float32)
        unit = jnp.where(code > 0, unit, 0.0)
        shift = code.astype(jnp.int32) - 1
        for bit in (1, 2, 4):
            unit = jnp.where(jnp.bitwise_and(shift, bit) > 0, pltpu.roll(unit, bit, 0), unit)
        unit = jnp.where(lag == 112, code, unit)
        bank[index] = unit.astype(jnp.bfloat16)

    def build(number):
        wide = jnp.dot(bank[number], expand[...], preferred_element_type=jnp.float32)
        for slot in range(slots):
            spreaded = wide[:, slot * LANES : (slot + 1) * LANES]
            code = spreaded[112:113, :].astype(jnp.int32)
            usable = code > 0
            shift = code - 1
            moves = shift // 8 + ahead
            taps = spreaded[0:112, :]
            for bit in (1, 2, 4, 8):
                gap = jnp.zeros((8 * bit, LANES), jnp.float32)
                taps = jnp.where(
                    jnp.bitwise_and(moves, bit) > 0,
                    jnp.concatenate([gap, taps], axis=0),
                    jnp.concatenate([taps, gap], axis=0),
                )[0:top]
            taps = taps.astype(jnp.bfloat16)
            item = number * slots + slot
            pick = jnp.logical_and(lag == shift + 8 * ahead, usable)
            pick = jnp.where(pick, 1.0, 0.0).astype(jnp.bfloat16)
            for index in range(tile_count):
                skip = 8 * offset_count * index
                lanes = slice(LANES * index, LANES * (index + 1))
                if skip:
                    weight_a[item, 0:skip, lanes] = jnp.zeros((skip, LANES), jnp.bfloat16)
                    pick = jnp.concatenate(
                        [jnp.zeros((skip, LANES), jnp.bfloat16), pick[0 : LANES - skip]], axis=0
                    )
                weight_a[item, skip : skip + top, lanes] = taps
                rest = DEPTH - top - skip
                if rest:
                    weight_a[item, skip + top :, lanes] = jnp.zeros((rest, LANES), jnp.bfloat16)
                weight_r[item, 0:LANES, lanes] = pick
                weight_r[item, LANES : 2 * LANES, lanes] = pick

    def apply(number, count):
        for slot in range(count):
            item = number * slots + slot
            both = [left_a[base + item, 0:rows, :], left_a[base + item, 16 : rows + 16, :]]
            corr = jnp.dot(
                jnp.concatenate(both, axis=1), weight_a[item], preferred_element_type=jnp.float32
            )
            factor = jnp.dot(
                left_r[base + item], weight_r[item], preferred_element_type=jnp.float32
            )
            total[...] += corr * factor

    total[...] = before[...] if side else jnp.zeros_like(total)
    build(0)

    for number in range(1, banks):
        apply(number - 1, slots)
        build(number)

    apply(banks - 1, half - slots * (banks - 1))

    if not side:
        outs[0][...] = total[...]
        return
    rows_out = outs[0].shape[0]
    station = lax.axis_index("sta") % len(outs)
    for step, out in enumerate(outs):
        part = jnp.bitwise_xor(station, step)
        out[...] = total[pl.ds(pl.multiple_of(part * rows_out, rows_out), rows_out), :].astype(
            jnp.bfloat16
        )


def correlate(side, tlen, group, count, piece, left_a, left_r, *before):
    channels, rows, _ = left_r.shape
    width = OFFSETS * group
    half = channels // 2
    if side:
        out = [jax.ShapeDtypeStruct((rows // count, width), jnp.bfloat16)] * count
    else:
        out = [jax.ShapeDtypeStruct((rows, width), jnp.float32)]
    return pl.pallas_call(
        functools.partial(main_kernel, side, tlen, group),
        out_shape=out,
        in_specs=[VMEM] * (3 + len(before)),
        out_specs=[VMEM] * len(out),
        scratch_shapes=[
            pltpu.VMEM(((half + 1) * group // LANES, LANES, LANES), jnp.bfloat16),
            pltpu.VMEM((LANES, LANES // group * LANES), jnp.bfloat16),
            pltpu.VMEM((half + 1, DEPTH, width), jnp.bfloat16),
            pltpu.VMEM((half + 1, DEPTH, width), jnp.bfloat16),
            pltpu.VMEM((rows, width), jnp.float32),
        ],
        compiler_params=params(),
        cost_estimate=cost(3),
        name="correlate_" + ("second" if side else "first"),
    )(piece, left_a, left_r, *before)


def add_kernel(*refs):
    parts, keep, send = refs[:-2], refs[-2], refs[-1]
    rows = keep.shape[0]
    core = lax.axis_index("tm") % 2
    for out, which in ((keep, core), (send, 1 - core)):
        place = pl.ds(pl.multiple_of(which * rows, rows), rows)
        value = parts[0][place, :].astype(jnp.float32)
        for part in parts[1:]:
            value = value + part[place, :].astype(jnp.float32)
        out[...] = value


def add(parts):
    rows, width = parts[0].shape
    out = jax.ShapeDtypeStruct((rows // 2, width), jnp.float32)
    return pl.pallas_call(
        add_kernel,
        out_shape=[out, out],
        in_specs=[VMEM] * len(parts),
        out_specs=[VMEM, VMEM],
        compiler_params=params(),
        cost_estimate=cost(0.5),
        name="add",
    )(*parts)


def finish_kernel(group, ours, received, out):
    samples = out.shape[1]
    rows = ours.shape[0]
    value = ours[...] + received[...]
    high = value.astype(jnp.bfloat16).astype(jnp.float32)
    both = jnp.concatenate([high, value - high], axis=0).T.astype(jnp.bfloat16)
    row = lax.broadcasted_iota(jnp.int32, (2 * rows, samples), 0) % rows
    lane = lax.broadcasted_iota(jnp.int32, (2 * rows, samples), 1)
    place = jnp.logical_and(lane // STRIDE == row // 8, lane % 8 == 7 - row % 8)
    place = jnp.where(place, 1.0, 0.0).astype(jnp.bfloat16)
    wide = jnp.dot(both, place, preferred_element_type=jnp.float32)
    lane = lax.broadcasted_iota(jnp.int32, (group, samples), 1) // 8 % OFFSETS
    result = jnp.zeros((group, samples), jnp.float32)
    for offset in range(OFFSETS):
        result = jnp.where(lane == offset, wide[offset * group : (offset + 1) * group], result)
    out[...] = result


def finish(group, samples, ours, received):
    return pl.pallas_call(
        functools.partial(finish_kernel, group),
        out_shape=jax.ShapeDtypeStruct((group, samples), jnp.float32),
        in_specs=[VMEM, VMEM],
        out_specs=VMEM,
        compiler_params=params(),
        cost_estimate=cost(1),
        name="finish",
    )(ours, received)


def shards(waveforms, templates, available, moveout, bank_blocks):
    channels, samples = waveforms.shape
    blocks, events, _, tlen = templates.shape
    count_tm = lax.axis_size("tm")
    count_sta = lax.axis_size("sta")
    chips = count_tm // 2
    near = chips // 2
    group = 2 * events // chips

    def swap(array):
        return lax.ppermute(array, "tm", [(i, i ^ 1) for i in range(count_tm)])

    def across(array, step):
        return lax.ppermute(array, "tm", [(i, i ^ (2 * step)) for i in range(count_tm)])

    partner = swap(waveforms)
    mine, theirs, owners = pack(
        chips,
        group,
        bank_blocks,
        jnp.transpose(templates, (0, 2, 1, 3)),
        jnp.transpose(available, (2, 0, 1)),
        jnp.transpose(moveout, (2, 0, 1)),
    )
    theirs, partner = lax.optimization_barrier((theirs, partner))
    other = swap(theirs)
    pair = pair_waves(waveforms, partner)
    far = []
    for number in range(near - 1):
        steps = (chips - 1 - 2 * number, chips - 2 - 2 * number)
        route = [(2 * z + c, 2 * (z ^ steps[c]) + c) for z in range(chips) for c in range(2)]
        far.append(lax.ppermute(pair, "tm", route))
    beside = across(waveforms, 1)
    merged = list(merge(owners, mine, other))
    pieces = [across(merged[step], step) for step in reversed(range(1, chips))]
    pieces = [merged[0]] + pieces[::-1]
    swapped = swap(choose_waves(pair, beside, far))
    left_a, left_r = prepare_waves(tlen, swapped, pair, beside, far)

    left_a, left_r, *pieces = lax.optimization_barrier((left_a, left_r, *pieces[::-1]))
    pieces = pieces[::-1]
    first = choose_piece(owners, pieces)
    second = swap(first)
    total = correlate(0, tlen, group, near, first, left_a, left_r)
    parts = correlate(1, tlen, group, near, second, left_a, left_r, *total)
    gathered = []
    for step in range(near):
        route = []
        for d in range(count_tm):
            for s in range(count_sta):
                dest = near * (d % 2) + (s % near ^ step)
                route.append((d * count_sta + s, (2 * dest + s // near) * count_sta + d // 2))
        gathered.append(lax.ppermute(parts[step], ("tm", "sta"), route))
    ours, send = add(gathered)
    return finish(group, samples, ours, swap(send))


def solution(mesh):
    in_specs = (
        P("sta", "tm"),
        P("tm", None, "sta", None),
        P("tm", None, "sta"),
        P("tm", None, "sta"),
        P(),
    )
    out_specs = P("sta", "tm")
    return jax.shard_map(shards, mesh=mesh, in_specs=in_specs, out_specs=out_specs, check_vma=False)
```

```python
import functools

import jax
import jax.numpy as jnp
from jax import lax
from jax.experimental import pallas as pl
from jax.experimental.pallas import tpu as pltpu
from jax.sharding import PartitionSpec as P

EPSILON = 1e-06
LANES = 128
OFFSETS = 8
TILES = 12
QUARTER = 25
STRIDE = 64
DEPTH = 256
VMEM_LIMIT = 28 * 1024 * 1024

VMEM = pl.BlockSpec(memory_space=pltpu.VMEM)
ANY = pl.BlockSpec(memory_space=pl.ANY)


def params():
    return pltpu.CompilerParams(vmem_limit_bytes=VMEM_LIMIT)


def cost(micros):
    return pl.CostEstimate(
        flops=int(micros * 1e9), bytes_accessed=int(micros * 1e6), transcendentals=0
    )


def pack_kernel(bank_blocks, templates, available, moveout, mine, theirs, owners, chosen, raw, usable, shifts, square, sems):
    blocks, channels, events, tlen = templates.shape
    chips, _, group, _ = mine.shape
    half = channels // 2
    me = lax.axis_index("tm") % 2
    station = lax.axis_index("sta")
    fetch = [
        pltpu.make_async_copy(source, target, sems.at[index])
        for index, (source, target) in enumerate(
            ((bank_blocks, chosen), (available, usable), (moveout, shifts), (templates, raw))
        )
    ]
    for copy in fetch:
        copy.start()
    mine[...] = jnp.zeros_like(mine)
    theirs[...] = jnp.zeros_like(theirs)
    square[...] = jnp.zeros_like(square)
    for copy in fetch[:3]:
        copy.wait()
    slots = [chosen[which] % blocks for which in range(2)]
    row = lax.broadcasted_iota(jnp.int32, owners.shape, 0)
    owners[...] = jnp.where(row == 0, chosen[0] // blocks, chosen[1] // blocks)
    flags = jnp.where(usable[...] > 0, shifts[...] + 1, 0).astype(jnp.float32)
    codes = []
    for which in range(2):
        code = flags[:, 0, :]
        for block in range(1, blocks):
            code = jnp.where(slots[which] == block, flags[:, block, :], code)
        square[0:channels, 0:events] = code
        turned = square[...].T
        later = pltpu.roll(turned, LANES - half, 1)
        codes.append([jnp.where(me == core, turned, later) for core in range(2)])
    fetch[3].wait()
    for which in range(2):
        for side, out in enumerate((mine, theirs)):
            first = half * jnp.where(me == side, 0, 1)
            code = codes[which][side].astype(jnp.bfloat16)
            for tile in range(TILES):
                extra = TILES + tile // 4
                start = QUARTER * (tile % 4)
                for index in range(events // group):
                    chip = jnp.bitwise_xor(station, which * (events // group) + index)
                    rows = slice(index * group, (index + 1) * group)
                    out[chip, tile, :, 0:tlen] = raw[slots[which], first + tile, rows, :]
                    out[chip, tile, :, tlen : tlen + QUARTER] = raw[
                        slots[which], first + extra, rows, start : start + QUARTER
                    ]
                    out[chip, tile, :, 125:126] = code[rows, tile : tile + 1]
                    if tile < half - TILES:
                        beyond = TILES + tile
                        out[chip, tile, :, 126:127] = code[rows, beyond : beyond + 1]


def pack(chips, group, bank_blocks, templates, available, moveout):
    shape = (chips, TILES, group, LANES)
    held = [
        pltpu.with_memory_space_constraint(array, pltpu.HBM)
        for array in (bank_blocks, templates, available, moveout)
    ]
    return pl.pallas_call(
        pack_kernel,
        out_shape=[jax.ShapeDtypeStruct(shape, jnp.bfloat16)] * 2
        + [jax.ShapeDtypeStruct((8, LANES), jnp.int32)],
        in_specs=[ANY] * 4,
        out_specs=[VMEM] * 3,
        scratch_shapes=[
            pltpu.SMEM(bank_blocks.shape, jnp.int32),
            pltpu.VMEM(templates.shape, jnp.bfloat16),
            pltpu.VMEM(available.shape, jnp.int32),
            pltpu.VMEM(moveout.shape, jnp.int32),
            pltpu.VMEM((LANES, LANES), jnp.float32),
            pltpu.SemaphoreType.DMA((4,)),
        ],
        compiler_params=params(),
        cost_estimate=cost(2),
        name="pack",
    )(*held)


def merge_kernel(owners, mine, other, *outs):
    chips = len(outs)
    me = lax.axis_index("tm")
    station = lax.axis_index("sta")
    for step, out in enumerate(outs):
        dest = jnp.bitwise_xor(me // 2, step)
        first = jnp.bitwise_xor(dest, station) < chips // 2
        owner = jnp.where(first, owners[0, 0], owners[1, 0])
        here = owner % 2 == me % 2

        @pl.when(here)
        def _():
            out[...] = mine[dest]

        @pl.when(jnp.logical_not(here))
        def _():
            out[...] = other[dest]


def merge(owners, mine, other):
    chips = mine.shape[0]
    return pl.pallas_call(
        merge_kernel,
        out_shape=[jax.ShapeDtypeStruct(mine.shape[1:], mine.dtype)] * chips,
        in_specs=[VMEM] * 3,
        out_specs=[VMEM] * chips,
        compiler_params=params(),
        cost_estimate=cost(0.3),
        name="merge",
    )(owners, mine, other)


def lagged(row, ahead):
    copies = jnp.broadcast_to(row, (8, row.shape[1]))
    return pltpu.roll(copies, row.shape[1] - 7 - ahead, 1, stride=1, stride_axis=0)


def segment(me, other, parity, pair, beside, far, default):
    chip, core = me // 2, me % 2
    chips = 2 * len(far) + 2
    step = jnp.bitwise_xor(chip, other)
    value = default[...]
    value = jnp.where(jnp.logical_and(step == 1, core == parity), beside[...], value)
    value = jnp.where(step == 0, pair[parity], value)
    for number, array in enumerate(far):
        value = jnp.where(step == chips - 1 - 2 * number - core, array[parity], value)
    return value


def pair_kernel(own, partner, out):
    core = lax.axis_index("tm") % 2
    out[core] = own[...]
    out[1 - core] = partner[...]


def pair_waves(own, partner):
    return pl.pallas_call(
        pair_kernel,
        out_shape=jax.ShapeDtypeStruct((2,) + own.shape, own.dtype),
        in_specs=[VMEM] * 2,
        out_specs=VMEM,
        compiler_params=params(),
        cost_estimate=cost(0.05),
        name="pair_waves",
    )(own, partner)


def choose_kernel(pair, beside, *rest):
    far, out = rest[:-1], rest[-1]
    near = out.shape[0] - 1
    me = lax.axis_index("tm")
    chip, core = me // 2, me % 2
    for entry in range(near):
        number, parity = divmod(entry, 2)
        step = jnp.bitwise_xor(chip, near * (1 - core) + 2 * number) // 2
        value = beside[...]
        for place, array in enumerate(far):
            value = jnp.where(step == near - 1 - place, array[parity], value)
        out[entry] = value
    out[near] = segment(me, near, 0, pair, beside, far, beside)


def choose_waves(pair, beside, far):
    return pl.pallas_call(
        choose_kernel,
        out_shape=jax.ShapeDtypeStruct((len(far) + 2,) + beside.shape, beside.dtype),
        in_specs=[VMEM] * (2 + len(far)),
        out_specs=VMEM,
        compiler_params=params(),
        cost_estimate=cost(0.05),
        name="choose_waves",
    )(pair, beside, *far)


def own_kernel(owners, *refs):
    pieces, out = refs[:-1], refs[-1]
    chip = lax.axis_index("tm") // 2
    first = jnp.bitwise_xor(chip, lax.axis_index("sta")) < len(pieces) // 2
    owner = jnp.where(first, owners[0, 0], owners[1, 0])
    source = jnp.bitwise_xor(owner // 2, chip)
    value = pieces[0][...]
    for number, piece in enumerate(pieces[1:], 1):
        value = jnp.where(source == number, piece[...], value)
    out[...] = value


def choose_piece(owners, pieces):
    return pl.pallas_call(
        own_kernel,
        out_shape=jax.ShapeDtypeStruct(pieces[0].shape, pieces[0].dtype),
        in_specs=[VMEM] * (1 + len(pieces)),
        out_specs=VMEM,
        compiler_params=params(),
        cost_estimate=cost(0.3),
        name="choose_piece",
    )(owners, *pieces)


def waves_kernel(channels, tlen, unroll, swapped, pair, beside, *rest):
    far = rest[:-4]
    left_a, left_r, padded, inverse = rest[-4:]
    samples = beside.shape[1]
    near = swapped.shape[0] - 1
    length = 2 * near * samples
    count = padded.shape[1] // LANES
    me = lax.axis_index("tm")
    core = me % 2
    padded[...] = jnp.zeros_like(padded)
    for index in range(2 * near):
        entry, parity = divmod(index, 2)
        given = swapped.at[2 * (entry // 2) + parity]
        wave = segment(me, near * core + entry, parity, pair, beside, far, given)
        padded[0:channels, samples * index : samples * (index + 1)] = wave.astype(jnp.float32)
    rim = segment(me, near * core + near, 0, pair, beside, far, swapped.at[near])
    rim = rim[:, 0 : padded.shape[1] - length].astype(jnp.float32)
    padded[0:channels, length:] = jnp.where(core == 0, rim, 0.0)

    rows = 32 * count
    values = [padded[:, LANES * tile : LANES * (tile + 1)] for tile in range(count)]
    values = jnp.concatenate(values + [jnp.zeros((32, LANES), jnp.float32)], axis=0)
    square = values * values
    high = square.astype(jnp.bfloat16)
    low = (square - high.astype(jnp.float32)).astype(jnp.bfloat16)
    values = values.astype(jnp.bfloat16)
    lag = lax.broadcasted_iota(jnp.int32, (2 * LANES, LANES), 0)
    lag = lag - lax.broadcasted_iota(jnp.int32, (2 * LANES, LANES), 1)
    band = jnp.where(jnp.logical_and(lag >= 0, lag < tlen), 1.0, 0.0).astype(jnp.bfloat16)

    def windows(array):
        both = jnp.concatenate([array[0:rows], array[32 : rows + 32]], axis=1)
        return jnp.dot(both, band, preferred_element_type=jnp.float32)

    mean = windows(values) / tlen
    scale = lax.rsqrt((windows(high) + windows(low)) / tlen - mean * mean + EPSILON)
    for tile in range(count):
        inverse[:, LANES * tile : LANES * (tile + 1)] = scale[32 * tile : 32 * (tile + 1)]

    def interleaved(row, tiles):
        even, odd = lagged(row, 0), lagged(row, STRIDE)
        parts = []
        for tile in range(tiles):
            lanes = slice(LANES * tile, LANES * (tile + 1))
            parts += [even[:, lanes], odd[:, lanes]]
        return jnp.concatenate(parts, axis=0)

    @pl.loop(0, channels // unroll)
    def _(step):
        for item in range(unroll):
            channel = step * unroll + item
            value = interleaved(padded[pl.ds(channel, 1), :], length // LANES + 1)
            left_a[channel] = value.astype(jnp.bfloat16)
            value = interleaved(inverse[pl.ds(channel, 1), :], length // LANES)
            high = value.astype(jnp.bfloat16)
            left_r[channel, :, 0:LANES] = high
            left_r[channel, :, LANES:] = (value - high.astype(jnp.float32)).astype(jnp.bfloat16)


def prepare_waves(tlen, swapped, pair, beside, far):
    channels, samples = beside.shape
    length = 2 * (swapped.shape[0] - 1) * samples
    rows = length // OFFSETS
    unroll = max(step for step in (1, 2, 3) if channels % step == 0)
    return pl.pallas_call(
        functools.partial(waves_kernel, channels, tlen, unroll),
        out_shape=[
            jax.ShapeDtypeStruct((channels, rows + 16, LANES), jnp.bfloat16),
            jax.ShapeDtypeStruct((channels, rows, 2 * LANES), jnp.bfloat16),
        ],
        in_specs=[VMEM] * (3 + len(far)),
        out_specs=[VMEM, VMEM],
        scratch_shapes=[
            pltpu.VMEM((32, length + 2 * LANES), jnp.float32),
            pltpu.VMEM((32, length + 2 * LANES), jnp.float32),
        ],
        compiler_params=params(),
        cost_estimate=cost(0.05),
        name="prepare_waves",
    )(swapped, pair, beside, *far)


def main_kernel(side, tlen, group, piece, left_a, left_r, *rest):
    outs = rest[:-5]
    if side:
        before, outs = outs[0], outs[1:]
    bank, expand, weight_a, weight_r, total = rest[-5:]
    core = lax.axis_index("tm") % 2
    channels, rows, _ = left_r.shape
    half = channels // 2
    base = half * jnp.where(core == side, 0, 1)
    slots = LANES // group
    banks = (half + 1) // slots
    offset_count = LANES // group
    tile_count = OFFSETS // offset_count
    top = 112 + 8 * (7 + offset_count - 1)
    top = top + top % 16

    lag = lax.broadcasted_iota(jnp.int32, (LANES, LANES), 0)
    target = lax.broadcasted_iota(jnp.int32, (LANES, LANES), 1)
    lane = lax.broadcasted_iota(jnp.int32, (1, LANES), 1)
    used = lag < tlen
    ahead = lane // group
    for slot in range(slots):
        chosen = jnp.where(lag == target % group + slot * group, 1.0, 0.0)
        expand[:, slot * LANES : (slot + 1) * LANES] = chosen.astype(jnp.bfloat16)
    turned = []
    for index in range(banks):
        count = min(slots, max(TILES - slots * index, 0))
        values = jnp.zeros((LANES, LANES), jnp.float32)
        if count:
            values = piece[slots * index : slots * index + count].astype(jnp.float32)
            values = values.reshape(count * group, LANES)
            if count < slots:
                gap = jnp.zeros((LANES - count * group, LANES), jnp.float32)
                values = jnp.concatenate([values, gap], axis=0)
            values = values.T
        turned.append(values)
    codes = [values[125:126, :] for values in turned]
    heads = [jnp.where(used, values, 0.0) for values in turned]
    for extra in range(half - TILES):
        place, slot = divmod(TILES + extra, slots)
        mask = ahead == slot
        code = pltpu.roll(turned[0][126:127, :], (slot - extra) * group % LANES, 1)
        codes[place] = jnp.where(mask, code, codes[place])
        for quarter in range(4):
            source, lanes = divmod(4 * extra + quarter, slots)
            values = turned[source][96:128]
            sample = lag[96:128]
            inside = jnp.logical_and(sample >= tlen, sample < tlen + QUARTER)
            values = jnp.where(inside, values, 0.0)
            values = pltpu.roll(values, (slot - lanes) * group % LANES, 1)
            start = QUARTER * quarter - (tlen - 96)
            values = jnp.concatenate([values, jnp.zeros((8, LANES), jnp.float32)], axis=0)
            values = pltpu.roll(values, start % 8, 0)
            start -= start % 8
            if start < 0:
                values, start = values[8:], 0
            below = LANES - start - values.shape[0]
            if start:
                values = jnp.concatenate([jnp.zeros((start, LANES), jnp.float32), values], axis=0)
            if below > 0:
                values = jnp.concatenate([values, jnp.zeros((below, LANES), jnp.float32)], axis=0)
            heads[place] = heads[place] + jnp.where(mask, values[0:LANES], 0.0)
    for index, (values, code) in enumerate(zip(heads, codes)):
        code = jnp.where(slots * index + ahead < half, code, 0.0)
        center = jnp.sum(values, axis=0, keepdims=True) / tlen
        deviate = jnp.where(used, values - center, 0.0)
        spread = jnp.sqrt(jnp.sum(deviate * deviate, axis=0, keepdims=True) / tlen + EPSILON)
        unit = (deviate / (spread * tlen)).astype(jnp.bfloat16).astype(jnp.float32)
        unit = jnp.where(code > 0, unit, 0.0)
        shift = code.astype(jnp.int32) - 1
        for bit in (1, 2, 4):
            unit = jnp.where(jnp.bitwise_and(shift, bit) > 0, pltpu.roll(unit, bit, 0), unit)
        unit = jnp.where(lag == 112, code, unit)
        bank[index] = unit.astype(jnp.bfloat16)

    def build(number):
        wide = jnp.dot(bank[number], expand[...], preferred_element_type=jnp.float32)
        for slot in range(slots):
            spreaded = wide[:, slot * LANES : (slot + 1) * LANES]
            code = spreaded[112:113, :].astype(jnp.int32)
            usable = code > 0
            shift = code - 1
            moves = shift // 8 + ahead
            taps = spreaded[0:112, :]
            for bit in (1, 2, 4, 8):
                gap = jnp.zeros((8 * bit, LANES), jnp.float32)
                taps = jnp.where(
                    jnp.bitwise_and(moves, bit) > 0,
                    jnp.concatenate([gap, taps], axis=0),
                    jnp.concatenate([taps, gap], axis=0),
                )[0:top]
            taps = taps.astype(jnp.bfloat16)
            item = number * slots + slot
            pick = jnp.logical_and(lag == shift + 8 * ahead, usable)
            pick = jnp.where(pick, 1.0, 0.0).astype(jnp.bfloat16)
            for index in range(tile_count):
                skip = 8 * offset_count * index
                lanes = slice(LANES * index, LANES * (index + 1))
                if skip:
                    weight_a[item, 0:skip, lanes] = jnp.zeros((skip, LANES), jnp.bfloat16)
                    pick = jnp.concatenate(
                        [jnp.zeros((skip, LANES), jnp.bfloat16), pick[0 : LANES - skip]], axis=0
                    )
                weight_a[item, skip : skip + top, lanes] = taps
                rest = DEPTH - top - skip
                if rest:
                    weight_a[item, skip + top :, lanes] = jnp.zeros((rest, LANES), jnp.bfloat16)
                weight_r[item, 0:LANES, lanes] = pick
                weight_r[item, LANES : 2 * LANES, lanes] = pick

    def apply(number, count):
        for slot in range(count):
            item = number * slots + slot
            both = [left_a[base + item, 0:rows, :], left_a[base + item, 16 : rows + 16, :]]
            corr = jnp.dot(
                jnp.concatenate(both, axis=1), weight_a[item], preferred_element_type=jnp.float32
            )
            factor = jnp.dot(
                left_r[base + item], weight_r[item], preferred_element_type=jnp.float32
            )
            total[...] += corr * factor

    total[...] = before[...] if side else jnp.zeros_like(total)
    build(0)

    for number in range(1, banks):
        apply(number - 1, slots)
        build(number)

    apply(banks - 1, half - slots * (banks - 1))

    if not side:
        outs[0][...] = total[...]
        return
    rows_out = outs[0].shape[0]
    station = lax.axis_index("sta") % len(outs)
    for step, out in enumerate(outs):
        part = jnp.bitwise_xor(station, step)
        out[...] = total[pl.ds(pl.multiple_of(part * rows_out, rows_out), rows_out), :].astype(
            jnp.bfloat16
        )


def correlate(side, tlen, group, count, piece, left_a, left_r, *before):
    channels, rows, _ = left_r.shape
    width = OFFSETS * group
    half = channels // 2
    if side:
        out = [jax.ShapeDtypeStruct((rows // count, width), jnp.bfloat16)] * count
    else:
        out = [jax.ShapeDtypeStruct((rows, width), jnp.float32)]
    return pl.pallas_call(
        functools.partial(main_kernel, side, tlen, group),
        out_shape=out,
        in_specs=[VMEM] * (3 + len(before)),
        out_specs=[VMEM] * len(out),
        scratch_shapes=[
            pltpu.VMEM(((half + 1) * group // LANES, LANES, LANES), jnp.bfloat16),
            pltpu.VMEM((LANES, LANES // group * LANES), jnp.bfloat16),
            pltpu.VMEM((half + 1, DEPTH, width), jnp.bfloat16),
            pltpu.VMEM((half + 1, DEPTH, width), jnp.bfloat16),
            pltpu.VMEM((rows, width), jnp.float32),
        ],
        compiler_params=params(),
        cost_estimate=cost(3),
        name="correlate_" + ("second" if side else "first"),
    )(piece, left_a, left_r, *before)


def add_kernel(*refs):
    parts, keep, send = refs[:-2], refs[-2], refs[-1]
    rows = keep.shape[0]
    core = lax.axis_index("tm") % 2
    for out, which in ((keep, core), (send, 1 - core)):
        place = pl.ds(pl.multiple_of(which * rows, rows), rows)
        value = parts[0][place, :].astype(jnp.float32)
        for part in parts[1:]:
            value = value + part[place, :].astype(jnp.float32)
        out[...] = value


def add(parts):
    rows, width = parts[0].shape
    out = jax.ShapeDtypeStruct((rows // 2, width), jnp.float32)
    return pl.pallas_call(
        add_kernel,
        out_shape=[out, out],
        in_specs=[VMEM] * len(parts),
        out_specs=[VMEM, VMEM],
        compiler_params=params(),
        cost_estimate=cost(0.5),
        name="add",
    )(*parts)


def finish_kernel(group, ours, received, out):
    samples = out.shape[1]
    rows = ours.shape[0]
    value = ours[...] + received[...]
    high = value.astype(jnp.bfloat16).astype(jnp.float32)
    both = jnp.concatenate([high, value - high], axis=0).T.astype(jnp.bfloat16)
    row = lax.broadcasted_iota(jnp.int32, (2 * rows, samples), 0) % rows
    lane = lax.broadcasted_iota(jnp.int32, (2 * rows, samples), 1)
    place = jnp.logical_and(lane // STRIDE == row // 8, lane % 8 == 7 - row % 8)
    place = jnp.where(place, 1.0, 0.0).astype(jnp.bfloat16)
    wide = jnp.dot(both, place, preferred_element_type=jnp.float32)
    lane = lax.broadcasted_iota(jnp.int32, (group, samples), 1) // 8 % OFFSETS
    result = jnp.zeros((group, samples), jnp.float32)
    for offset in range(OFFSETS):
        result = jnp.where(lane == offset, wide[offset * group : (offset + 1) * group], result)
    out[...] = result


def finish(group, samples, ours, received):
    return pl.pallas_call(
        functools.partial(finish_kernel, group),
        out_shape=jax.ShapeDtypeStruct((group, samples), jnp.float32),
        in_specs=[VMEM, VMEM],
        out_specs=VMEM,
        compiler_params=params(),
        cost_estimate=cost(1),
        name="finish",
    )(ours, received)


def shards(waveforms, templates, available, moveout, bank_blocks):
    channels, samples = waveforms.shape
    blocks, events, _, tlen = templates.shape
    count_tm = lax.axis_size("tm")
    count_sta = lax.axis_size("sta")
    chips = count_tm // 2
    near = chips // 2
    group = 2 * events // chips

    def swap(array):
        return lax.ppermute(array, "tm", [(i, i ^ 1) for i in range(count_tm)])

    def across(array, step):
        return lax.ppermute(array, "tm", [(i, i ^ (2 * step)) for i in range(count_tm)])

    partner = swap(waveforms)
    mine, theirs, owners = pack(
        chips,
        group,
        bank_blocks,
        jnp.transpose(templates, (0, 2, 1, 3)),
        jnp.transpose(available, (2, 0, 1)),
        jnp.transpose(moveout, (2, 0, 1)),
    )
    theirs, partner = lax.optimization_barrier((theirs, partner))
    other = swap(theirs)
    pair = pair_waves(waveforms, partner)
    far = []
    for number in range(near - 1):
        steps = (chips - 1 - 2 * number, chips - 2 - 2 * number)
        route = [(2 * z + c, 2 * (z ^ steps[c]) + c) for z in range(chips) for c in range(2)]
        far.append(lax.ppermute(pair, "tm", route))
    beside = across(waveforms, 1)
    merged = list(merge(owners, mine, other))
    pieces = [across(merged[step], step) for step in reversed(range(1, chips))]
    pieces = [merged[0]] + pieces[::-1]
    swapped = swap(choose_waves(pair, beside, far))
    left_a, left_r = prepare_waves(tlen, swapped, pair, beside, far)

    left_a, left_r, *pieces = lax.optimization_barrier((left_a, left_r, *pieces[::-1]))
    pieces = pieces[::-1]
    first = choose_piece(owners, pieces)
    second = swap(first)
    total = correlate(0, tlen, group, near, first, left_a, left_r)
    parts = correlate(1, tlen, group, near, second, left_a, left_r, *total)
    gathered = []
    for step in range(near):
        route = []
        for d in range(count_tm):
            for s in range(count_sta):
                dest = near * (d % 2) + (s % near ^ step)
                sta = d // 2 ^ s
                route.append((d * count_sta + s, (2 * dest + s // near) * count_sta + sta))
        gathered.append(lax.ppermute(parts[step], ("tm", "sta"), route))
    ours, send = add(gathered)
    return finish(group, samples, ours, swap(send))


def solution(mesh):
    in_specs = (
        P("sta", "tm"),
        P("tm", None, "sta", None),
        P("tm", None, "sta"),
        P("tm", None, "sta"),
        P(),
    )
    out_specs = P("sta", "tm")
    return jax.shard_map(shards, mesh=mesh, in_specs=in_specs, out_specs=out_specs, check_vma=False)
```

```python
import functools

import jax
import jax.numpy as jnp
from jax import lax
from jax.experimental import pallas as pl
from jax.experimental.pallas import tpu as pltpu
from jax.sharding import PartitionSpec as P

EPSILON = 1e-06
LANES = 128
OFFSETS = 8
TILES = 12
QUARTER = 25
STRIDE = 64
DEPTH = 256
VMEM_LIMIT = 28 * 1024 * 1024

VMEM = pl.BlockSpec(memory_space=pltpu.VMEM)
ANY = pl.BlockSpec(memory_space=pl.ANY)


def params():
    return pltpu.CompilerParams(vmem_limit_bytes=VMEM_LIMIT)


def cost(micros):
    return pl.CostEstimate(
        flops=int(micros * 1e9), bytes_accessed=int(micros * 1e6), transcendentals=0
    )


def pack_kernel(bank_blocks, templates, available, moveout, mine, theirs, owners, chosen, raw, usable, shifts, square, sems):
    blocks, channels, events, tlen = templates.shape
    chips, _, group, _ = mine.shape
    half = channels // 2
    me = lax.axis_index("tm") % 2
    fetch = [
        pltpu.make_async_copy(source, target, sems.at[index])
        for index, (source, target) in enumerate(
            ((bank_blocks, chosen), (available, usable), (moveout, shifts), (templates, raw))
        )
    ]
    for copy in fetch:
        copy.start()
    mine[...] = jnp.zeros_like(mine)
    theirs[...] = jnp.zeros_like(theirs)
    square[...] = jnp.zeros_like(square)
    for copy in fetch[:3]:
        copy.wait()
    slots = [chosen[which] % blocks for which in range(2)]
    row = lax.broadcasted_iota(jnp.int32, owners.shape, 0)
    owners[...] = jnp.where(row == 0, chosen[0] // blocks, chosen[1] // blocks)
    flags = jnp.where(usable[...] > 0, shifts[...] + 1, 0).astype(jnp.float32)
    codes = []
    for which in range(2):
        code = flags[:, 0, :]
        for block in range(1, blocks):
            code = jnp.where(slots[which] == block, flags[:, block, :], code)
        square[0:channels, 0:events] = code
        turned = square[...].T
        later = pltpu.roll(turned, LANES - half, 1)
        codes.append([jnp.where(me == core, turned, later) for core in range(2)])
    fetch[3].wait()
    for which in range(2):
        for side, out in enumerate((mine, theirs)):
            first = half * jnp.where(me == side, 0, 1)
            code = codes[which][side].astype(jnp.bfloat16)
            for tile in range(TILES):
                extra = TILES + tile // 4
                start = QUARTER * (tile % 4)
                for index in range(events // group):
                    chip = which * (events // group) + index
                    rows = slice(index * group, (index + 1) * group)
                    out[chip, tile, :, 0:tlen] = raw[slots[which], first + tile, rows, :]
                    out[chip, tile, :, tlen : tlen + QUARTER] = raw[
                        slots[which], first + extra, rows, start : start + QUARTER
                    ]
                    out[chip, tile, :, 125:126] = code[rows, tile : tile + 1]
                    if tile < half - TILES:
                        beyond = TILES + tile
                        out[chip, tile, :, 126:127] = code[rows, beyond : beyond + 1]


def pack(chips, group, bank_blocks, templates, available, moveout):
    shape = (chips, TILES, group, LANES)
    held = [
        pltpu.with_memory_space_constraint(array, pltpu.HBM)
        for array in (bank_blocks, templates, available, moveout)
    ]
    return pl.pallas_call(
        pack_kernel,
        out_shape=[jax.ShapeDtypeStruct(shape, jnp.bfloat16)] * 2
        + [jax.ShapeDtypeStruct((8, LANES), jnp.int32)],
        in_specs=[ANY] * 4,
        out_specs=[VMEM] * 3,
        scratch_shapes=[
            pltpu.SMEM(bank_blocks.shape, jnp.int32),
            pltpu.VMEM(templates.shape, jnp.bfloat16),
            pltpu.VMEM(available.shape, jnp.int32),
            pltpu.VMEM(moveout.shape, jnp.int32),
            pltpu.VMEM((LANES, LANES), jnp.float32),
            pltpu.SemaphoreType.DMA((4,)),
        ],
        compiler_params=params(),
        cost_estimate=cost(2),
        name="pack",
    )(*held)


def owner_chip(owners, dest, chips):
    return jnp.where(dest < chips // 2, owners[0, 0], owners[1, 0]) // 2


def merge_kernel(owners, mine, other, *outs):
    chips = mine.shape[0]
    size = TILES // 2
    me = lax.axis_index("tm")
    for step in range(chips):
        dest = jnp.bitwise_xor(me // 2, step)
        owner = jnp.where(dest < chips // 2, owners[0, 0], owners[1, 0])
        for source, taken in ((mine, owner % 2 == me % 2), (other, owner % 2 != me % 2)):

            @pl.when(taken)
            def _():
                for part in range(2):
                    tiles = slice(size * part, size * (part + 1))
                    outs[2 * part + step % 2][step // 2] = source[dest, tiles]


def merge(owners, mine, other):
    chips, _, group, _ = mine.shape
    out = jax.ShapeDtypeStruct((chips // 2, TILES // 2, group, LANES), mine.dtype)
    return pl.pallas_call(
        merge_kernel,
        out_shape=[out] * 4,
        in_specs=[VMEM] * 3,
        out_specs=[VMEM] * 4,
        compiler_params=params(),
        cost_estimate=cost(0.3),
        name="merge",
    )(owners, mine, other)


def halve_kernel(bit, chips, owners, keep, received, *outs):
    chip = lax.axis_index("tm") // 2
    for entry in range(keep.shape[0]):
        dest = jnp.bitwise_xor(chip, 2 * bit * entry)
        owner = owner_chip(owners, dest, chips)
        there = jnp.bitwise_and(jnp.bitwise_xor(owner, chip), bit) > 0
        outs[entry % 2][entry // 2] = jnp.where(there, received[entry], keep[entry])


def halve(bit, chips, owners, keep, received):
    count = keep.shape[0] // 2
    out = jax.ShapeDtypeStruct((count,) + keep.shape[1:], keep.dtype)
    return pl.pallas_call(
        functools.partial(halve_kernel, bit, chips),
        out_shape=[out] * 2,
        in_specs=[VMEM] * 3,
        out_specs=[VMEM] * 2,
        compiler_params=params(),
        cost_estimate=cost(0.05),
        name="halve",
    )(owners, keep, received)


def own_kernel(chips, owners, *refs):
    parts, out = refs[:-1], refs[-1]
    chip = lax.axis_index("tm") // 2
    owner = owner_chip(owners, chip, chips)
    there = jnp.bitwise_and(jnp.bitwise_xor(owner, chip), chips // 2) > 0
    size = parts[0].shape[1]
    for part in range(2):
        keep, received = parts[2 * part : 2 * part + 2]
        out[size * part : size * (part + 1)] = jnp.where(there, received[0], keep[0])


def choose_piece(chips, owners, parts):
    _, size, group, lanes = parts[0].shape
    return pl.pallas_call(
        functools.partial(own_kernel, chips),
        out_shape=jax.ShapeDtypeStruct((2 * size, group, lanes), parts[0].dtype),
        in_specs=[VMEM] * 5,
        out_specs=VMEM,
        compiler_params=params(),
        cost_estimate=cost(0.3),
        name="choose_piece",
    )(owners, *parts)


def lagged(row, ahead):
    copies = jnp.broadcast_to(row, (8, row.shape[1]))
    return pltpu.roll(copies, row.shape[1] - 7 - ahead, 1, stride=1, stride_axis=0)


def segment(me, other, parity, pair, beside, far, default):
    chip, core = me // 2, me % 2
    chips = 2 * len(far) + 2
    step = jnp.bitwise_xor(chip, other)
    value = default[...]
    value = jnp.where(jnp.logical_and(step == 1, core == parity), beside[...], value)
    value = jnp.where(step == 0, pair[parity], value)
    for number, array in enumerate(far):
        value = jnp.where(step == chips - 1 - 2 * number - core, array[parity], value)
    return value


def pair_kernel(own, partner, out):
    core = lax.axis_index("tm") % 2
    out[core] = own[...]
    out[1 - core] = partner[...]


def pair_waves(own, partner):
    return pl.pallas_call(
        pair_kernel,
        out_shape=jax.ShapeDtypeStruct((2,) + own.shape, own.dtype),
        in_specs=[VMEM] * 2,
        out_specs=VMEM,
        compiler_params=params(),
        cost_estimate=cost(0.05),
        name="pair_waves",
    )(own, partner)


def choose_kernel(pair, beside, *rest):
    far, out = rest[:-1], rest[-1]
    near = out.shape[0] - 1
    me = lax.axis_index("tm")
    chip, core = me // 2, me % 2
    for entry in range(near):
        number, parity = divmod(entry, 2)
        step = jnp.bitwise_xor(chip, near * (1 - core) + 2 * number) // 2
        value = beside[...]
        for place, array in enumerate(far):
            value = jnp.where(step == near - 1 - place, array[parity], value)
        out[entry] = value
    out[near] = segment(me, near, 0, pair, beside, far, beside)


def choose_waves(pair, beside, far):
    return pl.pallas_call(
        choose_kernel,
        out_shape=jax.ShapeDtypeStruct((len(far) + 2,) + beside.shape, beside.dtype),
        in_specs=[VMEM] * (2 + len(far)),
        out_specs=VMEM,
        compiler_params=params(),
        cost_estimate=cost(0.05),
        name="choose_waves",
    )(pair, beside, *far)


def waves_kernel(channels, tlen, unroll, swapped, pair, beside, *rest):
    far = rest[:-4]
    left_a, left_r, padded, inverse = rest[-4:]
    samples = beside.shape[1]
    near = swapped.shape[0] - 1
    length = 2 * near * samples
    count = padded.shape[1] // LANES
    me = lax.axis_index("tm")
    core = me % 2
    padded[...] = jnp.zeros_like(padded)
    for index in range(2 * near):
        entry, parity = divmod(index, 2)
        given = swapped.at[2 * (entry // 2) + parity]
        wave = segment(me, near * core + entry, parity, pair, beside, far, given)
        padded[0:channels, samples * index : samples * (index + 1)] = wave.astype(jnp.float32)
    rim = segment(me, near * core + near, 0, pair, beside, far, swapped.at[near])
    rim = rim[:, 0 : padded.shape[1] - length].astype(jnp.float32)
    padded[0:channels, length:] = jnp.where(core == 0, rim, 0.0)

    rows = 32 * count
    values = [padded[:, LANES * tile : LANES * (tile + 1)] for tile in range(count)]
    values = jnp.concatenate(values + [jnp.zeros((32, LANES), jnp.float32)], axis=0)
    square = values * values
    high = square.astype(jnp.bfloat16)
    low = (square - high.astype(jnp.float32)).astype(jnp.bfloat16)
    values = values.astype(jnp.bfloat16)
    lag = lax.broadcasted_iota(jnp.int32, (2 * LANES, LANES), 0)
    lag = lag - lax.broadcasted_iota(jnp.int32, (2 * LANES, LANES), 1)
    band = jnp.where(jnp.logical_and(lag >= 0, lag < tlen), 1.0, 0.0).astype(jnp.bfloat16)

    def windows(array):
        both = jnp.concatenate([array[0:rows], array[32 : rows + 32]], axis=1)
        return jnp.dot(both, band, preferred_element_type=jnp.float32)

    mean = windows(values) / tlen
    scale = lax.rsqrt((windows(high) + windows(low)) / tlen - mean * mean + EPSILON)
    for tile in range(count):
        inverse[:, LANES * tile : LANES * (tile + 1)] = scale[32 * tile : 32 * (tile + 1)]

    def interleaved(row, tiles):
        even, odd = lagged(row, 0), lagged(row, STRIDE)
        parts = []
        for tile in range(tiles):
            lanes = slice(LANES * tile, LANES * (tile + 1))
            parts += [even[:, lanes], odd[:, lanes]]
        return jnp.concatenate(parts, axis=0)

    @pl.loop(0, channels // unroll)
    def _(step):
        for item in range(unroll):
            channel = step * unroll + item
            value = interleaved(padded[pl.ds(channel, 1), :], length // LANES + 1)
            left_a[channel] = value.astype(jnp.bfloat16)
            value = interleaved(inverse[pl.ds(channel, 1), :], length // LANES)
            high = value.astype(jnp.bfloat16)
            left_r[channel, :, 0:LANES] = high
            left_r[channel, :, LANES:] = (value - high.astype(jnp.float32)).astype(jnp.bfloat16)


def prepare_waves(tlen, swapped, pair, beside, far):
    channels, samples = beside.shape
    length = 2 * (swapped.shape[0] - 1) * samples
    rows = length // OFFSETS
    unroll = max(step for step in (1, 2, 3) if channels % step == 0)
    return pl.pallas_call(
        functools.partial(waves_kernel, channels, tlen, unroll),
        out_shape=[
            jax.ShapeDtypeStruct((channels, rows + 16, LANES), jnp.bfloat16),
            jax.ShapeDtypeStruct((channels, rows, 2 * LANES), jnp.bfloat16),
        ],
        in_specs=[VMEM] * (3 + len(far)),
        out_specs=[VMEM, VMEM],
        scratch_shapes=[
            pltpu.VMEM((32, length + 2 * LANES), jnp.float32),
            pltpu.VMEM((32, length + 2 * LANES), jnp.float32),
        ],
        compiler_params=params(),
        cost_estimate=cost(0.05),
        name="prepare_waves",
    )(swapped, pair, beside, *far)


def main_kernel(side, tlen, group, piece, left_a, left_r, *rest):
    outs = rest[:-5]
    if side:
        before, outs = outs[0], outs[1:]
    bank, expand, weight_a, weight_r, total = rest[-5:]
    core = lax.axis_index("tm") % 2
    channels, rows, _ = left_r.shape
    half = channels // 2
    base = half * jnp.where(core == side, 0, 1)
    slots = LANES // group
    banks = (half + 1) // slots
    offset_count = LANES // group
    tile_count = OFFSETS // offset_count
    top = 112 + 8 * (7 + offset_count - 1)
    top = top + top % 16

    lag = lax.broadcasted_iota(jnp.int32, (LANES, LANES), 0)
    target = lax.broadcasted_iota(jnp.int32, (LANES, LANES), 1)
    lane = lax.broadcasted_iota(jnp.int32, (1, LANES), 1)
    used = lag < tlen
    ahead = lane // group
    for slot in range(slots):
        chosen = jnp.where(lag == target % group + slot * group, 1.0, 0.0)
        expand[:, slot * LANES : (slot + 1) * LANES] = chosen.astype(jnp.bfloat16)
    turned = []
    for index in range(banks):
        count = min(slots, max(TILES - slots * index, 0))
        values = jnp.zeros((LANES, LANES), jnp.float32)
        if count:
            values = piece[slots * index : slots * index + count].astype(jnp.float32)
            values = values.reshape(count * group, LANES)
            if count < slots:
                gap = jnp.zeros((LANES - count * group, LANES), jnp.float32)
                values = jnp.concatenate([values, gap], axis=0)
            values = values.T
        turned.append(values)
    codes = [values[125:126, :] for values in turned]
    heads = [jnp.where(used, values, 0.0) for values in turned]
    for extra in range(half - TILES):
        place, slot = divmod(TILES + extra, slots)
        mask = ahead == slot
        code = pltpu.roll(turned[0][126:127, :], (slot - extra) * group % LANES, 1)
        codes[place] = jnp.where(mask, code, codes[place])
        for quarter in range(4):
            source, lanes = divmod(4 * extra + quarter, slots)
            values = turned[source][96:128]
            sample = lag[96:128]
            inside = jnp.logical_and(sample >= tlen, sample < tlen + QUARTER)
            values = jnp.where(inside, values, 0.0)
            values = pltpu.roll(values, (slot - lanes) * group % LANES, 1)
            start = QUARTER * quarter - (tlen - 96)
            values = jnp.concatenate([values, jnp.zeros((8, LANES), jnp.float32)], axis=0)
            values = pltpu.roll(values, start % 8, 0)
            start -= start % 8
            if start < 0:
                values, start = values[8:], 0
            below = LANES - start - values.shape[0]
            if start:
                values = jnp.concatenate([jnp.zeros((start, LANES), jnp.float32), values], axis=0)
            if below > 0:
                values = jnp.concatenate([values, jnp.zeros((below, LANES), jnp.float32)], axis=0)
            heads[place] = heads[place] + jnp.where(mask, values[0:LANES], 0.0)
    for index, (values, code) in enumerate(zip(heads, codes)):
        code = jnp.where(slots * index + ahead < half, code, 0.0)
        center = jnp.sum(values, axis=0, keepdims=True) / tlen
        deviate = jnp.where(used, values - center, 0.0)
        spread = jnp.sqrt(jnp.sum(deviate * deviate, axis=0, keepdims=True) / tlen + EPSILON)
        unit = (deviate / (spread * tlen)).astype(jnp.bfloat16).astype(jnp.float32)
        unit = jnp.where(code > 0, unit, 0.0)
        shift = code.astype(jnp.int32) - 1
        for bit in (1, 2, 4):
            unit = jnp.where(jnp.bitwise_and(shift, bit) > 0, pltpu.roll(unit, bit, 0), unit)
        unit = jnp.where(lag == 112, code, unit)
        bank[index] = unit.astype(jnp.bfloat16)

    def build(number):
        wide = jnp.dot(bank[number], expand[...], preferred_element_type=jnp.float32)
        for slot in range(slots):
            spreaded = wide[:, slot * LANES : (slot + 1) * LANES]
            code = spreaded[112:113, :].astype(jnp.int32)
            usable = code > 0
            shift = code - 1
            moves = shift // 8 + ahead
            taps = spreaded[0:112, :]
            for bit in (1, 2, 4, 8):
                gap = jnp.zeros((8 * bit, LANES), jnp.float32)
                taps = jnp.where(
                    jnp.bitwise_and(moves, bit) > 0,
                    jnp.concatenate([gap, taps], axis=0),
                    jnp.concatenate([taps, gap], axis=0),
                )[0:top]
            taps = taps.astype(jnp.bfloat16)
            item = number * slots + slot
            pick = jnp.logical_and(lag == shift + 8 * ahead, usable)
            pick = jnp.where(pick, 1.0, 0.0).astype(jnp.bfloat16)
            for index in range(tile_count):
                skip = 8 * offset_count * index
                lanes = slice(LANES * index, LANES * (index + 1))
                if skip:
                    weight_a[item, 0:skip, lanes] = jnp.zeros((skip, LANES), jnp.bfloat16)
                    pick = jnp.concatenate(
                        [jnp.zeros((skip, LANES), jnp.bfloat16), pick[0 : LANES - skip]], axis=0
                    )
                weight_a[item, skip : skip + top, lanes] = taps
                rest = DEPTH - top - skip
                if rest:
                    weight_a[item, skip + top :, lanes] = jnp.zeros((rest, LANES), jnp.bfloat16)
                weight_r[item, 0:LANES, lanes] = pick
                weight_r[item, LANES : 2 * LANES, lanes] = pick

    def apply(number, count):
        for slot in range(count):
            item = number * slots + slot
            both = [left_a[base + item, 0:rows, :], left_a[base + item, 16 : rows + 16, :]]
            corr = jnp.dot(
                jnp.concatenate(both, axis=1), weight_a[item], preferred_element_type=jnp.float32
            )
            factor = jnp.dot(
                left_r[base + item], weight_r[item], preferred_element_type=jnp.float32
            )
            total[...] += corr * factor

    total[...] = before[...] if side else jnp.zeros_like(total)
    build(0)

    for number in range(1, banks):
        apply(number - 1, slots)
        build(number)

    apply(banks - 1, half - slots * (banks - 1))

    if not side:
        outs[0][...] = total[...]
        return
    rows_out = outs[0].shape[0]
    station = lax.axis_index("sta") % len(outs)
    for step, out in enumerate(outs):
        part = jnp.bitwise_xor(station, step)
        out[...] = total[pl.ds(pl.multiple_of(part * rows_out, rows_out), rows_out), :].astype(
            jnp.bfloat16
        )


def correlate(side, tlen, group, count, piece, left_a, left_r, *before):
    channels, rows, _ = left_r.shape
    width = OFFSETS * group
    half = channels // 2
    if side:
        out = [jax.ShapeDtypeStruct((rows // count, width), jnp.bfloat16)] * count
    else:
        out = [jax.ShapeDtypeStruct((rows, width), jnp.float32)]
    return pl.pallas_call(
        functools.partial(main_kernel, side, tlen, group),
        out_shape=out,
        in_specs=[VMEM] * (3 + len(before)),
        out_specs=[VMEM] * len(out),
        scratch_shapes=[
            pltpu.VMEM(((half + 1) * group // LANES, LANES, LANES), jnp.bfloat16),
            pltpu.VMEM((LANES, LANES // group * LANES), jnp.bfloat16),
            pltpu.VMEM((half + 1, DEPTH, width), jnp.bfloat16),
            pltpu.VMEM((half + 1, DEPTH, width), jnp.bfloat16),
            pltpu.VMEM((rows, width), jnp.float32),
        ],
        compiler_params=params(),
        cost_estimate=cost(3),
        name="correlate_" + ("second" if side else "first"),
    )(piece, left_a, left_r, *before)


def add_kernel(*refs):
    parts, keep, send = refs[:-2], refs[-2], refs[-1]
    rows = keep.shape[0]
    core = lax.axis_index("tm") % 2
    for out, which in ((keep, core), (send, 1 - core)):
        place = pl.ds(pl.multiple_of(which * rows, rows), rows)
        value = parts[0][place, :].astype(jnp.float32)
        for part in parts[1:]:
            value = value + part[place, :].astype(jnp.float32)
        out[...] = value


def add(parts):
    rows, width = parts[0].shape
    out = jax.ShapeDtypeStruct((rows // 2, width), jnp.float32)
    return pl.pallas_call(
        add_kernel,
        out_shape=[out, out],
        in_specs=[VMEM] * len(parts),
        out_specs=[VMEM, VMEM],
        compiler_params=params(),
        cost_estimate=cost(0.5),
        name="add",
    )(*parts)


def finish_kernel(group, ours, received, out):
    samples = out.shape[1]
    rows = ours.shape[0]
    value = ours[...] + received[...]
    high = value.astype(jnp.bfloat16).astype(jnp.float32)
    both = jnp.concatenate([high, value - high], axis=0).T.astype(jnp.bfloat16)
    row = lax.broadcasted_iota(jnp.int32, (2 * rows, samples), 0) % rows
    lane = lax.broadcasted_iota(jnp.int32, (2 * rows, samples), 1)
    place = jnp.logical_and(lane // STRIDE == row // 8, lane % 8 == 7 - row % 8)
    place = jnp.where(place, 1.0, 0.0).astype(jnp.bfloat16)
    wide = jnp.dot(both, place, preferred_element_type=jnp.float32)
    lane = lax.broadcasted_iota(jnp.int32, (group, samples), 1) // 8 % OFFSETS
    result = jnp.zeros((group, samples), jnp.float32)
    for offset in range(OFFSETS):
        result = jnp.where(lane == offset, wide[offset * group : (offset + 1) * group], result)
    out[...] = result


def finish(group, samples, ours, received):
    return pl.pallas_call(
        functools.partial(finish_kernel, group),
        out_shape=jax.ShapeDtypeStruct((group, samples), jnp.float32),
        in_specs=[VMEM, VMEM],
        out_specs=VMEM,
        compiler_params=params(),
        cost_estimate=cost(1),
        name="finish",
    )(ours, received)


def shards(waveforms, templates, available, moveout, bank_blocks):
    channels, samples = waveforms.shape
    blocks, events, _, tlen = templates.shape
    count_tm = lax.axis_size("tm")
    count_sta = lax.axis_size("sta")
    chips = count_tm // 2
    near = chips // 2
    group = 2 * events // chips

    def swap(array):
        return lax.ppermute(array, "tm", [(i, i ^ 1) for i in range(count_tm)])

    def across(array, step):
        return lax.ppermute(array, "tm", [(i, i ^ (2 * step)) for i in range(count_tm)])

    partner = swap(waveforms)
    mine, theirs, owners = pack(
        chips,
        group,
        bank_blocks,
        jnp.transpose(templates, (0, 2, 1, 3)),
        jnp.transpose(available, (2, 0, 1)),
        jnp.transpose(moveout, (2, 0, 1)),
    )
    theirs, partner = lax.optimization_barrier((theirs, partner))
    other = swap(theirs)
    pair = pair_waves(waveforms, partner)
    far = []
    for number in range(near - 1):
        steps = (chips - 1 - 2 * number, chips - 2 - 2 * number)
        route = [(2 * z + c, 2 * (z ^ steps[c]) + c) for z in range(chips) for c in range(2)]
        far.append(lax.ppermute(pair, "tm", route))
    beside = across(waveforms, 1)
    kept_0, sent_0, kept_1, sent_1 = merge(owners, mine, other)
    parts = [(kept_0, sent_0), (kept_1, sent_1)]
    bit = 1
    while 2 * bit < chips:
        parts = [halve(bit, chips, owners, kept, across(sent, bit)) for kept, sent in parts]
        bit *= 2
    pieces = [piece for kept, sent in parts for piece in (kept, across(sent, bit))]
    swapped = swap(choose_waves(pair, beside, far))
    left_a, left_r = prepare_waves(tlen, swapped, pair, beside, far)

    left_a, left_r, *pieces = lax.optimization_barrier((left_a, left_r, *pieces))
    first = choose_piece(chips, owners, pieces)
    second = swap(first)
    total = correlate(0, tlen, group, near, first, left_a, left_r)
    parts = correlate(1, tlen, group, near, second, left_a, left_r, *total)
    gathered = []
    for step in range(near):
        route = []
        for d in range(count_tm):
            for s in range(count_sta):
                dest = near * (d % 2) + (s % near ^ step)
                route.append((d * count_sta + s, (2 * dest + s // near) * count_sta + d // 2))
        gathered.append(lax.ppermute(parts[step], ("tm", "sta"), route))
    ours, send = add(gathered)
    return finish(group, samples, ours, swap(send))


def solution(mesh):
    in_specs = (
        P("sta", "tm"),
        P("tm", None, "sta", None),
        P("tm", None, "sta"),
        P("tm", None, "sta"),
        P(),
    )
    out_specs = P("sta", "tm")
    return jax.shard_map(shards, mesh=mesh, in_specs=in_specs, out_specs=out_specs, check_vma=False)
```

```python
import functools

import jax
import jax.numpy as jnp
from jax import lax
from jax.experimental import pallas as pl
from jax.experimental.pallas import tpu as pltpu
from jax.sharding import PartitionSpec as P

EPSILON = 1e-06
LANES = 128
OFFSETS = 8
TILES = 12
QUARTER = 25
STRIDE = 64
DEPTH = 256
VMEM_LIMIT = 28 * 1024 * 1024

VMEM = pl.BlockSpec(memory_space=pltpu.VMEM)
ANY = pl.BlockSpec(memory_space=pl.ANY)


def params():
    return pltpu.CompilerParams(vmem_limit_bytes=VMEM_LIMIT)


def cost(micros):
    return pl.CostEstimate(
        flops=int(micros * 1e9), bytes_accessed=int(micros * 1e6), transcendentals=0
    )


def pack_kernel(bank_blocks, templates, available, moveout, mine, theirs, owners, chosen, raw, usable, shifts, square, sems):
    blocks, channels, events, tlen = templates.shape
    chips, _, group, _ = mine.shape
    half = channels // 2
    me = lax.axis_index("tm") % 2
    fetch = [
        pltpu.make_async_copy(source, target, sems.at[index])
        for index, (source, target) in enumerate(
            ((bank_blocks, chosen), (available, usable), (moveout, shifts), (templates, raw))
        )
    ]
    for copy in fetch:
        copy.start()
    mine[...] = jnp.zeros_like(mine)
    theirs[...] = jnp.zeros_like(theirs)
    square[...] = jnp.zeros_like(square)
    for copy in fetch[:3]:
        copy.wait()
    slots = [chosen[which] % blocks for which in range(2)]
    row = lax.broadcasted_iota(jnp.int32, owners.shape, 0)
    owners[...] = jnp.where(row == 0, chosen[0] // blocks, chosen[1] // blocks)
    flags = jnp.where(usable[...] > 0, shifts[...] + 1, 0).astype(jnp.float32)
    codes = []
    for which in range(2):
        code = flags[:, 0, :]
        for block in range(1, blocks):
            code = jnp.where(slots[which] == block, flags[:, block, :], code)
        square[0:channels, 0:events] = code
        turned = square[...].T
        later = pltpu.roll(turned, LANES - half, 1)
        codes.append([jnp.where(me == core, turned, later) for core in range(2)])
    fetch[3].wait()
    for which in range(2):
        for side, out in enumerate((mine, theirs)):
            first = half * jnp.where(me == side, 0, 1)
            code = codes[which][side].astype(jnp.bfloat16)
            for tile in range(TILES):
                extra = TILES + tile // 4
                start = QUARTER * (tile % 4)
                for index in range(events // group):
                    chip = which * (events // group) + index
                    rows = slice(index * group, (index + 1) * group)
                    out[chip, tile, :, 0:tlen] = raw[slots[which], first + tile, rows, :]
                    out[chip, tile, :, tlen : tlen + QUARTER] = raw[
                        slots[which], first + extra, rows, start : start + QUARTER
                    ]
                    out[chip, tile, :, 125:126] = code[rows, tile : tile + 1]
                    if tile < half - TILES:
                        beyond = TILES + tile
                        out[chip, tile, :, 126:127] = code[rows, beyond : beyond + 1]


def pack(chips, group, bank_blocks, templates, available, moveout):
    shape = (chips, TILES, group, LANES)
    held = [
        pltpu.with_memory_space_constraint(array, pltpu.HBM)
        for array in (bank_blocks, templates, available, moveout)
    ]
    return pl.pallas_call(
        pack_kernel,
        out_shape=[jax.ShapeDtypeStruct(shape, jnp.bfloat16)] * 2
        + [jax.ShapeDtypeStruct((8, LANES), jnp.int32)],
        in_specs=[ANY] * 4,
        out_specs=[VMEM] * 3,
        scratch_shapes=[
            pltpu.SMEM(bank_blocks.shape, jnp.int32),
            pltpu.VMEM(templates.shape, jnp.bfloat16),
            pltpu.VMEM(available.shape, jnp.int32),
            pltpu.VMEM(moveout.shape, jnp.int32),
            pltpu.VMEM((LANES, LANES), jnp.float32),
            pltpu.SemaphoreType.DMA((4,)),
        ],
        compiler_params=params(),
        cost_estimate=cost(2),
        name="pack",
    )(*held)


def merge_kernel(owners, mine, other, *outs):
    chips = len(outs)
    me = lax.axis_index("tm")
    for step, out in enumerate(outs):
        dest = jnp.bitwise_xor(me // 2, step)
        owner = jnp.where(dest < chips // 2, owners[0, 0], owners[1, 0])
        here = owner % 2 == me % 2

        @pl.when(here)
        def _():
            out[...] = mine[dest]

        @pl.when(jnp.logical_not(here))
        def _():
            out[...] = other[dest]


def merge(owners, mine, other):
    chips = mine.shape[0]
    return pl.pallas_call(
        merge_kernel,
        out_shape=[jax.ShapeDtypeStruct(mine.shape[1:], mine.dtype)] * chips,
        in_specs=[VMEM] * 3,
        out_specs=[VMEM] * chips,
        compiler_params=params(),
        cost_estimate=cost(0.3),
        name="merge",
    )(owners, mine, other)


def lagged(row, ahead):
    copies = jnp.broadcast_to(row, (8, row.shape[1]))
    return pltpu.roll(copies, row.shape[1] - 7 - ahead, 1, stride=1, stride_axis=0)


def segment(me, other, parity, pair, beside, far, default):
    chip, core = me // 2, me % 2
    chips = 2 * len(far) + 2
    step = jnp.bitwise_xor(chip, other)
    value = default[...]
    value = jnp.where(jnp.logical_and(step == 1, core == parity), beside[...], value)
    value = jnp.where(step == 0, pair[parity], value)
    for number, array in enumerate(far):
        value = jnp.where(step == chips - 1 - 2 * number - core, array[parity], value)
    return value


def pair_kernel(own, partner, out):
    core = lax.axis_index("tm") % 2
    out[core] = own[...]
    out[1 - core] = partner[...]


def pair_waves(own, partner):
    return pl.pallas_call(
        pair_kernel,
        out_shape=jax.ShapeDtypeStruct((2,) + own.shape, own.dtype),
        in_specs=[VMEM] * 2,
        out_specs=VMEM,
        compiler_params=params(),
        cost_estimate=cost(0.05),
        name="pair_waves",
    )(own, partner)


def choose_kernel(pair, beside, *rest):
    far, out = rest[:-1], rest[-1]
    near = out.shape[0] - 1
    me = lax.axis_index("tm")
    chip, core = me // 2, me % 2
    for entry in range(near):
        number, parity = divmod(entry, 2)
        step = jnp.bitwise_xor(chip, near * (1 - core) + 2 * number) // 2
        value = beside[...]
        for place, array in enumerate(far):
            value = jnp.where(step == near - 1 - place, array[parity], value)
        out[entry] = value
    out[near] = segment(me, near, 0, pair, beside, far, beside)


def choose_waves(pair, beside, far):
    return pl.pallas_call(
        choose_kernel,
        out_shape=jax.ShapeDtypeStruct((len(far) + 2,) + beside.shape, beside.dtype),
        in_specs=[VMEM] * (2 + len(far)),
        out_specs=VMEM,
        compiler_params=params(),
        cost_estimate=cost(0.05),
        name="choose_waves",
    )(pair, beside, *far)


def own_kernel(owners, *refs):
    pieces, out = refs[:-1], refs[-1]
    chip = lax.axis_index("tm") // 2
    owner = jnp.where(chip < len(pieces) // 2, owners[0, 0], owners[1, 0])
    source = jnp.bitwise_xor(owner // 2, chip)
    value = pieces[0][...]
    for number, piece in enumerate(pieces[1:], 1):
        value = jnp.where(source == number, piece[...], value)
    out[...] = value


def choose_piece(owners, pieces):
    return pl.pallas_call(
        own_kernel,
        out_shape=jax.ShapeDtypeStruct(pieces[0].shape, pieces[0].dtype),
        in_specs=[VMEM] * (1 + len(pieces)),
        out_specs=VMEM,
        compiler_params=params(),
        cost_estimate=cost(0.3),
        name="choose_piece",
    )(owners, *pieces)


def waves_kernel(channels, tlen, unroll, swapped, pair, beside, *rest):
    far = rest[:-4]
    left_a, left_r, padded, inverse = rest[-4:]
    samples = beside.shape[1]
    near = swapped.shape[0] - 1
    length = 2 * near * samples
    count = padded.shape[1] // LANES
    me = lax.axis_index("tm")
    core = me % 2
    padded[...] = jnp.zeros_like(padded)
    for index in range(2 * near):
        entry, parity = divmod(index, 2)
        given = swapped.at[2 * (entry // 2) + parity]
        wave = segment(me, near * core + entry, parity, pair, beside, far, given)
        padded[0:channels, samples * index : samples * (index + 1)] = wave.astype(jnp.float32)
    rim = segment(me, near * core + near, 0, pair, beside, far, swapped.at[near])
    rim = rim[:, 0 : padded.shape[1] - length].astype(jnp.float32)
    padded[0:channels, length:] = jnp.where(core == 0, rim, 0.0)

    rows = 32 * count
    values = [padded[:, LANES * tile : LANES * (tile + 1)] for tile in range(count)]
    values = jnp.concatenate(values + [jnp.zeros((32, LANES), jnp.float32)], axis=0)
    square = values * values
    high = square.astype(jnp.bfloat16)
    low = (square - high.astype(jnp.float32)).astype(jnp.bfloat16)
    values = values.astype(jnp.bfloat16)
    lag = lax.broadcasted_iota(jnp.int32, (2 * LANES, LANES), 0)
    lag = lag - lax.broadcasted_iota(jnp.int32, (2 * LANES, LANES), 1)
    band = jnp.where(jnp.logical_and(lag >= 0, lag < tlen), 1.0, 0.0).astype(jnp.bfloat16)

    def windows(array):
        both = jnp.concatenate([array[0:rows], array[32 : rows + 32]], axis=1)
        return jnp.dot(both, band, preferred_element_type=jnp.float32)

    mean = windows(values) / tlen
    scale = lax.rsqrt((windows(high) + windows(low)) / tlen - mean * mean + EPSILON)
    for tile in range(count):
        inverse[:, LANES * tile : LANES * (tile + 1)] = scale[32 * tile : 32 * (tile + 1)]

    def interleaved(row, tiles):
        even, odd = lagged(row, 0), lagged(row, STRIDE)
        parts = []
        for tile in range(tiles):
            lanes = slice(LANES * tile, LANES * (tile + 1))
            parts += [even[:, lanes], odd[:, lanes]]
        return jnp.concatenate(parts, axis=0)

    @pl.loop(0, channels // unroll)
    def _(step):
        for item in range(unroll):
            channel = step * unroll + item
            value = interleaved(padded[pl.ds(channel, 1), :], length // LANES + 1)
            left_a[channel] = value.astype(jnp.bfloat16)
            value = interleaved(inverse[pl.ds(channel, 1), :], length // LANES)
            high = value.astype(jnp.bfloat16)
            left_r[channel, :, 0:LANES] = high
            left_r[channel, :, LANES:] = (value - high.astype(jnp.float32)).astype(jnp.bfloat16)


def prepare_waves(tlen, swapped, pair, beside, far):
    channels, samples = beside.shape
    length = 2 * (swapped.shape[0] - 1) * samples
    rows = length // OFFSETS
    unroll = max(step for step in (1, 2, 3) if channels % step == 0)
    return pl.pallas_call(
        functools.partial(waves_kernel, channels, tlen, unroll),
        out_shape=[
            jax.ShapeDtypeStruct((channels, rows + 16, LANES), jnp.bfloat16),
            jax.ShapeDtypeStruct((channels, rows, 2 * LANES), jnp.bfloat16),
        ],
        in_specs=[VMEM] * (3 + len(far)),
        out_specs=[VMEM, VMEM],
        scratch_shapes=[
            pltpu.VMEM((32, length + 2 * LANES), jnp.float32),
            pltpu.VMEM((32, length + 2 * LANES), jnp.float32),
        ],
        compiler_params=params(),
        cost_estimate=cost(0.05),
        name="prepare_waves",
    )(swapped, pair, beside, *far)


def main_kernel(side, tlen, group, piece, left_a, left_r, *rest):
    outs = rest[:-5]
    if side:
        before, outs = outs[0], outs[1:]
    bank, expand, weight_a, weight_r, total = rest[-5:]
    core = lax.axis_index("tm") % 2
    channels, rows, _ = left_r.shape
    half = channels // 2
    base = half * jnp.where(core == side, 0, 1)
    slots = LANES // group
    banks = (half + 1) // slots
    offset_count = LANES // group
    tile_count = OFFSETS // offset_count
    top = 112 + 8 * (7 + offset_count - 1)
    top = top + top % 16

    lag = lax.broadcasted_iota(jnp.int32, (LANES, LANES), 0)
    target = lax.broadcasted_iota(jnp.int32, (LANES, LANES), 1)
    lane = lax.broadcasted_iota(jnp.int32, (1, LANES), 1)
    used = lag < tlen
    ahead = lane // group
    for slot in range(slots):
        chosen = jnp.where(lag == target % group + slot * group, 1.0, 0.0)
        expand[:, slot * LANES : (slot + 1) * LANES] = chosen.astype(jnp.bfloat16)
    turned = []
    for index in range(banks):
        count = min(slots, max(TILES - slots * index, 0))
        values = jnp.zeros((LANES, LANES), jnp.float32)
        if count:
            values = piece[slots * index : slots * index + count].astype(jnp.float32)
            values = values.reshape(count * group, LANES)
            if count < slots:
                gap = jnp.zeros((LANES - count * group, LANES), jnp.float32)
                values = jnp.concatenate([values, gap], axis=0)
            values = values.T
        turned.append(values)
    codes = [values[125:126, :] for values in turned]
    heads = [jnp.where(used, values, 0.0) for values in turned]
    for extra in range(half - TILES):
        place, slot = divmod(TILES + extra, slots)
        mask = ahead == slot
        code = pltpu.roll(turned[0][126:127, :], (slot - extra) * group % LANES, 1)
        codes[place] = jnp.where(mask, code, codes[place])
        for quarter in range(4):
            source, lanes = divmod(4 * extra + quarter, slots)
            values = turned[source][96:128]
            sample = lag[96:128]
            inside = jnp.logical_and(sample >= tlen, sample < tlen + QUARTER)
            values = jnp.where(inside, values, 0.0)
            values = pltpu.roll(values, (slot - lanes) * group % LANES, 1)
            start = QUARTER * quarter - (tlen - 96)
            values = jnp.concatenate([values, jnp.zeros((8, LANES), jnp.float32)], axis=0)
            values = pltpu.roll(values, start % 8, 0)
            start -= start % 8
            if start < 0:
                values, start = values[8:], 0
            below = LANES - start - values.shape[0]
            if start:
                values = jnp.concatenate([jnp.zeros((start, LANES), jnp.float32), values], axis=0)
            if below > 0:
                values = jnp.concatenate([values, jnp.zeros((below, LANES), jnp.float32)], axis=0)
            heads[place] = heads[place] + jnp.where(mask, values[0:LANES], 0.0)
    for index, (values, code) in enumerate(zip(heads, codes)):
        code = jnp.where(slots * index + ahead < half, code, 0.0)
        center = jnp.sum(values, axis=0, keepdims=True) / tlen
        deviate = jnp.where(used, values - center, 0.0)
        spread = jnp.sqrt(jnp.sum(deviate * deviate, axis=0, keepdims=True) / tlen + EPSILON)
        unit = (deviate / (spread * tlen)).astype(jnp.bfloat16).astype(jnp.float32)
        unit = jnp.where(code > 0, unit, 0.0)
        shift = code.astype(jnp.int32) - 1
        for bit in (1, 2, 4):
            unit = jnp.where(jnp.bitwise_and(shift, bit) > 0, pltpu.roll(unit, bit, 0), unit)
        unit = jnp.where(lag == 112, code, unit)
        bank[index] = unit.astype(jnp.bfloat16)

    def build(number):
        wide = jnp.dot(bank[number], expand[...], preferred_element_type=jnp.float32)
        for slot in range(slots):
            spreaded = wide[:, slot * LANES : (slot + 1) * LANES]
            code = spreaded[112:113, :].astype(jnp.int32)
            usable = code > 0
            shift = code - 1
            moves = shift // 8 + ahead
            taps = spreaded[0:112, :]
            for bit in (1, 2, 4, 8):
                gap = jnp.zeros((8 * bit, LANES), jnp.float32)
                taps = jnp.where(
                    jnp.bitwise_and(moves, bit) > 0,
                    jnp.concatenate([gap, taps], axis=0),
                    jnp.concatenate([taps, gap], axis=0),
                )[0:top]
            taps = taps.astype(jnp.bfloat16)
            item = number * slots + slot
            pick = jnp.logical_and(lag == shift + 8 * ahead, usable)
            pick = jnp.where(pick, 1.0, 0.0).astype(jnp.bfloat16)
            for index in range(tile_count):
                skip = 8 * offset_count * index
                lanes = slice(LANES * index, LANES * (index + 1))
                if skip:
                    weight_a[item, 0:skip, lanes] = jnp.zeros((skip, LANES), jnp.bfloat16)
                    pick = jnp.concatenate(
                        [jnp.zeros((skip, LANES), jnp.bfloat16), pick[0 : LANES - skip]], axis=0
                    )
                weight_a[item, skip : skip + top, lanes] = taps
                rest = DEPTH - top - skip
                if rest:
                    weight_a[item, skip + top :, lanes] = jnp.zeros((rest, LANES), jnp.bfloat16)
                weight_r[item, 0:LANES, lanes] = pick
                weight_r[item, LANES : 2 * LANES, lanes] = pick

    def apply(number, count):
        for slot in range(count):
            item = number * slots + slot
            both = [left_a[base + item, 0:rows, :], left_a[base + item, 16 : rows + 16, :]]
            corr = jnp.dot(
                jnp.concatenate(both, axis=1), weight_a[item], preferred_element_type=jnp.float32
            )
            factor = jnp.dot(
                left_r[base + item], weight_r[item], preferred_element_type=jnp.float32
            )
            total[...] += corr * factor

    total[...] = before[...] if side else jnp.zeros_like(total)
    build(0)

    for number in range(1, banks):
        apply(number - 1, slots)
        build(number)

    apply(banks - 1, half - slots * (banks - 1))

    if not side:
        outs[0][...] = total[...]
        return
    rows_out = outs[0].shape[0]
    station = lax.axis_index("sta") % len(outs)
    for step, out in enumerate(outs):
        part = jnp.bitwise_xor(station, len(outs) - 1 - step)
        out[...] = total[pl.ds(pl.multiple_of(part * rows_out, rows_out), rows_out), :].astype(
            jnp.bfloat16
        )


def correlate(side, tlen, group, count, piece, left_a, left_r, *before):
    channels, rows, _ = left_r.shape
    width = OFFSETS * group
    half = channels // 2
    if side:
        out = [jax.ShapeDtypeStruct((rows // count, width), jnp.bfloat16)] * count
    else:
        out = [jax.ShapeDtypeStruct((rows, width), jnp.float32)]
    return pl.pallas_call(
        functools.partial(main_kernel, side, tlen, group),
        out_shape=out,
        in_specs=[VMEM] * (3 + len(before)),
        out_specs=[VMEM] * len(out),
        scratch_shapes=[
            pltpu.VMEM(((half + 1) * group // LANES, LANES, LANES), jnp.bfloat16),
            pltpu.VMEM((LANES, LANES // group * LANES), jnp.bfloat16),
            pltpu.VMEM((half + 1, DEPTH, width), jnp.bfloat16),
            pltpu.VMEM((half + 1, DEPTH, width), jnp.bfloat16),
            pltpu.VMEM((rows, width), jnp.float32),
        ],
        compiler_params=params(),
        cost_estimate=cost(3),
        name="correlate_" + ("second" if side else "first"),
    )(piece, left_a, left_r, *before)


def add_kernel(*refs):
    parts, keep, send = refs[:-2], refs[-2], refs[-1]
    rows = keep.shape[0]
    core = lax.axis_index("tm") % 2
    for out, which in ((keep, core), (send, 1 - core)):
        place = pl.ds(pl.multiple_of(which * rows, rows), rows)
        value = parts[0][place, :].astype(jnp.float32)
        for part in parts[1:]:
            value = value + part[place, :].astype(jnp.float32)
        out[...] = value


def add(parts):
    rows, width = parts[0].shape
    out = jax.ShapeDtypeStruct((rows // 2, width), jnp.float32)
    return pl.pallas_call(
        add_kernel,
        out_shape=[out, out],
        in_specs=[VMEM] * len(parts),
        out_specs=[VMEM, VMEM],
        compiler_params=params(),
        cost_estimate=cost(0.5),
        name="add",
    )(*parts)


def finish_kernel(group, ours, received, out, result, sems):
    samples = out.shape[1]
    rows = ours.shape[0]
    value = ours[...] + received[...]
    high = value.astype(jnp.bfloat16).astype(jnp.float32)
    both = jnp.concatenate([high, value - high], axis=0).T.astype(jnp.bfloat16)
    half = samples // 2
    copies = []
    for number in range(2):
        row = lax.broadcasted_iota(jnp.int32, (2 * rows, half), 0) % rows
        lane = lax.broadcasted_iota(jnp.int32, (2 * rows, half), 1) + half * number
        place = jnp.logical_and(lane // STRIDE == row // 8, lane % 8 == 7 - row % 8)
        place = jnp.where(place, 1.0, 0.0).astype(jnp.bfloat16)
        wide = jnp.dot(both, place, preferred_element_type=jnp.float32)
        lane = lax.broadcasted_iota(jnp.int32, (group, half), 1) // 8 % OFFSETS
        piece = jnp.zeros((group, half), jnp.float32)
        for offset in range(OFFSETS):
            piece = jnp.where(lane == offset, wide[offset * group : (offset + 1) * group], piece)
        lanes = pl.ds(half * number, half)
        result[:, lanes] = piece
        copy = pltpu.make_async_copy(result.at[:, lanes], out.at[:, lanes], sems.at[number])
        copy.start()
        copies.append(copy)
    for copy in copies:
        copy.wait()


def finish(group, samples, ours, received):
    return pl.pallas_call(
        functools.partial(finish_kernel, group),
        out_shape=jax.ShapeDtypeStruct((group, samples), jnp.float32),
        in_specs=[VMEM, VMEM],
        out_specs=ANY,
        scratch_shapes=[
            pltpu.VMEM((group, samples), jnp.float32),
            pltpu.SemaphoreType.DMA((2,)),
        ],
        compiler_params=params(),
        cost_estimate=cost(1),
        name="finish",
    )(ours, received)


def shards(waveforms, templates, available, moveout, bank_blocks):
    channels, samples = waveforms.shape
    blocks, events, _, tlen = templates.shape
    count_tm = lax.axis_size("tm")
    count_sta = lax.axis_size("sta")
    chips = count_tm // 2
    near = chips // 2
    group = 2 * events // chips

    def swap(array):
        return lax.ppermute(array, "tm", [(i, i ^ 1) for i in range(count_tm)])

    def across(array, step):
        return lax.ppermute(array, "tm", [(i, i ^ (2 * step)) for i in range(count_tm)])

    partner = swap(waveforms)
    mine, theirs, owners = pack(
        chips,
        group,
        bank_blocks,
        jnp.transpose(templates, (0, 2, 1, 3)),
        jnp.transpose(available, (2, 0, 1)),
        jnp.transpose(moveout, (2, 0, 1)),
    )
    theirs, partner = lax.optimization_barrier((theirs, partner))
    other = swap(theirs)
    pair = pair_waves(waveforms, partner)
    far = []
    for number in range(near - 1):
        steps = (chips - 1 - 2 * number, chips - 2 - 2 * number)
        route = [(2 * z + c, 2 * (z ^ steps[c]) + c) for z in range(chips) for c in range(2)]
        far.append(lax.ppermute(pair, "tm", route))
    beside = across(waveforms, 1)
    merged = list(merge(owners, mine, other))
    pieces = [across(merged[step], step) for step in reversed(range(1, chips))]
    pieces = [merged[0]] + pieces[::-1]
    swapped = swap(choose_waves(pair, beside, far))
    left_a, left_r = prepare_waves(tlen, swapped, pair, beside, far)

    left_a, left_r, *pieces = lax.optimization_barrier((left_a, left_r, *pieces[::-1]))
    pieces = pieces[::-1]
    first = choose_piece(owners, pieces)
    second = swap(first)
    total = correlate(0, tlen, group, near, first, left_a, left_r)
    parts = correlate(1, tlen, group, near, second, left_a, left_r, *total)
    gathered = []
    for step in range(near):
        route = []
        for d in range(count_tm):
            for s in range(count_sta):
                dest = near * (d % 2) + (s % near ^ (near - 1 - step))
                route.append((d * count_sta + s, (2 * dest + s // near) * count_sta + d // 2))
        gathered.append(lax.ppermute(parts[step], ("tm", "sta"), route))
    ours, send = add(gathered)
    return finish(group, samples, ours, swap(send))


def solution(mesh):
    in_specs = (
        P("sta", "tm"),
        P("tm", None, "sta", None),
        P("tm", None, "sta"),
        P("tm", None, "sta"),
        P(),
    )
    out_specs = P("sta", "tm")
    return jax.shard_map(shards, mesh=mesh, in_specs=in_specs, out_specs=out_specs, check_vma=False)
```

```python
import functools

import jax
import jax.numpy as jnp
from jax import lax
from jax.experimental import pallas as pl
from jax.experimental.pallas import tpu as pltpu
from jax.sharding import PartitionSpec as P

EPSILON = 1e-06
LANES = 128
OFFSETS = 8
TILES = 12
QUARTER = 25
STRIDE = 64
DEPTH = 256
VMEM_LIMIT = 28 * 1024 * 1024

VMEM = pl.BlockSpec(memory_space=pltpu.VMEM)
ANY = pl.BlockSpec(memory_space=pl.ANY)


def params():
    return pltpu.CompilerParams(vmem_limit_bytes=VMEM_LIMIT)


def cost(micros):
    return pl.CostEstimate(
        flops=int(micros * 1e9), bytes_accessed=int(micros * 1e6), transcendentals=0
    )


def pack_kernel(bank_blocks, templates, available, moveout, mine, theirs, owners, chosen, raw, usable, shifts, square, sems):
    blocks, channels, events, tlen = templates.shape
    chips, _, group, _ = mine.shape
    half = channels // 2
    me = lax.axis_index("tm") % 2
    fetch = [
        pltpu.make_async_copy(source, target, sems.at[index])
        for index, (source, target) in enumerate(
            ((bank_blocks, chosen), (available, usable), (moveout, shifts))
        )
    ]
    for block in range(blocks):
        for part in range(2):
            place = (block, pl.ds(half * part, half))
            fetch.append(
                pltpu.make_async_copy(
                    templates.at[place], raw.at[place], sems.at[3 + 2 * block + part]
                )
            )
    for copy in fetch:
        copy.start()
    mine[...] = jnp.zeros_like(mine)
    theirs[...] = jnp.zeros_like(theirs)
    square[...] = jnp.zeros_like(square)
    for copy in fetch[:3]:
        copy.wait()
    slots = [chosen[which] % blocks for which in range(2)]
    row = lax.broadcasted_iota(jnp.int32, owners.shape, 0)
    owners[...] = jnp.where(row == 0, chosen[0] // blocks, chosen[1] // blocks)
    flags = jnp.where(usable[...] > 0, shifts[...] + 1, 0).astype(jnp.float32)
    codes = []
    for which in range(2):
        code = flags[:, 0, :]
        for block in range(1, blocks):
            code = jnp.where(slots[which] == block, flags[:, block, :], code)
        square[0:channels, 0:events] = code
        turned = square[...].T
        later = pltpu.roll(turned, LANES - half, 1)
        codes.append([jnp.where(me == core, turned, later) for core in range(2)])
    for copy in fetch[3:]:
        copy.wait()
    for which in range(2):
        for side, out in enumerate((mine, theirs)):
            first = half * jnp.where(me == side, 0, 1)
            code = codes[which][side].astype(jnp.bfloat16)
            for tile in range(TILES):
                extra = TILES + tile // 4
                start = QUARTER * (tile % 4)
                for index in range(events // group):
                    chip = which * (events // group) + index
                    rows = slice(index * group, (index + 1) * group)
                    out[chip, tile, :, 0:tlen] = raw[slots[which], first + tile, rows, :]
                    out[chip, tile, :, tlen : tlen + QUARTER] = raw[
                        slots[which], first + extra, rows, start : start + QUARTER
                    ]
                    out[chip, tile, :, 125:126] = code[rows, tile : tile + 1]
                    if tile < half - TILES:
                        beyond = TILES + tile
                        out[chip, tile, :, 126:127] = code[rows, beyond : beyond + 1]


def pack(chips, group, bank_blocks, templates, available, moveout):
    shape = (chips, TILES, group, LANES)
    held = [
        pltpu.with_memory_space_constraint(array, pltpu.HBM)
        for array in (bank_blocks, templates, available, moveout)
    ]
    return pl.pallas_call(
        pack_kernel,
        out_shape=[jax.ShapeDtypeStruct(shape, jnp.bfloat16)] * 2
        + [jax.ShapeDtypeStruct((8, LANES), jnp.int32)],
        in_specs=[ANY] * 4,
        out_specs=[VMEM] * 3,
        scratch_shapes=[
            pltpu.SMEM(bank_blocks.shape, jnp.int32),
            pltpu.VMEM(templates.shape, jnp.bfloat16),
            pltpu.VMEM(available.shape, jnp.int32),
            pltpu.VMEM(moveout.shape, jnp.int32),
            pltpu.VMEM((LANES, LANES), jnp.float32),
            pltpu.SemaphoreType.DMA((3 + 2 * templates.shape[0],)),
        ],
        compiler_params=params(),
        cost_estimate=cost(2),
        name="pack",
    )(*held)


def merge_kernel(owners, mine, other, *outs):
    chips = len(outs)
    me = lax.axis_index("tm")
    for step, out in enumerate(outs):
        dest = jnp.bitwise_xor(me // 2, step)
        owner = jnp.where(dest < chips // 2, owners[0, 0], owners[1, 0])
        here = owner % 2 == me % 2

        @pl.when(here)
        def _():
            out[...] = mine[dest]

        @pl.when(jnp.logical_not(here))
        def _():
            out[...] = other[dest]


def merge(owners, mine, other):
    chips = mine.shape[0]
    return pl.pallas_call(
        merge_kernel,
        out_shape=[jax.ShapeDtypeStruct(mine.shape[1:], mine.dtype)] * chips,
        in_specs=[VMEM] * 3,
        out_specs=[VMEM] * chips,
        compiler_params=params(),
        cost_estimate=cost(0.3),
        name="merge",
    )(owners, mine, other)


def lagged(row, ahead):
    copies = jnp.broadcast_to(row, (8, row.shape[1]))
    return pltpu.roll(copies, row.shape[1] - 7 - ahead, 1, stride=1, stride_axis=0)


def segment(me, other, parity, pair, beside, far, default):
    chip, core = me // 2, me % 2
    chips = 2 * len(far) + 2
    step = jnp.bitwise_xor(chip, other)
    value = default[...]
    value = jnp.where(jnp.logical_and(step == 1, core == parity), beside[...], value)
    value = jnp.where(step == 0, pair[parity], value)
    for number, array in enumerate(far):
        value = jnp.where(step == chips - 1 - 2 * number - core, array[parity], value)
    return value


def pair_kernel(own, partner, out):
    core = lax.axis_index("tm") % 2
    out[core] = own[...]
    out[1 - core] = partner[...]


def pair_waves(own, partner):
    return pl.pallas_call(
        pair_kernel,
        out_shape=jax.ShapeDtypeStruct((2,) + own.shape, own.dtype),
        in_specs=[VMEM] * 2,
        out_specs=VMEM,
        compiler_params=params(),
        cost_estimate=cost(0.05),
        name="pair_waves",
    )(own, partner)


def choose_kernel(pair, beside, *rest):
    far, out = rest[:-1], rest[-1]
    near = out.shape[0] - 1
    me = lax.axis_index("tm")
    chip, core = me // 2, me % 2
    for entry in range(near):
        number, parity = divmod(entry, 2)
        step = jnp.bitwise_xor(chip, near * (1 - core) + 2 * number) // 2
        value = beside[...]
        for place, array in enumerate(far):
            value = jnp.where(step == near - 1 - place, array[parity], value)
        out[entry] = value
    out[near] = segment(me, near, 0, pair, beside, far, beside)


def choose_waves(pair, beside, far):
    return pl.pallas_call(
        choose_kernel,
        out_shape=jax.ShapeDtypeStruct((len(far) + 2,) + beside.shape, beside.dtype),
        in_specs=[VMEM] * (2 + len(far)),
        out_specs=VMEM,
        compiler_params=params(),
        cost_estimate=cost(0.05),
        name="choose_waves",
    )(pair, beside, *far)


def own_kernel(owners, *refs):
    pieces, out = refs[:-1], refs[-1]
    chip = lax.axis_index("tm") // 2
    owner = jnp.where(chip < len(pieces) // 2, owners[0, 0], owners[1, 0])
    source = jnp.bitwise_xor(owner // 2, chip)
    value = pieces[0][...]
    for number, piece in enumerate(pieces[1:], 1):
        value = jnp.where(source == number, piece[...], value)
    out[...] = value


def choose_piece(owners, pieces):
    return pl.pallas_call(
        own_kernel,
        out_shape=jax.ShapeDtypeStruct(pieces[0].shape, pieces[0].dtype),
        in_specs=[VMEM] * (1 + len(pieces)),
        out_specs=VMEM,
        compiler_params=params(),
        cost_estimate=cost(0.3),
        name="choose_piece",
    )(owners, *pieces)


def waves_kernel(channels, tlen, unroll, swapped, pair, beside, *rest):
    far = rest[:-4]
    left_a, left_r, padded, inverse = rest[-4:]
    samples = beside.shape[1]
    near = swapped.shape[0] - 1
    length = 2 * near * samples
    count = padded.shape[1] // LANES
    me = lax.axis_index("tm")
    core = me % 2
    padded[...] = jnp.zeros_like(padded)
    for index in range(2 * near):
        entry, parity = divmod(index, 2)
        given = swapped.at[2 * (entry // 2) + parity]
        wave = segment(me, near * core + entry, parity, pair, beside, far, given)
        padded[0:channels, samples * index : samples * (index + 1)] = wave.astype(jnp.float32)
    rim = segment(me, near * core + near, 0, pair, beside, far, swapped.at[near])
    rim = rim[:, 0 : padded.shape[1] - length].astype(jnp.float32)
    padded[0:channels, length:] = jnp.where(core == 0, rim, 0.0)

    rows = 32 * count
    values = [padded[:, LANES * tile : LANES * (tile + 1)] for tile in range(count)]
    values = jnp.concatenate(values + [jnp.zeros((32, LANES), jnp.float32)], axis=0)
    square = values * values
    high = square.astype(jnp.bfloat16)
    low = (square - high.astype(jnp.float32)).astype(jnp.bfloat16)
    values = values.astype(jnp.bfloat16)
    lag = lax.broadcasted_iota(jnp.int32, (2 * LANES, LANES), 0)
    lag = lag - lax.broadcasted_iota(jnp.int32, (2 * LANES, LANES), 1)
    band = jnp.where(jnp.logical_and(lag >= 0, lag < tlen), 1.0, 0.0).astype(jnp.bfloat16)

    def windows(array):
        both = jnp.concatenate([array[0:rows], array[32 : rows + 32]], axis=1)
        return jnp.dot(both, band, preferred_element_type=jnp.float32)

    first_sum = windows(values)
    second_sum = windows(high) + windows(low)
    variance = (second_sum * tlen - first_sum * first_sum) * (1.0 / tlen**2)
    scale = lax.rsqrt(variance + EPSILON)
    for tile in range(count):
        inverse[:, LANES * tile : LANES * (tile + 1)] = scale[32 * tile : 32 * (tile + 1)]

    def interleaved(row, tiles):
        even, odd = lagged(row, 0), lagged(row, STRIDE)
        parts = []
        for tile in range(tiles):
            lanes = slice(LANES * tile, LANES * (tile + 1))
            parts += [even[:, lanes], odd[:, lanes]]
        return jnp.concatenate(parts, axis=0)

    @pl.loop(0, channels // unroll)
    def _(step):
        for item in range(unroll):
            channel = step * unroll + item
            value = interleaved(padded[pl.ds(channel, 1), :], length // LANES + 1)
            left_a[channel] = value.astype(jnp.bfloat16)
            value = interleaved(inverse[pl.ds(channel, 1), :], length // LANES)
            high = value.astype(jnp.bfloat16)
            left_r[channel, :, 0:LANES] = high
            left_r[channel, :, LANES:] = (value - high.astype(jnp.float32)).astype(jnp.bfloat16)


def prepare_waves(tlen, swapped, pair, beside, far):
    channels, samples = beside.shape
    length = 2 * (swapped.shape[0] - 1) * samples
    rows = length // OFFSETS
    unroll = max(step for step in (1, 2, 3) if channels % step == 0)
    return pl.pallas_call(
        functools.partial(waves_kernel, channels, tlen, unroll),
        out_shape=[
            jax.ShapeDtypeStruct((channels, rows + 16, LANES), jnp.bfloat16),
            jax.ShapeDtypeStruct((channels, rows, 2 * LANES), jnp.bfloat16),
        ],
        in_specs=[VMEM] * (3 + len(far)),
        out_specs=[VMEM, VMEM],
        scratch_shapes=[
            pltpu.VMEM((32, length + 2 * LANES), jnp.float32),
            pltpu.VMEM((32, length + 2 * LANES), jnp.float32),
        ],
        compiler_params=params(),
        cost_estimate=cost(0.05),
        name="prepare_waves",
    )(swapped, pair, beside, *far)


def main_kernel(side, tlen, group, piece, left_a, left_r, *rest):
    outs = rest[:-5]
    if side:
        before, outs = outs[0], outs[1:]
    bank, expand, weight_a, weight_r, total = rest[-5:]
    core = lax.axis_index("tm") % 2
    channels, rows, _ = left_r.shape
    half = channels // 2
    base = half * jnp.where(core == side, 0, 1)
    slots = LANES // group
    banks = (half + 1) // slots
    offset_count = LANES // group
    tile_count = OFFSETS // offset_count
    top = 112 + 8 * (7 + offset_count - 1)
    top = top + top % 16

    lag = lax.broadcasted_iota(jnp.int32, (LANES, LANES), 0)
    target = lax.broadcasted_iota(jnp.int32, (LANES, LANES), 1)
    lane = lax.broadcasted_iota(jnp.int32, (1, LANES), 1)
    used = lag < tlen
    ahead = lane // group
    for slot in range(slots):
        chosen = jnp.where(lag == target % group + slot * group, 1.0, 0.0)
        expand[:, slot * LANES : (slot + 1) * LANES] = chosen.astype(jnp.bfloat16)
    turned = []
    for index in range(banks):
        count = min(slots, max(TILES - slots * index, 0))
        values = jnp.zeros((LANES, LANES), jnp.float32)
        if count:
            values = piece[slots * index : slots * index + count].astype(jnp.float32)
            values = values.reshape(count * group, LANES)
            if count < slots:
                gap = jnp.zeros((LANES - count * group, LANES), jnp.float32)
                values = jnp.concatenate([values, gap], axis=0)
            values = values.T
        turned.append(values)
    codes = [values[125:126, :] for values in turned]
    heads = [jnp.where(used, values, 0.0) for values in turned]
    for extra in range(half - TILES):
        place, slot = divmod(TILES + extra, slots)
        mask = ahead == slot
        code = pltpu.roll(turned[0][126:127, :], (slot - extra) * group % LANES, 1)
        codes[place] = jnp.where(mask, code, codes[place])
        for quarter in range(4):
            source, lanes = divmod(4 * extra + quarter, slots)
            values = turned[source][96:128]
            sample = lag[96:128]
            inside = jnp.logical_and(sample >= tlen, sample < tlen + QUARTER)
            values = jnp.where(inside, values, 0.0)
            values = pltpu.roll(values, (slot - lanes) * group % LANES, 1)
            start = QUARTER * quarter - (tlen - 96)
            values = jnp.concatenate([values, jnp.zeros((8, LANES), jnp.float32)], axis=0)
            values = pltpu.roll(values, start % 8, 0)
            start -= start % 8
            if start < 0:
                values, start = values[8:], 0
            below = LANES - start - values.shape[0]
            if start:
                values = jnp.concatenate([jnp.zeros((start, LANES), jnp.float32), values], axis=0)
            if below > 0:
                values = jnp.concatenate([values, jnp.zeros((below, LANES), jnp.float32)], axis=0)
            heads[place] = heads[place] + jnp.where(mask, values[0:LANES], 0.0)
    for index, (values, code) in enumerate(zip(heads, codes)):
        code = jnp.where(slots * index + ahead < half, code, 0.0)
        deviate = jnp.where(used, values * tlen - jnp.sum(values, axis=0, keepdims=True), 0.0)
        square = jnp.sum(deviate * deviate, axis=0, keepdims=True) * (1.0 / tlen**3)
        unit = deviate / (jnp.sqrt(square + EPSILON) * tlen**2)
        unit = unit.astype(jnp.bfloat16).astype(jnp.float32)
        unit = jnp.where(code > 0, unit, 0.0)
        shift = code.astype(jnp.int32) - 1
        for bit in (1, 2, 4):
            unit = jnp.where(jnp.bitwise_and(shift, bit) > 0, pltpu.roll(unit, bit, 0), unit)
        unit = jnp.where(lag == 112, code, unit)
        bank[index] = unit.astype(jnp.bfloat16)

    def build(number):
        wide = jnp.dot(bank[number], expand[...], preferred_element_type=jnp.float32)
        for slot in range(slots):
            spreaded = wide[:, slot * LANES : (slot + 1) * LANES]
            code = spreaded[112:113, :].astype(jnp.int32)
            usable = code > 0
            shift = code - 1
            moves = shift // 8 + ahead
            taps = spreaded[0:112, :]
            for bit in (1, 2, 4, 8):
                gap = jnp.zeros((8 * bit, LANES), jnp.float32)
                taps = jnp.where(
                    jnp.bitwise_and(moves, bit) > 0,
                    jnp.concatenate([gap, taps], axis=0),
                    jnp.concatenate([taps, gap], axis=0),
                )[0:top]
            taps = taps.astype(jnp.bfloat16)
            item = number * slots + slot
            pick = jnp.logical_and(lag == shift + 8 * ahead, usable)
            pick = jnp.where(pick, 1.0, 0.0).astype(jnp.bfloat16)
            for index in range(tile_count):
                skip = 8 * offset_count * index
                lanes = slice(LANES * index, LANES * (index + 1))
                if skip:
                    weight_a[item, 0:skip, lanes] = jnp.zeros((skip, LANES), jnp.bfloat16)
                    pick = jnp.concatenate(
                        [jnp.zeros((skip, LANES), jnp.bfloat16), pick[0 : LANES - skip]], axis=0
                    )
                weight_a[item, skip : skip + top, lanes] = taps
                rest = DEPTH - top - skip
                if rest:
                    weight_a[item, skip + top :, lanes] = jnp.zeros((rest, LANES), jnp.bfloat16)
                weight_r[item, 0:LANES, lanes] = pick
                weight_r[item, LANES : 2 * LANES, lanes] = pick

    def apply(number, count):
        for slot in range(count):
            item = number * slots + slot
            both = [left_a[base + item, 0:rows, :], left_a[base + item, 16 : rows + 16, :]]
            corr = jnp.dot(
                jnp.concatenate(both, axis=1), weight_a[item], preferred_element_type=jnp.float32
            )
            factor = jnp.dot(
                left_r[base + item], weight_r[item], preferred_element_type=jnp.float32
            )
            total[...] += corr * factor

    total[...] = before[...] if side else jnp.zeros_like(total)
    build(0)

    for number in range(1, banks):
        apply(number - 1, slots)
        build(number)

    apply(banks - 1, half - slots * (banks - 1))

    if not side:
        outs[0][...] = total[...]
        return
    rows_out = outs[0].shape[0]
    station = lax.axis_index("sta") % len(outs)
    for step, out in enumerate(outs):
        part = jnp.bitwise_xor(station, step)
        out[...] = total[pl.ds(pl.multiple_of(part * rows_out, rows_out), rows_out), :].astype(
            jnp.bfloat16
        )


def correlate(side, tlen, group, count, piece, left_a, left_r, *before):
    channels, rows, _ = left_r.shape
    width = OFFSETS * group
    half = channels // 2
    if side:
        out = [jax.ShapeDtypeStruct((rows // count, width), jnp.bfloat16)] * count
    else:
        out = [jax.ShapeDtypeStruct((rows, width), jnp.float32)]
    return pl.pallas_call(
        functools.partial(main_kernel, side, tlen, group),
        out_shape=out,
        in_specs=[VMEM] * (3 + len(before)),
        out_specs=[VMEM] * len(out),
        scratch_shapes=[
            pltpu.VMEM(((half + 1) * group // LANES, LANES, LANES), jnp.bfloat16),
            pltpu.VMEM((LANES, LANES // group * LANES), jnp.bfloat16),
            pltpu.VMEM((half + 1, DEPTH, width), jnp.bfloat16),
            pltpu.VMEM((half + 1, DEPTH, width), jnp.bfloat16),
            pltpu.VMEM((rows, width), jnp.float32),
        ],
        compiler_params=params(),
        cost_estimate=cost(3),
        name="correlate_" + ("second" if side else "first"),
    )(piece, left_a, left_r, *before)


def add_kernel(*refs):
    parts, keep, send = refs[:-2], refs[-2], refs[-1]
    rows = keep.shape[0]
    core = lax.axis_index("tm") % 2
    for out, which in ((keep, core), (send, 1 - core)):
        place = pl.ds(pl.multiple_of(which * rows, rows), rows)
        value = parts[0][place, :].astype(jnp.float32)
        for part in parts[1:]:
            value = value + part[place, :].astype(jnp.float32)
        out[...] = value


def add(parts):
    rows, width = parts[0].shape
    out = jax.ShapeDtypeStruct((rows // 2, width), jnp.float32)
    return pl.pallas_call(
        add_kernel,
        out_shape=[out, out],
        in_specs=[VMEM] * len(parts),
        out_specs=[VMEM, VMEM],
        compiler_params=params(),
        cost_estimate=cost(0.5),
        name="add",
    )(*parts)


def finish_kernel(group, ours, received, out):
    samples = out.shape[1]
    rows = ours.shape[0]
    value = ours[...] + received[...]
    high = value.astype(jnp.bfloat16).astype(jnp.float32)
    both = jnp.concatenate([high, value - high], axis=0).T.astype(jnp.bfloat16)
    row = lax.broadcasted_iota(jnp.int32, (2 * rows, samples), 0) % rows
    lane = lax.broadcasted_iota(jnp.int32, (2 * rows, samples), 1)
    place = jnp.logical_and(lane // STRIDE == row // 8, lane % 8 == 7 - row % 8)
    place = jnp.where(place, 1.0, 0.0).astype(jnp.bfloat16)
    wide = jnp.dot(both, place, preferred_element_type=jnp.float32)
    lane = lax.broadcasted_iota(jnp.int32, (group, samples), 1) // 8 % OFFSETS
    result = jnp.zeros((group, samples), jnp.float32)
    for offset in range(OFFSETS):
        result = jnp.where(lane == offset, wide[offset * group : (offset + 1) * group], result)
    out[...] = result


def finish(group, samples, ours, received):
    return pl.pallas_call(
        functools.partial(finish_kernel, group),
        out_shape=jax.ShapeDtypeStruct((group, samples), jnp.float32),
        in_specs=[VMEM, VMEM],
        out_specs=VMEM,
        compiler_params=params(),
        cost_estimate=cost(1),
        name="finish",
    )(ours, received)


def shards(waveforms, templates, available, moveout, bank_blocks):
    channels, samples = waveforms.shape
    blocks, events, _, tlen = templates.shape
    count_tm = lax.axis_size("tm")
    count_sta = lax.axis_size("sta")
    chips = count_tm // 2
    near = chips // 2
    group = 2 * events // chips

    def swap(array):
        return lax.ppermute(array, "tm", [(i, i ^ 1) for i in range(count_tm)])

    def across(array, step):
        return lax.ppermute(array, "tm", [(i, i ^ (2 * step)) for i in range(count_tm)])

    partner = swap(waveforms)
    mine, theirs, owners = pack(
        chips,
        group,
        bank_blocks,
        jnp.transpose(templates, (0, 2, 1, 3)),
        jnp.transpose(available, (2, 0, 1)),
        jnp.transpose(moveout, (2, 0, 1)),
    )
    theirs, partner = lax.optimization_barrier((theirs, partner))
    other = swap(theirs)
    pair = pair_waves(waveforms, partner)
    far = []
    for number in range(near - 1):
        steps = (chips - 1 - 2 * number, chips - 2 - 2 * number)
        route = [(2 * z + c, 2 * (z ^ steps[c]) + c) for z in range(chips) for c in range(2)]
        far.append(lax.ppermute(pair, "tm", route))
    beside = across(waveforms, 1)
    merged = list(merge(owners, mine, other))
    pieces = [across(merged[step], step) for step in reversed(range(1, chips))]
    pieces = [merged[0]] + pieces[::-1]
    swapped = swap(choose_waves(pair, beside, far))
    left_a, left_r = prepare_waves(tlen, swapped, pair, beside, far)

    left_a, left_r, *pieces = lax.optimization_barrier((left_a, left_r, *pieces[::-1]))
    pieces = pieces[::-1]
    first = choose_piece(owners, pieces)
    second = swap(first)
    total = correlate(0, tlen, group, near, first, left_a, left_r)
    parts = correlate(1, tlen, group, near, second, left_a, left_r, *total)
    gathered = []
    for step in range(near):
        route = []
        for d in range(count_tm):
            for s in range(count_sta):
                dest = near * (d % 2) + (s % near ^ step)
                route.append((d * count_sta + s, (2 * dest + s // near) * count_sta + d // 2))
        gathered.append(lax.ppermute(parts[step], ("tm", "sta"), route))
    ours, send = add(gathered)
    return finish(group, samples, ours, swap(send))


def solution(mesh):
    in_specs = (
        P("sta", "tm"),
        P("tm", None, "sta", None),
        P("tm", None, "sta"),
        P("tm", None, "sta"),
        P(),
    )
    out_specs = P("sta", "tm")
    return jax.shard_map(shards, mesh=mesh, in_specs=in_specs, out_specs=out_specs, check_vma=False)
```

```python
import functools

import jax
import jax.numpy as jnp
from jax import lax
from jax.experimental import pallas as pl
from jax.experimental.pallas import tpu as pltpu
from jax.sharding import PartitionSpec as P

EPSILON = 1e-06
LANES = 128
OFFSETS = 8
TILES = 12
QUARTER = 25
STRIDE = 64
DEPTH = 256
VMEM_LIMIT = 28 * 1024 * 1024

VMEM = pl.BlockSpec(memory_space=pltpu.VMEM)
ANY = pl.BlockSpec(memory_space=pl.ANY)


def params():
    return pltpu.CompilerParams(vmem_limit_bytes=VMEM_LIMIT)


def cost(micros):
    return pl.CostEstimate(
        flops=int(micros * 1e9), bytes_accessed=int(micros * 1e6), transcendentals=0
    )


def pack_kernel(bank_blocks, templates, available, moveout, mine, theirs, owners, chosen, raw, usable, shifts, square, sems):
    blocks, channels, events, tlen = templates.shape
    chips, _, group, _ = mine.shape
    half = channels // 2
    me = lax.axis_index("tm") % 2
    fetch = [
        pltpu.make_async_copy(source, target, sems.at[index])
        for index, (source, target) in enumerate(
            ((bank_blocks, chosen), (available, usable), (moveout, shifts))
        )
    ]
    for block in range(blocks):
        for part in range(2):
            place = (block, pl.ds(half * part, half))
            fetch.append(
                pltpu.make_async_copy(
                    templates.at[place], raw.at[place], sems.at[3 + 2 * block + part]
                )
            )
    for copy in fetch:
        copy.start()
    mine[...] = jnp.zeros_like(mine)
    theirs[...] = jnp.zeros_like(theirs)
    square[...] = jnp.zeros_like(square)
    for copy in fetch[:3]:
        copy.wait()
    slots = [chosen[which] % blocks for which in range(2)]
    row = lax.broadcasted_iota(jnp.int32, owners.shape, 0)
    owners[...] = jnp.where(row == 0, chosen[0] // blocks, chosen[1] // blocks)
    flags = jnp.where(usable[...] > 0, shifts[...] + 1, 0).astype(jnp.float32)
    codes = []
    for which in range(2):
        code = flags[:, 0, :]
        for block in range(1, blocks):
            code = jnp.where(slots[which] == block, flags[:, block, :], code)
        square[0:channels, 0:events] = code
        turned = square[...].T
        later = pltpu.roll(turned, LANES - half, 1)
        codes.append([jnp.where(me == core, turned, later) for core in range(2)])
    for copy in fetch[3:]:
        copy.wait()
    for which in range(2):
        for side, out in enumerate((mine, theirs)):
            first = half * jnp.where(me == side, 0, 1)
            code = codes[which][side].astype(jnp.bfloat16)
            for tile in range(TILES):
                extra = TILES + tile // 4
                start = QUARTER * (tile % 4)
                for index in range(events // group):
                    chip = which * (events // group) + index
                    rows = slice(index * group, (index + 1) * group)
                    out[chip, tile, :, 0:tlen] = raw[slots[which], first + tile, rows, :]
                    out[chip, tile, :, tlen : tlen + QUARTER] = raw[
                        slots[which], first + extra, rows, start : start + QUARTER
                    ]
                    out[chip, tile, :, 125:126] = code[rows, tile : tile + 1]
                    if tile < half - TILES:
                        beyond = TILES + tile
                        out[chip, tile, :, 126:127] = code[rows, beyond : beyond + 1]


def pack(chips, group, bank_blocks, templates, available, moveout):
    shape = (chips, TILES, group, LANES)
    held = [
        pltpu.with_memory_space_constraint(array, pltpu.HBM)
        for array in (bank_blocks, templates, available, moveout)
    ]
    return pl.pallas_call(
        pack_kernel,
        out_shape=[jax.ShapeDtypeStruct(shape, jnp.bfloat16)] * 2
        + [jax.ShapeDtypeStruct((8, LANES), jnp.int32)],
        in_specs=[ANY] * 4,
        out_specs=[VMEM] * 3,
        scratch_shapes=[
            pltpu.SMEM(bank_blocks.shape, jnp.int32),
            pltpu.VMEM(templates.shape, jnp.bfloat16),
            pltpu.VMEM(available.shape, jnp.int32),
            pltpu.VMEM(moveout.shape, jnp.int32),
            pltpu.VMEM((LANES, LANES), jnp.float32),
            pltpu.SemaphoreType.DMA((3 + 2 * templates.shape[0],)),
        ],
        compiler_params=params(),
        cost_estimate=cost(2),
        name="pack",
    )(*held)


def merge_kernel(owners, mine, other, *outs):
    chips = len(outs)
    me = lax.axis_index("tm")
    for step, out in enumerate(outs):
        dest = jnp.bitwise_xor(me // 2, step)
        owner = jnp.where(dest < chips // 2, owners[0, 0], owners[1, 0])
        here = owner % 2 == me % 2

        @pl.when(here)
        def _():
            out[...] = mine[dest]

        @pl.when(jnp.logical_not(here))
        def _():
            out[...] = other[dest]


def merge(owners, mine, other):
    chips = mine.shape[0]
    return pl.pallas_call(
        merge_kernel,
        out_shape=[jax.ShapeDtypeStruct(mine.shape[1:], mine.dtype)] * chips,
        in_specs=[VMEM] * 3,
        out_specs=[VMEM] * chips,
        compiler_params=params(),
        cost_estimate=cost(0.3),
        name="merge",
    )(owners, mine, other)


def lagged(row, ahead):
    copies = jnp.broadcast_to(row, (8, row.shape[1]))
    return pltpu.roll(copies, row.shape[1] - 7 - ahead, 1, stride=1, stride_axis=0)


def segment(me, other, parity, pair, beside, far, default):
    chip, core = me // 2, me % 2
    chips = 2 * len(far) + 2
    step = jnp.bitwise_xor(chip, other)
    value = default[...]
    value = jnp.where(jnp.logical_and(step == 1, core == parity), beside[...], value)
    value = jnp.where(step == 0, pair[parity], value)
    for number, array in enumerate(far):
        value = jnp.where(step == chips - 1 - 2 * number - core, array[parity], value)
    return value


def pair_kernel(own, partner, out):
    core = lax.axis_index("tm") % 2
    out[core] = own[...]
    out[1 - core] = partner[...]


def pair_waves(own, partner):
    return pl.pallas_call(
        pair_kernel,
        out_shape=jax.ShapeDtypeStruct((2,) + own.shape, own.dtype),
        in_specs=[VMEM] * 2,
        out_specs=VMEM,
        compiler_params=params(),
        cost_estimate=cost(0.05),
        name="pair_waves",
    )(own, partner)


def choose_kernel(pair, beside, *rest):
    far, out = rest[:-1], rest[-1]
    near = out.shape[0] - 1
    me = lax.axis_index("tm")
    chip, core = me // 2, me % 2
    for entry in range(near):
        number, parity = divmod(entry, 2)
        step = jnp.bitwise_xor(chip, near * (1 - core) + 2 * number) // 2
        value = beside[...]
        for place, array in enumerate(far):
            value = jnp.where(step == near - 1 - place, array[parity], value)
        out[entry] = value
    out[near] = segment(me, near, 0, pair, beside, far, beside)


def choose_waves(pair, beside, far):
    return pl.pallas_call(
        choose_kernel,
        out_shape=jax.ShapeDtypeStruct((len(far) + 2,) + beside.shape, beside.dtype),
        in_specs=[VMEM] * (2 + len(far)),
        out_specs=VMEM,
        compiler_params=params(),
        cost_estimate=cost(0.05),
        name="choose_waves",
    )(pair, beside, *far)


def own_kernel(owners, *refs):
    pieces, out = refs[:-1], refs[-1]
    chip = lax.axis_index("tm") // 2
    owner = jnp.where(chip < len(pieces) // 2, owners[0, 0], owners[1, 0])
    source = jnp.bitwise_xor(owner // 2, chip)
    value = pieces[0][...]
    for number, piece in enumerate(pieces[1:], 1):
        value = jnp.where(source == number, piece[...], value)
    out[...] = value


def choose_piece(owners, pieces):
    return pl.pallas_call(
        own_kernel,
        out_shape=jax.ShapeDtypeStruct(pieces[0].shape, pieces[0].dtype),
        in_specs=[VMEM] * (1 + len(pieces)),
        out_specs=VMEM,
        compiler_params=params(),
        cost_estimate=cost(0.3),
        name="choose_piece",
    )(owners, *pieces)


def waves_kernel(channels, tlen, unroll, swapped, pair, beside, *rest):
    far = rest[:-4]
    left_a, left_r, padded, inverse = rest[-4:]
    samples = beside.shape[1]
    near = swapped.shape[0] - 1
    length = 2 * near * samples
    count = padded.shape[1] // LANES
    me = lax.axis_index("tm")
    core = me % 2
    padded[...] = jnp.zeros_like(padded)
    for index in range(2 * near):
        entry, parity = divmod(index, 2)
        given = swapped.at[2 * (entry // 2) + parity]
        wave = segment(me, near * core + entry, parity, pair, beside, far, given)
        padded[0:channels, samples * index : samples * (index + 1)] = wave.astype(jnp.float32)
    rim = segment(me, near * core + near, 0, pair, beside, far, swapped.at[near])
    rim = rim[:, 0 : padded.shape[1] - length].astype(jnp.float32)
    padded[0:channels, length:] = jnp.where(core == 0, rim, 0.0)

    rows = 32 * count
    values = [padded[:, LANES * tile : LANES * (tile + 1)] for tile in range(count)]
    values = jnp.concatenate(values + [jnp.zeros((32, LANES), jnp.float32)], axis=0)
    square = values * values
    high = square.astype(jnp.bfloat16)
    low = (square - high.astype(jnp.float32)).astype(jnp.bfloat16)
    values = values.astype(jnp.bfloat16)
    lag = lax.broadcasted_iota(jnp.int32, (2 * LANES, LANES), 0)
    lag = lag - lax.broadcasted_iota(jnp.int32, (2 * LANES, LANES), 1)
    band = jnp.where(jnp.logical_and(lag >= 0, lag < tlen), 1.0, 0.0).astype(jnp.bfloat16)

    def windows(array):
        both = jnp.concatenate([array[0:rows], array[32 : rows + 32]], axis=1)
        return jnp.dot(both, band, preferred_element_type=jnp.float32)

    first_sum = windows(values)
    second_sum = windows(high) + windows(low)
    variance = (second_sum * tlen - first_sum * first_sum) * (1.0 / tlen**2)
    scale = lax.rsqrt(variance + EPSILON)
    for tile in range(count):
        inverse[:, LANES * tile : LANES * (tile + 1)] = scale[32 * tile : 32 * (tile + 1)]

    def interleaved(row, tiles):
        even, odd = lagged(row, 0), lagged(row, STRIDE)
        parts = []
        for tile in range(tiles):
            lanes = slice(LANES * tile, LANES * (tile + 1))
            parts += [even[:, lanes], odd[:, lanes]]
        return jnp.concatenate(parts, axis=0)

    @pl.loop(0, channels // unroll)
    def _(step):
        for item in range(unroll):
            channel = step * unroll + item
            value = interleaved(padded[pl.ds(channel, 1), :], length // LANES + 1)
            left_a[channel] = value.astype(jnp.bfloat16)
            value = interleaved(inverse[pl.ds(channel, 1), :], length // LANES)
            high = value.astype(jnp.bfloat16)
            left_r[channel, :, 0:LANES] = high
            left_r[channel, :, LANES:] = (value - high.astype(jnp.float32)).astype(jnp.bfloat16)


def prepare_waves(tlen, swapped, pair, beside, far):
    channels, samples = beside.shape
    length = 2 * (swapped.shape[0] - 1) * samples
    rows = length // OFFSETS
    unroll = max(step for step in (1, 2, 3) if channels % step == 0)
    return pl.pallas_call(
        functools.partial(waves_kernel, channels, tlen, unroll),
        out_shape=[
            jax.ShapeDtypeStruct((channels, rows + 16, LANES), jnp.bfloat16),
            jax.ShapeDtypeStruct((channels, rows, 2 * LANES), jnp.bfloat16),
        ],
        in_specs=[VMEM] * (3 + len(far)),
        out_specs=[VMEM, VMEM],
        scratch_shapes=[
            pltpu.VMEM((32, length + 2 * LANES), jnp.float32),
            pltpu.VMEM((32, length + 2 * LANES), jnp.float32),
        ],
        compiler_params=params(),
        cost_estimate=cost(0.05),
        name="prepare_waves",
    )(swapped, pair, beside, *far)


def main_kernel(side, tlen, group, piece, left_a, left_r, *rest):
    outs = rest[:-5]
    if side:
        before, outs = outs[0], outs[1:]
    bank, expand, weight_a, weight_r, total = rest[-5:]
    core = lax.axis_index("tm") % 2
    channels, rows, _ = left_r.shape
    half = channels // 2
    base = half * jnp.where(core == side, 0, 1)
    slots = LANES // group
    banks = (half + 1) // slots
    offset_count = LANES // group
    tile_count = OFFSETS // offset_count
    top = 112 + 8 * (7 + offset_count - 1)
    top = top + top % 16

    lag = lax.broadcasted_iota(jnp.int32, (LANES, LANES), 0)
    target = lax.broadcasted_iota(jnp.int32, (LANES, LANES), 1)
    lane = lax.broadcasted_iota(jnp.int32, (1, LANES), 1)
    used = lag < tlen
    ahead = lane // group
    for slot in range(slots):
        chosen = jnp.where(lag == target % group + slot * group, 1.0, 0.0)
        expand[:, slot * LANES : (slot + 1) * LANES] = chosen.astype(jnp.bfloat16)
    turned = []
    for index in range(banks):
        count = min(slots, max(TILES - slots * index, 0))
        values = jnp.zeros((LANES, LANES), jnp.float32)
        if count:
            values = piece[slots * index : slots * index + count].astype(jnp.float32)
            values = values.reshape(count * group, LANES)
            if count < slots:
                gap = jnp.zeros((LANES - count * group, LANES), jnp.float32)
                values = jnp.concatenate([values, gap], axis=0)
            values = values.T
        turned.append(values)
    codes = [values[125:126, :] for values in turned]
    heads = [jnp.where(used, values, 0.0) for values in turned]
    for extra in range(half - TILES):
        place, slot = divmod(TILES + extra, slots)
        mask = ahead == slot
        code = pltpu.roll(turned[0][126:127, :], (slot - extra) * group % LANES, 1)
        codes[place] = jnp.where(mask, code, codes[place])
        for quarter in range(4):
            source, lanes = divmod(4 * extra + quarter, slots)
            values = turned[source][96:128]
            sample = lag[96:128]
            inside = jnp.logical_and(sample >= tlen, sample < tlen + QUARTER)
            values = jnp.where(inside, values, 0.0)
            values = pltpu.roll(values, (slot - lanes) * group % LANES, 1)
            start = QUARTER * quarter - (tlen - 96)
            values = jnp.concatenate([values, jnp.zeros((8, LANES), jnp.float32)], axis=0)
            values = pltpu.roll(values, start % 8, 0)
            start -= start % 8
            if start < 0:
                values, start = values[8:], 0
            below = LANES - start - values.shape[0]
            if start:
                values = jnp.concatenate([jnp.zeros((start, LANES), jnp.float32), values], axis=0)
            if below > 0:
                values = jnp.concatenate([values, jnp.zeros((below, LANES), jnp.float32)], axis=0)
            heads[place] = heads[place] + jnp.where(mask, values[0:LANES], 0.0)
    for index, (values, code) in enumerate(zip(heads, codes)):
        code = jnp.where(slots * index + ahead < half, code, 0.0)
        deviate = jnp.where(used, values * tlen - jnp.sum(values, axis=0, keepdims=True), 0.0)
        square = jnp.sum(deviate * deviate, axis=0, keepdims=True) * (1.0 / tlen**3)
        unit = deviate / (jnp.sqrt(square + EPSILON) * tlen**2)
        unit = unit.astype(jnp.bfloat16).astype(jnp.float32)
        unit = jnp.where(code > 0, unit, 0.0)
        shift = code.astype(jnp.int32) - 1
        for bit in (1, 2, 4):
            unit = jnp.where(jnp.bitwise_and(shift, bit) > 0, pltpu.roll(unit, bit, 0), unit)
        unit = jnp.where(lag == 112, code, unit)
        bank[index] = unit.astype(jnp.bfloat16)

    def build(number):
        wide = jnp.dot(bank[number], expand[...], preferred_element_type=jnp.float32)
        for slot in range(slots):
            spreaded = wide[:, slot * LANES : (slot + 1) * LANES]
            code = spreaded[112:113, :].astype(jnp.int32)
            usable = code > 0
            shift = code - 1
            moves = shift // 8 + ahead
            taps = spreaded[0:112, :]
            for bit in (1, 2, 4, 8):
                gap = jnp.zeros((8 * bit, LANES), jnp.float32)
                taps = jnp.where(
                    jnp.bitwise_and(moves, bit) > 0,
                    jnp.concatenate([gap, taps], axis=0),
                    jnp.concatenate([taps, gap], axis=0),
                )[0:top]
            taps = taps.astype(jnp.bfloat16)
            item = number * slots + slot
            pick = jnp.logical_and(lag == shift + 8 * ahead, usable)
            pick = jnp.where(pick, 1.0, 0.0).astype(jnp.bfloat16)
            for index in range(tile_count):
                skip = 8 * offset_count * index
                lanes = slice(LANES * index, LANES * (index + 1))
                if skip:
                    weight_a[item, 0:skip, lanes] = jnp.zeros((skip, LANES), jnp.bfloat16)
                    pick = jnp.concatenate(
                        [jnp.zeros((skip, LANES), jnp.bfloat16), pick[0 : LANES - skip]], axis=0
                    )
                weight_a[item, skip : skip + top, lanes] = taps
                rest = DEPTH - top - skip
                if rest:
                    weight_a[item, skip + top :, lanes] = jnp.zeros((rest, LANES), jnp.bfloat16)
                weight_r[item, 0:LANES, lanes] = pick
                weight_r[item, LANES : 2 * LANES, lanes] = pick

    def products(item):
        both = [left_a[base + item, 0:rows, :], left_a[base + item, 16 : rows + 16, :]]
        corr = jnp.dot(
            jnp.concatenate(both, axis=1), weight_a[item], preferred_element_type=jnp.float32
        )
        factor = jnp.dot(left_r[base + item], weight_r[item], preferred_element_type=jnp.float32)
        return corr * factor

    def apply(number, count):
        for item in range(number * slots, number * slots + count, 2):
            value = products(item)
            if item + 1 < number * slots + count:
                value = value + products(item + 1)
            if item:
                value = value + total[...]
            elif side:
                value = value + before[...]
            total[...] = value

    build(0)

    for number in range(1, banks):
        apply(number - 1, slots)
        build(number)

    apply(banks - 1, half - slots * (banks - 1))

    if not side:
        outs[0][...] = total[...]
        return
    rows_out = outs[0].shape[0]
    station = lax.axis_index("sta") % len(outs)
    for step, out in enumerate(outs):
        part = jnp.bitwise_xor(station, step)
        out[...] = total[pl.ds(pl.multiple_of(part * rows_out, rows_out), rows_out), :].astype(
            jnp.bfloat16
        )


def correlate(side, tlen, group, count, piece, left_a, left_r, *before):
    channels, rows, _ = left_r.shape
    width = OFFSETS * group
    half = channels // 2
    if side:
        out = [jax.ShapeDtypeStruct((rows // count, width), jnp.bfloat16)] * count
    else:
        out = [jax.ShapeDtypeStruct((rows, width), jnp.float32)]
    return pl.pallas_call(
        functools.partial(main_kernel, side, tlen, group),
        out_shape=out,
        in_specs=[VMEM] * (3 + len(before)),
        out_specs=[VMEM] * len(out),
        scratch_shapes=[
            pltpu.VMEM(((half + 1) * group // LANES, LANES, LANES), jnp.bfloat16),
            pltpu.VMEM((LANES, LANES // group * LANES), jnp.bfloat16),
            pltpu.VMEM((half + 1, DEPTH, width), jnp.bfloat16),
            pltpu.VMEM((half + 1, DEPTH, width), jnp.bfloat16),
            pltpu.VMEM((rows, width), jnp.float32),
        ],
        compiler_params=params(),
        cost_estimate=cost(3),
        name="correlate_" + ("second" if side else "first"),
    )(piece, left_a, left_r, *before)


def add_kernel(*refs):
    parts, keep, send = refs[:-2], refs[-2], refs[-1]
    rows = keep.shape[0]
    core = lax.axis_index("tm") % 2
    for out, which in ((keep, core), (send, 1 - core)):
        place = pl.ds(pl.multiple_of(which * rows, rows), rows)
        value = parts[0][place, :].astype(jnp.float32)
        for part in parts[1:]:
            value = value + part[place, :].astype(jnp.float32)
        out[...] = value


def add(parts):
    rows, width = parts[0].shape
    out = jax.ShapeDtypeStruct((rows // 2, width), jnp.float32)
    return pl.pallas_call(
        add_kernel,
        out_shape=[out, out],
        in_specs=[VMEM] * len(parts),
        out_specs=[VMEM, VMEM],
        compiler_params=params(),
        cost_estimate=cost(0.5),
        name="add",
    )(*parts)


def finish_kernel(group, ours, received, out):
    samples = out.shape[1]
    rows = ours.shape[0]
    value = ours[...] + received[...]
    high = value.astype(jnp.bfloat16).astype(jnp.float32)
    both = jnp.concatenate([high, value - high], axis=0).T.astype(jnp.bfloat16)
    row = lax.broadcasted_iota(jnp.int32, (2 * rows, samples), 0) % rows
    lane = lax.broadcasted_iota(jnp.int32, (2 * rows, samples), 1)
    place = jnp.logical_and(lane // STRIDE == row // 8, lane % 8 == 7 - row % 8)
    place = jnp.where(place, 1.0, 0.0).astype(jnp.bfloat16)
    wide = jnp.dot(both, place, preferred_element_type=jnp.float32)
    lane = lax.broadcasted_iota(jnp.int32, (group, samples), 1) // 8 % OFFSETS
    result = jnp.zeros((group, samples), jnp.float32)
    for offset in range(OFFSETS):
        result = jnp.where(lane == offset, wide[offset * group : (offset + 1) * group], result)
    out[...] = result


def finish(group, samples, ours, received):
    return pl.pallas_call(
        functools.partial(finish_kernel, group),
        out_shape=jax.ShapeDtypeStruct((group, samples), jnp.float32),
        in_specs=[VMEM, VMEM],
        out_specs=VMEM,
        compiler_params=params(),
        cost_estimate=cost(1),
        name="finish",
    )(ours, received)


def shards(waveforms, templates, available, moveout, bank_blocks):
    channels, samples = waveforms.shape
    blocks, events, _, tlen = templates.shape
    count_tm = lax.axis_size("tm")
    count_sta = lax.axis_size("sta")
    chips = count_tm // 2
    near = chips // 2
    group = 2 * events // chips

    def swap(array):
        return lax.ppermute(array, "tm", [(i, i ^ 1) for i in range(count_tm)])

    def across(array, step):
        return lax.ppermute(array, "tm", [(i, i ^ (2 * step)) for i in range(count_tm)])

    partner = swap(waveforms)
    mine, theirs, owners = pack(
        chips,
        group,
        bank_blocks,
        jnp.transpose(templates, (0, 2, 1, 3)),
        jnp.transpose(available, (2, 0, 1)),
        jnp.transpose(moveout, (2, 0, 1)),
    )
    theirs, partner = lax.optimization_barrier((theirs, partner))
    other = swap(theirs)
    pair = pair_waves(waveforms, partner)
    far = []
    for number in range(near - 1):
        steps = (chips - 1 - 2 * number, chips - 2 - 2 * number)
        route = [(2 * z + c, 2 * (z ^ steps[c]) + c) for z in range(chips) for c in range(2)]
        far.append(lax.ppermute(pair, "tm", route))
    beside = across(waveforms, 1)
    merged = list(merge(owners, mine, other))
    pieces = [across(merged[step], step) for step in reversed(range(1, chips))]
    pieces = [merged[0]] + pieces[::-1]
    swapped = swap(choose_waves(pair, beside, far))
    left_a, left_r = prepare_waves(tlen, swapped, pair, beside, far)

    left_a, left_r, *pieces = lax.optimization_barrier((left_a, left_r, *pieces[::-1]))
    pieces = pieces[::-1]
    first = choose_piece(owners, pieces)
    second = swap(first)
    total = correlate(0, tlen, group, near, first, left_a, left_r)
    parts = correlate(1, tlen, group, near, second, left_a, left_r, *total)
    gathered = []
    for step in range(near):
        route = []
        for d in range(count_tm):
            for s in range(count_sta):
                dest = near * (d % 2) + (s % near ^ step)
                route.append((d * count_sta + s, (2 * dest + s // near) * count_sta + d // 2))
        gathered.append(lax.ppermute(parts[step], ("tm", "sta"), route))
    ours, send = add(gathered)
    return finish(group, samples, ours, swap(send))


def solution(mesh):
    in_specs = (
        P("sta", "tm"),
        P("tm", None, "sta", None),
        P("tm", None, "sta"),
        P("tm", None, "sta"),
        P(),
    )
    out_specs = P("sta", "tm")
    return jax.shard_map(shards, mesh=mesh, in_specs=in_specs, out_specs=out_specs, check_vma=False)
```

```python
import functools

import jax
import jax.numpy as jnp
from jax import lax
from jax.experimental import pallas as pl
from jax.experimental.pallas import tpu as pltpu
from jax.sharding import PartitionSpec as P

EPSILON = 1e-06
LANES = 128
OFFSETS = 8
TILES = 12
QUARTER = 25
STRIDE = 64
DEPTH = 256
VMEM_LIMIT = 28 * 1024 * 1024

VMEM = pl.BlockSpec(memory_space=pltpu.VMEM)
ANY = pl.BlockSpec(memory_space=pl.ANY)


def params():
    return pltpu.CompilerParams(vmem_limit_bytes=VMEM_LIMIT)


def cost(micros):
    return pl.CostEstimate(
        flops=int(micros * 1e9), bytes_accessed=int(micros * 1e6), transcendentals=0
    )


def pack_kernel(bank_blocks, templates, available, moveout, mine, theirs, owners, chosen, raw, usable, shifts, square, sems):
    blocks, channels, events, tlen = templates.shape
    chips, _, group, _ = mine.shape
    half = channels // 2
    me = lax.axis_index("tm") % 2
    fetch = [
        pltpu.make_async_copy(source, target, sems.at[index])
        for index, (source, target) in enumerate(
            ((bank_blocks, chosen), (available, usable), (moveout, shifts))
        )
    ]
    for block in range(blocks):
        for part in range(2):
            place = (block, pl.ds(half * part, half))
            fetch.append(
                pltpu.make_async_copy(
                    templates.at[place], raw.at[place], sems.at[3 + 2 * block + part]
                )
            )
    for copy in fetch:
        copy.start()
    mine[...] = jnp.zeros_like(mine)
    theirs[...] = jnp.zeros_like(theirs)
    square[...] = jnp.zeros_like(square)
    for copy in fetch[:3]:
        copy.wait()
    slots = [chosen[which] % blocks for which in range(2)]
    row = lax.broadcasted_iota(jnp.int32, owners.shape, 0)
    owners[...] = jnp.where(row == 0, chosen[0] // blocks, chosen[1] // blocks)
    flags = jnp.where(usable[...] > 0, shifts[...] + 1, 0).astype(jnp.float32)
    codes = []
    for which in range(2):
        code = flags[:, 0, :]
        for block in range(1, blocks):
            code = jnp.where(slots[which] == block, flags[:, block, :], code)
        square[0:channels, 0:events] = code
        turned = square[...].T
        later = pltpu.roll(turned, LANES - half, 1)
        codes.append([jnp.where(me == core, turned, later) for core in range(2)])
    for copy in fetch[3:]:
        copy.wait()
    for which in range(2):
        for side, out in enumerate((mine, theirs)):
            first = half * jnp.where(me == side, 0, 1)
            code = codes[which][side].astype(jnp.bfloat16)
            for tile in range(TILES):
                extra = TILES + tile // 4
                start = QUARTER * (tile % 4)
                for index in range(events // group):
                    chip = which * (events // group) + index
                    rows = slice(index * group, (index + 1) * group)
                    out[chip, tile, :, 0:tlen] = raw[slots[which], first + tile, rows, :]
                    out[chip, tile, :, tlen : tlen + QUARTER] = raw[
                        slots[which], first + extra, rows, start : start + QUARTER
                    ]
                    out[chip, tile, :, 125:126] = code[rows, tile : tile + 1]
                    if tile < half - TILES:
                        beyond = TILES + tile
                        out[chip, tile, :, 126:127] = code[rows, beyond : beyond + 1]


def pack(chips, group, bank_blocks, templates, available, moveout):
    shape = (chips, TILES, group, LANES)
    held = [
        pltpu.with_memory_space_constraint(array, pltpu.HBM)
        for array in (bank_blocks, templates, available, moveout)
    ]
    return pl.pallas_call(
        pack_kernel,
        out_shape=[jax.ShapeDtypeStruct(shape, jnp.bfloat16)] * 2
        + [jax.ShapeDtypeStruct((8, LANES), jnp.int32)],
        in_specs=[ANY] * 4,
        out_specs=[VMEM] * 3,
        scratch_shapes=[
            pltpu.SMEM(bank_blocks.shape, jnp.int32),
            pltpu.VMEM(templates.shape, jnp.bfloat16),
            pltpu.VMEM(available.shape, jnp.int32),
            pltpu.VMEM(moveout.shape, jnp.int32),
            pltpu.VMEM((LANES, LANES), jnp.float32),
            pltpu.SemaphoreType.DMA((3 + 2 * templates.shape[0],)),
        ],
        compiler_params=params(),
        cost_estimate=cost(2),
        name="pack",
    )(*held)


def merge_kernel(owners, mine, other, *outs):
    chips = len(outs)
    me = lax.axis_index("tm")
    for step, out in enumerate(outs):
        dest = jnp.bitwise_xor(me // 2, step)
        owner = jnp.where(dest < chips // 2, owners[0, 0], owners[1, 0])
        here = owner % 2 == me % 2

        @pl.when(here)
        def _():
            out[...] = mine[dest]

        @pl.when(jnp.logical_not(here))
        def _():
            out[...] = other[dest]


def merge(owners, mine, other):
    chips = mine.shape[0]
    return pl.pallas_call(
        merge_kernel,
        out_shape=[jax.ShapeDtypeStruct(mine.shape[1:], mine.dtype)] * chips,
        in_specs=[VMEM] * 3,
        out_specs=[VMEM] * chips,
        compiler_params=params(),
        cost_estimate=cost(0.3),
        name="merge",
    )(owners, mine, other)


def lagged(row, ahead):
    copies = jnp.broadcast_to(row, (8, row.shape[1]))
    return pltpu.roll(copies, row.shape[1] - 7 - ahead, 1, stride=1, stride_axis=0)


def segment(me, other, parity, pair, beside, far, default):
    chip, core = me // 2, me % 2
    chips = 2 * len(far) + 2
    step = jnp.bitwise_xor(chip, other)
    value = default[...]
    value = jnp.where(jnp.logical_and(step == 1, core == parity), beside[...], value)
    value = jnp.where(step == 0, pair[parity], value)
    for number, array in enumerate(far):
        value = jnp.where(step == chips - 1 - 2 * number - core, array[parity], value)
    return value


def pair_kernel(own, partner, out):
    core = lax.axis_index("tm") % 2
    out[core] = own[...]
    out[1 - core] = partner[...]


def pair_waves(own, partner):
    return pl.pallas_call(
        pair_kernel,
        out_shape=jax.ShapeDtypeStruct((2,) + own.shape, own.dtype),
        in_specs=[VMEM] * 2,
        out_specs=VMEM,
        compiler_params=params(),
        cost_estimate=cost(0.05),
        name="pair_waves",
    )(own, partner)


def choose_kernel(pair, beside, *rest):
    far, out = rest[:-1], rest[-1]
    near = out.shape[0] - 1
    me = lax.axis_index("tm")
    chip, core = me // 2, me % 2
    for entry in range(near):
        number, parity = divmod(entry, 2)
        step = jnp.bitwise_xor(chip, near * (1 - core) + 2 * number) // 2
        value = beside[...]
        for place, array in enumerate(far):
            value = jnp.where(step == near - 1 - place, array[parity], value)
        out[entry] = value
    out[near] = segment(me, near, 0, pair, beside, far, beside)


def choose_waves(pair, beside, far):
    return pl.pallas_call(
        choose_kernel,
        out_shape=jax.ShapeDtypeStruct((len(far) + 2,) + beside.shape, beside.dtype),
        in_specs=[VMEM] * (2 + len(far)),
        out_specs=VMEM,
        compiler_params=params(),
        cost_estimate=cost(0.05),
        name="choose_waves",
    )(pair, beside, *far)


def own_kernel(owners, *refs):
    pieces, out = refs[:-1], refs[-1]
    chip = lax.axis_index("tm") // 2
    owner = jnp.where(chip < len(pieces) // 2, owners[0, 0], owners[1, 0])
    source = jnp.bitwise_xor(owner // 2, chip)
    value = pieces[0][...]
    for number, piece in enumerate(pieces[1:], 1):
        value = jnp.where(source == number, piece[...], value)
    out[...] = value


def choose_piece(owners, pieces):
    return pl.pallas_call(
        own_kernel,
        out_shape=jax.ShapeDtypeStruct(pieces[0].shape, pieces[0].dtype),
        in_specs=[VMEM] * (1 + len(pieces)),
        out_specs=VMEM,
        compiler_params=params(),
        cost_estimate=cost(0.3),
        name="choose_piece",
    )(owners, *pieces)


def waves_kernel(channels, tlen, unroll, swapped, pair, beside, *rest):
    far = rest[:-3]
    left_a, inverse, padded = rest[-3:]
    samples = beside.shape[1]
    near = swapped.shape[0] - 1
    length = 2 * near * samples
    count = padded.shape[1] // LANES
    me = lax.axis_index("tm")
    core = me % 2
    padded[...] = jnp.zeros_like(padded)
    for index in range(2 * near):
        entry, parity = divmod(index, 2)
        given = swapped.at[2 * (entry // 2) + parity]
        wave = segment(me, near * core + entry, parity, pair, beside, far, given)
        padded[0:channels, samples * index : samples * (index + 1)] = wave.astype(jnp.float32)
    rim = segment(me, near * core + near, 0, pair, beside, far, swapped.at[near])
    rim = rim[:, 0 : padded.shape[1] - length].astype(jnp.float32)
    padded[0:channels, length:] = jnp.where(core == 0, rim, 0.0)

    rows = 32 * count
    values = [padded[:, LANES * tile : LANES * (tile + 1)] for tile in range(count)]
    values = jnp.concatenate(values + [jnp.zeros((32, LANES), jnp.float32)], axis=0)
    square = values * values
    high = square.astype(jnp.bfloat16)
    low = (square - high.astype(jnp.float32)).astype(jnp.bfloat16)
    values = values.astype(jnp.bfloat16)
    lag = lax.broadcasted_iota(jnp.int32, (2 * LANES, LANES), 0)
    lag = lag - lax.broadcasted_iota(jnp.int32, (2 * LANES, LANES), 1)
    band = jnp.where(jnp.logical_and(lag >= 0, lag < tlen), 1.0, 0.0).astype(jnp.bfloat16)

    def windows(array):
        both = jnp.concatenate([array[0:rows], array[32 : rows + 32]], axis=1)
        return jnp.dot(both, band, preferred_element_type=jnp.float32)

    first_sum = windows(values)
    second_sum = windows(high) + windows(low)
    variance = (second_sum * tlen - first_sum * first_sum) * (1.0 / tlen**2)
    scale = lax.rsqrt(variance + EPSILON)
    for tile in range(length // LANES):
        part = scale[32 * tile : 32 * (tile + 1)]
        after = scale[32 * (tile + 1) : 32 * (tile + 2)]
        inverse[2 * tile] = part
        lane = lax.broadcasted_iota(jnp.int32, part.shape, 1)
        both = jnp.where(lane < STRIDE, after, part)
        inverse[2 * tile + 1] = pltpu.roll(both, LANES - STRIDE, 1)

    def interleaved(row, tiles):
        even, odd = lagged(row, 0), lagged(row, STRIDE)
        parts = []
        for tile in range(tiles):
            lanes = slice(LANES * tile, LANES * (tile + 1))
            parts += [even[:, lanes], odd[:, lanes]]
        return jnp.concatenate(parts, axis=0)

    @pl.loop(0, channels // unroll)
    def _(step):
        for item in range(unroll):
            channel = step * unroll + item
            value = interleaved(padded[pl.ds(channel, 1), :], length // LANES + 1)
            left_a[channel] = value.astype(jnp.bfloat16)


def prepare_waves(tlen, swapped, pair, beside, far):
    channels, samples = beside.shape
    length = 2 * (swapped.shape[0] - 1) * samples
    rows = length // OFFSETS
    unroll = max(step for step in (1, 2, 3) if channels % step == 0)
    return pl.pallas_call(
        functools.partial(waves_kernel, channels, tlen, unroll),
        out_shape=[
            jax.ShapeDtypeStruct((channels, rows + 16, LANES), jnp.bfloat16),
            jax.ShapeDtypeStruct((length // STRIDE, 32, LANES), jnp.float32),
        ],
        in_specs=[VMEM] * (3 + len(far)),
        out_specs=[VMEM, VMEM],
        scratch_shapes=[
            pltpu.VMEM((32, length + 2 * LANES), jnp.float32),
        ],
        compiler_params=params(),
        cost_estimate=cost(0.05),
        name="prepare_waves",
    )(swapped, pair, beside, *far)


def main_kernel(side, tlen, group, piece, left_a, inverse, *rest):
    outs = rest[:-5]
    if side:
        before, outs = outs[0], outs[1:]
    bank, expand, weight_a, reach, total = rest[-5:]
    core = lax.axis_index("tm") % 2
    channels = left_a.shape[0]
    rows = left_a.shape[1] - 16
    half = channels // 2
    base = half * jnp.where(core == side, 0, 1)
    slots = LANES // group
    banks = (half + 1) // slots
    offset_count = LANES // group
    tile_count = OFFSETS // offset_count
    top = 112 + 8 * (7 + offset_count - 1)
    top = top + top % 16

    lag = lax.broadcasted_iota(jnp.int32, (LANES, LANES), 0)
    target = lax.broadcasted_iota(jnp.int32, (LANES, LANES), 1)
    lane = lax.broadcasted_iota(jnp.int32, (1, LANES), 1)
    used = lag < tlen
    ahead = lane // group
    for slot in range(slots):
        chosen = jnp.where(lag == target % group + slot * group, 1.0, 0.0)
        expand[:, slot * LANES : (slot + 1) * LANES] = chosen.astype(jnp.bfloat16)
    turned = []
    for index in range(banks):
        count = min(slots, max(TILES - slots * index, 0))
        values = jnp.zeros((LANES, LANES), jnp.float32)
        if count:
            values = piece[slots * index : slots * index + count].astype(jnp.float32)
            values = values.reshape(count * group, LANES)
            if count < slots:
                gap = jnp.zeros((LANES - count * group, LANES), jnp.float32)
                values = jnp.concatenate([values, gap], axis=0)
            values = values.T
        turned.append(values)
    codes = [values[125:126, :] for values in turned]
    heads = [jnp.where(used, values, 0.0) for values in turned]
    for extra in range(half - TILES):
        place, slot = divmod(TILES + extra, slots)
        mask = ahead == slot
        code = pltpu.roll(turned[0][126:127, :], (slot - extra) * group % LANES, 1)
        codes[place] = jnp.where(mask, code, codes[place])
        for quarter in range(4):
            source, lanes = divmod(4 * extra + quarter, slots)
            values = turned[source][96:128]
            sample = lag[96:128]
            inside = jnp.logical_and(sample >= tlen, sample < tlen + QUARTER)
            values = jnp.where(inside, values, 0.0)
            values = pltpu.roll(values, (slot - lanes) * group % LANES, 1)
            start = QUARTER * quarter - (tlen - 96)
            values = jnp.concatenate([values, jnp.zeros((8, LANES), jnp.float32)], axis=0)
            values = pltpu.roll(values, start % 8, 0)
            start -= start % 8
            if start < 0:
                values, start = values[8:], 0
            below = LANES - start - values.shape[0]
            if start:
                values = jnp.concatenate([jnp.zeros((start, LANES), jnp.float32), values], axis=0)
            if below > 0:
                values = jnp.concatenate([values, jnp.zeros((below, LANES), jnp.float32)], axis=0)
            heads[place] = heads[place] + jnp.where(mask, values[0:LANES], 0.0)
    for index, (values, code) in enumerate(zip(heads, codes)):
        code = jnp.where(slots * index + ahead < half, code, 0.0)
        deviate = jnp.where(used, values * tlen - jnp.sum(values, axis=0, keepdims=True), 0.0)
        square = jnp.sum(deviate * deviate, axis=0, keepdims=True) * (1.0 / tlen**3)
        unit = deviate / (jnp.sqrt(square + EPSILON) * tlen**2)
        unit = unit.astype(jnp.bfloat16).astype(jnp.float32)
        unit = jnp.where(code > 0, unit, 0.0)
        shift = code.astype(jnp.int32) - 1
        for bit in (1, 2, 4):
            unit = jnp.where(jnp.bitwise_and(shift, bit) > 0, pltpu.roll(unit, bit, 0), unit)
        unit = jnp.where(lag == 112, code, unit)
        bank[index] = unit.astype(jnp.bfloat16)

    def build(number):
        wide = jnp.dot(bank[number], expand[...], preferred_element_type=jnp.float32)
        for slot in range(slots):
            spreaded = wide[:, slot * LANES : (slot + 1) * LANES]
            code = spreaded[112:113, :].astype(jnp.int32)
            shift = code - 1
            moves = shift // 8 + ahead
            taps = spreaded[0:112, :]
            for bit in (1, 2, 4, 8):
                gap = jnp.zeros((8 * bit, LANES), jnp.float32)
                taps = jnp.where(
                    jnp.bitwise_and(moves, bit) > 0,
                    jnp.concatenate([gap, taps], axis=0),
                    jnp.concatenate([taps, gap], axis=0),
                )[0:top]
            taps = taps.astype(jnp.bfloat16)
            item = number * slots + slot
            reach[item] = jnp.maximum(shift, 0) + 8 * ahead + 7 - lag[0:8]
            for tile in range(tile_count):
                skip = 8 * offset_count * tile
                lanes = slice(LANES * tile, LANES * (tile + 1))
                if skip:
                    weight_a[item, 0:skip, lanes] = jnp.zeros((skip, LANES), jnp.bfloat16)
                weight_a[item, skip : skip + top, lanes] = taps
                rest = DEPTH - top - skip
                if rest:
                    weight_a[item, skip + top :, lanes] = jnp.zeros((rest, LANES), jnp.bfloat16)

    def products(item):
        both = [left_a[base + item, 0:rows, :], left_a[base + item, 16 : rows + 16, :]]
        corr = jnp.dot(
            jnp.concatenate(both, axis=1), weight_a[item], preferred_element_type=jnp.float32
        )
        columns = []
        for tile in range(tile_count):
            place = reach[item] + 8 * offset_count * tile
            parts = []
            for step in range(rows // 8):
                window = inverse[step, pl.ds(base + item, 1), :]
                window = jnp.broadcast_to(window, (8, LANES))
                parts.append(jnp.take_along_axis(window, place, axis=1, mode="promise_in_bounds"))
            columns.append(jnp.concatenate(parts, axis=0))
        return corr * jnp.concatenate(columns, axis=1)

    def apply(number, count):
        for item in range(number * slots, number * slots + count, 2):
            value = products(item)
            if item + 1 < number * slots + count:
                value = value + products(item + 1)
            if item:
                value = value + total[...]
            elif side:
                value = value + before[...]
            total[...] = value

    build(0)

    for number in range(1, banks):
        apply(number - 1, slots)
        build(number)

    apply(banks - 1, half - slots * (banks - 1))

    if not side:
        outs[0][...] = total[...]
        return
    rows_out = outs[0].shape[0]
    station = lax.axis_index("sta") % len(outs)
    for step, out in enumerate(outs):
        part = jnp.bitwise_xor(station, step)
        out[...] = total[pl.ds(pl.multiple_of(part * rows_out, rows_out), rows_out), :].astype(
            jnp.bfloat16
        )


def correlate(side, tlen, group, count, piece, left_a, inverse, *before):
    channels = left_a.shape[0]
    rows = left_a.shape[1] - 16
    width = OFFSETS * group
    half = channels // 2
    if side:
        out = [jax.ShapeDtypeStruct((rows // count, width), jnp.bfloat16)] * count
    else:
        out = [jax.ShapeDtypeStruct((rows, width), jnp.float32)]
    return pl.pallas_call(
        functools.partial(main_kernel, side, tlen, group),
        out_shape=out,
        in_specs=[VMEM] * (3 + len(before)),
        out_specs=[VMEM] * len(out),
        scratch_shapes=[
            pltpu.VMEM(((half + 1) * group // LANES, LANES, LANES), jnp.bfloat16),
            pltpu.VMEM((LANES, LANES // group * LANES), jnp.bfloat16),
            pltpu.VMEM((half + 1, DEPTH, width), jnp.bfloat16),
            pltpu.VMEM((half + 1, 8, LANES), jnp.int32),
            pltpu.VMEM((rows, width), jnp.float32),
        ],
        compiler_params=params(),
        cost_estimate=cost(3),
        name="correlate_" + ("second" if side else "first"),
    )(piece, left_a, inverse, *before)


def add_kernel(*refs):
    parts, keep, send = refs[:-2], refs[-2], refs[-1]
    rows = keep.shape[0]
    core = lax.axis_index("tm") % 2
    for out, which in ((keep, core), (send, 1 - core)):
        place = pl.ds(pl.multiple_of(which * rows, rows), rows)
        value = parts[0][place, :].astype(jnp.float32)
        for part in parts[1:]:
            value = value + part[place, :].astype(jnp.float32)
        out[...] = value


def add(parts):
    rows, width = parts[0].shape
    out = jax.ShapeDtypeStruct((rows // 2, width), jnp.float32)
    return pl.pallas_call(
        add_kernel,
        out_shape=[out, out],
        in_specs=[VMEM] * len(parts),
        out_specs=[VMEM, VMEM],
        compiler_params=params(),
        cost_estimate=cost(0.5),
        name="add",
    )(*parts)


def finish_kernel(group, ours, received, out):
    samples = out.shape[1]
    rows = ours.shape[0]
    value = ours[...] + received[...]
    high = value.astype(jnp.bfloat16).astype(jnp.float32)
    both = jnp.concatenate([high, value - high], axis=0).T.astype(jnp.bfloat16)
    row = lax.broadcasted_iota(jnp.int32, (2 * rows, samples), 0) % rows
    lane = lax.broadcasted_iota(jnp.int32, (2 * rows, samples), 1)
    place = jnp.logical_and(lane // STRIDE == row // 8, lane % 8 == 7 - row % 8)
    place = jnp.where(place, 1.0, 0.0).astype(jnp.bfloat16)
    wide = jnp.dot(both, place, preferred_element_type=jnp.float32)
    lane = lax.broadcasted_iota(jnp.int32, (group, samples), 1) // 8 % OFFSETS
    result = jnp.zeros((group, samples), jnp.float32)
    for offset in range(OFFSETS):
        result = jnp.where(lane == offset, wide[offset * group : (offset + 1) * group], result)
    out[...] = result


def finish(group, samples, ours, received):
    return pl.pallas_call(
        functools.partial(finish_kernel, group),
        out_shape=jax.ShapeDtypeStruct((group, samples), jnp.float32),
        in_specs=[VMEM, VMEM],
        out_specs=VMEM,
        compiler_params=params(),
        cost_estimate=cost(1),
        name="finish",
    )(ours, received)


def shards(waveforms, templates, available, moveout, bank_blocks):
    channels, samples = waveforms.shape
    blocks, events, _, tlen = templates.shape
    count_tm = lax.axis_size("tm")
    count_sta = lax.axis_size("sta")
    chips = count_tm // 2
    near = chips // 2
    group = 2 * events // chips

    def swap(array):
        return lax.ppermute(array, "tm", [(i, i ^ 1) for i in range(count_tm)])

    def across(array, step):
        return lax.ppermute(array, "tm", [(i, i ^ (2 * step)) for i in range(count_tm)])

    partner = swap(waveforms)
    mine, theirs, owners = pack(
        chips,
        group,
        bank_blocks,
        jnp.transpose(templates, (0, 2, 1, 3)),
        jnp.transpose(available, (2, 0, 1)),
        jnp.transpose(moveout, (2, 0, 1)),
    )
    theirs, partner = lax.optimization_barrier((theirs, partner))
    other = swap(theirs)
    pair = pair_waves(waveforms, partner)
    far = []
    for number in range(near - 1):
        steps = (chips - 1 - 2 * number, chips - 2 - 2 * number)
        route = [(2 * z + c, 2 * (z ^ steps[c]) + c) for z in range(chips) for c in range(2)]
        far.append(lax.ppermute(pair, "tm", route))
    beside = across(waveforms, 1)
    merged = list(merge(owners, mine, other))
    pieces = [across(merged[step], step) for step in reversed(range(1, chips))]
    pieces = [merged[0]] + pieces[::-1]
    swapped = swap(choose_waves(pair, beside, far))
    left_a, inverse = prepare_waves(tlen, swapped, pair, beside, far)

    left_a, inverse, *pieces = lax.optimization_barrier((left_a, inverse, *pieces[::-1]))
    pieces = pieces[::-1]
    first = choose_piece(owners, pieces)
    second = swap(first)
    total = correlate(0, tlen, group, near, first, left_a, inverse)
    parts = correlate(1, tlen, group, near, second, left_a, inverse, *total)
    gathered = []
    for step in range(near):
        route = []
        for d in range(count_tm):
            for s in range(count_sta):
                dest = near * (d % 2) + (s % near ^ step)
                route.append((d * count_sta + s, (2 * dest + s // near) * count_sta + d // 2))
        gathered.append(lax.ppermute(parts[step], ("tm", "sta"), route))
    ours, send = add(gathered)
    return finish(group, samples, ours, swap(send))


def solution(mesh):
    in_specs = (
        P("sta", "tm"),
        P("tm", None, "sta", None),
        P("tm", None, "sta"),
        P("tm", None, "sta"),
        P(),
    )
    out_specs = P("sta", "tm")
    return jax.shard_map(shards, mesh=mesh, in_specs=in_specs, out_specs=out_specs, check_vma=False)
```

```python
import functools

import jax
import jax.numpy as jnp
from jax import lax
from jax.experimental import pallas as pl
from jax.experimental.pallas import tpu as pltpu
from jax.sharding import PartitionSpec as P

EPSILON = 1e-06
LANES = 128
OFFSETS = 8
TILES = 12
QUARTER = 25
STRIDE = 64
DEPTH = 256
VMEM_LIMIT = 28 * 1024 * 1024

VMEM = pl.BlockSpec(memory_space=pltpu.VMEM)
ANY = pl.BlockSpec(memory_space=pl.ANY)


def params():
    return pltpu.CompilerParams(vmem_limit_bytes=VMEM_LIMIT)


def cost(micros):
    return pl.CostEstimate(
        flops=int(micros * 1e9), bytes_accessed=int(micros * 1e6), transcendentals=0
    )


def pack_kernel(bank_blocks, templates, available, moveout, mine, theirs, owners, chosen, raw, usable, shifts, square, sems):
    blocks, channels, events, tlen = templates.shape
    chips, _, group, _ = mine.shape
    half = channels // 2
    me = lax.axis_index("tm") % 2
    fetch = [
        pltpu.make_async_copy(source, target, sems.at[index])
        for index, (source, target) in enumerate(
            ((bank_blocks, chosen), (available, usable), (moveout, shifts))
        )
    ]
    for block in range(blocks):
        for part in range(2):
            place = (block, pl.ds(half * part, half))
            fetch.append(
                pltpu.make_async_copy(
                    templates.at[place], raw.at[place], sems.at[3 + 2 * block + part]
                )
            )
    for copy in fetch:
        copy.start()
    mine[...] = jnp.zeros_like(mine)
    theirs[...] = jnp.zeros_like(theirs)
    square[...] = jnp.zeros_like(square)
    for copy in fetch:
        copy.wait()
    slots = [chosen[which] % blocks for which in range(2)]
    row = lax.broadcasted_iota(jnp.int32, owners.shape, 0)
    owners[...] = jnp.where(row == 0, chosen[0] // blocks, chosen[1] // blocks)
    flags = jnp.where(usable[...] > 0, shifts[...] + 1, 0).astype(jnp.float32)
    codes = []
    for which in range(2):
        code = flags[:, 0, :]
        for block in range(1, blocks):
            code = jnp.where(slots[which] == block, flags[:, block, :], code)
        square[0:channels, 0:events] = code
        turned = square[...].T
        later = pltpu.roll(turned, LANES - half, 1)
        codes.append([jnp.where(me == core, turned, later) for core in range(2)])
    for which in range(2):
        for side, out in enumerate((mine, theirs)):
            first = half * jnp.where(me == side, 0, 1)
            code = codes[which][side].astype(jnp.bfloat16)
            for tile in range(TILES):
                extra = TILES + tile // 4
                start = QUARTER * (tile % 4)
                for index in range(events // group):
                    chip = which * (events // group) + index
                    rows = slice(index * group, (index + 1) * group)
                    out[chip, tile, :, 0:tlen] = raw[slots[which], first + tile, rows, :]
                    out[chip, tile, :, tlen : tlen + QUARTER] = raw[
                        slots[which], first + extra, rows, start : start + QUARTER
                    ]
                    out[chip, tile, :, 125:126] = code[rows, tile : tile + 1]
                    if tile < half - TILES:
                        beyond = TILES + tile
                        out[chip, tile, :, 126:127] = code[rows, beyond : beyond + 1]


def pack(chips, group, bank_blocks, templates, available, moveout):
    shape = (chips, TILES, group, LANES)
    held = [
        pltpu.with_memory_space_constraint(array, pltpu.HBM)
        for array in (bank_blocks, templates, available, moveout)
    ]
    return pl.pallas_call(
        pack_kernel,
        out_shape=[jax.ShapeDtypeStruct(shape, jnp.bfloat16)] * 2
        + [jax.ShapeDtypeStruct((8, LANES), jnp.int32)],
        in_specs=[ANY] * 4,
        out_specs=[VMEM] * 3,
        scratch_shapes=[
            pltpu.SMEM(bank_blocks.shape, jnp.int32),
            pltpu.VMEM(templates.shape, jnp.bfloat16),
            pltpu.VMEM(available.shape, jnp.int32),
            pltpu.VMEM(moveout.shape, jnp.int32),
            pltpu.VMEM((LANES, LANES), jnp.float32),
            pltpu.SemaphoreType.DMA((3 + 2 * templates.shape[0],)),
        ],
        compiler_params=params(),
        cost_estimate=cost(2),
        name="pack",
    )(*held)


def merge_kernel(owners, mine, other, *outs):
    chips = len(outs)
    me = lax.axis_index("tm")
    for step, out in enumerate(outs):
        dest = jnp.bitwise_xor(me // 2, step)
        owner = jnp.where(dest < chips // 2, owners[0, 0], owners[1, 0])
        here = owner % 2 == me % 2

        @pl.when(here)
        def _():
            out[...] = mine[dest]

        @pl.when(jnp.logical_not(here))
        def _():
            out[...] = other[dest]


def merge(owners, mine, other):
    chips = mine.shape[0]
    return pl.pallas_call(
        merge_kernel,
        out_shape=[jax.ShapeDtypeStruct(mine.shape[1:], mine.dtype)] * chips,
        in_specs=[VMEM] * 3,
        out_specs=[VMEM] * chips,
        compiler_params=params(),
        cost_estimate=cost(0.3),
        name="merge",
    )(owners, mine, other)


def lagged(row, ahead):
    copies = jnp.broadcast_to(row, (8, row.shape[1]))
    return pltpu.roll(copies, row.shape[1] - 7 - ahead, 1, stride=1, stride_axis=0)


def segment(me, other, parity, pair, beside, far, default):
    chip, core = me // 2, me % 2
    chips = 2 * len(far) + 2
    step = jnp.bitwise_xor(chip, other)
    value = default[...]
    value = jnp.where(jnp.logical_and(step == 1, core == parity), beside[...], value)
    value = jnp.where(step == 0, pair[parity], value)
    for number, array in enumerate(far):
        value = jnp.where(step == chips - 1 - 2 * number - core, array[parity], value)
    return value


def pair_kernel(own, partner, out):
    core = lax.axis_index("tm") % 2
    out[core] = own[...]
    out[1 - core] = partner[...]


def pair_waves(own, partner):
    return pl.pallas_call(
        pair_kernel,
        out_shape=jax.ShapeDtypeStruct((2,) + own.shape, own.dtype),
        in_specs=[VMEM] * 2,
        out_specs=VMEM,
        compiler_params=params(),
        cost_estimate=cost(0.05),
        name="pair_waves",
    )(own, partner)


def choose_kernel(pair, beside, *rest):
    far, out = rest[:-1], rest[-1]
    near = out.shape[0] - 1
    me = lax.axis_index("tm")
    chip, core = me // 2, me % 2
    for entry in range(near):
        number, parity = divmod(entry, 2)
        step = jnp.bitwise_xor(chip, near * (1 - core) + 2 * number) // 2
        value = beside[...]
        for place, array in enumerate(far):
            value = jnp.where(step == near - 1 - place, array[parity], value)
        out[entry] = value
    out[near] = segment(me, near, 0, pair, beside, far, beside)


def choose_waves(pair, beside, far):
    return pl.pallas_call(
        choose_kernel,
        out_shape=jax.ShapeDtypeStruct((len(far) + 2,) + beside.shape, beside.dtype),
        in_specs=[VMEM] * (2 + len(far)),
        out_specs=VMEM,
        compiler_params=params(),
        cost_estimate=cost(0.05),
        name="choose_waves",
    )(pair, beside, *far)


def own_kernel(owners, *refs):
    pieces, out = refs[:-1], refs[-1]
    chip = lax.axis_index("tm") // 2
    owner = jnp.where(chip < len(pieces) // 2, owners[0, 0], owners[1, 0])
    source = jnp.bitwise_xor(owner // 2, chip)
    value = pieces[0][...]
    for number, piece in enumerate(pieces[1:], 1):
        value = jnp.where(source == number, piece[...], value)
    out[...] = value


def choose_piece(owners, pieces):
    return pl.pallas_call(
        own_kernel,
        out_shape=jax.ShapeDtypeStruct(pieces[0].shape, pieces[0].dtype),
        in_specs=[VMEM] * (1 + len(pieces)),
        out_specs=VMEM,
        compiler_params=params(),
        cost_estimate=cost(0.3),
        name="choose_piece",
    )(owners, *pieces)


def waves_kernel(channels, tlen, unroll, swapped, pair, beside, *rest):
    far = rest[:-3]
    left_a, inverse, padded = rest[-3:]
    samples = beside.shape[1]
    near = swapped.shape[0] - 1
    length = 2 * near * samples
    count = padded.shape[1] // LANES
    me = lax.axis_index("tm")
    core = me % 2
    padded[...] = jnp.zeros_like(padded)
    for index in range(2 * near):
        entry, parity = divmod(index, 2)
        given = swapped.at[2 * (entry // 2) + parity]
        wave = segment(me, near * core + entry, parity, pair, beside, far, given)
        padded[0:channels, samples * index : samples * (index + 1)] = wave.astype(jnp.float32)
    rim = segment(me, near * core + near, 0, pair, beside, far, swapped.at[near])
    rim = rim[:, 0 : padded.shape[1] - length].astype(jnp.float32)
    padded[0:channels, length:] = jnp.where(core == 0, rim, 0.0)

    rows = 32 * count
    values = [padded[:, LANES * tile : LANES * (tile + 1)] for tile in range(count)]
    values = jnp.concatenate(values + [jnp.zeros((32, LANES), jnp.float32)], axis=0)
    square = values * values
    high = square.astype(jnp.bfloat16)
    low = (square - high.astype(jnp.float32)).astype(jnp.bfloat16)
    values = values.astype(jnp.bfloat16)
    lag = lax.broadcasted_iota(jnp.int32, (2 * LANES, LANES), 0)
    lag = lag - lax.broadcasted_iota(jnp.int32, (2 * LANES, LANES), 1)
    band = jnp.where(jnp.logical_and(lag >= 0, lag < tlen), 1.0, 0.0).astype(jnp.bfloat16)

    def windows(array):
        both = jnp.concatenate([array[0:rows], array[32 : rows + 32]], axis=1)
        return jnp.dot(both, band, preferred_element_type=jnp.float32)

    first_sum = windows(values)
    second_sum = windows(high) + windows(low)
    variance = (second_sum * tlen - first_sum * first_sum) * (1.0 / tlen**2)
    scale = lax.rsqrt(variance + EPSILON)
    for tile in range(length // LANES):
        part = scale[32 * tile : 32 * (tile + 1)]
        after = scale[32 * (tile + 1) : 32 * (tile + 2)]
        inverse[2 * tile] = part
        lane = lax.broadcasted_iota(jnp.int32, part.shape, 1)
        both = jnp.where(lane < STRIDE, after, part)
        inverse[2 * tile + 1] = pltpu.roll(both, LANES - STRIDE, 1)

    def interleaved(row, tiles):
        even, odd = lagged(row, 0), lagged(row, STRIDE)
        parts = []
        for tile in range(tiles):
            lanes = slice(LANES * tile, LANES * (tile + 1))
            parts += [even[:, lanes], odd[:, lanes]]
        return jnp.concatenate(parts, axis=0)

    @pl.loop(0, channels // unroll)
    def _(step):
        for item in range(unroll):
            channel = step * unroll + item
            value = interleaved(padded[pl.ds(channel, 1), :], length // LANES + 1)
            left_a[channel] = value.astype(jnp.bfloat16)


def prepare_waves(tlen, swapped, pair, beside, far):
    channels, samples = beside.shape
    length = 2 * (swapped.shape[0] - 1) * samples
    rows = length // OFFSETS
    unroll = max(step for step in (1, 2, 3) if channels % step == 0)
    return pl.pallas_call(
        functools.partial(waves_kernel, channels, tlen, unroll),
        out_shape=[
            jax.ShapeDtypeStruct((channels, rows + 16, LANES), jnp.bfloat16),
            jax.ShapeDtypeStruct((length // STRIDE, 32, LANES), jnp.float32),
        ],
        in_specs=[VMEM] * (3 + len(far)),
        out_specs=[VMEM, VMEM],
        scratch_shapes=[
            pltpu.VMEM((32, length + 2 * LANES), jnp.float32),
        ],
        compiler_params=params(),
        cost_estimate=cost(0.05),
        name="prepare_waves",
    )(swapped, pair, beside, *far)


def main_kernel(side, tlen, group, piece, left_a, inverse, *rest):
    outs = rest[:-5]
    if side:
        before, outs = outs[0], outs[1:]
    bank, expand, weight_a, reach, total = rest[-5:]
    core = lax.axis_index("tm") % 2
    channels = left_a.shape[0]
    rows = left_a.shape[1] - 16
    half = channels // 2
    base = half * jnp.where(core == side, 0, 1)
    slots = LANES // group
    banks = (half + 1) // slots
    offset_count = LANES // group
    tile_count = OFFSETS // offset_count
    top = 112 + 8 * (7 + offset_count - 1)
    top = top + top % 16

    lag = lax.broadcasted_iota(jnp.int32, (LANES, LANES), 0)
    target = lax.broadcasted_iota(jnp.int32, (LANES, LANES), 1)
    lane = lax.broadcasted_iota(jnp.int32, (1, LANES), 1)
    used = lag < tlen
    ahead = lane // group
    for slot in range(slots):
        chosen = jnp.where(lag == target % group + slot * group, 1.0, 0.0)
        expand[:, slot * LANES : (slot + 1) * LANES] = chosen.astype(jnp.bfloat16)
    turned = []
    for index in range(banks):
        count = min(slots, max(TILES - slots * index, 0))
        values = jnp.zeros((LANES, LANES), jnp.float32)
        if count:
            values = piece[slots * index : slots * index + count].astype(jnp.float32)
            values = values.reshape(count * group, LANES)
            if count < slots:
                gap = jnp.zeros((LANES - count * group, LANES), jnp.float32)
                values = jnp.concatenate([values, gap], axis=0)
            values = values.T
        turned.append(values)
    codes = [values[125:126, :] for values in turned]
    heads = [jnp.where(used, values, 0.0) for values in turned]
    for extra in range(half - TILES):
        place, slot = divmod(TILES + extra, slots)
        mask = ahead == slot
        code = pltpu.roll(turned[0][126:127, :], (slot - extra) * group % LANES, 1)
        codes[place] = jnp.where(mask, code, codes[place])
        for quarter in range(4):
            source, lanes = divmod(4 * extra + quarter, slots)
            values = turned[source][96:128]
            sample = lag[96:128]
            inside = jnp.logical_and(sample >= tlen, sample < tlen + QUARTER)
            values = jnp.where(inside, values, 0.0)
            values = pltpu.roll(values, (slot - lanes) * group % LANES, 1)
            start = QUARTER * quarter - (tlen - 96)
            values = jnp.concatenate([values, jnp.zeros((8, LANES), jnp.float32)], axis=0)
            values = pltpu.roll(values, start % 8, 0)
            start -= start % 8
            if start < 0:
                values, start = values[8:], 0
            below = LANES - start - values.shape[0]
            if start:
                values = jnp.concatenate([jnp.zeros((start, LANES), jnp.float32), values], axis=0)
            if below > 0:
                values = jnp.concatenate([values, jnp.zeros((below, LANES), jnp.float32)], axis=0)
            heads[place] = heads[place] + jnp.where(mask, values[0:LANES], 0.0)
    for index, (values, code) in enumerate(zip(heads, codes)):
        code = jnp.where(slots * index + ahead < half, code, 0.0)
        deviate = jnp.where(used, values * tlen - jnp.sum(values, axis=0, keepdims=True), 0.0)
        square = jnp.sum(deviate * deviate, axis=0, keepdims=True) * (1.0 / tlen**3)
        unit = deviate / (jnp.sqrt(square + EPSILON) * tlen**2)
        unit = unit.astype(jnp.bfloat16).astype(jnp.float32)
        unit = jnp.where(code > 0, unit, 0.0)
        shift = code.astype(jnp.int32) - 1
        for bit in (1, 2, 4):
            unit = jnp.where(jnp.bitwise_and(shift, bit) > 0, pltpu.roll(unit, bit, 0), unit)
        unit = jnp.where(lag == 112, code, unit)
        bank[index] = unit.astype(jnp.bfloat16)

    def build(number):
        wide = jnp.dot(bank[number], expand[...], preferred_element_type=jnp.float32)
        for slot in range(slots):
            spreaded = wide[:, slot * LANES : (slot + 1) * LANES]
            code = spreaded[112:113, :].astype(jnp.int32)
            shift = code - 1
            moves = shift // 8 + ahead
            taps = spreaded[0:112, :]
            for bit in (1, 2, 4, 8):
                gap = jnp.zeros((8 * bit, LANES), jnp.float32)
                taps = jnp.where(
                    jnp.bitwise_and(moves, bit) > 0,
                    jnp.concatenate([gap, taps], axis=0),
                    jnp.concatenate([taps, gap], axis=0),
                )[0:top]
            taps = taps.astype(jnp.bfloat16)
            item = number * slots + slot
            reach[item] = jnp.maximum(shift, 0) + 8 * ahead + 7 - lag[0:8]
            for tile in range(tile_count):
                skip = 8 * offset_count * tile
                lanes = slice(LANES * tile, LANES * (tile + 1))
                if skip:
                    weight_a[item, 0:skip, lanes] = jnp.zeros((skip, LANES), jnp.bfloat16)
                weight_a[item, skip : skip + top, lanes] = taps
                rest = DEPTH - top - skip
                if rest:
                    weight_a[item, skip + top :, lanes] = jnp.zeros((rest, LANES), jnp.bfloat16)

    def products(item):
        both = [left_a[base + item, 0:rows, :], left_a[base + item, 16 : rows + 16, :]]
        corr = jnp.dot(
            jnp.concatenate(both, axis=1), weight_a[item], preferred_element_type=jnp.float32
        )
        columns = []
        for tile in range(tile_count):
            place = reach[item] + 8 * offset_count * tile
            parts = []
            for step in range(rows // 8):
                window = inverse[step, pl.ds(base + item, 1), :]
                window = jnp.broadcast_to(window, (8, LANES))
                parts.append(jnp.take_along_axis(window, place, axis=1, mode="promise_in_bounds"))
            columns.append(jnp.concatenate(parts, axis=0))
        return corr * jnp.concatenate(columns, axis=1)

    def apply(number, count):
        for item in range(number * slots, number * slots + count, 2):
            value = products(item)
            if item + 1 < number * slots + count:
                value = value + products(item + 1)
            if item:
                value = value + total[...]
            elif side:
                value = value + before[...]
            total[...] = value

    build(0)

    for number in range(1, banks):
        apply(number - 1, slots)
        build(number)

    apply(banks - 1, half - slots * (banks - 1))

    if not side:
        outs[0][...] = total[...]
        return
    rows_out = outs[0].shape[0]
    station = lax.axis_index("sta") % len(outs)
    for step, out in enumerate(outs):
        part = jnp.bitwise_xor(station, step)
        out[...] = total[pl.ds(pl.multiple_of(part * rows_out, rows_out), rows_out), :].astype(
            jnp.bfloat16
        )


def correlate(side, tlen, group, count, piece, left_a, inverse, *before):
    channels = left_a.shape[0]
    rows = left_a.shape[1] - 16
    width = OFFSETS * group
    half = channels // 2
    if side:
        out = [jax.ShapeDtypeStruct((rows // count, width), jnp.bfloat16)] * count
    else:
        out = [jax.ShapeDtypeStruct((rows, width), jnp.float32)]
    return pl.pallas_call(
        functools.partial(main_kernel, side, tlen, group),
        out_shape=out,
        in_specs=[VMEM] * (3 + len(before)),
        out_specs=[VMEM] * len(out),
        scratch_shapes=[
            pltpu.VMEM(((half + 1) * group // LANES, LANES, LANES), jnp.bfloat16),
            pltpu.VMEM((LANES, LANES // group * LANES), jnp.bfloat16),
            pltpu.VMEM((half + 1, DEPTH, width), jnp.bfloat16),
            pltpu.VMEM((half + 1, 8, LANES), jnp.int32),
            pltpu.VMEM((rows, width), jnp.float32),
        ],
        compiler_params=params(),
        cost_estimate=cost(3),
        name="correlate_" + ("second" if side else "first"),
    )(piece, left_a, inverse, *before)


def add_kernel(*refs):
    parts, keep, send = refs[:-2], refs[-2], refs[-1]
    rows = keep.shape[0]
    core = lax.axis_index("tm") % 2
    for out, which in ((keep, core), (send, 1 - core)):
        place = pl.ds(pl.multiple_of(which * rows, rows), rows)
        value = parts[0][place, :].astype(jnp.float32)
        for part in parts[1:]:
            value = value + part[place, :].astype(jnp.float32)
        out[...] = value


def add(parts):
    rows, width = parts[0].shape
    out = jax.ShapeDtypeStruct((rows // 2, width), jnp.float32)
    return pl.pallas_call(
        add_kernel,
        out_shape=[out, out],
        in_specs=[VMEM] * len(parts),
        out_specs=[VMEM, VMEM],
        compiler_params=params(),
        cost_estimate=cost(0.5),
        name="add",
    )(*parts)


def finish_kernel(group, ours, received, out):
    samples = out.shape[1]
    rows = ours.shape[0]
    value = ours[...] + received[...]
    high = value.astype(jnp.bfloat16).astype(jnp.float32)
    both = jnp.concatenate([high, value - high], axis=0).T.astype(jnp.bfloat16)
    row = lax.broadcasted_iota(jnp.int32, (2 * rows, samples), 0) % rows
    lane = lax.broadcasted_iota(jnp.int32, (2 * rows, samples), 1)
    place = jnp.logical_and(lane // STRIDE == row // 8, lane % 8 == 7 - row % 8)
    place = jnp.where(place, 1.0, 0.0).astype(jnp.bfloat16)
    wide = jnp.dot(both, place, preferred_element_type=jnp.float32)
    lane = lax.broadcasted_iota(jnp.int32, (group, samples), 1) // 8 % OFFSETS
    result = jnp.zeros((group, samples), jnp.float32)
    for offset in range(OFFSETS):
        result = jnp.where(lane == offset, wide[offset * group : (offset + 1) * group], result)
    out[...] = result


def finish(group, samples, ours, received):
    return pl.pallas_call(
        functools.partial(finish_kernel, group),
        out_shape=jax.ShapeDtypeStruct((group, samples), jnp.float32),
        in_specs=[VMEM, VMEM],
        out_specs=VMEM,
        compiler_params=params(),
        cost_estimate=cost(1),
        name="finish",
    )(ours, received)


def shards(waveforms, templates, available, moveout, bank_blocks):
    channels, samples = waveforms.shape
    blocks, events, _, tlen = templates.shape
    count_tm = lax.axis_size("tm")
    count_sta = lax.axis_size("sta")
    chips = count_tm // 2
    near = chips // 2
    group = 2 * events // chips

    def swap(array):
        return lax.ppermute(array, "tm", [(i, i ^ 1) for i in range(count_tm)])

    def across(array, step):
        return lax.ppermute(array, "tm", [(i, i ^ (2 * step)) for i in range(count_tm)])

    partner = swap(waveforms)
    mine, theirs, owners = pack(
        chips,
        group,
        bank_blocks,
        jnp.transpose(templates, (0, 2, 1, 3)),
        jnp.transpose(available, (2, 0, 1)),
        jnp.transpose(moveout, (2, 0, 1)),
    )
    theirs, partner = lax.optimization_barrier((theirs, partner))
    other = swap(theirs)
    pair = pair_waves(waveforms, partner)
    far = []
    for number in range(near - 1):
        steps = (chips - 1 - 2 * number, chips - 2 - 2 * number)
        route = [(2 * z + c, 2 * (z ^ steps[c]) + c) for z in range(chips) for c in range(2)]
        far.append(lax.ppermute(pair, "tm", route))
    beside = across(waveforms, 1)
    merged = list(merge(owners, mine, other))
    pieces = [across(merged[step], step) for step in reversed(range(1, chips))]
    pieces = [merged[0]] + pieces[::-1]
    swapped = swap(choose_waves(pair, beside, far))
    left_a, inverse = prepare_waves(tlen, swapped, pair, beside, far)

    left_a, inverse, *pieces = lax.optimization_barrier((left_a, inverse, *pieces[::-1]))
    pieces = pieces[::-1]
    first = choose_piece(owners, pieces)
    second = swap(first)
    total = correlate(0, tlen, group, near, first, left_a, inverse)
    parts = correlate(1, tlen, group, near, second, left_a, inverse, *total)
    gathered = []
    for step in range(near):
        route = []
        for d in range(count_tm):
            for s in range(count_sta):
                dest = near * (d % 2) + (s % near ^ step)
                route.append((d * count_sta + s, (2 * dest + s // near) * count_sta + d // 2))
        gathered.append(lax.ppermute(parts[step], ("tm", "sta"), route))
    ours, send = add(gathered)
    return finish(group, samples, ours, swap(send))


def solution(mesh):
    in_specs = (
        P("sta", "tm"),
        P("tm", None, "sta", None),
        P("tm", None, "sta"),
        P("tm", None, "sta"),
        P(),
    )
    out_specs = P("sta", "tm")
    return jax.shard_map(shards, mesh=mesh, in_specs=in_specs, out_specs=out_specs, check_vma=False)
```

```python
import functools

import jax
import jax.numpy as jnp
from jax import lax
from jax.experimental import pallas as pl
from jax.experimental.pallas import tpu as pltpu
from jax.sharding import PartitionSpec as P

EPSILON = 1e-06
LANES = 128
OFFSETS = 8
TILES = 12
QUARTER = 25
STRIDE = 64
DEPTH = 256
VMEM_LIMIT = 28 * 1024 * 1024

VMEM = pl.BlockSpec(memory_space=pltpu.VMEM)
ANY = pl.BlockSpec(memory_space=pl.ANY)


def params():
    return pltpu.CompilerParams(vmem_limit_bytes=VMEM_LIMIT)


def cost(micros):
    return pl.CostEstimate(
        flops=int(micros * 1e9), bytes_accessed=int(micros * 1e6), transcendentals=0
    )


def pack_kernel(bank_blocks, templates, available, moveout, mine, theirs, owners, chosen, raw, usable, shifts, square, sems):
    blocks, channels, events, tlen = templates.shape
    chips, _, group, _ = mine.shape
    half = channels // 2
    me = lax.axis_index("tm") % 2
    fetch = [
        pltpu.make_async_copy(source, target, sems.at[index])
        for index, (source, target) in enumerate(
            ((bank_blocks, chosen), (available, usable), (moveout, shifts))
        )
    ]
    for side in (1, 0):
        first = half * jnp.where(me == side, 0, 1)
        for block in range(blocks):
            place = (block, pl.ds(first, half))
            number = 3 + blocks * (1 - side) + block
            fetch.append(
                pltpu.make_async_copy(templates.at[place], raw.at[place], sems.at[number])
            )
    for copy in fetch:
        copy.start()
    mine[...] = jnp.zeros_like(mine)
    theirs[...] = jnp.zeros_like(theirs)
    square[...] = jnp.zeros_like(square)
    for copy in fetch[:3]:
        copy.wait()
    slots = [chosen[which] % blocks for which in range(2)]
    row = lax.broadcasted_iota(jnp.int32, owners.shape, 0)
    owners[...] = jnp.where(row == 0, chosen[0] // blocks, chosen[1] // blocks)
    flags = jnp.where(usable[...] > 0, shifts[...] + 1, 0).astype(jnp.float32)
    codes = []
    for which in range(2):
        code = flags[:, 0, :]
        for block in range(1, blocks):
            code = jnp.where(slots[which] == block, flags[:, block, :], code)
        square[0:channels, 0:events] = code
        turned = square[...].T
        later = pltpu.roll(turned, LANES - half, 1)
        codes.append([jnp.where(me == core, turned, later) for core in range(2)])
    for side, out in ((1, theirs), (0, mine)):
        for block in range(blocks):
            fetch[3 + blocks * (1 - side) + block].wait()
        for which in range(2):
            first = half * jnp.where(me == side, 0, 1)
            code = codes[which][side].astype(jnp.bfloat16)
            for tile in range(TILES):
                extra = TILES + tile // 4
                start = QUARTER * (tile % 4)
                for index in range(events // group):
                    chip = which * (events // group) + index
                    rows = slice(index * group, (index + 1) * group)
                    out[chip, tile, :, 0:tlen] = raw[slots[which], first + tile, rows, :]
                    out[chip, tile, :, tlen : tlen + QUARTER] = raw[
                        slots[which], first + extra, rows, start : start + QUARTER
                    ]
                    out[chip, tile, :, 125:126] = code[rows, tile : tile + 1]
                    if tile < half - TILES:
                        beyond = TILES + tile
                        out[chip, tile, :, 126:127] = code[rows, beyond : beyond + 1]


def pack(chips, group, bank_blocks, templates, available, moveout):
    shape = (chips, TILES, group, LANES)
    held = [
        pltpu.with_memory_space_constraint(array, pltpu.HBM)
        for array in (bank_blocks, templates, available, moveout)
    ]
    return pl.pallas_call(
        pack_kernel,
        out_shape=[jax.ShapeDtypeStruct(shape, jnp.bfloat16)] * 2
        + [jax.ShapeDtypeStruct((8, LANES), jnp.int32)],
        in_specs=[ANY] * 4,
        out_specs=[VMEM] * 3,
        scratch_shapes=[
            pltpu.SMEM(bank_blocks.shape, jnp.int32),
            pltpu.VMEM(templates.shape, jnp.bfloat16),
            pltpu.VMEM(available.shape, jnp.int32),
            pltpu.VMEM(moveout.shape, jnp.int32),
            pltpu.VMEM((LANES, LANES), jnp.float32),
            pltpu.SemaphoreType.DMA((3 + 2 * templates.shape[0],)),
        ],
        compiler_params=params(),
        cost_estimate=cost(2),
        name="pack",
    )(*held)


def merge_kernel(owners, mine, other, *outs):
    chips = len(outs)
    me = lax.axis_index("tm")
    for step, out in enumerate(outs):
        dest = jnp.bitwise_xor(me // 2, step)
        owner = jnp.where(dest < chips // 2, owners[0, 0], owners[1, 0])
        here = owner % 2 == me % 2

        @pl.when(here)
        def _():
            out[...] = mine[dest]

        @pl.when(jnp.logical_not(here))
        def _():
            out[...] = other[dest]


def merge(owners, mine, other):
    chips = mine.shape[0]
    return pl.pallas_call(
        merge_kernel,
        out_shape=[jax.ShapeDtypeStruct(mine.shape[1:], mine.dtype)] * chips,
        in_specs=[VMEM] * 3,
        out_specs=[VMEM] * chips,
        compiler_params=params(),
        cost_estimate=cost(0.3),
        name="merge",
    )(owners, mine, other)


def lagged(row, ahead):
    copies = jnp.broadcast_to(row, (8, row.shape[1]))
    return pltpu.roll(copies, row.shape[1] - 7 - ahead, 1, stride=1, stride_axis=0)


def segment(me, other, parity, pair, beside, far, default):
    chip, core = me // 2, me % 2
    chips = 2 * len(far) + 2
    step = jnp.bitwise_xor(chip, other)
    value = default[...]
    value = jnp.where(jnp.logical_and(step == 1, core == parity), beside[...], value)
    value = jnp.where(step == 0, pair[parity], value)
    for number, array in enumerate(far):
        value = jnp.where(step == chips - 1 - 2 * number - core, array[parity], value)
    return value


def pair_kernel(own, partner, out):
    core = lax.axis_index("tm") % 2
    out[core] = own[...]
    out[1 - core] = partner[...]


def pair_waves(own, partner):
    return pl.pallas_call(
        pair_kernel,
        out_shape=jax.ShapeDtypeStruct((2,) + own.shape, own.dtype),
        in_specs=[VMEM] * 2,
        out_specs=VMEM,
        compiler_params=params(),
        cost_estimate=cost(0.05),
        name="pair_waves",
    )(own, partner)


def choose_kernel(pair, beside, *rest):
    far, out = rest[:-1], rest[-1]
    near = out.shape[0] - 1
    me = lax.axis_index("tm")
    chip, core = me // 2, me % 2
    for entry in range(near):
        number, parity = divmod(entry, 2)
        step = jnp.bitwise_xor(chip, near * (1 - core) + 2 * number) // 2
        value = beside[...]
        for place, array in enumerate(far):
            value = jnp.where(step == near - 1 - place, array[parity], value)
        out[entry] = value
    out[near] = segment(me, near, 0, pair, beside, far, beside)


def choose_waves(pair, beside, far):
    return pl.pallas_call(
        choose_kernel,
        out_shape=jax.ShapeDtypeStruct((len(far) + 2,) + beside.shape, beside.dtype),
        in_specs=[VMEM] * (2 + len(far)),
        out_specs=VMEM,
        compiler_params=params(),
        cost_estimate=cost(0.05),
        name="choose_waves",
    )(pair, beside, *far)


def own_kernel(owners, *refs):
    pieces, out = refs[:-1], refs[-1]
    chip = lax.axis_index("tm") // 2
    owner = jnp.where(chip < len(pieces) // 2, owners[0, 0], owners[1, 0])
    source = jnp.bitwise_xor(owner // 2, chip)
    value = pieces[0][...]
    for number, piece in enumerate(pieces[1:], 1):
        value = jnp.where(source == number, piece[...], value)
    out[...] = value


def choose_piece(owners, pieces):
    return pl.pallas_call(
        own_kernel,
        out_shape=jax.ShapeDtypeStruct(pieces[0].shape, pieces[0].dtype),
        in_specs=[VMEM] * (1 + len(pieces)),
        out_specs=VMEM,
        compiler_params=params(),
        cost_estimate=cost(0.3),
        name="choose_piece",
    )(owners, *pieces)


def waves_kernel(channels, tlen, unroll, swapped, pair, beside, *rest):
    far = rest[:-3]
    left_a, inverse, padded = rest[-3:]
    samples = beside.shape[1]
    near = swapped.shape[0] - 1
    length = 2 * near * samples
    count = padded.shape[1] // LANES
    me = lax.axis_index("tm")
    core = me % 2
    padded[...] = jnp.zeros_like(padded)
    for index in range(2 * near):
        entry, parity = divmod(index, 2)
        given = swapped.at[2 * (entry // 2) + parity]
        wave = segment(me, near * core + entry, parity, pair, beside, far, given)
        padded[0:channels, samples * index : samples * (index + 1)] = wave.astype(jnp.float32)
    rim = segment(me, near * core + near, 0, pair, beside, far, swapped.at[near])
    rim = rim[:, 0 : padded.shape[1] - length].astype(jnp.float32)
    padded[0:channels, length:] = jnp.where(core == 0, rim, 0.0)

    rows = 32 * count
    values = [padded[:, LANES * tile : LANES * (tile + 1)] for tile in range(count)]
    values = jnp.concatenate(values + [jnp.zeros((32, LANES), jnp.float32)], axis=0)
    square = values * values
    high = square.astype(jnp.bfloat16)
    low = (square - high.astype(jnp.float32)).astype(jnp.bfloat16)
    values = values.astype(jnp.bfloat16)
    lag = lax.broadcasted_iota(jnp.int32, (2 * LANES, LANES), 0)
    lag = lag - lax.broadcasted_iota(jnp.int32, (2 * LANES, LANES), 1)
    band = jnp.where(jnp.logical_and(lag >= 0, lag < tlen), 1.0, 0.0).astype(jnp.bfloat16)

    def windows(array):
        both = jnp.concatenate([array[0:rows], array[32 : rows + 32]], axis=1)
        return jnp.dot(both, band, preferred_element_type=jnp.float32)

    first_sum = windows(values)
    second_sum = windows(high) + windows(low)
    variance = (second_sum * tlen - first_sum * first_sum) * (1.0 / tlen**2)
    scale = lax.rsqrt(variance + EPSILON)
    for tile in range(length // LANES):
        part = scale[32 * tile : 32 * (tile + 1)]
        after = scale[32 * (tile + 1) : 32 * (tile + 2)]
        inverse[2 * tile] = part
        lane = lax.broadcasted_iota(jnp.int32, part.shape, 1)
        both = jnp.where(lane < STRIDE, after, part)
        inverse[2 * tile + 1] = pltpu.roll(both, LANES - STRIDE, 1)

    def interleaved(row, tiles):
        even, odd = lagged(row, 0), lagged(row, STRIDE)
        parts = []
        for tile in range(tiles):
            lanes = slice(LANES * tile, LANES * (tile + 1))
            parts += [even[:, lanes], odd[:, lanes]]
        return jnp.concatenate(parts, axis=0)

    @pl.loop(0, channels // unroll)
    def _(step):
        for item in range(unroll):
            channel = step * unroll + item
            value = interleaved(padded[pl.ds(channel, 1), :], length // LANES + 1)
            left_a[channel] = value.astype(jnp.bfloat16)


def prepare_waves(tlen, swapped, pair, beside, far):
    channels, samples = beside.shape
    length = 2 * (swapped.shape[0] - 1) * samples
    rows = length // OFFSETS
    unroll = max(step for step in (1, 2, 3) if channels % step == 0)
    return pl.pallas_call(
        functools.partial(waves_kernel, channels, tlen, unroll),
        out_shape=[
            jax.ShapeDtypeStruct((channels, rows + 16, LANES), jnp.bfloat16),
            jax.ShapeDtypeStruct((length // STRIDE, 32, LANES), jnp.float32),
        ],
        in_specs=[VMEM] * (3 + len(far)),
        out_specs=[VMEM, VMEM],
        scratch_shapes=[
            pltpu.VMEM((32, length + 2 * LANES), jnp.float32),
        ],
        compiler_params=params(),
        cost_estimate=cost(0.05),
        name="prepare_waves",
    )(swapped, pair, beside, *far)


def main_kernel(side, tlen, group, piece, left_a, inverse, *rest):
    outs = rest[:-5]
    if side:
        before, outs = outs[0], outs[1:]
    bank, expand, weight_a, reach, total = rest[-5:]
    core = lax.axis_index("tm") % 2
    channels = left_a.shape[0]
    rows = left_a.shape[1] - 16
    half = channels // 2
    base = half * jnp.where(core == side, 0, 1)
    slots = LANES // group
    banks = (half + 1) // slots
    offset_count = LANES // group
    tile_count = OFFSETS // offset_count
    top = 112 + 8 * (7 + offset_count - 1)
    top = top + top % 16

    lag = lax.broadcasted_iota(jnp.int32, (LANES, LANES), 0)
    target = lax.broadcasted_iota(jnp.int32, (LANES, LANES), 1)
    lane = lax.broadcasted_iota(jnp.int32, (1, LANES), 1)
    used = lag < tlen
    ahead = lane // group
    for slot in range(slots):
        chosen = jnp.where(lag == target % group + slot * group, 1.0, 0.0)
        expand[:, slot * LANES : (slot + 1) * LANES] = chosen.astype(jnp.bfloat16)
    turned = []
    for index in range(banks):
        count = min(slots, max(TILES - slots * index, 0))
        values = jnp.zeros((LANES, LANES), jnp.float32)
        if count:
            values = piece[slots * index : slots * index + count].astype(jnp.float32)
            values = values.reshape(count * group, LANES)
            if count < slots:
                gap = jnp.zeros((LANES - count * group, LANES), jnp.float32)
                values = jnp.concatenate([values, gap], axis=0)
            values = values.T
        turned.append(values)
    codes = [values[125:126, :] for values in turned]
    heads = [jnp.where(used, values, 0.0) for values in turned]
    for extra in range(half - TILES):
        place, slot = divmod(TILES + extra, slots)
        mask = ahead == slot
        code = pltpu.roll(turned[0][126:127, :], (slot - extra) * group % LANES, 1)
        codes[place] = jnp.where(mask, code, codes[place])
        for quarter in range(4):
            source, lanes = divmod(4 * extra + quarter, slots)
            values = turned[source][96:128]
            sample = lag[96:128]
            inside = jnp.logical_and(sample >= tlen, sample < tlen + QUARTER)
            values = jnp.where(inside, values, 0.0)
            values = pltpu.roll(values, (slot - lanes) * group % LANES, 1)
            start = QUARTER * quarter - (tlen - 96)
            values = jnp.concatenate([values, jnp.zeros((8, LANES), jnp.float32)], axis=0)
            values = pltpu.roll(values, start % 8, 0)
            start -= start % 8
            if start < 0:
                values, start = values[8:], 0
            below = LANES - start - values.shape[0]
            if start:
                values = jnp.concatenate([jnp.zeros((start, LANES), jnp.float32), values], axis=0)
            if below > 0:
                values = jnp.concatenate([values, jnp.zeros((below, LANES), jnp.float32)], axis=0)
            heads[place] = heads[place] + jnp.where(mask, values[0:LANES], 0.0)
    for index, (values, code) in enumerate(zip(heads, codes)):
        code = jnp.where(slots * index + ahead < half, code, 0.0)
        deviate = jnp.where(used, values * tlen - jnp.sum(values, axis=0, keepdims=True), 0.0)
        square = jnp.sum(deviate * deviate, axis=0, keepdims=True) * (1.0 / tlen**3)
        unit = deviate / (jnp.sqrt(square + EPSILON) * tlen**2)
        unit = unit.astype(jnp.bfloat16).astype(jnp.float32)
        unit = jnp.where(code > 0, unit, 0.0)
        shift = code.astype(jnp.int32) - 1
        for bit in (1, 2, 4):
            unit = jnp.where(jnp.bitwise_and(shift, bit) > 0, pltpu.roll(unit, bit, 0), unit)
        unit = jnp.where(lag == 112, code, unit)
        bank[index] = unit.astype(jnp.bfloat16)

    def build(number):
        wide = jnp.dot(bank[number], expand[...], preferred_element_type=jnp.float32)
        for slot in range(slots):
            spreaded = wide[:, slot * LANES : (slot + 1) * LANES]
            code = spreaded[112:113, :].astype(jnp.int32)
            shift = code - 1
            moves = shift // 8 + ahead
            taps = spreaded[0:112, :]
            for bit in (1, 2, 4, 8):
                gap = jnp.zeros((8 * bit, LANES), jnp.float32)
                taps = jnp.where(
                    jnp.bitwise_and(moves, bit) > 0,
                    jnp.concatenate([gap, taps], axis=0),
                    jnp.concatenate([taps, gap], axis=0),
                )[0:top]
            taps = taps.astype(jnp.bfloat16)
            item = number * slots + slot
            reach[item] = jnp.maximum(shift, 0) + 8 * ahead + 7 - lag[0:8]
            for tile in range(tile_count):
                skip = 8 * offset_count * tile
                lanes = slice(LANES * tile, LANES * (tile + 1))
                if skip:
                    weight_a[item, 0:skip, lanes] = jnp.zeros((skip, LANES), jnp.bfloat16)
                weight_a[item, skip : skip + top, lanes] = taps
                rest = DEPTH - top - skip
                if rest:
                    weight_a[item, skip + top :, lanes] = jnp.zeros((rest, LANES), jnp.bfloat16)

    def products(item):
        both = [left_a[base + item, 0:rows, :], left_a[base + item, 16 : rows + 16, :]]
        corr = jnp.dot(
            jnp.concatenate(both, axis=1), weight_a[item], preferred_element_type=jnp.float32
        )
        columns = []
        for tile in range(tile_count):
            place = reach[item] + 8 * offset_count * tile
            parts = []
            for step in range(rows // 8):
                window = inverse[step, pl.ds(base + item, 1), :]
                window = jnp.broadcast_to(window, (8, LANES))
                parts.append(jnp.take_along_axis(window, place, axis=1, mode="promise_in_bounds"))
            columns.append(jnp.concatenate(parts, axis=0))
        return corr * jnp.concatenate(columns, axis=1)

    def apply(number, count):
        for item in range(number * slots, number * slots + count, 2):
            value = products(item)
            if item + 1 < number * slots + count:
                value = value + products(item + 1)
            if item:
                value = value + total[...]
            elif side:
                value = value + before[...]
            total[...] = value

    build(0)

    for number in range(1, banks):
        apply(number - 1, slots)
        build(number)

    apply(banks - 1, half - slots * (banks - 1))

    if not side:
        outs[0][...] = total[...]
        return
    rows_out = outs[0].shape[0]
    station = lax.axis_index("sta") % len(outs)
    for step, out in enumerate(outs):
        part = jnp.bitwise_xor(station, step)
        out[...] = total[pl.ds(pl.multiple_of(part * rows_out, rows_out), rows_out), :].astype(
            jnp.bfloat16
        )


def correlate(side, tlen, group, count, piece, left_a, inverse, *before):
    channels = left_a.shape[0]
    rows = left_a.shape[1] - 16
    width = OFFSETS * group
    half = channels // 2
    if side:
        out = [jax.ShapeDtypeStruct((rows // count, width), jnp.bfloat16)] * count
    else:
        out = [jax.ShapeDtypeStruct((rows, width), jnp.float32)]
    return pl.pallas_call(
        functools.partial(main_kernel, side, tlen, group),
        out_shape=out,
        in_specs=[VMEM] * (3 + len(before)),
        out_specs=[VMEM] * len(out),
        scratch_shapes=[
            pltpu.VMEM(((half + 1) * group // LANES, LANES, LANES), jnp.bfloat16),
            pltpu.VMEM((LANES, LANES // group * LANES), jnp.bfloat16),
            pltpu.VMEM((half + 1, DEPTH, width), jnp.bfloat16),
            pltpu.VMEM((half + 1, 8, LANES), jnp.int32),
            pltpu.VMEM((rows, width), jnp.float32),
        ],
        compiler_params=params(),
        cost_estimate=cost(3),
        name="correlate_" + ("second" if side else "first"),
    )(piece, left_a, inverse, *before)


def add_kernel(*refs):
    parts, keep, send = refs[:-2], refs[-2], refs[-1]
    rows = keep.shape[0]
    core = lax.axis_index("tm") % 2
    for out, which in ((keep, core), (send, 1 - core)):
        place = pl.ds(pl.multiple_of(which * rows, rows), rows)
        value = parts[0][place, :].astype(jnp.float32)
        for part in parts[1:]:
            value = value + part[place, :].astype(jnp.float32)
        out[...] = value


def add(parts):
    rows, width = parts[0].shape
    out = jax.ShapeDtypeStruct((rows // 2, width), jnp.float32)
    return pl.pallas_call(
        add_kernel,
        out_shape=[out, out],
        in_specs=[VMEM] * len(parts),
        out_specs=[VMEM, VMEM],
        compiler_params=params(),
        cost_estimate=cost(0.5),
        name="add",
    )(*parts)


def finish_kernel(group, ours, received, out):
    samples = out.shape[1]
    rows = ours.shape[0]
    value = ours[...] + received[...]
    high = value.astype(jnp.bfloat16).astype(jnp.float32)
    both = jnp.concatenate([high, value - high], axis=0).T.astype(jnp.bfloat16)
    row = lax.broadcasted_iota(jnp.int32, (2 * rows, samples), 0) % rows
    lane = lax.broadcasted_iota(jnp.int32, (2 * rows, samples), 1)
    place = jnp.logical_and(lane // STRIDE == row // 8, lane % 8 == 7 - row % 8)
    place = jnp.where(place, 1.0, 0.0).astype(jnp.bfloat16)
    wide = jnp.dot(both, place, preferred_element_type=jnp.float32)
    lane = lax.broadcasted_iota(jnp.int32, (group, samples), 1) // 8 % OFFSETS
    result = jnp.zeros((group, samples), jnp.float32)
    for offset in range(OFFSETS):
        result = jnp.where(lane == offset, wide[offset * group : (offset + 1) * group], result)
    out[...] = result


def finish(group, samples, ours, received):
    return pl.pallas_call(
        functools.partial(finish_kernel, group),
        out_shape=jax.ShapeDtypeStruct((group, samples), jnp.float32),
        in_specs=[VMEM, VMEM],
        out_specs=VMEM,
        compiler_params=params(),
        cost_estimate=cost(1),
        name="finish",
    )(ours, received)


def shards(waveforms, templates, available, moveout, bank_blocks):
    channels, samples = waveforms.shape
    blocks, events, _, tlen = templates.shape
    count_tm = lax.axis_size("tm")
    count_sta = lax.axis_size("sta")
    chips = count_tm // 2
    near = chips // 2
    group = 2 * events // chips

    def swap(array):
        return lax.ppermute(array, "tm", [(i, i ^ 1) for i in range(count_tm)])

    def across(array, step):
        return lax.ppermute(array, "tm", [(i, i ^ (2 * step)) for i in range(count_tm)])

    partner = swap(waveforms)
    mine, theirs, owners = pack(
        chips,
        group,
        bank_blocks,
        jnp.transpose(templates, (0, 2, 1, 3)),
        jnp.transpose(available, (2, 0, 1)),
        jnp.transpose(moveout, (2, 0, 1)),
    )
    theirs, partner = lax.optimization_barrier((theirs, partner))
    other = swap(theirs)
    pair = pair_waves(waveforms, partner)
    far = []
    for number in range(near - 1):
        steps = (chips - 1 - 2 * number, chips - 2 - 2 * number)
        route = [(2 * z + c, 2 * (z ^ steps[c]) + c) for z in range(chips) for c in range(2)]
        far.append(lax.ppermute(pair, "tm", route))
    beside = across(waveforms, 1)
    merged = list(merge(owners, mine, other))
    pieces = [across(merged[step], step) for step in reversed(range(1, chips))]
    pieces = [merged[0]] + pieces[::-1]
    swapped = swap(choose_waves(pair, beside, far))
    left_a, inverse = prepare_waves(tlen, swapped, pair, beside, far)

    left_a, inverse, *pieces = lax.optimization_barrier((left_a, inverse, *pieces[::-1]))
    pieces = pieces[::-1]
    first = choose_piece(owners, pieces)
    second = swap(first)
    total = correlate(0, tlen, group, near, first, left_a, inverse)
    parts = correlate(1, tlen, group, near, second, left_a, inverse, *total)
    gathered = []
    for step in range(near):
        route = []
        for d in range(count_tm):
            for s in range(count_sta):
                dest = near * (d % 2) + (s % near ^ step)
                route.append((d * count_sta + s, (2 * dest + s // near) * count_sta + d // 2))
        gathered.append(lax.ppermute(parts[step], ("tm", "sta"), route))
    ours, send = add(gathered)
    return finish(group, samples, ours, swap(send))


def solution(mesh):
    in_specs = (
        P("sta", "tm"),
        P("tm", None, "sta", None),
        P("tm", None, "sta"),
        P("tm", None, "sta"),
        P(),
    )
    out_specs = P("sta", "tm")
    return jax.shard_map(shards, mesh=mesh, in_specs=in_specs, out_specs=out_specs, check_vma=False)
```

```python
import functools

import jax
import jax.numpy as jnp
from jax import lax
from jax.experimental import pallas as pl
from jax.experimental.pallas import tpu as pltpu
from jax.sharding import PartitionSpec as P

EPSILON = 1e-06
LANES = 128
OFFSETS = 8
TILES = 12
QUARTER = 25
STRIDE = 64
DEPTH = 256
VMEM_LIMIT = 28 * 1024 * 1024

VMEM = pl.BlockSpec(memory_space=pltpu.VMEM)
ANY = pl.BlockSpec(memory_space=pl.ANY)


def params():
    return pltpu.CompilerParams(vmem_limit_bytes=VMEM_LIMIT)


def cost(micros):
    return pl.CostEstimate(
        flops=int(micros * 1e9), bytes_accessed=int(micros * 1e6), transcendentals=0
    )


def pack_kernel(bank_blocks, templates, available, moveout, mine, theirs, owners, chosen, raw, usable, shifts, square, sems):
    blocks, channels, events, tlen = templates.shape
    chips, _, group, _ = mine.shape
    half = channels // 2
    me = lax.axis_index("tm") % 2
    fetch = [
        pltpu.make_async_copy(source, target, sems.at[index])
        for index, (source, target) in enumerate(
            ((bank_blocks, chosen), (available, usable), (moveout, shifts))
        )
    ]
    for side in (1, 0):
        first = half * jnp.where(me == side, 0, 1)
        for block in range(blocks):
            place = (block, pl.ds(first, half))
            number = 3 + blocks * (1 - side) + block
            fetch.append(
                pltpu.make_async_copy(templates.at[place], raw.at[place], sems.at[number])
            )
    for copy in fetch:
        copy.start()
    mine[...] = jnp.zeros_like(mine)
    theirs[...] = jnp.zeros_like(theirs)
    square[...] = jnp.zeros_like(square)
    for copy in fetch[:3]:
        copy.wait()
    slots = [chosen[which] % blocks for which in range(2)]
    row = lax.broadcasted_iota(jnp.int32, owners.shape, 0)
    owners[...] = jnp.where(row == 0, chosen[0] // blocks, chosen[1] // blocks)
    flags = jnp.where(usable[...] > 0, shifts[...] + 1, 0).astype(jnp.float32)
    codes = []
    for which in range(2):
        code = flags[:, 0, :]
        for block in range(1, blocks):
            code = jnp.where(slots[which] == block, flags[:, block, :], code)
        square[0:channels, 0:events] = code
        turned = square[...].T
        later = pltpu.roll(turned, LANES - half, 1)
        codes.append([jnp.where(me == core, turned, later) for core in range(2)])
    for side, out in ((1, theirs), (0, mine)):
        for block in range(blocks):
            fetch[3 + blocks * (1 - side) + block].wait()
        for which in range(2):
            first = half * jnp.where(me == side, 0, 1)
            code = codes[which][side].astype(jnp.bfloat16)
            for tile in range(TILES):
                extra = TILES + tile // 4
                start = QUARTER * (tile % 4)
                for index in range(events // group):
                    chip = which * (events // group) + index
                    rows = slice(index * group, (index + 1) * group)
                    out[chip, tile, :, 0:tlen] = raw[slots[which], first + tile, rows, :]
                    out[chip, tile, :, tlen : tlen + QUARTER] = raw[
                        slots[which], first + extra, rows, start : start + QUARTER
                    ]
                    out[chip, tile, :, 125:126] = code[rows, tile : tile + 1]
                    if tile < half - TILES:
                        beyond = TILES + tile
                        out[chip, tile, :, 126:127] = code[rows, beyond : beyond + 1]


def pack(chips, group, bank_blocks, templates, available, moveout):
    shape = (chips, TILES, group, LANES)
    held = [
        pltpu.with_memory_space_constraint(array, pltpu.HBM)
        for array in (bank_blocks, templates, available, moveout)
    ]
    return pl.pallas_call(
        pack_kernel,
        out_shape=[jax.ShapeDtypeStruct(shape, jnp.bfloat16)] * 2
        + [jax.ShapeDtypeStruct((8, LANES), jnp.int32)],
        in_specs=[ANY] * 4,
        out_specs=[VMEM] * 3,
        scratch_shapes=[
            pltpu.SMEM(bank_blocks.shape, jnp.int32),
            pltpu.VMEM(templates.shape, jnp.bfloat16),
            pltpu.VMEM(available.shape, jnp.int32),
            pltpu.VMEM(moveout.shape, jnp.int32),
            pltpu.VMEM((LANES, LANES), jnp.float32),
            pltpu.SemaphoreType.DMA((3 + 2 * templates.shape[0],)),
        ],
        compiler_params=params(),
        cost_estimate=cost(2),
        name="pack",
    )(*held)


def merge_kernel(owners, mine, other, *outs):
    chips = len(outs)
    me = lax.axis_index("tm")
    for step, out in enumerate(outs):
        dest = jnp.bitwise_xor(me // 2, step)
        owner = jnp.where(dest < chips // 2, owners[0, 0], owners[1, 0])
        here = owner % 2 == me % 2

        @pl.when(here)
        def _():
            out[...] = mine[dest]

        @pl.when(jnp.logical_not(here))
        def _():
            out[...] = other[dest]


def merge(owners, mine, other):
    chips = mine.shape[0]
    return pl.pallas_call(
        merge_kernel,
        out_shape=[jax.ShapeDtypeStruct(mine.shape[1:], mine.dtype)] * chips,
        in_specs=[VMEM] * 3,
        out_specs=[VMEM] * chips,
        compiler_params=params(),
        cost_estimate=cost(0.3),
        name="merge",
    )(owners, mine, other)


def lagged(row, ahead):
    copies = jnp.broadcast_to(row, (8, row.shape[1]))
    return pltpu.roll(copies, row.shape[1] - 7 - ahead, 1, stride=1, stride_axis=0)


def segment(me, other, parity, pair, beside, far, default):
    chip, core = me // 2, me % 2
    chips = 2 * len(far) + 2
    step = jnp.bitwise_xor(chip, other)
    value = default[...]
    value = jnp.where(jnp.logical_and(step == 1, core == parity), beside[...], value)
    value = jnp.where(step == 0, pair[parity], value)
    for number, array in enumerate(far):
        value = jnp.where(step == chips - 1 - 2 * number - core, array[parity], value)
    return value


def pair_kernel(own, partner, out):
    core = lax.axis_index("tm") % 2
    out[core] = own[...]
    out[1 - core] = partner[...]


def pair_waves(own, partner):
    return pl.pallas_call(
        pair_kernel,
        out_shape=jax.ShapeDtypeStruct((2,) + own.shape, own.dtype),
        in_specs=[VMEM] * 2,
        out_specs=VMEM,
        compiler_params=params(),
        cost_estimate=cost(0.05),
        name="pair_waves",
    )(own, partner)


def choose_kernel(pair, beside, *rest):
    far, out = rest[:-1], rest[-1]
    near = out.shape[0] - 1
    me = lax.axis_index("tm")
    chip, core = me // 2, me % 2
    for entry in range(near):
        number, parity = divmod(entry, 2)
        step = jnp.bitwise_xor(chip, near * (1 - core) + 2 * number) // 2
        value = beside[...]
        for place, array in enumerate(far):
            value = jnp.where(step == near - 1 - place, array[parity], value)
        out[entry] = value
    out[near] = segment(me, near, 0, pair, beside, far, beside)


def choose_waves(pair, beside, far):
    return pl.pallas_call(
        choose_kernel,
        out_shape=jax.ShapeDtypeStruct((len(far) + 2,) + beside.shape, beside.dtype),
        in_specs=[VMEM] * (2 + len(far)),
        out_specs=VMEM,
        compiler_params=params(),
        cost_estimate=cost(0.05),
        name="choose_waves",
    )(pair, beside, *far)


def own_kernel(owners, *refs):
    pieces, out = refs[:-1], refs[-1]
    chip = lax.axis_index("tm") // 2
    owner = jnp.where(chip < len(pieces) // 2, owners[0, 0], owners[1, 0])
    source = jnp.bitwise_xor(owner // 2, chip)
    value = pieces[0][...]
    for number, piece in enumerate(pieces[1:], 1):
        value = jnp.where(source == number, piece[...], value)
    out[...] = value


def choose_piece(owners, pieces):
    return pl.pallas_call(
        own_kernel,
        out_shape=jax.ShapeDtypeStruct(pieces[0].shape, pieces[0].dtype),
        in_specs=[VMEM] * (1 + len(pieces)),
        out_specs=VMEM,
        compiler_params=params(),
        cost_estimate=cost(0.3),
        name="choose_piece",
    )(owners, *pieces)


def waves_kernel(channels, tlen, unroll, swapped, pair, beside, *rest):
    far = rest[:-3]
    left_a, inverse, padded = rest[-3:]
    samples = beside.shape[1]
    near = swapped.shape[0] - 1
    length = 2 * near * samples
    count = padded.shape[1] // LANES
    me = lax.axis_index("tm")
    core = me % 2
    padded[...] = jnp.zeros_like(padded)
    for index in range(2 * near):
        entry, parity = divmod(index, 2)
        given = swapped.at[2 * (entry // 2) + parity]
        wave = segment(me, near * core + entry, parity, pair, beside, far, given)
        padded[0:channels, samples * index : samples * (index + 1)] = wave.astype(jnp.float32)
    rim = segment(me, near * core + near, 0, pair, beside, far, swapped.at[near])
    rim = rim[:, 0 : padded.shape[1] - length].astype(jnp.float32)
    padded[0:channels, length:] = jnp.where(core == 0, rim, 0.0)

    rows = 32 * count
    values = [padded[:, LANES * tile : LANES * (tile + 1)] for tile in range(count)]
    values = jnp.concatenate(values + [jnp.zeros((32, LANES), jnp.float32)], axis=0)
    square = values * values
    high = square.astype(jnp.bfloat16)
    low = (square - high.astype(jnp.float32)).astype(jnp.bfloat16)
    values = values.astype(jnp.bfloat16)
    lag = lax.broadcasted_iota(jnp.int32, (2 * LANES, LANES), 0)
    lag = lag - lax.broadcasted_iota(jnp.int32, (2 * LANES, LANES), 1)
    band = jnp.where(jnp.logical_and(lag >= 0, lag < tlen), 1.0, 0.0).astype(jnp.bfloat16)

    def windows(array):
        both = jnp.concatenate([array[0:rows], array[32 : rows + 32]], axis=1)
        return jnp.dot(both, band, preferred_element_type=jnp.float32)

    first_sum = windows(values)
    second_sum = windows(high) + windows(low)
    variance = (second_sum * tlen - first_sum * first_sum) * (1.0 / tlen**2)
    scale = lax.rsqrt(variance + EPSILON)
    for tile in range(length // LANES):
        part = scale[32 * tile : 32 * (tile + 1)]
        after = scale[32 * (tile + 1) : 32 * (tile + 2)]
        inverse[2 * tile] = part
        lane = lax.broadcasted_iota(jnp.int32, part.shape, 1)
        both = jnp.where(lane < STRIDE, after, part)
        inverse[2 * tile + 1] = pltpu.roll(both, LANES - STRIDE, 1)

    def interleaved(row, tiles):
        even, odd = lagged(row, 0), lagged(row, STRIDE)
        parts = []
        for tile in range(tiles):
            lanes = slice(LANES * tile, LANES * (tile + 1))
            parts += [even[:, lanes], odd[:, lanes]]
        return jnp.concatenate(parts, axis=0)

    @pl.loop(0, channels // unroll)
    def _(step):
        for item in range(unroll):
            channel = step * unroll + item
            value = interleaved(padded[pl.ds(channel, 1), :], length // LANES + 1)
            left_a[channel] = value.astype(jnp.bfloat16)


def prepare_waves(tlen, swapped, pair, beside, far):
    channels, samples = beside.shape
    length = 2 * (swapped.shape[0] - 1) * samples
    rows = length // OFFSETS
    unroll = max(step for step in (1, 2, 3) if channels % step == 0)
    return pl.pallas_call(
        functools.partial(waves_kernel, channels, tlen, unroll),
        out_shape=[
            jax.ShapeDtypeStruct((channels, rows + 16, LANES), jnp.bfloat16),
            jax.ShapeDtypeStruct((length // STRIDE, 32, LANES), jnp.float32),
        ],
        in_specs=[VMEM] * (3 + len(far)),
        out_specs=[VMEM, VMEM],
        scratch_shapes=[
            pltpu.VMEM((32, length + 2 * LANES), jnp.float32),
        ],
        compiler_params=params(),
        cost_estimate=cost(0.05),
        name="prepare_waves",
    )(swapped, pair, beside, *far)


def main_kernel(side, tlen, group, piece, left_a, inverse, *rest):
    outs = rest[:-5]
    if side:
        before, outs = outs[0], outs[1:]
    bank, expand, weight_a, reach, total = rest[-5:]
    core = lax.axis_index("tm") % 2
    channels = left_a.shape[0]
    rows = left_a.shape[1] - 16
    half = channels // 2
    base = half * jnp.where(core == side, 0, 1)
    slots = LANES // group
    banks = (half + 1) // slots
    offset_count = LANES // group
    tile_count = OFFSETS // offset_count
    top = 112 + 8 * (7 + offset_count - 1)
    top = top + top % 16

    lag = lax.broadcasted_iota(jnp.int32, (LANES, LANES), 0)
    target = lax.broadcasted_iota(jnp.int32, (LANES, LANES), 1)
    lane = lax.broadcasted_iota(jnp.int32, (1, LANES), 1)
    used = lag < tlen
    ahead = lane // group
    for slot in range(slots):
        chosen = jnp.where(lag == target % group + slot * group, 1.0, 0.0)
        expand[:, slot * LANES : (slot + 1) * LANES] = chosen.astype(jnp.bfloat16)
    turned = []
    for index in range(banks):
        count = min(slots, max(TILES - slots * index, 0))
        values = jnp.zeros((LANES, LANES), jnp.float32)
        if count:
            values = piece[slots * index : slots * index + count].astype(jnp.float32)
            values = values.reshape(count * group, LANES)
            if count < slots:
                gap = jnp.zeros((LANES - count * group, LANES), jnp.float32)
                values = jnp.concatenate([values, gap], axis=0)
            values = values.T
        turned.append(values)
    codes = [values[125:126, :] for values in turned]
    heads = [jnp.where(used, values, 0.0) for values in turned]
    for extra in range(half - TILES):
        place, slot = divmod(TILES + extra, slots)
        mask = ahead == slot
        code = pltpu.roll(turned[0][126:127, :], (slot - extra) * group % LANES, 1)
        codes[place] = jnp.where(mask, code, codes[place])
        for quarter in range(4):
            source, lanes = divmod(4 * extra + quarter, slots)
            values = turned[source][96:128]
            sample = lag[96:128]
            inside = jnp.logical_and(sample >= tlen, sample < tlen + QUARTER)
            values = jnp.where(inside, values, 0.0)
            values = pltpu.roll(values, (slot - lanes) * group % LANES, 1)
            start = QUARTER * quarter - (tlen - 96)
            values = jnp.concatenate([values, jnp.zeros((8, LANES), jnp.float32)], axis=0)
            values = pltpu.roll(values, start % 8, 0)
            start -= start % 8
            if start < 0:
                values, start = values[8:], 0
            below = LANES - start - values.shape[0]
            if start:
                values = jnp.concatenate([jnp.zeros((start, LANES), jnp.float32), values], axis=0)
            if below > 0:
                values = jnp.concatenate([values, jnp.zeros((below, LANES), jnp.float32)], axis=0)
            heads[place] = heads[place] + jnp.where(mask, values[0:LANES], 0.0)
    for index, (values, code) in enumerate(zip(heads, codes)):
        code = jnp.where(slots * index + ahead < half, code, 0.0)
        deviate = jnp.where(used, values * tlen - jnp.sum(values, axis=0, keepdims=True), 0.0)
        square = jnp.sum(deviate * deviate, axis=0, keepdims=True) * (1.0 / tlen**3)
        unit = deviate / (jnp.sqrt(square + EPSILON) * tlen**2)
        unit = unit.astype(jnp.bfloat16).astype(jnp.float32)
        unit = jnp.where(code > 0, unit, 0.0)
        shift = code.astype(jnp.int32) - 1
        for bit in (1, 2, 4):
            unit = jnp.where(jnp.bitwise_and(shift, bit) > 0, pltpu.roll(unit, bit, 0), unit)
        unit = jnp.where(lag == 112, code, unit)
        bank[index] = unit.astype(jnp.bfloat16)

    def build(number):
        wide = jnp.dot(bank[number], expand[...], preferred_element_type=jnp.float32)
        for slot in range(slots):
            spreaded = wide[:, slot * LANES : (slot + 1) * LANES]
            code = spreaded[112:113, :].astype(jnp.int32)
            shift = code - 1
            moves = shift // 8 + ahead
            taps = spreaded[0:112, :]
            for bit in (1, 2, 4, 8):
                gap = jnp.zeros((8 * bit, LANES), jnp.float32)
                taps = jnp.where(
                    jnp.bitwise_and(moves, bit) > 0,
                    jnp.concatenate([gap, taps], axis=0),
                    jnp.concatenate([taps, gap], axis=0),
                )[0:top]
            taps = taps.astype(jnp.bfloat16)
            item = number * slots + slot
            reach[item] = jnp.maximum(shift, 0) + 8 * ahead + 7 - lag[0:8]
            for tile in range(tile_count):
                skip = 8 * offset_count * tile
                lanes = slice(LANES * tile, LANES * (tile + 1))
                if skip:
                    weight_a[item, 0:skip, lanes] = jnp.zeros((skip, LANES), jnp.bfloat16)
                weight_a[item, skip : skip + top, lanes] = taps
                rest = DEPTH - top - skip
                if rest:
                    weight_a[item, skip + top :, lanes] = jnp.zeros((rest, LANES), jnp.bfloat16)

    def products(item):
        both = [left_a[base + item, 0:rows, :], left_a[base + item, 16 : rows + 16, :]]
        corr = jnp.dot(
            jnp.concatenate(both, axis=1), weight_a[item], preferred_element_type=jnp.float32
        )
        columns = []
        for tile in range(tile_count):
            place = reach[item] + 8 * offset_count * tile
            parts = []
            for step in range(rows // 8):
                window = inverse[step, pl.ds(base + item, 1), :]
                window = jnp.broadcast_to(window, (8, LANES))
                parts.append(jnp.take_along_axis(window, place, axis=1, mode="promise_in_bounds"))
            columns.append(jnp.concatenate(parts, axis=0))
        return corr * jnp.concatenate(columns, axis=1)

    def apply(number, count):
        for item in range(number * slots, number * slots + count, 2):
            value = products(item)
            if item + 1 < number * slots + count:
                value = value + products(item + 1)
            if item:
                value = value + total[...]
            elif side:
                value = value + before[...]
            total[...] = value

    build(0)

    for number in range(1, banks):
        apply(number - 1, slots)
        build(number)

    apply(banks - 1, half - slots * (banks - 1))

    if not side:
        outs[0][...] = total[...]
        return
    rows_out = outs[0].shape[0]
    station = lax.axis_index("sta") % len(outs)
    for step, out in enumerate(outs):
        part = jnp.bitwise_xor(station, step)
        out[...] = total[pl.ds(pl.multiple_of(part * rows_out, rows_out), rows_out), :].astype(
            jnp.bfloat16
        )


def correlate(side, tlen, group, count, piece, left_a, inverse, *before):
    channels = left_a.shape[0]
    rows = left_a.shape[1] - 16
    width = OFFSETS * group
    half = channels // 2
    if side:
        out = [jax.ShapeDtypeStruct((rows // count, width), jnp.bfloat16)] * count
    else:
        out = [jax.ShapeDtypeStruct((rows, width), jnp.float32)]
    return pl.pallas_call(
        functools.partial(main_kernel, side, tlen, group),
        out_shape=out,
        in_specs=[VMEM] * (3 + len(before)),
        out_specs=[VMEM] * len(out),
        scratch_shapes=[
            pltpu.VMEM(((half + 1) * group // LANES, LANES, LANES), jnp.bfloat16),
            pltpu.VMEM((LANES, LANES // group * LANES), jnp.bfloat16),
            pltpu.VMEM((half + 1, DEPTH, width), jnp.bfloat16),
            pltpu.VMEM((half + 1, 8, LANES), jnp.int32),
            pltpu.VMEM((rows, width), jnp.float32),
        ],
        compiler_params=params(),
        cost_estimate=cost(3),
        name="correlate_" + ("second" if side else "first"),
    )(piece, left_a, inverse, *before)


def add_kernel(*refs):
    parts, keep, send = refs[:-2], refs[-2], refs[-1]
    rows = keep.shape[0]
    core = lax.axis_index("tm") % 2
    for out, which in ((keep, core), (send, 1 - core)):
        place = pl.ds(pl.multiple_of(which * rows, rows), rows)
        value = parts[0][place, :].astype(jnp.float32)
        for part in parts[1:]:
            value = value + part[place, :].astype(jnp.float32)
        out[...] = value


def add(parts):
    rows, width = parts[0].shape
    out = jax.ShapeDtypeStruct((rows // 2, width), jnp.float32)
    return pl.pallas_call(
        add_kernel,
        out_shape=[out, out],
        in_specs=[VMEM] * len(parts),
        out_specs=[VMEM, VMEM],
        compiler_params=params(),
        cost_estimate=cost(0.5),
        name="add",
    )(*parts)


def finish_kernel(group, ours, received, out):
    samples = out.shape[1]
    rows = ours.shape[0]
    value = ours[...] + received[...]
    high = value.astype(jnp.bfloat16).astype(jnp.float32)
    both = jnp.concatenate([high, value - high], axis=0).T.astype(jnp.bfloat16)
    row = lax.broadcasted_iota(jnp.int32, (2 * rows, samples), 0) % rows
    lane = lax.broadcasted_iota(jnp.int32, (2 * rows, samples), 1)
    place = jnp.logical_and(lane // STRIDE == row // 8, lane % 8 == 7 - row % 8)
    place = jnp.where(place, 1.0, 0.0).astype(jnp.bfloat16)
    wide = jnp.dot(both, place, preferred_element_type=jnp.float32)
    lane = lax.broadcasted_iota(jnp.int32, (group, samples), 1) // 8 % OFFSETS
    result = jnp.zeros((group, samples), jnp.float32)
    for offset in range(OFFSETS):
        result = jnp.where(lane == offset, wide[offset * group : (offset + 1) * group], result)
    out[...] = result


def finish(group, samples, ours, received):
    return pl.pallas_call(
        functools.partial(finish_kernel, group),
        out_shape=jax.ShapeDtypeStruct((group, samples), jnp.float32),
        in_specs=[VMEM, VMEM],
        out_specs=VMEM,
        compiler_params=params(),
        cost_estimate=cost(1),
        name="finish",
    )(ours, received)


def shards(waveforms, templates, available, moveout, bank_blocks):
    channels, samples = waveforms.shape
    blocks, events, _, tlen = templates.shape
    count_tm = lax.axis_size("tm")
    count_sta = lax.axis_size("sta")
    chips = count_tm // 2
    near = chips // 2
    group = 2 * events // chips

    def swap(array):
        return lax.ppermute(array, "tm", [(i, i ^ 1) for i in range(count_tm)])

    def across(array, step):
        return lax.ppermute(array, "tm", [(i, i ^ (2 * step)) for i in range(count_tm)])

    partner = swap(waveforms)
    mine, theirs, owners = pack(
        chips,
        group,
        bank_blocks,
        jnp.transpose(templates, (0, 2, 1, 3)),
        jnp.transpose(available, (2, 0, 1)),
        jnp.transpose(moveout, (2, 0, 1)),
    )
    theirs, partner = lax.optimization_barrier((theirs, partner))
    other = swap(theirs)
    pair = pair_waves(waveforms, partner)
    far = []
    for number in range(near - 1):
        steps = (chips - 1 - 2 * number, chips - 2 - 2 * number)
        route = [(2 * z + c, 2 * (z ^ steps[c]) + c) for z in range(chips) for c in range(2)]
        far.append(lax.ppermute(pair, "tm", route))
    beside = across(waveforms, 1)
    merged = list(merge(owners, mine, other))
    pieces = [across(merged[step], step) for step in reversed(range(1, chips))]
    pieces = [merged[0]] + pieces[::-1]
    swapped = swap(choose_waves(pair, beside, far))
    left_a, inverse = prepare_waves(tlen, swapped, pair, beside, far)

    order = sorted(range(chips), key=lambda step: (step < 2, step))
    placed = lax.optimization_barrier((left_a, inverse, *[pieces[step] for step in order]))
    left_a, inverse = placed[:2]
    pieces = [placed[2 + order.index(step)] for step in range(chips)]
    first = choose_piece(owners, pieces)
    second = swap(first)
    total = correlate(0, tlen, group, near, first, left_a, inverse)
    parts = correlate(1, tlen, group, near, second, left_a, inverse, *total)
    gathered = []
    for step in range(near):
        route = []
        for d in range(count_tm):
            for s in range(count_sta):
                dest = near * (d % 2) + (s % near ^ step)
                route.append((d * count_sta + s, (2 * dest + s // near) * count_sta + d // 2))
        gathered.append(lax.ppermute(parts[step], ("tm", "sta"), route))
    ours, send = add(gathered)
    return finish(group, samples, ours, swap(send))


def solution(mesh):
    in_specs = (
        P("sta", "tm"),
        P("tm", None, "sta", None),
        P("tm", None, "sta"),
        P("tm", None, "sta"),
        P(),
    )
    out_specs = P("sta", "tm")
    return jax.shard_map(shards, mesh=mesh, in_specs=in_specs, out_specs=out_specs, check_vma=False)
```

```python
import functools

import jax
import jax.numpy as jnp
from jax import lax
from jax.experimental import pallas as pl
from jax.experimental.pallas import tpu as pltpu
from jax.sharding import PartitionSpec as P

EPSILON = 1e-06
LANES = 128
OFFSETS = 8
TILES = 12
QUARTER = 25
STRIDE = 64
DEPTH = 256
VMEM_LIMIT = 28 * 1024 * 1024

VMEM = pl.BlockSpec(memory_space=pltpu.VMEM)
ANY = pl.BlockSpec(memory_space=pl.ANY)


def params():
    return pltpu.CompilerParams(vmem_limit_bytes=VMEM_LIMIT)


def cost(micros):
    return pl.CostEstimate(
        flops=int(micros * 1e9), bytes_accessed=int(micros * 1e6), transcendentals=0
    )


def pack_kernel(bank_blocks, templates, available, moveout, mine, theirs, owners, chosen, raw, usable, shifts, square, sems):
    blocks, channels, events, tlen = templates.shape
    chips, _, group, _ = mine.shape
    half = channels // 2
    me = lax.axis_index("tm") % 2
    fetch = [
        pltpu.make_async_copy(source, target, sems.at[index])
        for index, (source, target) in enumerate(
            ((bank_blocks, chosen), (available, usable), (moveout, shifts))
        )
    ]
    for side in (1, 0):
        first = half * jnp.where(me == side, 0, 1)
        for block in range(blocks):
            place = (block, pl.ds(first, half))
            number = 3 + blocks * (1 - side) + block
            fetch.append(
                pltpu.make_async_copy(templates.at[place], raw.at[place], sems.at[number])
            )
    for copy in fetch:
        copy.start()
    mine[...] = jnp.zeros_like(mine)
    theirs[...] = jnp.zeros_like(theirs)
    square[...] = jnp.zeros_like(square)
    for copy in fetch[:3]:
        copy.wait()
    slots = [chosen[which] % blocks for which in range(2)]
    row = lax.broadcasted_iota(jnp.int32, owners.shape, 0)
    owners[...] = jnp.where(row == 0, chosen[0] // blocks, chosen[1] // blocks)
    flags = jnp.where(usable[...] > 0, shifts[...] + 1, 0).astype(jnp.float32)
    codes = []
    for which in range(2):
        code = flags[:, 0, :]
        for block in range(1, blocks):
            code = jnp.where(slots[which] == block, flags[:, block, :], code)
        square[0:channels, 0:events] = code
        turned = square[...].T
        later = pltpu.roll(turned, LANES - half, 1)
        codes.append([jnp.where(me == core, turned, later) for core in range(2)])
    for side, out in ((1, theirs), (0, mine)):
        for block in range(blocks):
            fetch[3 + blocks * (1 - side) + block].wait()
        for which in range(2):
            first = half * jnp.where(me == side, 0, 1)
            code = codes[which][side].astype(jnp.bfloat16)
            for tile in range(TILES):
                extra = TILES + tile // 4
                start = QUARTER * (tile % 4)
                for index in range(events // group):
                    chip = which * (events // group) + index
                    rows = slice(index * group, (index + 1) * group)
                    out[chip, tile, :, 0:tlen] = raw[slots[which], first + tile, rows, :]
                    out[chip, tile, :, tlen : tlen + QUARTER] = raw[
                        slots[which], first + extra, rows, start : start + QUARTER
                    ]
                    out[chip, tile, :, 125:126] = code[rows, tile : tile + 1]
                    if tile < half - TILES:
                        beyond = TILES + tile
                        out[chip, tile, :, 126:127] = code[rows, beyond : beyond + 1]


def pack(chips, group, bank_blocks, templates, available, moveout):
    shape = (chips, TILES, group, LANES)
    held = [
        pltpu.with_memory_space_constraint(array, pltpu.HBM)
        for array in (bank_blocks, templates, available, moveout)
    ]
    return pl.pallas_call(
        pack_kernel,
        out_shape=[jax.ShapeDtypeStruct(shape, jnp.bfloat16)] * 2
        + [jax.ShapeDtypeStruct((8, LANES), jnp.int32)],
        in_specs=[ANY] * 4,
        out_specs=[VMEM] * 3,
        scratch_shapes=[
            pltpu.SMEM(bank_blocks.shape, jnp.int32),
            pltpu.VMEM(templates.shape, jnp.bfloat16),
            pltpu.VMEM(available.shape, jnp.int32),
            pltpu.VMEM(moveout.shape, jnp.int32),
            pltpu.VMEM((LANES, LANES), jnp.float32),
            pltpu.SemaphoreType.DMA((3 + 2 * templates.shape[0],)),
        ],
        compiler_params=params(),
        cost_estimate=cost(2),
        name="pack",
    )(*held)


def merge_kernel(owners, mine, other, *outs):
    chips = len(outs)
    me = lax.axis_index("tm")
    for step, out in enumerate(outs):
        dest = jnp.bitwise_xor(me // 2, step)
        owner = jnp.where(dest < chips // 2, owners[0, 0], owners[1, 0])
        here = owner % 2 == me % 2

        @pl.when(here)
        def _():
            out[...] = mine[dest]

        @pl.when(jnp.logical_not(here))
        def _():
            out[...] = other[dest]


def merge(owners, mine, other):
    chips = mine.shape[0]
    return pl.pallas_call(
        merge_kernel,
        out_shape=[jax.ShapeDtypeStruct(mine.shape[1:], mine.dtype)] * chips,
        in_specs=[VMEM] * 3,
        out_specs=[VMEM] * chips,
        compiler_params=params(),
        cost_estimate=cost(0.3),
        name="merge",
    )(owners, mine, other)


def lagged(row, ahead):
    copies = jnp.broadcast_to(row, (8, row.shape[1]))
    return pltpu.roll(copies, row.shape[1] - 7 - ahead, 1, stride=1, stride_axis=0)


def segment(me, other, parity, pair, beside, far, default):
    chip, core = me // 2, me % 2
    chips = 2 * len(far) + 2
    step = jnp.bitwise_xor(chip, other)
    value = default[...]
    value = jnp.where(jnp.logical_and(step == 1, core == parity), beside[...], value)
    value = jnp.where(step == 0, pair[parity], value)
    for number, array in enumerate(far):
        value = jnp.where(step == chips - 1 - 2 * number - core, array[parity], value)
    return value


def pair_kernel(own, partner, out):
    core = lax.axis_index("tm") % 2
    out[core] = own[...]
    out[1 - core] = partner[...]


def pair_waves(own, partner):
    return pl.pallas_call(
        pair_kernel,
        out_shape=jax.ShapeDtypeStruct((2,) + own.shape, own.dtype),
        in_specs=[VMEM] * 2,
        out_specs=VMEM,
        compiler_params=params(),
        cost_estimate=cost(0.05),
        name="pair_waves",
    )(own, partner)


def choose_kernel(pair, beside, *rest):
    far, out = rest[:-1], rest[-1]
    near = out.shape[0] - 1
    me = lax.axis_index("tm")
    chip, core = me // 2, me % 2
    for entry in range(near):
        number, parity = divmod(entry, 2)
        step = jnp.bitwise_xor(chip, near * (1 - core) + 2 * number) // 2
        value = beside[...]
        for place, array in enumerate(far):
            value = jnp.where(step == near - 1 - place, array[parity], value)
        out[entry] = value
    out[near] = segment(me, near, 0, pair, beside, far, beside)


def choose_waves(pair, beside, far):
    return pl.pallas_call(
        choose_kernel,
        out_shape=jax.ShapeDtypeStruct((len(far) + 2,) + beside.shape, beside.dtype),
        in_specs=[VMEM] * (2 + len(far)),
        out_specs=VMEM,
        compiler_params=params(),
        cost_estimate=cost(0.05),
        name="choose_waves",
    )(pair, beside, *far)


def own_kernel(owners, *refs):
    pieces, out = refs[:-1], refs[-1]
    chip = lax.axis_index("tm") // 2
    owner = jnp.where(chip < len(pieces) // 2, owners[0, 0], owners[1, 0])
    source = jnp.bitwise_xor(owner // 2, chip)
    value = pieces[0][...]
    for number, piece in enumerate(pieces[1:], 1):
        value = jnp.where(source == number, piece[...], value)
    out[...] = value


def choose_piece(owners, pieces):
    return pl.pallas_call(
        own_kernel,
        out_shape=jax.ShapeDtypeStruct(pieces[0].shape, pieces[0].dtype),
        in_specs=[VMEM] * (1 + len(pieces)),
        out_specs=VMEM,
        compiler_params=params(),
        cost_estimate=cost(0.3),
        name="choose_piece",
    )(owners, *pieces)


def waves_kernel(channels, tlen, unroll, swapped, pair, beside, *rest):
    far = rest[:-3]
    left_a, inverse, padded = rest[-3:]
    samples = beside.shape[1]
    near = swapped.shape[0] - 1
    length = 2 * near * samples
    count = padded.shape[1] // LANES
    me = lax.axis_index("tm")
    core = me % 2
    padded[...] = jnp.zeros_like(padded)
    for index in range(2 * near):
        entry, parity = divmod(index, 2)
        given = swapped.at[2 * (entry // 2) + parity]
        wave = segment(me, near * core + entry, parity, pair, beside, far, given)
        padded[0:channels, samples * index : samples * (index + 1)] = wave.astype(jnp.float32)
    rim = segment(me, near * core + near, 0, pair, beside, far, swapped.at[near])
    rim = rim[:, 0 : padded.shape[1] - length].astype(jnp.float32)
    padded[0:channels, length:] = jnp.where(core == 0, rim, 0.0)

    rows = 32 * count
    values = [padded[:, LANES * tile : LANES * (tile + 1)] for tile in range(count)]
    values = jnp.concatenate(values + [jnp.zeros((32, LANES), jnp.float32)], axis=0)
    square = values * values
    high = square.astype(jnp.bfloat16)
    low = (square - high.astype(jnp.float32)).astype(jnp.bfloat16)
    values = values.astype(jnp.bfloat16)
    lag = lax.broadcasted_iota(jnp.int32, (2 * LANES, LANES), 0)
    lag = lag - lax.broadcasted_iota(jnp.int32, (2 * LANES, LANES), 1)
    band = jnp.where(jnp.logical_and(lag >= 0, lag < tlen), 1.0, 0.0).astype(jnp.bfloat16)

    def windows(array):
        both = jnp.concatenate([array[0:rows], array[32 : rows + 32]], axis=1)
        return jnp.dot(both, band, preferred_element_type=jnp.float32)

    first_sum = windows(values)
    second_sum = windows(high) + windows(low)
    variance = (second_sum * tlen - first_sum * first_sum) * (1.0 / tlen**2)
    scale = lax.rsqrt(variance + EPSILON)
    for tile in range(length // LANES):
        part = scale[32 * tile : 32 * (tile + 1)]
        after = scale[32 * (tile + 1) : 32 * (tile + 2)]
        inverse[2 * tile] = part
        lane = lax.broadcasted_iota(jnp.int32, part.shape, 1)
        both = jnp.where(lane < STRIDE, after, part)
        inverse[2 * tile + 1] = pltpu.roll(both, LANES - STRIDE, 1)

    def interleaved(row, tiles):
        even, odd = lagged(row, 0), lagged(row, STRIDE)
        parts = []
        for tile in range(tiles):
            lanes = slice(LANES * tile, LANES * (tile + 1))
            parts += [even[:, lanes], odd[:, lanes]]
        return jnp.concatenate(parts, axis=0)

    @pl.loop(0, channels // unroll)
    def _(step):
        for item in range(unroll):
            channel = step * unroll + item
            value = interleaved(padded[pl.ds(channel, 1), :], length // LANES + 1)
            left_a[channel] = value.astype(jnp.bfloat16)


def prepare_waves(tlen, swapped, pair, beside, far):
    channels, samples = beside.shape
    length = 2 * (swapped.shape[0] - 1) * samples
    rows = length // OFFSETS
    unroll = max(step for step in (1, 2, 3) if channels % step == 0)
    return pl.pallas_call(
        functools.partial(waves_kernel, channels, tlen, unroll),
        out_shape=[
            jax.ShapeDtypeStruct((channels, rows + 16, LANES), jnp.bfloat16),
            jax.ShapeDtypeStruct((length // STRIDE, 32, LANES), jnp.float32),
        ],
        in_specs=[VMEM] * (3 + len(far)),
        out_specs=[VMEM, VMEM],
        scratch_shapes=[
            pltpu.VMEM((32, length + 2 * LANES), jnp.float32),
        ],
        compiler_params=params(),
        cost_estimate=cost(0.05),
        name="prepare_waves",
    )(swapped, pair, beside, *far)


def main_kernel(side, tlen, group, piece, left_a, inverse, *rest):
    outs = rest[:-5]
    if side:
        before, outs = outs[0], outs[1:]
    bank, expand, weight_a, reach, total = rest[-5:]
    core = lax.axis_index("tm") % 2
    channels = left_a.shape[0]
    rows = left_a.shape[1] - 16
    half = channels // 2
    base = half * jnp.where(core == side, 0, 1)
    slots = LANES // group
    banks = (half + 1) // slots
    offset_count = LANES // group
    tile_count = OFFSETS // offset_count
    top = 112 + 8 * (7 + offset_count - 1)
    top = top + top % 16

    lag = lax.broadcasted_iota(jnp.int32, (LANES, LANES), 0)
    target = lax.broadcasted_iota(jnp.int32, (LANES, LANES), 1)
    lane = lax.broadcasted_iota(jnp.int32, (1, LANES), 1)
    used = lag < tlen
    ahead = lane // group
    for slot in range(slots):
        chosen = jnp.where(lag == target % group + slot * group, 1.0, 0.0)
        expand[:, slot * LANES : (slot + 1) * LANES] = chosen.astype(jnp.bfloat16)
    turned = []
    for index in range(banks):
        count = min(slots, max(TILES - slots * index, 0))
        values = jnp.zeros((LANES, LANES), jnp.float32)
        if count:
            values = piece[slots * index : slots * index + count].astype(jnp.float32)
            values = values.reshape(count * group, LANES)
            if count < slots:
                gap = jnp.zeros((LANES - count * group, LANES), jnp.float32)
                values = jnp.concatenate([values, gap], axis=0)
            values = values.T
        turned.append(values)
    codes = [values[125:126, :] for values in turned]
    heads = [jnp.where(used, values, 0.0) for values in turned]
    for extra in range(half - TILES):
        place, slot = divmod(TILES + extra, slots)
        mask = ahead == slot
        code = pltpu.roll(turned[0][126:127, :], (slot - extra) * group % LANES, 1)
        codes[place] = jnp.where(mask, code, codes[place])
        for quarter in range(4):
            source, lanes = divmod(4 * extra + quarter, slots)
            values = turned[source][96:128]
            sample = lag[96:128]
            inside = jnp.logical_and(sample >= tlen, sample < tlen + QUARTER)
            values = jnp.where(inside, values, 0.0)
            values = pltpu.roll(values, (slot - lanes) * group % LANES, 1)
            start = QUARTER * quarter - (tlen - 96)
            values = jnp.concatenate([values, jnp.zeros((8, LANES), jnp.float32)], axis=0)
            values = pltpu.roll(values, start % 8, 0)
            start -= start % 8
            if start < 0:
                values, start = values[8:], 0
            below = LANES - start - values.shape[0]
            if start:
                values = jnp.concatenate([jnp.zeros((start, LANES), jnp.float32), values], axis=0)
            if below > 0:
                values = jnp.concatenate([values, jnp.zeros((below, LANES), jnp.float32)], axis=0)
            heads[place] = heads[place] + jnp.where(mask, values[0:LANES], 0.0)
    for index, (values, code) in enumerate(zip(heads, codes)):
        code = jnp.where(slots * index + ahead < half, code, 0.0)
        deviate = jnp.where(used, values * tlen - jnp.sum(values, axis=0, keepdims=True), 0.0)
        square = jnp.sum(deviate * deviate, axis=0, keepdims=True) * (1.0 / tlen**3)
        unit = deviate / (jnp.sqrt(square + EPSILON) * tlen**2)
        unit = unit.astype(jnp.bfloat16).astype(jnp.float32)
        unit = jnp.where(code > 0, unit, 0.0)
        shift = code.astype(jnp.int32) - 1
        for bit in (1, 2, 4):
            unit = jnp.where(jnp.bitwise_and(shift, bit) > 0, pltpu.roll(unit, bit, 0), unit)
        unit = jnp.where(lag == 112, code, unit)
        bank[index] = unit.astype(jnp.bfloat16)

    def build(number):
        wide = jnp.dot(bank[number], expand[...], preferred_element_type=jnp.float32)
        for slot in range(slots):
            spreaded = wide[:, slot * LANES : (slot + 1) * LANES]
            code = spreaded[112:113, :].astype(jnp.int32)
            shift = code - 1
            moves = shift // 8 + ahead
            taps = spreaded[0:112, :]
            for bit in (1, 2, 4, 8):
                gap = jnp.zeros((8 * bit, LANES), jnp.float32)
                taps = jnp.where(
                    jnp.bitwise_and(moves, bit) > 0,
                    jnp.concatenate([gap, taps], axis=0),
                    jnp.concatenate([taps, gap], axis=0),
                )[0:top]
            taps = taps.astype(jnp.bfloat16)
            item = number * slots + slot
            reach[item] = jnp.maximum(shift, 0) + 8 * ahead + 7 - lag[0:8]
            for tile in range(tile_count):
                skip = 8 * offset_count * tile
                lanes = slice(LANES * tile, LANES * (tile + 1))
                if skip:
                    weight_a[item, 0:skip, lanes] = jnp.zeros((skip, LANES), jnp.bfloat16)
                weight_a[item, skip : skip + top, lanes] = taps
                rest = DEPTH - top - skip
                if rest:
                    weight_a[item, skip + top :, lanes] = jnp.zeros((rest, LANES), jnp.bfloat16)

    def products(item):
        both = [left_a[base + item, 0:rows, :], left_a[base + item, 16 : rows + 16, :]]
        corr = jnp.dot(
            jnp.concatenate(both, axis=1), weight_a[item], preferred_element_type=jnp.float32
        )
        columns = []
        for tile in range(tile_count):
            place = reach[item] + 8 * offset_count * tile
            parts = []
            for step in range(rows // 8):
                window = inverse[step, pl.ds(base + item, 1), :]
                window = jnp.broadcast_to(window, (8, LANES))
                parts.append(jnp.take_along_axis(window, place, axis=1, mode="promise_in_bounds"))
            columns.append(jnp.concatenate(parts, axis=0))
        return corr * jnp.concatenate(columns, axis=1)

    def apply(number, count):
        for item in range(number * slots, number * slots + count, 2):
            value = products(item)
            if item + 1 < number * slots + count:
                value = value + products(item + 1)
            if item:
                value = value + total[...]
            elif side:
                value = value + before[...]
            total[...] = value

    build(0)

    for number in range(1, banks):
        apply(number - 1, slots)
        build(number)

    apply(banks - 1, half - slots * (banks - 1))

    if not side:
        outs[0][...] = total[...]
        return
    rows_out = outs[0].shape[0]
    station = lax.axis_index("sta") // 2
    for step, out in enumerate(outs):
        part = jnp.bitwise_xor(station, step)
        out[...] = total[pl.ds(pl.multiple_of(part * rows_out, rows_out), rows_out), :].astype(
            jnp.bfloat16
        )


def correlate(side, tlen, group, count, piece, left_a, inverse, *before):
    channels = left_a.shape[0]
    rows = left_a.shape[1] - 16
    width = OFFSETS * group
    half = channels // 2
    if side:
        out = [jax.ShapeDtypeStruct((rows // count, width), jnp.bfloat16)] * count
    else:
        out = [jax.ShapeDtypeStruct((rows, width), jnp.float32)]
    return pl.pallas_call(
        functools.partial(main_kernel, side, tlen, group),
        out_shape=out,
        in_specs=[VMEM] * (3 + len(before)),
        out_specs=[VMEM] * len(out),
        scratch_shapes=[
            pltpu.VMEM(((half + 1) * group // LANES, LANES, LANES), jnp.bfloat16),
            pltpu.VMEM((LANES, LANES // group * LANES), jnp.bfloat16),
            pltpu.VMEM((half + 1, DEPTH, width), jnp.bfloat16),
            pltpu.VMEM((half + 1, 8, LANES), jnp.int32),
            pltpu.VMEM((rows, width), jnp.float32),
        ],
        compiler_params=params(),
        cost_estimate=cost(3),
        name="correlate_" + ("second" if side else "first"),
    )(piece, left_a, inverse, *before)


def add_kernel(*refs):
    parts, keep, send = refs[:-2], refs[-2], refs[-1]
    rows = keep.shape[0]
    core = lax.axis_index("tm") % 2
    for out, which in ((keep, core), (send, 1 - core)):
        place = pl.ds(pl.multiple_of(which * rows, rows), rows)
        value = parts[0][place, :].astype(jnp.float32)
        for part in parts[1:]:
            value = value + part[place, :].astype(jnp.float32)
        out[...] = value


def add(parts):
    rows, width = parts[0].shape
    out = jax.ShapeDtypeStruct((rows // 2, width), jnp.float32)
    return pl.pallas_call(
        add_kernel,
        out_shape=[out, out],
        in_specs=[VMEM] * len(parts),
        out_specs=[VMEM, VMEM],
        compiler_params=params(),
        cost_estimate=cost(0.5),
        name="add",
    )(*parts)


def finish_kernel(group, ours, received, out):
    samples = out.shape[1]
    rows = ours.shape[0]
    value = ours[...] + received[...]
    high = value.astype(jnp.bfloat16).astype(jnp.float32)
    both = jnp.concatenate([high, value - high], axis=0).T.astype(jnp.bfloat16)
    row = lax.broadcasted_iota(jnp.int32, (2 * rows, samples), 0) % rows
    lane = lax.broadcasted_iota(jnp.int32, (2 * rows, samples), 1)
    place = jnp.logical_and(lane // STRIDE == row // 8, lane % 8 == 7 - row % 8)
    place = jnp.where(place, 1.0, 0.0).astype(jnp.bfloat16)
    wide = jnp.dot(both, place, preferred_element_type=jnp.float32)
    lane = lax.broadcasted_iota(jnp.int32, (group, samples), 1) // 8 % OFFSETS
    result = jnp.zeros((group, samples), jnp.float32)
    for offset in range(OFFSETS):
        result = jnp.where(lane == offset, wide[offset * group : (offset + 1) * group], result)
    out[...] = result


def finish(group, samples, ours, received):
    return pl.pallas_call(
        functools.partial(finish_kernel, group),
        out_shape=jax.ShapeDtypeStruct((group, samples), jnp.float32),
        in_specs=[VMEM, VMEM],
        out_specs=VMEM,
        compiler_params=params(),
        cost_estimate=cost(1),
        name="finish",
    )(ours, received)


def shards(waveforms, templates, available, moveout, bank_blocks):
    channels, samples = waveforms.shape
    blocks, events, _, tlen = templates.shape
    count_tm = lax.axis_size("tm")
    count_sta = lax.axis_size("sta")
    chips = count_tm // 2
    near = chips // 2
    group = 2 * events // chips

    def swap(array):
        return lax.ppermute(array, "tm", [(i, i ^ 1) for i in range(count_tm)])

    def across(array, step):
        return lax.ppermute(array, "tm", [(i, i ^ (2 * step)) for i in range(count_tm)])

    partner = swap(waveforms)
    mine, theirs, owners = pack(
        chips,
        group,
        bank_blocks,
        jnp.transpose(templates, (0, 2, 1, 3)),
        jnp.transpose(available, (2, 0, 1)),
        jnp.transpose(moveout, (2, 0, 1)),
    )
    theirs, partner = lax.optimization_barrier((theirs, partner))
    other = swap(theirs)
    pair = pair_waves(waveforms, partner)
    far = []
    for number in range(near - 1):
        steps = (chips - 1 - 2 * number, chips - 2 - 2 * number)
        route = [(2 * z + c, 2 * (z ^ steps[c]) + c) for z in range(chips) for c in range(2)]
        far.append(lax.ppermute(pair, "tm", route))
    beside = across(waveforms, 1)
    merged = list(merge(owners, mine, other))
    pieces = [across(merged[step], step) for step in reversed(range(1, chips))]
    pieces = [merged[0]] + pieces[::-1]
    swapped = swap(choose_waves(pair, beside, far))
    left_a, inverse = prepare_waves(tlen, swapped, pair, beside, far)

    order = sorted(range(chips), key=lambda step: (step < 2, step))
    placed = lax.optimization_barrier((left_a, inverse, *[pieces[step] for step in order]))
    left_a, inverse = placed[:2]
    pieces = [placed[2 + order.index(step)] for step in range(chips)]
    first = choose_piece(owners, pieces)
    second = swap(first)
    total = correlate(0, tlen, group, near, first, left_a, inverse)
    parts = correlate(1, tlen, group, near, second, left_a, inverse, *total)
    gathered = []
    for step in range(near):
        route = []
        for d in range(count_tm):
            for s in range(count_sta):
                dest = near * (d % 2) + (s // 2 ^ step)
                route.append((d * count_sta + s, (2 * dest + s % 2) * count_sta + d // 2))
        gathered.append(lax.ppermute(parts[step], ("tm", "sta"), route))
    ours, send = add(gathered)
    return finish(group, samples, ours, swap(send))


def solution(mesh):
    in_specs = (
        P("sta", "tm"),
        P("tm", None, "sta", None),
        P("tm", None, "sta"),
        P("tm", None, "sta"),
        P(),
    )
    out_specs = P("sta", "tm")
    return jax.shard_map(shards, mesh=mesh, in_specs=in_specs, out_specs=out_specs, check_vma=False)
```

```python
import functools

import jax
import jax.numpy as jnp
from jax import lax
from jax.experimental import pallas as pl
from jax.experimental.pallas import tpu as pltpu
from jax.sharding import PartitionSpec as P

EPSILON = 1e-06
LANES = 128
OFFSETS = 8
TILES = 12
QUARTER = 25
STRIDE = 64
DEPTH = 256
VMEM_LIMIT = 28 * 1024 * 1024

VMEM = pl.BlockSpec(memory_space=pltpu.VMEM)
ANY = pl.BlockSpec(memory_space=pl.ANY)


def params():
    return pltpu.CompilerParams(vmem_limit_bytes=VMEM_LIMIT)


def cost(micros):
    return pl.CostEstimate(
        flops=int(micros * 1e9), bytes_accessed=int(micros * 1e6), transcendentals=0
    )


def pack_kernel(bank_blocks, templates, available, moveout, mine, theirs, owners, chosen, raw, usable, shifts, square, sems):
    blocks, channels, events, tlen = templates.shape
    chips, _, group, _ = mine.shape
    half = channels // 2
    me = lax.axis_index("tm") % 2
    fetch = [
        pltpu.make_async_copy(source, target, sems.at[index])
        for index, (source, target) in enumerate(
            ((bank_blocks, chosen), (available, usable), (moveout, shifts))
        )
    ]
    for side in (1, 0):
        first = half * jnp.where(me == side, 0, 1)
        for block in range(blocks):
            place = (block, pl.ds(first, half))
            number = 3 + blocks * (1 - side) + block
            fetch.append(
                pltpu.make_async_copy(templates.at[place], raw.at[place], sems.at[number])
            )
    for copy in fetch:
        copy.start()
    mine[...] = jnp.zeros_like(mine)
    theirs[...] = jnp.zeros_like(theirs)
    square[...] = jnp.zeros_like(square)
    for copy in fetch[:3]:
        copy.wait()
    slots = [chosen[which] % blocks for which in range(2)]
    row = lax.broadcasted_iota(jnp.int32, owners.shape, 0)
    owners[...] = jnp.where(row == 0, chosen[0] // blocks, chosen[1] // blocks)
    flags = jnp.where(usable[...] > 0, shifts[...] + 1, 0).astype(jnp.float32)
    codes = []
    for which in range(2):
        code = flags[:, 0, :]
        for block in range(1, blocks):
            code = jnp.where(slots[which] == block, flags[:, block, :], code)
        square[0:channels, 0:events] = code
        turned = square[...].T
        later = pltpu.roll(turned, LANES - half, 1)
        codes.append([jnp.where(me == core, turned, later) for core in range(2)])
    for side, out in ((1, theirs), (0, mine)):
        for block in range(blocks):
            fetch[3 + blocks * (1 - side) + block].wait()
        for which in range(2):
            first = half * jnp.where(me == side, 0, 1)
            code = codes[which][side].astype(jnp.bfloat16)
            for tile in range(TILES):
                extra = TILES + tile // 4
                start = QUARTER * (tile % 4)
                for index in range(events // group):
                    chip = which * (events // group) + index
                    rows = slice(index * group, (index + 1) * group)
                    out[chip, tile, :, 0:tlen] = raw[slots[which], first + tile, rows, :]
                    out[chip, tile, :, tlen : tlen + QUARTER] = raw[
                        slots[which], first + extra, rows, start : start + QUARTER
                    ]
                    out[chip, tile, :, 125:126] = code[rows, tile : tile + 1]
                    if tile < half - TILES:
                        beyond = TILES + tile
                        out[chip, tile, :, 126:127] = code[rows, beyond : beyond + 1]


def pack(chips, group, bank_blocks, templates, available, moveout):
    shape = (chips, TILES, group, LANES)
    held = [
        pltpu.with_memory_space_constraint(array, pltpu.HBM)
        for array in (bank_blocks, templates, available, moveout)
    ]
    return pl.pallas_call(
        pack_kernel,
        out_shape=[jax.ShapeDtypeStruct(shape, jnp.bfloat16)] * 2
        + [jax.ShapeDtypeStruct((8, LANES), jnp.int32)],
        in_specs=[ANY] * 4,
        out_specs=[VMEM] * 3,
        scratch_shapes=[
            pltpu.SMEM(bank_blocks.shape, jnp.int32),
            pltpu.VMEM(templates.shape, jnp.bfloat16),
            pltpu.VMEM(available.shape, jnp.int32),
            pltpu.VMEM(moveout.shape, jnp.int32),
            pltpu.VMEM((LANES, LANES), jnp.float32),
            pltpu.SemaphoreType.DMA((3 + 2 * templates.shape[0],)),
        ],
        compiler_params=params(),
        cost_estimate=cost(2),
        name="pack",
    )(*held)


def merge_kernel(owners, mine, other, *outs):
    chips = len(outs)
    me = lax.axis_index("tm")
    for step, out in enumerate(outs):
        dest = jnp.bitwise_xor(me // 2, step)
        owner = jnp.where(dest < chips // 2, owners[0, 0], owners[1, 0])
        here = owner % 2 == me % 2

        @pl.when(here)
        def _():
            out[...] = mine[dest]

        @pl.when(jnp.logical_not(here))
        def _():
            out[...] = other[dest]


def merge(owners, mine, other):
    chips = mine.shape[0]
    return pl.pallas_call(
        merge_kernel,
        out_shape=[jax.ShapeDtypeStruct(mine.shape[1:], mine.dtype)] * chips,
        in_specs=[VMEM] * 3,
        out_specs=[VMEM] * chips,
        compiler_params=params(),
        cost_estimate=cost(0.3),
        name="merge",
    )(owners, mine, other)


def lagged(row, ahead):
    copies = jnp.broadcast_to(row, (8, row.shape[1]))
    return pltpu.roll(copies, row.shape[1] - 7 - ahead, 1, stride=1, stride_axis=0)


def segment(me, other, parity, pair, beside, far, default):
    chip, core = me // 2, me % 2
    chips = 2 * len(far) + 2
    step = jnp.bitwise_xor(chip, other)
    value = default[...]
    value = jnp.where(jnp.logical_and(step == 1, core == parity), beside[...], value)
    value = jnp.where(step == 0, pair[parity], value)
    for number, array in enumerate(far):
        value = jnp.where(step == chips - 1 - 2 * number - core, array[parity], value)
    return value


def pair_kernel(own, partner, out):
    core = lax.axis_index("tm") % 2
    out[core] = own[...]
    out[1 - core] = partner[...]


def pair_waves(own, partner):
    return pl.pallas_call(
        pair_kernel,
        out_shape=jax.ShapeDtypeStruct((2,) + own.shape, own.dtype),
        in_specs=[VMEM] * 2,
        out_specs=VMEM,
        compiler_params=params(),
        cost_estimate=cost(0.05),
        name="pair_waves",
    )(own, partner)


def choose_kernel(pair, beside, *rest):
    far, out = rest[:-1], rest[-1]
    near = out.shape[0] - 1
    me = lax.axis_index("tm")
    chip, core = me // 2, me % 2
    for entry in range(near):
        number, parity = divmod(entry, 2)
        step = jnp.bitwise_xor(chip, near * (1 - core) + 2 * number) // 2
        value = beside[...]
        for place, array in enumerate(far):
            value = jnp.where(step == near - 1 - place, array[parity], value)
        out[entry] = value
    out[near] = segment(me, near, 0, pair, beside, far, beside)


def choose_waves(pair, beside, far):
    return pl.pallas_call(
        choose_kernel,
        out_shape=jax.ShapeDtypeStruct((len(far) + 2,) + beside.shape, beside.dtype),
        in_specs=[VMEM] * (2 + len(far)),
        out_specs=VMEM,
        compiler_params=params(),
        cost_estimate=cost(0.05),
        name="choose_waves",
    )(pair, beside, *far)


def own_kernel(owners, *refs):
    pieces, out = refs[:-1], refs[-1]
    chip = lax.axis_index("tm") // 2
    owner = jnp.where(chip < len(pieces) // 2, owners[0, 0], owners[1, 0])
    source = jnp.bitwise_xor(owner // 2, chip)
    value = pieces[0][...]
    for number, piece in enumerate(pieces[1:], 1):
        value = jnp.where(source == number, piece[...], value)
    out[...] = value


def choose_piece(owners, pieces):
    return pl.pallas_call(
        own_kernel,
        out_shape=jax.ShapeDtypeStruct(pieces[0].shape, pieces[0].dtype),
        in_specs=[VMEM] * (1 + len(pieces)),
        out_specs=VMEM,
        compiler_params=params(),
        cost_estimate=cost(0.3),
        name="choose_piece",
    )(owners, *pieces)


def waves_kernel(channels, tlen, unroll, swapped, pair, beside, *rest):
    far = rest[:-3]
    left_a, inverse, padded = rest[-3:]
    samples = beside.shape[1]
    near = swapped.shape[0] - 1
    length = 2 * near * samples
    count = padded.shape[1] // LANES
    me = lax.axis_index("tm")
    core = me % 2
    padded[...] = jnp.zeros_like(padded)
    for index in range(2 * near):
        entry, parity = divmod(index, 2)
        given = swapped.at[2 * (entry // 2) + parity]
        wave = segment(me, near * core + entry, parity, pair, beside, far, given)
        padded[0:channels, samples * index : samples * (index + 1)] = wave.astype(jnp.float32)
    rim = segment(me, near * core + near, 0, pair, beside, far, swapped.at[near])
    rim = rim[:, 0 : padded.shape[1] - length].astype(jnp.float32)
    padded[0:channels, length:] = jnp.where(core == 0, rim, 0.0)

    rows = 32 * count
    values = [padded[:, LANES * tile : LANES * (tile + 1)] for tile in range(count)]
    values = jnp.concatenate(values + [jnp.zeros((32, LANES), jnp.float32)], axis=0)
    square = values * values
    high = square.astype(jnp.bfloat16)
    low = (square - high.astype(jnp.float32)).astype(jnp.bfloat16)
    values = values.astype(jnp.bfloat16)
    lag = lax.broadcasted_iota(jnp.int32, (2 * LANES, LANES), 0)
    lag = lag - lax.broadcasted_iota(jnp.int32, (2 * LANES, LANES), 1)
    band = jnp.where(jnp.logical_and(lag >= 0, lag < tlen), 1.0, 0.0).astype(jnp.bfloat16)

    def windows(array):
        both = jnp.concatenate([array[0:rows], array[32 : rows + 32]], axis=1)
        return jnp.dot(both, band, preferred_element_type=jnp.float32)

    first_sum = windows(values)
    second_sum = windows(high) + windows(low)
    variance = (second_sum * tlen - first_sum * first_sum) * (1.0 / tlen**2)
    scale = lax.rsqrt(variance + EPSILON)
    for tile in range(length // LANES):
        part = scale[32 * tile : 32 * (tile + 1)]
        after = scale[32 * (tile + 1) : 32 * (tile + 2)]
        inverse[2 * tile] = part
        lane = lax.broadcasted_iota(jnp.int32, part.shape, 1)
        both = jnp.where(lane < STRIDE, after, part)
        inverse[2 * tile + 1] = pltpu.roll(both, LANES - STRIDE, 1)

    def interleaved(row, tiles):
        even, odd = lagged(row, 0), lagged(row, STRIDE)
        parts = []
        for tile in range(tiles):
            lanes = slice(LANES * tile, LANES * (tile + 1))
            parts += [even[:, lanes], odd[:, lanes]]
        return jnp.concatenate(parts, axis=0)

    @pl.loop(0, channels // unroll)
    def _(step):
        for item in range(unroll):
            channel = step * unroll + item
            value = interleaved(padded[pl.ds(channel, 1), :], length // LANES + 1)
            left_a[channel] = value.astype(jnp.bfloat16)


def prepare_waves(tlen, swapped, pair, beside, far):
    channels, samples = beside.shape
    length = 2 * (swapped.shape[0] - 1) * samples
    rows = length // OFFSETS
    unroll = max(step for step in (1, 2, 3) if channels % step == 0)
    return pl.pallas_call(
        functools.partial(waves_kernel, channels, tlen, unroll),
        out_shape=[
            jax.ShapeDtypeStruct((channels, rows + 16, LANES), jnp.bfloat16),
            jax.ShapeDtypeStruct((length // STRIDE, 32, LANES), jnp.float32),
        ],
        in_specs=[VMEM] * (3 + len(far)),
        out_specs=[VMEM, VMEM],
        scratch_shapes=[
            pltpu.VMEM((32, length + 2 * LANES), jnp.float32),
        ],
        compiler_params=params(),
        cost_estimate=cost(0.05),
        name="prepare_waves",
    )(swapped, pair, beside, *far)


def main_kernel(side, tlen, group, piece, left_a, inverse, *rest):
    outs = rest[:-5]
    if side:
        before, outs = outs[0], outs[1:]
    bank, expand, weight_a, reach, total = rest[-5:]
    core = lax.axis_index("tm") % 2
    channels = left_a.shape[0]
    rows = left_a.shape[1] - 16
    half = channels // 2
    base = half * jnp.where(core == side, 0, 1)
    slots = LANES // group
    banks = (half + 1) // slots
    offset_count = LANES // group
    tile_count = OFFSETS // offset_count
    top = 112 + 8 * (7 + offset_count - 1)
    top = top + top % 16

    lag = lax.broadcasted_iota(jnp.int32, (LANES, LANES), 0)
    target = lax.broadcasted_iota(jnp.int32, (LANES, LANES), 1)
    lane = lax.broadcasted_iota(jnp.int32, (1, LANES), 1)
    used = lag < tlen
    ahead = lane // group
    for slot in range(slots):
        chosen = jnp.where(lag == target % group + slot * group, 1.0, 0.0)
        expand[:, slot * LANES : (slot + 1) * LANES] = chosen.astype(jnp.bfloat16)
    turned = []
    for index in range(banks):
        count = min(slots, max(TILES - slots * index, 0))
        values = jnp.zeros((LANES, LANES), jnp.float32)
        if count:
            values = piece[slots * index : slots * index + count].astype(jnp.float32)
            values = values.reshape(count * group, LANES)
            if count < slots:
                gap = jnp.zeros((LANES - count * group, LANES), jnp.float32)
                values = jnp.concatenate([values, gap], axis=0)
            values = values.T
        turned.append(values)
    codes = [values[125:126, :] for values in turned]
    heads = [jnp.where(used, values, 0.0) for values in turned]
    for extra in range(half - TILES):
        place, slot = divmod(TILES + extra, slots)
        mask = ahead == slot
        code = pltpu.roll(turned[0][126:127, :], (slot - extra) * group % LANES, 1)
        codes[place] = jnp.where(mask, code, codes[place])
        for quarter in range(4):
            source, lanes = divmod(4 * extra + quarter, slots)
            values = turned[source][96:128]
            sample = lag[96:128]
            inside = jnp.logical_and(sample >= tlen, sample < tlen + QUARTER)
            values = jnp.where(inside, values, 0.0)
            values = pltpu.roll(values, (slot - lanes) * group % LANES, 1)
            start = QUARTER * quarter - (tlen - 96)
            values = jnp.concatenate([values, jnp.zeros((8, LANES), jnp.float32)], axis=0)
            values = pltpu.roll(values, start % 8, 0)
            start -= start % 8
            if start < 0:
                values, start = values[8:], 0
            below = LANES - start - values.shape[0]
            if start:
                values = jnp.concatenate([jnp.zeros((start, LANES), jnp.float32), values], axis=0)
            if below > 0:
                values = jnp.concatenate([values, jnp.zeros((below, LANES), jnp.float32)], axis=0)
            heads[place] = heads[place] + jnp.where(mask, values[0:LANES], 0.0)
    for index, (values, code) in enumerate(zip(heads, codes)):
        code = jnp.where(slots * index + ahead < half, code, 0.0)
        deviate = jnp.where(used, values * tlen - jnp.sum(values, axis=0, keepdims=True), 0.0)
        square = jnp.sum(deviate * deviate, axis=0, keepdims=True) * (1.0 / tlen**3)
        unit = deviate / (jnp.sqrt(square + EPSILON) * tlen**2)
        unit = unit.astype(jnp.bfloat16).astype(jnp.float32)
        unit = jnp.where(code > 0, unit, 0.0)
        shift = code.astype(jnp.int32) - 1
        for bit in (1, 2, 4):
            unit = jnp.where(jnp.bitwise_and(shift, bit) > 0, pltpu.roll(unit, bit, 0), unit)
        unit = jnp.where(lag == 112, code, unit)
        bank[index] = unit.astype(jnp.bfloat16)

    def build(number):
        wide = jnp.dot(bank[number], expand[...], preferred_element_type=jnp.float32)
        for slot in range(slots):
            spreaded = wide[:, slot * LANES : (slot + 1) * LANES]
            code = spreaded[112:113, :].astype(jnp.int32)
            shift = code - 1
            moves = shift // 8 + ahead
            taps = spreaded[0:112, :]
            for bit in (1, 2, 4, 8):
                gap = jnp.zeros((8 * bit, LANES), jnp.float32)
                taps = jnp.where(
                    jnp.bitwise_and(moves, bit) > 0,
                    jnp.concatenate([gap, taps], axis=0),
                    jnp.concatenate([taps, gap], axis=0),
                )[0:top]
            taps = taps.astype(jnp.bfloat16)
            item = number * slots + slot
            reach[item] = jnp.maximum(shift, 0) + 8 * ahead + 7 - lag[0:8]
            for tile in range(tile_count):
                skip = 8 * offset_count * tile
                lanes = slice(LANES * tile, LANES * (tile + 1))
                if skip:
                    weight_a[item, 0:skip, lanes] = jnp.zeros((skip, LANES), jnp.bfloat16)
                weight_a[item, skip : skip + top, lanes] = taps
                rest = DEPTH - top - skip
                if rest:
                    weight_a[item, skip + top :, lanes] = jnp.zeros((rest, LANES), jnp.bfloat16)

    def products(item):
        both = [left_a[base + item, 0:rows, :], left_a[base + item, 16 : rows + 16, :]]
        corr = jnp.dot(
            jnp.concatenate(both, axis=1), weight_a[item], preferred_element_type=jnp.float32
        )
        columns = []
        for tile in range(tile_count):
            place = reach[item] + 8 * offset_count * tile
            parts = []
            for step in range(rows // 8):
                window = inverse[step, pl.ds(base + item, 1), :]
                window = jnp.broadcast_to(window, (8, LANES))
                parts.append(jnp.take_along_axis(window, place, axis=1, mode="promise_in_bounds"))
            columns.append(jnp.concatenate(parts, axis=0))
        return corr * jnp.concatenate(columns, axis=1)

    def apply(number, count):
        for item in range(number * slots, number * slots + count, 2):
            value = products(item)
            if item + 1 < number * slots + count:
                value = value + products(item + 1)
            if item:
                value = value + total[...]
            elif side:
                value = value + before[...]
            total[...] = value

    build(0)

    for number in range(1, banks):
        apply(number - 1, slots)
        build(number)

    apply(banks - 1, half - slots * (banks - 1))

    if not side:
        outs[0][...] = total[...]
        return
    rows_out = outs[0].shape[0]
    station = lax.axis_index("sta") // 2
    for step, out in enumerate(outs):
        part = jnp.bitwise_xor(station, len(outs) - 1 - step)
        out[...] = total[pl.ds(pl.multiple_of(part * rows_out, rows_out), rows_out), :].astype(
            jnp.bfloat16
        )


def correlate(side, tlen, group, count, piece, left_a, inverse, *before):
    channels = left_a.shape[0]
    rows = left_a.shape[1] - 16
    width = OFFSETS * group
    half = channels // 2
    if side:
        out = [jax.ShapeDtypeStruct((rows // count, width), jnp.bfloat16)] * count
    else:
        out = [jax.ShapeDtypeStruct((rows, width), jnp.float32)]
    return pl.pallas_call(
        functools.partial(main_kernel, side, tlen, group),
        out_shape=out,
        in_specs=[VMEM] * (3 + len(before)),
        out_specs=[VMEM] * len(out),
        scratch_shapes=[
            pltpu.VMEM(((half + 1) * group // LANES, LANES, LANES), jnp.bfloat16),
            pltpu.VMEM((LANES, LANES // group * LANES), jnp.bfloat16),
            pltpu.VMEM((half + 1, DEPTH, width), jnp.bfloat16),
            pltpu.VMEM((half + 1, 8, LANES), jnp.int32),
            pltpu.VMEM((rows, width), jnp.float32),
        ],
        compiler_params=params(),
        cost_estimate=cost(3),
        name="correlate_" + ("second" if side else "first"),
    )(piece, left_a, inverse, *before)


def add_kernel(*refs):
    parts, keep, send = refs[:-2], refs[-2], refs[-1]
    rows = keep.shape[0]
    core = lax.axis_index("tm") % 2
    for out, which in ((keep, core), (send, 1 - core)):
        place = pl.ds(pl.multiple_of(which * rows, rows), rows)
        value = parts[0][place, :].astype(jnp.float32)
        for part in parts[1:]:
            value = value + part[place, :].astype(jnp.float32)
        out[...] = value


def add(parts):
    rows, width = parts[0].shape
    out = jax.ShapeDtypeStruct((rows // 2, width), jnp.float32)
    return pl.pallas_call(
        add_kernel,
        out_shape=[out, out],
        in_specs=[VMEM] * len(parts),
        out_specs=[VMEM, VMEM],
        compiler_params=params(),
        cost_estimate=cost(0.5),
        name="add",
    )(*parts)


def finish_kernel(group, ours, received, out):
    samples = out.shape[1]
    rows = ours.shape[0]
    value = ours[...] + received[...]
    high = value.astype(jnp.bfloat16).astype(jnp.float32)
    both = jnp.concatenate([high, value - high], axis=0).T.astype(jnp.bfloat16)
    row = lax.broadcasted_iota(jnp.int32, (2 * rows, samples), 0) % rows
    lane = lax.broadcasted_iota(jnp.int32, (2 * rows, samples), 1)
    place = jnp.logical_and(lane // STRIDE == row // 8, lane % 8 == 7 - row % 8)
    place = jnp.where(place, 1.0, 0.0).astype(jnp.bfloat16)
    wide = jnp.dot(both, place, preferred_element_type=jnp.float32)
    lane = lax.broadcasted_iota(jnp.int32, (group, samples), 1) // 8 % OFFSETS
    result = jnp.zeros((group, samples), jnp.float32)
    for offset in range(OFFSETS):
        result = jnp.where(lane == offset, wide[offset * group : (offset + 1) * group], result)
    out[...] = result


def finish(group, samples, ours, received):
    return pl.pallas_call(
        functools.partial(finish_kernel, group),
        out_shape=jax.ShapeDtypeStruct((group, samples), jnp.float32),
        in_specs=[VMEM, VMEM],
        out_specs=VMEM,
        compiler_params=params(),
        cost_estimate=cost(1),
        name="finish",
    )(ours, received)


def shards(waveforms, templates, available, moveout, bank_blocks):
    channels, samples = waveforms.shape
    blocks, events, _, tlen = templates.shape
    count_tm = lax.axis_size("tm")
    count_sta = lax.axis_size("sta")
    chips = count_tm // 2
    near = chips // 2
    group = 2 * events // chips

    def swap(array):
        return lax.ppermute(array, "tm", [(i, i ^ 1) for i in range(count_tm)])

    def across(array, step):
        return lax.ppermute(array, "tm", [(i, i ^ (2 * step)) for i in range(count_tm)])

    partner = swap(waveforms)
    mine, theirs, owners = pack(
        chips,
        group,
        bank_blocks,
        jnp.transpose(templates, (0, 2, 1, 3)),
        jnp.transpose(available, (2, 0, 1)),
        jnp.transpose(moveout, (2, 0, 1)),
    )
    theirs, partner = lax.optimization_barrier((theirs, partner))
    other = swap(theirs)
    pair = pair_waves(waveforms, partner)
    far = []
    for number in range(near - 1):
        steps = (chips - 1 - 2 * number, chips - 2 - 2 * number)
        route = [(2 * z + c, 2 * (z ^ steps[c]) + c) for z in range(chips) for c in range(2)]
        far.append(lax.ppermute(pair, "tm", route))
    beside = across(waveforms, 1)
    merged = list(merge(owners, mine, other))
    pieces = [across(merged[step], step) for step in reversed(range(1, chips))]
    pieces = [merged[0]] + pieces[::-1]
    swapped = swap(choose_waves(pair, beside, far))
    left_a, inverse = prepare_waves(tlen, swapped, pair, beside, far)

    order = sorted(range(chips), key=lambda step: (step < 2, step))
    placed = lax.optimization_barrier((left_a, inverse, *[pieces[step] for step in order]))
    left_a, inverse = placed[:2]
    pieces = [placed[2 + order.index(step)] for step in range(chips)]
    first = choose_piece(owners, pieces)
    second = swap(first)
    total = correlate(0, tlen, group, near, first, left_a, inverse)
    parts = correlate(1, tlen, group, near, second, left_a, inverse, *total)
    gathered = []
    for step in range(near):
        route = []
        for d in range(count_tm):
            for s in range(count_sta):
                dest = near * (d % 2) + (s // 2 ^ (near - 1 - step))
                route.append((d * count_sta + s, (2 * dest + s % 2) * count_sta + d // 2))
        gathered.append(lax.ppermute(parts[step], ("tm", "sta"), route))
    ours, send = add(gathered)
    return finish(group, samples, ours, swap(send))


def solution(mesh):
    in_specs = (
        P("sta", "tm"),
        P("tm", None, "sta", None),
        P("tm", None, "sta"),
        P("tm", None, "sta"),
        P(),
    )
    out_specs = P("sta", "tm")
    return jax.shard_map(shards, mesh=mesh, in_specs=in_specs, out_specs=out_specs, check_vma=False)
```

```python
import functools

import jax
import jax.numpy as jnp
from jax import lax
from jax.experimental import pallas as pl
from jax.experimental.pallas import tpu as pltpu
from jax.sharding import PartitionSpec as P

EPSILON = 1e-06
LANES = 128
OFFSETS = 8
TILES = 12
QUARTER = 25
STRIDE = 64
DEPTH = 256
VMEM_LIMIT = 28 * 1024 * 1024

VMEM = pl.BlockSpec(memory_space=pltpu.VMEM)
ANY = pl.BlockSpec(memory_space=pl.ANY)


def params():
    return pltpu.CompilerParams(vmem_limit_bytes=VMEM_LIMIT)


def cost(micros):
    return pl.CostEstimate(
        flops=int(micros * 1e9), bytes_accessed=int(micros * 1e6), transcendentals=0
    )


def pack_kernel(bank_blocks, templates, available, moveout, mine, theirs, owners, chosen, raw, usable, shifts, square, sems):
    blocks, channels, events, tlen = templates.shape
    chips, _, group, _ = mine.shape
    half = channels // 2
    me = lax.axis_index("tm") % 2
    fetch = [
        pltpu.make_async_copy(source, target, sems.at[index])
        for index, (source, target) in enumerate(
            ((bank_blocks, chosen), (available, usable), (moveout, shifts))
        )
    ]
    for side in (1, 0):
        first = half * jnp.where(me == side, 0, 1)
        for block in range(blocks):
            place = (block, pl.ds(first, half))
            number = 3 + blocks * (1 - side) + block
            fetch.append(
                pltpu.make_async_copy(templates.at[place], raw.at[place], sems.at[number])
            )
    for copy in fetch:
        copy.start()
    mine[...] = jnp.zeros_like(mine)
    theirs[...] = jnp.zeros_like(theirs)
    square[...] = jnp.zeros_like(square)
    for copy in fetch[:3]:
        copy.wait()
    slots = [chosen[which] % blocks for which in range(2)]
    row = lax.broadcasted_iota(jnp.int32, owners.shape, 0)
    owners[...] = jnp.where(row == 0, chosen[0] // blocks, chosen[1] // blocks)
    flags = jnp.where(usable[...] > 0, shifts[...] + 1, 0).astype(jnp.float32)
    codes = []
    for which in range(2):
        code = flags[:, 0, :]
        for block in range(1, blocks):
            code = jnp.where(slots[which] == block, flags[:, block, :], code)
        square[0:channels, 0:events] = code
        turned = square[...].T
        later = pltpu.roll(turned, LANES - half, 1)
        codes.append([jnp.where(me == core, turned, later) for core in range(2)])
    for side, out in ((1, theirs), (0, mine)):
        for block in range(blocks):
            fetch[3 + blocks * (1 - side) + block].wait()
        for which in range(2):
            first = half * jnp.where(me == side, 0, 1)
            code = codes[which][side].astype(jnp.bfloat16)
            for tile in range(TILES):
                extra = TILES + tile // 4
                start = QUARTER * (tile % 4)
                for index in range(events // group):
                    chip = which * (events // group) + index
                    rows = slice(index * group, (index + 1) * group)
                    out[chip, tile, :, 0:tlen] = raw[slots[which], first + tile, rows, :]
                    out[chip, tile, :, tlen : tlen + QUARTER] = raw[
                        slots[which], first + extra, rows, start : start + QUARTER
                    ]
                    out[chip, tile, :, 125:126] = code[rows, tile : tile + 1]
                    if tile < half - TILES:
                        beyond = TILES + tile
                        out[chip, tile, :, 126:127] = code[rows, beyond : beyond + 1]


def pack(chips, group, bank_blocks, templates, available, moveout):
    shape = (chips, TILES, group, LANES)
    held = [
        pltpu.with_memory_space_constraint(array, pltpu.HBM)
        for array in (bank_blocks, templates, available, moveout)
    ]
    return pl.pallas_call(
        pack_kernel,
        out_shape=[jax.ShapeDtypeStruct(shape, jnp.bfloat16)] * 2
        + [jax.ShapeDtypeStruct((8, LANES), jnp.int32)],
        in_specs=[ANY] * 4,
        out_specs=[VMEM] * 3,
        scratch_shapes=[
            pltpu.SMEM(bank_blocks.shape, jnp.int32),
            pltpu.VMEM(templates.shape, jnp.bfloat16),
            pltpu.VMEM(available.shape, jnp.int32),
            pltpu.VMEM(moveout.shape, jnp.int32),
            pltpu.VMEM((LANES, LANES), jnp.float32),
            pltpu.SemaphoreType.DMA((3 + 2 * templates.shape[0],)),
        ],
        compiler_params=params(),
        cost_estimate=cost(2),
        name="pack",
    )(*held)


def merge_kernel(owners, mine, other, *outs):
    chips = len(outs)
    me = lax.axis_index("tm")
    for step, out in enumerate(outs):
        dest = jnp.bitwise_xor(me // 2, step)
        owner = jnp.where(dest < chips // 2, owners[0, 0], owners[1, 0])
        here = owner % 2 == me % 2

        @pl.when(here)
        def _():
            out[...] = mine[dest]

        @pl.when(jnp.logical_not(here))
        def _():
            out[...] = other[dest]


def merge(owners, mine, other):
    chips = mine.shape[0]
    return pl.pallas_call(
        merge_kernel,
        out_shape=[jax.ShapeDtypeStruct(mine.shape[1:], mine.dtype)] * chips,
        in_specs=[VMEM] * 3,
        out_specs=[VMEM] * chips,
        compiler_params=params(),
        cost_estimate=cost(0.3),
        name="merge",
    )(owners, mine, other)


def lagged(row, ahead):
    copies = jnp.broadcast_to(row, (8, row.shape[1]))
    return pltpu.roll(copies, row.shape[1] - 7 - ahead, 1, stride=1, stride_axis=0)


def segment(me, other, parity, pair, beside, far, default):
    chip, core = me // 2, me % 2
    chips = 2 * len(far) + 2
    step = jnp.bitwise_xor(chip, other)
    value = default[...]
    value = jnp.where(jnp.logical_and(step == 1, core == parity), beside[...], value)
    value = jnp.where(step == 0, pair[parity], value)
    for number, array in enumerate(far):
        value = jnp.where(step == chips - 1 - 2 * number - core, array[parity], value)
    return value


def pair_kernel(own, partner, out):
    core = lax.axis_index("tm") % 2
    out[core] = own[...]
    out[1 - core] = partner[...]


def pair_waves(own, partner):
    return pl.pallas_call(
        pair_kernel,
        out_shape=jax.ShapeDtypeStruct((2,) + own.shape, own.dtype),
        in_specs=[VMEM] * 2,
        out_specs=VMEM,
        compiler_params=params(),
        cost_estimate=cost(0.05),
        name="pair_waves",
    )(own, partner)


def choose_kernel(pair, beside, *rest):
    far, out = rest[:-1], rest[-1]
    near = out.shape[0] - 1
    me = lax.axis_index("tm")
    chip, core = me // 2, me % 2
    for entry in range(near):
        number, parity = divmod(entry, 2)
        step = jnp.bitwise_xor(chip, near * (1 - core) + 2 * number) // 2
        value = beside[...]
        for place, array in enumerate(far):
            value = jnp.where(step == near - 1 - place, array[parity], value)
        out[entry] = value
    out[near] = segment(me, near, 0, pair, beside, far, beside)


def choose_waves(pair, beside, far):
    return pl.pallas_call(
        choose_kernel,
        out_shape=jax.ShapeDtypeStruct((len(far) + 2,) + beside.shape, beside.dtype),
        in_specs=[VMEM] * (2 + len(far)),
        out_specs=VMEM,
        compiler_params=params(),
        cost_estimate=cost(0.05),
        name="choose_waves",
    )(pair, beside, *far)


def own_kernel(owners, *refs):
    pieces, out = refs[:-1], refs[-1]
    chip = lax.axis_index("tm") // 2
    owner = jnp.where(chip < len(pieces) // 2, owners[0, 0], owners[1, 0])
    source = jnp.bitwise_xor(owner // 2, chip)
    value = pieces[0][...]
    for number, piece in enumerate(pieces[1:], 1):
        value = jnp.where(source == number, piece[...], value)
    out[...] = value


def choose_piece(owners, pieces):
    return pl.pallas_call(
        own_kernel,
        out_shape=jax.ShapeDtypeStruct(pieces[0].shape, pieces[0].dtype),
        in_specs=[VMEM] * (1 + len(pieces)),
        out_specs=VMEM,
        compiler_params=params(),
        cost_estimate=cost(0.3),
        name="choose_piece",
    )(owners, *pieces)


def waves_kernel(channels, tlen, unroll, swapped, pair, beside, *rest):
    far = rest[:-5]
    left_a, inverse, expand, place, padded = rest[-5:]
    samples = beside.shape[1]
    near = swapped.shape[0] - 1
    length = 2 * near * samples
    count = padded.shape[1] // LANES
    me = lax.axis_index("tm")
    core = me % 2
    padded[...] = jnp.zeros_like(padded)
    for index in range(2 * near):
        entry, parity = divmod(index, 2)
        given = swapped.at[2 * (entry // 2) + parity]
        wave = segment(me, near * core + entry, parity, pair, beside, far, given)
        padded[0:channels, samples * index : samples * (index + 1)] = wave.astype(jnp.float32)
    rim = segment(me, near * core + near, 0, pair, beside, far, swapped.at[near])
    rim = rim[:, 0 : padded.shape[1] - length].astype(jnp.float32)
    padded[0:channels, length:] = jnp.where(core == 0, rim, 0.0)

    group = expand.shape[1] // LANES
    group = LANES // group
    row = lax.broadcasted_iota(jnp.int32, expand.shape, 0)
    lane = lax.broadcasted_iota(jnp.int32, expand.shape, 1)
    chosen = row == lane % group + lane // LANES * group
    expand[...] = jnp.where(chosen, 1.0, 0.0).astype(jnp.bfloat16)
    row = lax.broadcasted_iota(jnp.int32, place.shape, 0) % (place.shape[0] // 2)
    lane = lax.broadcasted_iota(jnp.int32, place.shape, 1)
    chosen = jnp.logical_and(lane // STRIDE == row // 8, lane % 8 == 7 - row % 8)
    place[...] = jnp.where(chosen, 1.0, 0.0).astype(jnp.bfloat16)

    rows = 32 * count
    values = [padded[:, LANES * tile : LANES * (tile + 1)] for tile in range(count)]
    values = jnp.concatenate(values + [jnp.zeros((32, LANES), jnp.float32)], axis=0)
    square = values * values
    high = square.astype(jnp.bfloat16)
    low = (square - high.astype(jnp.float32)).astype(jnp.bfloat16)
    values = values.astype(jnp.bfloat16)
    lag = lax.broadcasted_iota(jnp.int32, (2 * LANES, LANES), 0)
    lag = lag - lax.broadcasted_iota(jnp.int32, (2 * LANES, LANES), 1)
    band = jnp.where(jnp.logical_and(lag >= 0, lag < tlen), 1.0, 0.0).astype(jnp.bfloat16)

    def windows(array):
        both = jnp.concatenate([array[0:rows], array[32 : rows + 32]], axis=1)
        return jnp.dot(both, band, preferred_element_type=jnp.float32)

    first_sum = windows(values)
    second_sum = windows(high) + windows(low)
    variance = (second_sum * tlen - first_sum * first_sum) * (1.0 / tlen**2)
    scale = lax.rsqrt(variance + EPSILON)
    for tile in range(length // LANES):
        part = scale[32 * tile : 32 * (tile + 1)]
        after = scale[32 * (tile + 1) : 32 * (tile + 2)]
        inverse[2 * tile] = part
        lane = lax.broadcasted_iota(jnp.int32, part.shape, 1)
        both = jnp.where(lane < STRIDE, after, part)
        inverse[2 * tile + 1] = pltpu.roll(both, LANES - STRIDE, 1)

    def interleaved(row, tiles):
        even, odd = lagged(row, 0), lagged(row, STRIDE)
        parts = []
        for tile in range(tiles):
            lanes = slice(LANES * tile, LANES * (tile + 1))
            parts += [even[:, lanes], odd[:, lanes]]
        return jnp.concatenate(parts, axis=0)

    @pl.loop(0, channels // unroll)
    def _(step):
        for item in range(unroll):
            channel = step * unroll + item
            value = interleaved(padded[pl.ds(channel, 1), :], length // LANES + 1)
            left_a[channel] = value.astype(jnp.bfloat16)


def prepare_waves(tlen, group, swapped, pair, beside, far):
    channels, samples = beside.shape
    length = 2 * (swapped.shape[0] - 1) * samples
    rows = length // OFFSETS
    unroll = max(step for step in (1, 2, 3) if channels % step == 0)
    return pl.pallas_call(
        functools.partial(waves_kernel, channels, tlen, unroll),
        out_shape=[
            jax.ShapeDtypeStruct((channels, rows + 16, LANES), jnp.bfloat16),
            jax.ShapeDtypeStruct((length // STRIDE, 32, LANES), jnp.float32),
            jax.ShapeDtypeStruct((LANES, LANES // group * LANES), jnp.bfloat16),
            jax.ShapeDtypeStruct((2 * samples // OFFSETS, samples), jnp.bfloat16),
        ],
        in_specs=[VMEM] * (3 + len(far)),
        out_specs=[VMEM] * 4,
        scratch_shapes=[
            pltpu.VMEM((32, length + 2 * LANES), jnp.float32),
        ],
        compiler_params=params(),
        cost_estimate=cost(0.05),
        name="prepare_waves",
    )(swapped, pair, beside, *far)


def main_kernel(side, tlen, group, piece, left_a, inverse, expand, *rest):
    outs = rest[:-4]
    if side:
        before, outs = outs[0], outs[1:]
    bank, weight_a, reach, total = rest[-4:]
    core = lax.axis_index("tm") % 2
    channels = left_a.shape[0]
    rows = left_a.shape[1] - 16
    half = channels // 2
    base = half * jnp.where(core == side, 0, 1)
    slots = LANES // group
    banks = (half + 1) // slots
    offset_count = LANES // group
    tile_count = OFFSETS // offset_count
    top = 112 + 8 * (7 + offset_count - 1)
    top = top + top % 16

    lag = lax.broadcasted_iota(jnp.int32, (LANES, LANES), 0)
    lane = lax.broadcasted_iota(jnp.int32, (1, LANES), 1)
    used = lag < tlen
    ahead = lane // group
    turned = []
    for index in range(banks):
        count = min(slots, max(TILES - slots * index, 0))
        values = jnp.zeros((LANES, LANES), jnp.float32)
        if count:
            values = piece[slots * index : slots * index + count].astype(jnp.float32)
            values = values.reshape(count * group, LANES)
            if count < slots:
                gap = jnp.zeros((LANES - count * group, LANES), jnp.float32)
                values = jnp.concatenate([values, gap], axis=0)
            values = values.T
        turned.append(values)
    codes = [values[125:126, :] for values in turned]
    heads = [jnp.where(used, values, 0.0) for values in turned]
    for extra in range(half - TILES):
        place, slot = divmod(TILES + extra, slots)
        mask = ahead == slot
        code = pltpu.roll(turned[0][126:127, :], (slot - extra) * group % LANES, 1)
        codes[place] = jnp.where(mask, code, codes[place])
        for quarter in range(4):
            source, lanes = divmod(4 * extra + quarter, slots)
            values = turned[source][96:128]
            sample = lag[96:128]
            inside = jnp.logical_and(sample >= tlen, sample < tlen + QUARTER)
            values = jnp.where(inside, values, 0.0)
            values = pltpu.roll(values, (slot - lanes) * group % LANES, 1)
            start = QUARTER * quarter - (tlen - 96)
            values = jnp.concatenate([values, jnp.zeros((8, LANES), jnp.float32)], axis=0)
            values = pltpu.roll(values, start % 8, 0)
            start -= start % 8
            if start < 0:
                values, start = values[8:], 0
            below = LANES - start - values.shape[0]
            if start:
                values = jnp.concatenate([jnp.zeros((start, LANES), jnp.float32), values], axis=0)
            if below > 0:
                values = jnp.concatenate([values, jnp.zeros((below, LANES), jnp.float32)], axis=0)
            heads[place] = heads[place] + jnp.where(mask, values[0:LANES], 0.0)
    for index, (values, code) in enumerate(zip(heads, codes)):
        code = jnp.where(slots * index + ahead < half, code, 0.0)
        deviate = jnp.where(used, values * tlen - jnp.sum(values, axis=0, keepdims=True), 0.0)
        square = jnp.sum(deviate * deviate, axis=0, keepdims=True) * (1.0 / tlen**3)
        unit = deviate / (jnp.sqrt(square + EPSILON) * tlen**2)
        unit = unit.astype(jnp.bfloat16).astype(jnp.float32)
        unit = jnp.where(code > 0, unit, 0.0)
        shift = code.astype(jnp.int32) - 1
        for bit in (1, 2, 4):
            unit = jnp.where(jnp.bitwise_and(shift, bit) > 0, pltpu.roll(unit, bit, 0), unit)
        unit = jnp.where(lag == 112, code, unit)
        bank[index] = unit.astype(jnp.bfloat16)

    def build(number):
        wide = jnp.dot(bank[number], expand[...], preferred_element_type=jnp.float32)
        for slot in range(slots):
            spreaded = wide[:, slot * LANES : (slot + 1) * LANES]
            code = spreaded[112:113, :].astype(jnp.int32)
            shift = code - 1
            moves = shift // 8 + ahead
            taps = spreaded[0:112, :]
            for bit in (1, 2, 4, 8):
                gap = jnp.zeros((8 * bit, LANES), jnp.float32)
                taps = jnp.where(
                    jnp.bitwise_and(moves, bit) > 0,
                    jnp.concatenate([gap, taps], axis=0),
                    jnp.concatenate([taps, gap], axis=0),
                )[0:top]
            taps = taps.astype(jnp.bfloat16)
            item = number * slots + slot
            reach[item] = jnp.maximum(shift, 0) + 8 * ahead + 7 - lag[0:8]
            for tile in range(tile_count):
                skip = 8 * offset_count * tile
                lanes = slice(LANES * tile, LANES * (tile + 1))
                if skip:
                    weight_a[item, 0:skip, lanes] = jnp.zeros((skip, LANES), jnp.bfloat16)
                weight_a[item, skip : skip + top, lanes] = taps
                rest = DEPTH - top - skip
                if rest:
                    weight_a[item, skip + top :, lanes] = jnp.zeros((rest, LANES), jnp.bfloat16)

    def products(item):
        both = [left_a[base + item, 0:rows, :], left_a[base + item, 16 : rows + 16, :]]
        corr = jnp.dot(
            jnp.concatenate(both, axis=1), weight_a[item], preferred_element_type=jnp.float32
        )
        columns = []
        for tile in range(tile_count):
            place = reach[item] + 8 * offset_count * tile
            parts = []
            for step in range(rows // 8):
                window = inverse[step, pl.ds(base + item, 1), :]
                window = jnp.broadcast_to(window, (8, LANES))
                parts.append(jnp.take_along_axis(window, place, axis=1, mode="promise_in_bounds"))
            columns.append(jnp.concatenate(parts, axis=0))
        return corr * jnp.concatenate(columns, axis=1)

    def apply(number, count):
        for item in range(number * slots, number * slots + count, 2):
            value = products(item)
            if item + 1 < number * slots + count:
                value = value + products(item + 1)
            if item:
                value = value + total[...]
            elif side:
                value = value + before[...]
            total[...] = value

    build(0)

    for number in range(1, banks):
        apply(number - 1, slots)
        build(number)

    apply(banks - 1, half - slots * (banks - 1))

    if not side:
        outs[0][...] = total[...]
        return
    rows_out = outs[0].shape[0]
    station = lax.axis_index("sta") // 2
    for step, out in enumerate(outs):
        part = jnp.bitwise_xor(station, step)
        out[...] = total[pl.ds(pl.multiple_of(part * rows_out, rows_out), rows_out), :].astype(
            jnp.bfloat16
        )


def correlate(side, tlen, group, count, piece, left_a, inverse, expand, *before):
    channels = left_a.shape[0]
    rows = left_a.shape[1] - 16
    width = OFFSETS * group
    half = channels // 2
    if side:
        out = [jax.ShapeDtypeStruct((rows // count, width), jnp.bfloat16)] * count
    else:
        out = [jax.ShapeDtypeStruct((rows, width), jnp.float32)]
    return pl.pallas_call(
        functools.partial(main_kernel, side, tlen, group),
        out_shape=out,
        in_specs=[VMEM] * (4 + len(before)),
        out_specs=[VMEM] * len(out),
        scratch_shapes=[
            pltpu.VMEM(((half + 1) * group // LANES, LANES, LANES), jnp.bfloat16),
            pltpu.VMEM((half + 1, DEPTH, width), jnp.bfloat16),
            pltpu.VMEM((half + 1, 8, LANES), jnp.int32),
            pltpu.VMEM((rows, width), jnp.float32),
        ],
        compiler_params=params(),
        cost_estimate=cost(3),
        name="correlate_" + ("second" if side else "first"),
    )(piece, left_a, inverse, expand, *before)


def add_kernel(*refs):
    parts, keep, send = refs[:-2], refs[-2], refs[-1]
    rows = keep.shape[0]
    core = lax.axis_index("tm") % 2
    for out, which in ((keep, core), (send, 1 - core)):
        place = pl.ds(pl.multiple_of(which * rows, rows), rows)
        value = parts[0][place, :].astype(jnp.float32)
        for part in parts[1:]:
            value = value + part[place, :].astype(jnp.float32)
        out[...] = value


def add(parts):
    rows, width = parts[0].shape
    out = jax.ShapeDtypeStruct((rows // 2, width), jnp.float32)
    return pl.pallas_call(
        add_kernel,
        out_shape=[out, out],
        in_specs=[VMEM] * len(parts),
        out_specs=[VMEM, VMEM],
        compiler_params=params(),
        cost_estimate=cost(0.5),
        name="add",
    )(*parts)


def finish_kernel(group, ours, received, place, out):
    samples = out.shape[1]
    value = ours[...] + received[...]
    high = value.astype(jnp.bfloat16).astype(jnp.float32)
    both = jnp.concatenate([high, value - high], axis=0).T.astype(jnp.bfloat16)
    wide = jnp.dot(both, place[...], preferred_element_type=jnp.float32)
    lane = lax.broadcasted_iota(jnp.int32, (group, samples), 1) // 8 % OFFSETS
    result = jnp.zeros((group, samples), jnp.float32)
    for offset in range(OFFSETS):
        result = jnp.where(lane == offset, wide[offset * group : (offset + 1) * group], result)
    out[...] = result


def finish(group, samples, ours, received, place):
    return pl.pallas_call(
        functools.partial(finish_kernel, group),
        out_shape=jax.ShapeDtypeStruct((group, samples), jnp.float32),
        in_specs=[VMEM] * 3,
        out_specs=VMEM,
        compiler_params=params(),
        cost_estimate=cost(1),
        name="finish",
    )(ours, received, place)


def shards(waveforms, templates, available, moveout, bank_blocks):
    channels, samples = waveforms.shape
    blocks, events, _, tlen = templates.shape
    count_tm = lax.axis_size("tm")
    count_sta = lax.axis_size("sta")
    chips = count_tm // 2
    near = chips // 2
    group = 2 * events // chips

    def swap(array):
        return lax.ppermute(array, "tm", [(i, i ^ 1) for i in range(count_tm)])

    def across(array, step):
        return lax.ppermute(array, "tm", [(i, i ^ (2 * step)) for i in range(count_tm)])

    partner = swap(waveforms)
    mine, theirs, owners = pack(
        chips,
        group,
        bank_blocks,
        jnp.transpose(templates, (0, 2, 1, 3)),
        jnp.transpose(available, (2, 0, 1)),
        jnp.transpose(moveout, (2, 0, 1)),
    )
    theirs, partner = lax.optimization_barrier((theirs, partner))
    other = swap(theirs)
    pair = pair_waves(waveforms, partner)
    far = []
    for number in range(near - 1):
        steps = (chips - 1 - 2 * number, chips - 2 - 2 * number)
        route = [(2 * z + c, 2 * (z ^ steps[c]) + c) for z in range(chips) for c in range(2)]
        far.append(lax.ppermute(pair, "tm", route))
    beside = across(waveforms, 1)
    merged = list(merge(owners, mine, other))
    pieces = [across(merged[step], step) for step in reversed(range(1, chips))]
    pieces = [merged[0]] + pieces[::-1]
    swapped = swap(choose_waves(pair, beside, far))
    left_a, inverse, expand, place = prepare_waves(tlen, group, swapped, pair, beside, far)

    order = sorted(range(chips), key=lambda step: (step < 2, step))
    placed = lax.optimization_barrier((left_a, inverse, *[pieces[step] for step in order]))
    left_a, inverse = placed[:2]
    pieces = [placed[2 + order.index(step)] for step in range(chips)]
    first = choose_piece(owners, pieces)
    second = swap(first)
    total = correlate(0, tlen, group, near, first, left_a, inverse, expand)
    parts = correlate(1, tlen, group, near, second, left_a, inverse, expand, *total)
    gathered = []
    for step in range(near):
        route = []
        for d in range(count_tm):
            for s in range(count_sta):
                dest = near * (d % 2) + (s // 2 ^ step)
                route.append((d * count_sta + s, (2 * dest + s % 2) * count_sta + d // 2))
        gathered.append(lax.ppermute(parts[step], ("tm", "sta"), route))
    ours, send = add(gathered)
    return finish(group, samples, ours, swap(send), place)


def solution(mesh):
    in_specs = (
        P("sta", "tm"),
        P("tm", None, "sta", None),
        P("tm", None, "sta"),
        P("tm", None, "sta"),
        P(),
    )
    out_specs = P("sta", "tm")
    return jax.shard_map(shards, mesh=mesh, in_specs=in_specs, out_specs=out_specs, check_vma=False)
```

```python
import functools

import jax
import jax.numpy as jnp
from jax import lax
from jax.experimental import pallas as pl
from jax.experimental.pallas import tpu as pltpu
from jax.sharding import PartitionSpec as P

EPSILON = 1e-06
LANES = 128
OFFSETS = 8
TILES = 12
QUARTER = 25
STRIDE = 64
DEPTH = 256
VMEM_LIMIT = 28 * 1024 * 1024

VMEM = pl.BlockSpec(memory_space=pltpu.VMEM)
ANY = pl.BlockSpec(memory_space=pl.ANY)


def params():
    return pltpu.CompilerParams(vmem_limit_bytes=VMEM_LIMIT)


def cost(micros):
    return pl.CostEstimate(
        flops=int(micros * 1e9), bytes_accessed=int(micros * 1e6), transcendentals=0
    )


def pack_kernel(bank_blocks, templates, available, moveout, mine, theirs, owners, chosen, raw, usable, shifts, square, sems):
    blocks, channels, events, tlen = templates.shape
    chips, _, group, _ = mine.shape
    half = channels // 2
    me = lax.axis_index("tm") % 2
    fetch = [
        pltpu.make_async_copy(source, target, sems.at[index])
        for index, (source, target) in enumerate(
            ((bank_blocks, chosen), (available, usable), (moveout, shifts))
        )
    ]
    for side in (1, 0):
        first = half * jnp.where(me == side, 0, 1)
        for block in range(blocks):
            place = (block, pl.ds(first, half))
            number = 3 + blocks * (1 - side) + block
            fetch.append(
                pltpu.make_async_copy(templates.at[place], raw.at[place], sems.at[number])
            )
    for copy in fetch:
        copy.start()
    mine[...] = jnp.zeros_like(mine)
    theirs[...] = jnp.zeros_like(theirs)
    square[...] = jnp.zeros_like(square)
    for copy in fetch[:3]:
        copy.wait()
    slots = [chosen[which] % blocks for which in range(2)]
    row = lax.broadcasted_iota(jnp.int32, owners.shape, 0)
    owners[...] = jnp.where(row == 0, chosen[0] // blocks, chosen[1] // blocks)
    flags = jnp.where(usable[...] > 0, shifts[...] + 1, 0).astype(jnp.float32)
    codes = []
    for which in range(2):
        code = flags[:, 0, :]
        for block in range(1, blocks):
            code = jnp.where(slots[which] == block, flags[:, block, :], code)
        square[0:channels, 0:events] = code
        turned = square[...].T
        later = pltpu.roll(turned, LANES - half, 1)
        codes.append([jnp.where(me == core, turned, later) for core in range(2)])
    for side, out in ((1, theirs), (0, mine)):
        for block in range(blocks):
            fetch[3 + blocks * (1 - side) + block].wait()
        for which in range(2):
            first = half * jnp.where(me == side, 0, 1)
            code = codes[which][side].astype(jnp.bfloat16)
            for tile in range(TILES):
                extra = TILES + tile // 4
                start = QUARTER * (tile % 4)
                for index in range(events // group):
                    chip = which * (events // group) + index
                    rows = slice(index * group, (index + 1) * group)
                    out[chip, tile, :, 0:tlen] = raw[slots[which], first + tile, rows, :]
                    out[chip, tile, :, tlen : tlen + QUARTER] = raw[
                        slots[which], first + extra, rows, start : start + QUARTER
                    ]
                    out[chip, tile, :, 125:126] = code[rows, tile : tile + 1]
                    if tile < half - TILES:
                        beyond = TILES + tile
                        out[chip, tile, :, 126:127] = code[rows, beyond : beyond + 1]


def pack(chips, group, bank_blocks, templates, available, moveout):
    shape = (chips, TILES, group, LANES)
    held = [
        pltpu.with_memory_space_constraint(array, pltpu.HBM)
        for array in (bank_blocks, templates, available, moveout)
    ]
    return pl.pallas_call(
        pack_kernel,
        out_shape=[jax.ShapeDtypeStruct(shape, jnp.bfloat16)] * 2
        + [jax.ShapeDtypeStruct((8, LANES), jnp.int32)],
        in_specs=[ANY] * 4,
        out_specs=[VMEM] * 3,
        scratch_shapes=[
            pltpu.SMEM(bank_blocks.shape, jnp.int32),
            pltpu.VMEM(templates.shape, jnp.bfloat16),
            pltpu.VMEM(available.shape, jnp.int32),
            pltpu.VMEM(moveout.shape, jnp.int32),
            pltpu.VMEM((LANES, LANES), jnp.float32),
            pltpu.SemaphoreType.DMA((3 + 2 * templates.shape[0],)),
        ],
        compiler_params=params(),
        cost_estimate=cost(2),
        name="pack",
    )(*held)


def step_of(number, chips, core):
    if number < 2:
        return number
    pair, second = divmod(number - 2, 2)
    high = chips - 1 - 2 * pair
    return high - 1 + core if second else high - core


def merge_kernel(owners, mine, other, *outs):
    chips = len(outs)
    me = lax.axis_index("tm")
    for number, out in enumerate(outs):
        dest = jnp.bitwise_xor(me // 2, step_of(number, chips, me % 2))
        owner = jnp.where(dest < chips // 2, owners[0, 0], owners[1, 0])
        here = owner % 2 == me % 2

        @pl.when(here)
        def _():
            out[...] = mine[dest]

        @pl.when(jnp.logical_not(here))
        def _():
            out[...] = other[dest]


def merge(owners, mine, other):
    chips = mine.shape[0]
    return pl.pallas_call(
        merge_kernel,
        out_shape=[jax.ShapeDtypeStruct(mine.shape[1:], mine.dtype)] * chips,
        in_specs=[VMEM] * 3,
        out_specs=[VMEM] * chips,
        compiler_params=params(),
        cost_estimate=cost(0.3),
        name="merge",
    )(owners, mine, other)


def lagged(row, ahead):
    copies = jnp.broadcast_to(row, (8, row.shape[1]))
    return pltpu.roll(copies, row.shape[1] - 7 - ahead, 1, stride=1, stride_axis=0)


def segment(me, other, parity, pair, beside, far, default):
    chip, core = me // 2, me % 2
    chips = 2 * len(far) + 2
    step = jnp.bitwise_xor(chip, other)
    value = default[...]
    value = jnp.where(jnp.logical_and(step == 1, core == parity), beside[...], value)
    value = jnp.where(step == 0, pair[parity], value)
    for number, array in enumerate(far):
        value = jnp.where(step == chips - 1 - 2 * number - core, array[parity], value)
    return value


def pair_kernel(own, partner, out):
    core = lax.axis_index("tm") % 2
    out[core] = own[...]
    out[1 - core] = partner[...]


def pair_waves(own, partner):
    return pl.pallas_call(
        pair_kernel,
        out_shape=jax.ShapeDtypeStruct((2,) + own.shape, own.dtype),
        in_specs=[VMEM] * 2,
        out_specs=VMEM,
        compiler_params=params(),
        cost_estimate=cost(0.05),
        name="pair_waves",
    )(own, partner)


def choose_kernel(pair, beside, *rest):
    far, out = rest[:-1], rest[-1]
    near = out.shape[0] - 1
    me = lax.axis_index("tm")
    chip, core = me // 2, me % 2
    for entry in range(near):
        number, parity = divmod(entry, 2)
        step = jnp.bitwise_xor(chip, near * (1 - core) + 2 * number) // 2
        value = beside[...]
        for place, array in enumerate(far):
            value = jnp.where(step == near - 1 - place, array[parity], value)
        out[entry] = value
    out[near] = segment(me, near, 0, pair, beside, far, beside)


def choose_waves(pair, beside, far):
    return pl.pallas_call(
        choose_kernel,
        out_shape=jax.ShapeDtypeStruct((len(far) + 2,) + beside.shape, beside.dtype),
        in_specs=[VMEM] * (2 + len(far)),
        out_specs=VMEM,
        compiler_params=params(),
        cost_estimate=cost(0.05),
        name="choose_waves",
    )(pair, beside, *far)


def own_kernel(owners, *refs):
    pieces, out = refs[:-1], refs[-1]
    me = lax.axis_index("tm")
    chip, chips = me // 2, len(pieces)
    owner = jnp.where(chip < chips // 2, owners[0, 0], owners[1, 0])
    source = jnp.bitwise_xor(owner // 2, chip)
    value = pieces[0][...]
    for number, piece in enumerate(pieces[1:], 1):
        value = jnp.where(source == step_of(number, chips, me % 2), piece[...], value)
    out[...] = value


def choose_piece(owners, pieces):
    return pl.pallas_call(
        own_kernel,
        out_shape=jax.ShapeDtypeStruct(pieces[0].shape, pieces[0].dtype),
        in_specs=[VMEM] * (1 + len(pieces)),
        out_specs=VMEM,
        compiler_params=params(),
        cost_estimate=cost(0.3),
        name="choose_piece",
    )(owners, *pieces)


def waves_kernel(channels, tlen, unroll, swapped, pair, beside, *rest):
    far = rest[:-5]
    left_a, inverse, expand, place, padded = rest[-5:]
    samples = beside.shape[1]
    near = swapped.shape[0] - 1
    length = 2 * near * samples
    count = padded.shape[1] // LANES
    me = lax.axis_index("tm")
    core = me % 2
    padded[...] = jnp.zeros_like(padded)
    for index in range(2 * near):
        entry, parity = divmod(index, 2)
        given = swapped.at[2 * (entry // 2) + parity]
        wave = segment(me, near * core + entry, parity, pair, beside, far, given)
        padded[0:channels, samples * index : samples * (index + 1)] = wave.astype(jnp.float32)
    rim = segment(me, near * core + near, 0, pair, beside, far, swapped.at[near])
    rim = rim[:, 0 : padded.shape[1] - length].astype(jnp.float32)
    padded[0:channels, length:] = jnp.where(core == 0, rim, 0.0)

    group = expand.shape[1] // LANES
    group = LANES // group
    row = lax.broadcasted_iota(jnp.int32, expand.shape, 0)
    lane = lax.broadcasted_iota(jnp.int32, expand.shape, 1)
    chosen = row == lane % group + lane // LANES * group
    expand[...] = jnp.where(chosen, 1.0, 0.0).astype(jnp.bfloat16)
    row = lax.broadcasted_iota(jnp.int32, place.shape, 0) % (place.shape[0] // 2)
    lane = lax.broadcasted_iota(jnp.int32, place.shape, 1)
    chosen = jnp.logical_and(lane // STRIDE == row // 8, lane % 8 == 7 - row % 8)
    place[...] = jnp.where(chosen, 1.0, 0.0).astype(jnp.bfloat16)

    rows = 32 * count
    values = [padded[:, LANES * tile : LANES * (tile + 1)] for tile in range(count)]
    values = jnp.concatenate(values + [jnp.zeros((32, LANES), jnp.float32)], axis=0)
    square = values * values
    high = square.astype(jnp.bfloat16)
    low = (square - high.astype(jnp.float32)).astype(jnp.bfloat16)
    values = values.astype(jnp.bfloat16)
    lag = lax.broadcasted_iota(jnp.int32, (2 * LANES, LANES), 0)
    lag = lag - lax.broadcasted_iota(jnp.int32, (2 * LANES, LANES), 1)
    band = jnp.where(jnp.logical_and(lag >= 0, lag < tlen), 1.0, 0.0).astype(jnp.bfloat16)

    def windows(array):
        both = jnp.concatenate([array[0:rows], array[32 : rows + 32]], axis=1)
        return jnp.dot(both, band, preferred_element_type=jnp.float32)

    first_sum = windows(values)
    second_sum = windows(high) + windows(low)
    variance = (second_sum * tlen - first_sum * first_sum) * (1.0 / tlen**2)
    scale = lax.rsqrt(variance + EPSILON)
    for tile in range(length // LANES):
        part = scale[32 * tile : 32 * (tile + 1)]
        after = scale[32 * (tile + 1) : 32 * (tile + 2)]
        inverse[2 * tile] = part
        lane = lax.broadcasted_iota(jnp.int32, part.shape, 1)
        both = jnp.where(lane < STRIDE, after, part)
        inverse[2 * tile + 1] = pltpu.roll(both, LANES - STRIDE, 1)

    def interleaved(row, tiles):
        even, odd = lagged(row, 0), lagged(row, STRIDE)
        parts = []
        for tile in range(tiles):
            lanes = slice(LANES * tile, LANES * (tile + 1))
            parts += [even[:, lanes], odd[:, lanes]]
        return jnp.concatenate(parts, axis=0)

    @pl.loop(0, channels // unroll)
    def _(step):
        for item in range(unroll):
            channel = step * unroll + item
            value = interleaved(padded[pl.ds(channel, 1), :], length // LANES + 1)
            left_a[channel] = value.astype(jnp.bfloat16)


def prepare_waves(tlen, group, swapped, pair, beside, far):
    channels, samples = beside.shape
    length = 2 * (swapped.shape[0] - 1) * samples
    rows = length // OFFSETS
    unroll = max(step for step in (1, 2, 3) if channels % step == 0)
    return pl.pallas_call(
        functools.partial(waves_kernel, channels, tlen, unroll),
        out_shape=[
            jax.ShapeDtypeStruct((channels, rows + 16, LANES), jnp.bfloat16),
            jax.ShapeDtypeStruct((length // STRIDE, 32, LANES), jnp.float32),
            jax.ShapeDtypeStruct((LANES, LANES // group * LANES), jnp.bfloat16),
            jax.ShapeDtypeStruct((2 * samples // OFFSETS, samples), jnp.bfloat16),
        ],
        in_specs=[VMEM] * (3 + len(far)),
        out_specs=[VMEM] * 4,
        scratch_shapes=[
            pltpu.VMEM((32, length + 2 * LANES), jnp.float32),
        ],
        compiler_params=params(),
        cost_estimate=cost(0.05),
        name="prepare_waves",
    )(swapped, pair, beside, *far)


def main_kernel(side, tlen, group, piece, left_a, inverse, expand, *rest):
    outs = rest[:-4]
    if side:
        before, outs = outs[0], outs[1:]
    bank, weight_a, reach, total = rest[-4:]
    core = lax.axis_index("tm") % 2
    channels = left_a.shape[0]
    rows = left_a.shape[1] - 16
    half = channels // 2
    base = half * jnp.where(core == side, 0, 1)
    slots = LANES // group
    banks = (half + 1) // slots
    offset_count = LANES // group
    tile_count = OFFSETS // offset_count
    top = 112 + 8 * (7 + offset_count - 1)
    top = top + top % 16

    lag = lax.broadcasted_iota(jnp.int32, (LANES, LANES), 0)
    lane = lax.broadcasted_iota(jnp.int32, (1, LANES), 1)
    used = lag < tlen
    ahead = lane // group
    turned = []
    for index in range(banks):
        count = min(slots, max(TILES - slots * index, 0))
        values = jnp.zeros((LANES, LANES), jnp.float32)
        if count:
            values = piece[slots * index : slots * index + count].astype(jnp.float32)
            values = values.reshape(count * group, LANES)
            if count < slots:
                gap = jnp.zeros((LANES - count * group, LANES), jnp.float32)
                values = jnp.concatenate([values, gap], axis=0)
            values = values.T
        turned.append(values)
    codes = [values[125:126, :] for values in turned]
    heads = [jnp.where(used, values, 0.0) for values in turned]
    for extra in range(half - TILES):
        place, slot = divmod(TILES + extra, slots)
        mask = ahead == slot
        code = pltpu.roll(turned[0][126:127, :], (slot - extra) * group % LANES, 1)
        codes[place] = jnp.where(mask, code, codes[place])
        for quarter in range(4):
            source, lanes = divmod(4 * extra + quarter, slots)
            values = turned[source][96:128]
            sample = lag[96:128]
            inside = jnp.logical_and(sample >= tlen, sample < tlen + QUARTER)
            values = jnp.where(inside, values, 0.0)
            values = pltpu.roll(values, (slot - lanes) * group % LANES, 1)
            start = QUARTER * quarter - (tlen - 96)
            values = jnp.concatenate([values, jnp.zeros((8, LANES), jnp.float32)], axis=0)
            values = pltpu.roll(values, start % 8, 0)
            start -= start % 8
            if start < 0:
                values, start = values[8:], 0
            below = LANES - start - values.shape[0]
            if start:
                values = jnp.concatenate([jnp.zeros((start, LANES), jnp.float32), values], axis=0)
            if below > 0:
                values = jnp.concatenate([values, jnp.zeros((below, LANES), jnp.float32)], axis=0)
            heads[place] = heads[place] + jnp.where(mask, values[0:LANES], 0.0)
    for index, (values, code) in enumerate(zip(heads, codes)):
        code = jnp.where(slots * index + ahead < half, code, 0.0)
        deviate = jnp.where(used, values * tlen - jnp.sum(values, axis=0, keepdims=True), 0.0)
        square = jnp.sum(deviate * deviate, axis=0, keepdims=True) * (1.0 / tlen**3)
        unit = deviate / (jnp.sqrt(square + EPSILON) * tlen**2)
        unit = unit.astype(jnp.bfloat16).astype(jnp.float32)
        unit = jnp.where(code > 0, unit, 0.0)
        shift = code.astype(jnp.int32) - 1
        for bit in (1, 2, 4):
            unit = jnp.where(jnp.bitwise_and(shift, bit) > 0, pltpu.roll(unit, bit, 0), unit)
        unit = jnp.where(lag == 112, code, unit)
        bank[index] = unit.astype(jnp.bfloat16)

    def build(number):
        wide = jnp.dot(bank[number], expand[...], preferred_element_type=jnp.float32)
        for slot in range(slots):
            spreaded = wide[:, slot * LANES : (slot + 1) * LANES]
            code = spreaded[112:113, :].astype(jnp.int32)
            shift = code - 1
            moves = shift // 8 + ahead
            taps = spreaded[0:112, :]
            for bit in (1, 2, 4, 8):
                gap = jnp.zeros((8 * bit, LANES), jnp.float32)
                taps = jnp.where(
                    jnp.bitwise_and(moves, bit) > 0,
                    jnp.concatenate([gap, taps], axis=0),
                    jnp.concatenate([taps, gap], axis=0),
                )[0:top]
            taps = taps.astype(jnp.bfloat16)
            item = number * slots + slot
            reach[item] = jnp.maximum(shift, 0) + 8 * ahead + 7 - lag[0:8]
            for tile in range(tile_count):
                skip = 8 * offset_count * tile
                lanes = slice(LANES * tile, LANES * (tile + 1))
                if skip:
                    weight_a[item, 0:skip, lanes] = jnp.zeros((skip, LANES), jnp.bfloat16)
                weight_a[item, skip : skip + top, lanes] = taps
                rest = DEPTH - top - skip
                if rest:
                    weight_a[item, skip + top :, lanes] = jnp.zeros((rest, LANES), jnp.bfloat16)

    def products(item):
        both = [left_a[base + item, 0:rows, :], left_a[base + item, 16 : rows + 16, :]]
        corr = jnp.dot(
            jnp.concatenate(both, axis=1), weight_a[item], preferred_element_type=jnp.float32
        )
        columns = []
        for tile in range(tile_count):
            place = reach[item] + 8 * offset_count * tile
            parts = []
            for step in range(rows // 8):
                window = inverse[step, pl.ds(base + item, 1), :]
                window = jnp.broadcast_to(window, (8, LANES))
                parts.append(jnp.take_along_axis(window, place, axis=1, mode="promise_in_bounds"))
            columns.append(jnp.concatenate(parts, axis=0))
        return corr * jnp.concatenate(columns, axis=1)

    def apply(number, count):
        for item in range(number * slots, number * slots + count, 2):
            value = products(item)
            if item + 1 < number * slots + count:
                value = value + products(item + 1)
            if item:
                value = value + total[...]
            elif side:
                value = value + before[...]
            total[...] = value

    build(0)

    for number in range(1, banks):
        apply(number - 1, slots)
        build(number)

    apply(banks - 1, half - slots * (banks - 1))

    if not side:
        outs[0][...] = total[...]
        return
    rows_out = outs[0].shape[0]
    station = lax.axis_index("sta") // 2
    for step, out in enumerate(outs):
        part = jnp.bitwise_xor(station, step)
        out[...] = total[pl.ds(pl.multiple_of(part * rows_out, rows_out), rows_out), :].astype(
            jnp.bfloat16
        )


def correlate(side, tlen, group, count, piece, left_a, inverse, expand, *before):
    channels = left_a.shape[0]
    rows = left_a.shape[1] - 16
    width = OFFSETS * group
    half = channels // 2
    if side:
        out = [jax.ShapeDtypeStruct((rows // count, width), jnp.bfloat16)] * count
    else:
        out = [jax.ShapeDtypeStruct((rows, width), jnp.float32)]
    return pl.pallas_call(
        functools.partial(main_kernel, side, tlen, group),
        out_shape=out,
        in_specs=[VMEM] * (4 + len(before)),
        out_specs=[VMEM] * len(out),
        scratch_shapes=[
            pltpu.VMEM(((half + 1) * group // LANES, LANES, LANES), jnp.bfloat16),
            pltpu.VMEM((half + 1, DEPTH, width), jnp.bfloat16),
            pltpu.VMEM((half + 1, 8, LANES), jnp.int32),
            pltpu.VMEM((rows, width), jnp.float32),
        ],
        compiler_params=params(),
        cost_estimate=cost(3),
        name="correlate_" + ("second" if side else "first"),
    )(piece, left_a, inverse, expand, *before)


def add_kernel(*refs):
    parts, keep, send = refs[:-2], refs[-2], refs[-1]
    rows = keep.shape[0]
    core = lax.axis_index("tm") % 2
    for out, which in ((keep, core), (send, 1 - core)):
        place = pl.ds(pl.multiple_of(which * rows, rows), rows)
        value = parts[0][place, :].astype(jnp.float32)
        for part in parts[1:]:
            value = value + part[place, :].astype(jnp.float32)
        out[...] = value


def add(parts):
    rows, width = parts[0].shape
    out = jax.ShapeDtypeStruct((rows // 2, width), jnp.float32)
    return pl.pallas_call(
        add_kernel,
        out_shape=[out, out],
        in_specs=[VMEM] * len(parts),
        out_specs=[VMEM, VMEM],
        compiler_params=params(),
        cost_estimate=cost(0.5),
        name="add",
    )(*parts)


def finish_kernel(group, ours, received, place, out):
    samples = out.shape[1]
    value = ours[...] + received[...]
    high = value.astype(jnp.bfloat16).astype(jnp.float32)
    both = jnp.concatenate([high, value - high], axis=0).T.astype(jnp.bfloat16)
    wide = jnp.dot(both, place[...], preferred_element_type=jnp.float32)
    lane = lax.broadcasted_iota(jnp.int32, (group, samples), 1) // 8 % OFFSETS
    result = jnp.zeros((group, samples), jnp.float32)
    for offset in range(OFFSETS):
        result = jnp.where(lane == offset, wide[offset * group : (offset + 1) * group], result)
    out[...] = result


def finish(group, samples, ours, received, place):
    return pl.pallas_call(
        functools.partial(finish_kernel, group),
        out_shape=jax.ShapeDtypeStruct((group, samples), jnp.float32),
        in_specs=[VMEM] * 3,
        out_specs=VMEM,
        compiler_params=params(),
        cost_estimate=cost(1),
        name="finish",
    )(ours, received, place)


def shards(waveforms, templates, available, moveout, bank_blocks):
    channels, samples = waveforms.shape
    blocks, events, _, tlen = templates.shape
    count_tm = lax.axis_size("tm")
    count_sta = lax.axis_size("sta")
    chips = count_tm // 2
    near = chips // 2
    group = 2 * events // chips

    def swap(array):
        return lax.ppermute(array, "tm", [(i, i ^ 1) for i in range(count_tm)])

    def across(array, step):
        return lax.ppermute(array, "tm", [(i, i ^ (2 * step)) for i in range(count_tm)])

    partner = swap(waveforms)
    mine, theirs, owners = pack(
        chips,
        group,
        bank_blocks,
        jnp.transpose(templates, (0, 2, 1, 3)),
        jnp.transpose(available, (2, 0, 1)),
        jnp.transpose(moveout, (2, 0, 1)),
    )
    theirs, partner = lax.optimization_barrier((theirs, partner))
    other = swap(theirs)
    pair = pair_waves(waveforms, partner)
    far = []
    for number in range(near - 1):
        steps = (chips - 1 - 2 * number, chips - 2 - 2 * number)
        route = [(2 * z + c, 2 * (z ^ steps[c]) + c) for z in range(chips) for c in range(2)]
        far.append(lax.ppermute(pair, "tm", route))
    beside = across(waveforms, 1)
    merged = list(merge(owners, mine, other))
    def exchange(number):
        route = [
            (2 * z + c, 2 * (z ^ step_of(number, chips, c)) + c) for z in range(chips) for c in range(2)
        ]
        return lax.ppermute(merged[number], "tm", route)

    pieces = [exchange(number) for number in reversed(range(1, chips))]
    pieces = [merged[0]] + pieces[::-1]
    swapped = swap(choose_waves(pair, beside, far))
    left_a, inverse, expand, place = prepare_waves(tlen, group, swapped, pair, beside, far)

    order = sorted(range(chips), key=lambda step: (step < 2, step))
    placed = lax.optimization_barrier((left_a, inverse, *[pieces[step] for step in order]))
    left_a, inverse = placed[:2]
    pieces = [placed[2 + order.index(step)] for step in range(chips)]
    first = choose_piece(owners, pieces)
    second = swap(first)
    total = correlate(0, tlen, group, near, first, left_a, inverse, expand)
    parts = correlate(1, tlen, group, near, second, left_a, inverse, expand, *total)
    gathered = []
    for step in range(near):
        route = []
        for d in range(count_tm):
            for s in range(count_sta):
                dest = near * (d % 2) + (s // 2 ^ step)
                route.append((d * count_sta + s, (2 * dest + s % 2) * count_sta + d // 2))
        gathered.append(lax.ppermute(parts[step], ("tm", "sta"), route))
    ours, send = add(gathered)
    return finish(group, samples, ours, swap(send), place)


def solution(mesh):
    in_specs = (
        P("sta", "tm"),
        P("tm", None, "sta", None),
        P("tm", None, "sta"),
        P("tm", None, "sta"),
        P(),
    )
    out_specs = P("sta", "tm")
    return jax.shard_map(shards, mesh=mesh, in_specs=in_specs, out_specs=out_specs, check_vma=False)
```

```python
import functools

import jax
import jax.numpy as jnp
from jax import lax
from jax.experimental import pallas as pl
from jax.experimental.pallas import tpu as pltpu
from jax.sharding import PartitionSpec as P

EPSILON = 1e-06
LANES = 128
OFFSETS = 8
TILES = 12
QUARTER = 25
STRIDE = 64
DEPTH = 256
VMEM_LIMIT = 28 * 1024 * 1024

VMEM = pl.BlockSpec(memory_space=pltpu.VMEM)
ANY = pl.BlockSpec(memory_space=pl.ANY)


def params():
    return pltpu.CompilerParams(vmem_limit_bytes=VMEM_LIMIT)


def cost(micros):
    return pl.CostEstimate(
        flops=int(micros * 1e9), bytes_accessed=int(micros * 1e6), transcendentals=0
    )


def pack_kernel(bank_blocks, templates, available, moveout, mine, theirs, owners, chosen, raw, usable, shifts, square, sems):
    blocks, channels, events, tlen = templates.shape
    chips, _, group, _ = mine.shape
    half = channels // 2
    me = lax.axis_index("tm") % 2
    fetch = [
        pltpu.make_async_copy(source, target, sems.at[index])
        for index, (source, target) in enumerate(
            ((bank_blocks, chosen), (available, usable), (moveout, shifts))
        )
    ]
    for side in (1, 0):
        first = half * jnp.where(me == side, 0, 1)
        for block in range(blocks):
            place = (block, pl.ds(first, half))
            number = 3 + blocks * (1 - side) + block
            fetch.append(
                pltpu.make_async_copy(templates.at[place], raw.at[place], sems.at[number])
            )
    for copy in fetch:
        copy.start()
    mine[...] = jnp.zeros_like(mine)
    theirs[...] = jnp.zeros_like(theirs)
    square[...] = jnp.zeros_like(square)
    for copy in fetch[:3]:
        copy.wait()
    slots = [chosen[which] % blocks for which in range(2)]
    row = lax.broadcasted_iota(jnp.int32, owners.shape, 0)
    owners[...] = jnp.where(row == 0, chosen[0] // blocks, chosen[1] // blocks)
    flags = jnp.where(usable[...] > 0, shifts[...] + 1, 0).astype(jnp.float32)
    codes = []
    for which in range(2):
        code = flags[:, 0, :]
        for block in range(1, blocks):
            code = jnp.where(slots[which] == block, flags[:, block, :], code)
        square[0:channels, 0:events] = code
        turned = square[...].T
        later = pltpu.roll(turned, LANES - half, 1)
        codes.append([jnp.where(me == core, turned, later) for core in range(2)])
    for side, out in ((1, theirs), (0, mine)):
        for block in range(blocks):
            fetch[3 + blocks * (1 - side) + block].wait()
        for which in range(2):
            first = half * jnp.where(me == side, 0, 1)
            code = codes[which][side].astype(jnp.bfloat16)
            for tile in range(TILES):
                extra = TILES + tile // 4
                start = QUARTER * (tile % 4)
                for index in range(events // group):
                    chip = which * (events // group) + index
                    rows = slice(index * group, (index + 1) * group)
                    out[chip, tile, :, 0:tlen] = raw[slots[which], first + tile, rows, :]
                    out[chip, tile, :, tlen : tlen + QUARTER] = raw[
                        slots[which], first + extra, rows, start : start + QUARTER
                    ]
                    out[chip, tile, :, 125:126] = code[rows, tile : tile + 1]
                    if tile < half - TILES:
                        beyond = TILES + tile
                        out[chip, tile, :, 126:127] = code[rows, beyond : beyond + 1]


def pack(chips, group, bank_blocks, templates, available, moveout):
    shape = (chips, TILES, group, LANES)
    held = [
        pltpu.with_memory_space_constraint(array, pltpu.HBM)
        for array in (bank_blocks, templates, available, moveout)
    ]
    return pl.pallas_call(
        pack_kernel,
        out_shape=[jax.ShapeDtypeStruct(shape, jnp.bfloat16)] * 2
        + [jax.ShapeDtypeStruct((8, LANES), jnp.int32)],
        in_specs=[ANY] * 4,
        out_specs=[VMEM] * 3,
        scratch_shapes=[
            pltpu.SMEM(bank_blocks.shape, jnp.int32),
            pltpu.VMEM(templates.shape, jnp.bfloat16),
            pltpu.VMEM(available.shape, jnp.int32),
            pltpu.VMEM(moveout.shape, jnp.int32),
            pltpu.VMEM((LANES, LANES), jnp.float32),
            pltpu.SemaphoreType.DMA((3 + 2 * templates.shape[0],)),
        ],
        compiler_params=params(),
        cost_estimate=cost(2),
        name="pack",
    )(*held)


def step_of(number, chips, core):
    if number < 2:
        return number
    pair, second = divmod(number - 2, 2)
    high = chips - 1 - 2 * pair
    return high - core if second else high - 1 + core


def merge_kernel(owners, mine, other, *outs):
    chips = len(outs)
    me = lax.axis_index("tm")
    for number, out in enumerate(outs):
        dest = jnp.bitwise_xor(me // 2, step_of(number, chips, me % 2))
        owner = jnp.where(dest < chips // 2, owners[0, 0], owners[1, 0])
        here = owner % 2 == me % 2

        @pl.when(here)
        def _():
            out[...] = mine[dest]

        @pl.when(jnp.logical_not(here))
        def _():
            out[...] = other[dest]


def merge(owners, mine, other):
    chips = mine.shape[0]
    return pl.pallas_call(
        merge_kernel,
        out_shape=[jax.ShapeDtypeStruct(mine.shape[1:], mine.dtype)] * chips,
        in_specs=[VMEM] * 3,
        out_specs=[VMEM] * chips,
        compiler_params=params(),
        cost_estimate=cost(0.3),
        name="merge",
    )(owners, mine, other)


def lagged(row, ahead):
    copies = jnp.broadcast_to(row, (8, row.shape[1]))
    return pltpu.roll(copies, row.shape[1] - 7 - ahead, 1, stride=1, stride_axis=0)


def segment(me, other, parity, pair, beside, far, default):
    chip, core = me // 2, me % 2
    chips = 2 * len(far) + 2
    step = jnp.bitwise_xor(chip, other)
    value = default[...]
    value = jnp.where(jnp.logical_and(step == 1, core == parity), beside[...], value)
    value = jnp.where(step == 0, pair[parity], value)
    for number, array in enumerate(far):
        value = jnp.where(step == chips - 1 - 2 * number - core, array[parity], value)
    return value


def pair_kernel(own, partner, out):
    core = lax.axis_index("tm") % 2
    out[core] = own[...]
    out[1 - core] = partner[...]


def pair_waves(own, partner):
    return pl.pallas_call(
        pair_kernel,
        out_shape=jax.ShapeDtypeStruct((2,) + own.shape, own.dtype),
        in_specs=[VMEM] * 2,
        out_specs=VMEM,
        compiler_params=params(),
        cost_estimate=cost(0.05),
        name="pair_waves",
    )(own, partner)


def choose_kernel(pair, beside, *rest):
    far, out = rest[:-1], rest[-1]
    near = out.shape[0] - 1
    me = lax.axis_index("tm")
    chip, core = me // 2, me % 2
    for entry in range(near):
        number, parity = divmod(entry, 2)
        step = jnp.bitwise_xor(chip, near * (1 - core) + 2 * number) // 2
        value = beside[...]
        for place, array in enumerate(far):
            value = jnp.where(step == near - 1 - place, array[parity], value)
        out[entry] = value
    out[near] = segment(me, near, 0, pair, beside, far, beside)


def choose_waves(pair, beside, far):
    return pl.pallas_call(
        choose_kernel,
        out_shape=jax.ShapeDtypeStruct((len(far) + 2,) + beside.shape, beside.dtype),
        in_specs=[VMEM] * (2 + len(far)),
        out_specs=VMEM,
        compiler_params=params(),
        cost_estimate=cost(0.05),
        name="choose_waves",
    )(pair, beside, *far)


def own_kernel(owners, *refs):
    pieces, out = refs[:-1], refs[-1]
    me = lax.axis_index("tm")
    chip, chips = me // 2, len(pieces)
    owner = jnp.where(chip < chips // 2, owners[0, 0], owners[1, 0])
    source = jnp.bitwise_xor(owner // 2, chip)
    value = pieces[0][...]
    for number, piece in enumerate(pieces[1:], 1):
        value = jnp.where(source == step_of(number, chips, me % 2), piece[...], value)
    out[...] = value


def choose_piece(owners, pieces):
    return pl.pallas_call(
        own_kernel,
        out_shape=jax.ShapeDtypeStruct(pieces[0].shape, pieces[0].dtype),
        in_specs=[VMEM] * (1 + len(pieces)),
        out_specs=VMEM,
        compiler_params=params(),
        cost_estimate=cost(0.3),
        name="choose_piece",
    )(owners, *pieces)


def waves_kernel(channels, tlen, unroll, swapped, pair, beside, *rest):
    far = rest[:-5]
    left_a, inverse, expand, place, padded = rest[-5:]
    samples = beside.shape[1]
    near = swapped.shape[0] - 1
    length = 2 * near * samples
    count = padded.shape[1] // LANES
    me = lax.axis_index("tm")
    core = me % 2
    padded[...] = jnp.zeros_like(padded)
    for index in range(2 * near):
        entry, parity = divmod(index, 2)
        given = swapped.at[2 * (entry // 2) + parity]
        wave = segment(me, near * core + entry, parity, pair, beside, far, given)
        padded[0:channels, samples * index : samples * (index + 1)] = wave.astype(jnp.float32)
    rim = segment(me, near * core + near, 0, pair, beside, far, swapped.at[near])
    rim = rim[:, 0 : padded.shape[1] - length].astype(jnp.float32)
    padded[0:channels, length:] = jnp.where(core == 0, rim, 0.0)

    group = expand.shape[1] // LANES
    group = LANES // group
    row = lax.broadcasted_iota(jnp.int32, expand.shape, 0)
    lane = lax.broadcasted_iota(jnp.int32, expand.shape, 1)
    chosen = row == lane % group + lane // LANES * group
    expand[...] = jnp.where(chosen, 1.0, 0.0).astype(jnp.bfloat16)
    row = lax.broadcasted_iota(jnp.int32, place.shape, 0) % (place.shape[0] // 2)
    lane = lax.broadcasted_iota(jnp.int32, place.shape, 1)
    chosen = jnp.logical_and(lane // STRIDE == row // 8, lane % 8 == 7 - row % 8)
    place[...] = jnp.where(chosen, 1.0, 0.0).astype(jnp.bfloat16)

    rows = 32 * count
    values = [padded[:, LANES * tile : LANES * (tile + 1)] for tile in range(count)]
    values = jnp.concatenate(values + [jnp.zeros((32, LANES), jnp.float32)], axis=0)
    square = values * values
    high = square.astype(jnp.bfloat16)
    low = (square - high.astype(jnp.float32)).astype(jnp.bfloat16)
    values = values.astype(jnp.bfloat16)
    lag = lax.broadcasted_iota(jnp.int32, (2 * LANES, LANES), 0)
    lag = lag - lax.broadcasted_iota(jnp.int32, (2 * LANES, LANES), 1)
    band = jnp.where(jnp.logical_and(lag >= 0, lag < tlen), 1.0, 0.0).astype(jnp.bfloat16)

    def windows(array):
        both = jnp.concatenate([array[0:rows], array[32 : rows + 32]], axis=1)
        return jnp.dot(both, band, preferred_element_type=jnp.float32)

    first_sum = windows(values)
    second_sum = windows(high) + windows(low)
    variance = (second_sum * tlen - first_sum * first_sum) * (1.0 / tlen**2)
    scale = lax.rsqrt(variance + EPSILON)
    for tile in range(length // LANES):
        part = scale[32 * tile : 32 * (tile + 1)]
        after = scale[32 * (tile + 1) : 32 * (tile + 2)]
        inverse[2 * tile] = part
        lane = lax.broadcasted_iota(jnp.int32, part.shape, 1)
        both = jnp.where(lane < STRIDE, after, part)
        inverse[2 * tile + 1] = pltpu.roll(both, LANES - STRIDE, 1)

    def interleaved(row, tiles):
        even, odd = lagged(row, 0), lagged(row, STRIDE)
        parts = []
        for tile in range(tiles):
            lanes = slice(LANES * tile, LANES * (tile + 1))
            parts += [even[:, lanes], odd[:, lanes]]
        return jnp.concatenate(parts, axis=0)

    @pl.loop(0, channels // unroll)
    def _(step):
        for item in range(unroll):
            channel = step * unroll + item
            value = interleaved(padded[pl.ds(channel, 1), :], length // LANES + 1)
            left_a[channel] = value.astype(jnp.bfloat16)


def prepare_waves(tlen, group, swapped, pair, beside, far):
    channels, samples = beside.shape
    length = 2 * (swapped.shape[0] - 1) * samples
    rows = length // OFFSETS
    unroll = max(step for step in (1, 2, 3) if channels % step == 0)
    return pl.pallas_call(
        functools.partial(waves_kernel, channels, tlen, unroll),
        out_shape=[
            jax.ShapeDtypeStruct((channels, rows + 16, LANES), jnp.bfloat16),
            jax.ShapeDtypeStruct((length // STRIDE, 32, LANES), jnp.float32),
            jax.ShapeDtypeStruct((LANES, LANES // group * LANES), jnp.bfloat16),
            jax.ShapeDtypeStruct((2 * samples // OFFSETS, samples), jnp.bfloat16),
        ],
        in_specs=[VMEM] * (3 + len(far)),
        out_specs=[VMEM] * 4,
        scratch_shapes=[
            pltpu.VMEM((32, length + 2 * LANES), jnp.float32),
        ],
        compiler_params=params(),
        cost_estimate=cost(0.05),
        name="prepare_waves",
    )(swapped, pair, beside, *far)


def main_kernel(side, tlen, group, piece, left_a, inverse, expand, *rest):
    outs = rest[:-4]
    if side:
        before, outs = outs[0], outs[1:]
    bank, weight_a, reach, total = rest[-4:]
    core = lax.axis_index("tm") % 2
    channels = left_a.shape[0]
    rows = left_a.shape[1] - 16
    half = channels // 2
    base = half * jnp.where(core == side, 0, 1)
    slots = LANES // group
    banks = (half + 1) // slots
    offset_count = LANES // group
    tile_count = OFFSETS // offset_count
    top = 112 + 8 * (7 + offset_count - 1)
    top = top + top % 16

    lag = lax.broadcasted_iota(jnp.int32, (LANES, LANES), 0)
    lane = lax.broadcasted_iota(jnp.int32, (1, LANES), 1)
    used = lag < tlen
    ahead = lane // group
    turned = []
    for index in range(banks):
        count = min(slots, max(TILES - slots * index, 0))
        values = jnp.zeros((LANES, LANES), jnp.float32)
        if count:
            values = piece[slots * index : slots * index + count].astype(jnp.float32)
            values = values.reshape(count * group, LANES)
            if count < slots:
                gap = jnp.zeros((LANES - count * group, LANES), jnp.float32)
                values = jnp.concatenate([values, gap], axis=0)
            values = values.T
        turned.append(values)
    codes = [values[125:126, :] for values in turned]
    heads = [jnp.where(used, values, 0.0) for values in turned]
    for extra in range(half - TILES):
        place, slot = divmod(TILES + extra, slots)
        mask = ahead == slot
        code = pltpu.roll(turned[0][126:127, :], (slot - extra) * group % LANES, 1)
        codes[place] = jnp.where(mask, code, codes[place])
        for quarter in range(4):
            source, lanes = divmod(4 * extra + quarter, slots)
            values = turned[source][96:128]
            sample = lag[96:128]
            inside = jnp.logical_and(sample >= tlen, sample < tlen + QUARTER)
            values = jnp.where(inside, values, 0.0)
            values = pltpu.roll(values, (slot - lanes) * group % LANES, 1)
            start = QUARTER * quarter - (tlen - 96)
            values = jnp.concatenate([values, jnp.zeros((8, LANES), jnp.float32)], axis=0)
            values = pltpu.roll(values, start % 8, 0)
            start -= start % 8
            if start < 0:
                values, start = values[8:], 0
            below = LANES - start - values.shape[0]
            if start:
                values = jnp.concatenate([jnp.zeros((start, LANES), jnp.float32), values], axis=0)
            if below > 0:
                values = jnp.concatenate([values, jnp.zeros((below, LANES), jnp.float32)], axis=0)
            heads[place] = heads[place] + jnp.where(mask, values[0:LANES], 0.0)
    for index, (values, code) in enumerate(zip(heads, codes)):
        code = jnp.where(slots * index + ahead < half, code, 0.0)
        deviate = jnp.where(used, values * tlen - jnp.sum(values, axis=0, keepdims=True), 0.0)
        square = jnp.sum(deviate * deviate, axis=0, keepdims=True) * (1.0 / tlen**3)
        unit = deviate / (jnp.sqrt(square + EPSILON) * tlen**2)
        unit = unit.astype(jnp.bfloat16).astype(jnp.float32)
        unit = jnp.where(code > 0, unit, 0.0)
        shift = code.astype(jnp.int32) - 1
        for bit in (1, 2, 4):
            unit = jnp.where(jnp.bitwise_and(shift, bit) > 0, pltpu.roll(unit, bit, 0), unit)
        unit = jnp.where(lag == 112, code, unit)
        bank[index] = unit.astype(jnp.bfloat16)

    def build(number):
        wide = jnp.dot(bank[number], expand[...], preferred_element_type=jnp.float32)
        for slot in range(slots):
            spreaded = wide[:, slot * LANES : (slot + 1) * LANES]
            code = spreaded[112:113, :].astype(jnp.int32)
            shift = code - 1
            moves = shift // 8 + ahead
            taps = spreaded[0:112, :]
            for bit in (1, 2, 4, 8):
                gap = jnp.zeros((8 * bit, LANES), jnp.float32)
                taps = jnp.where(
                    jnp.bitwise_and(moves, bit) > 0,
                    jnp.concatenate([gap, taps], axis=0),
                    jnp.concatenate([taps, gap], axis=0),
                )[0:top]
            taps = taps.astype(jnp.bfloat16)
            item = number * slots + slot
            reach[item] = jnp.maximum(shift, 0) + 8 * ahead + 7 - lag[0:8]
            for tile in range(tile_count):
                skip = 8 * offset_count * tile
                lanes = slice(LANES * tile, LANES * (tile + 1))
                if skip:
                    weight_a[item, 0:skip, lanes] = jnp.zeros((skip, LANES), jnp.bfloat16)
                weight_a[item, skip : skip + top, lanes] = taps
                rest = DEPTH - top - skip
                if rest:
                    weight_a[item, skip + top :, lanes] = jnp.zeros((rest, LANES), jnp.bfloat16)

    def products(item):
        both = [left_a[base + item, 0:rows, :], left_a[base + item, 16 : rows + 16, :]]
        corr = jnp.dot(
            jnp.concatenate(both, axis=1), weight_a[item], preferred_element_type=jnp.float32
        )
        columns = []
        for tile in range(tile_count):
            place = reach[item] + 8 * offset_count * tile
            parts = []
            for step in range(rows // 8):
                window = inverse[step, pl.ds(base + item, 1), :]
                window = jnp.broadcast_to(window, (8, LANES))
                parts.append(jnp.take_along_axis(window, place, axis=1, mode="promise_in_bounds"))
            columns.append(jnp.concatenate(parts, axis=0))
        return corr * jnp.concatenate(columns, axis=1)

    def apply(number, count):
        for item in range(number * slots, number * slots + count, 2):
            value = products(item)
            if item + 1 < number * slots + count:
                value = value + products(item + 1)
            if item:
                value = value + total[...]
            elif side:
                value = value + before[...]
            total[...] = value

    build(0)

    for number in range(1, banks):
        apply(number - 1, slots)
        build(number)

    apply(banks - 1, half - slots * (banks - 1))

    if not side:
        outs[0][...] = total[...]
        return
    rows_out = outs[0].shape[0]
    station = lax.axis_index("sta") // 2
    for step, out in enumerate(outs):
        part = jnp.bitwise_xor(station, step)
        out[...] = total[pl.ds(pl.multiple_of(part * rows_out, rows_out), rows_out), :].astype(
            jnp.bfloat16
        )


def correlate(side, tlen, group, count, piece, left_a, inverse, expand, *before):
    channels = left_a.shape[0]
    rows = left_a.shape[1] - 16
    width = OFFSETS * group
    half = channels // 2
    if side:
        out = [jax.ShapeDtypeStruct((rows // count, width), jnp.bfloat16)] * count
    else:
        out = [jax.ShapeDtypeStruct((rows, width), jnp.float32)]
    return pl.pallas_call(
        functools.partial(main_kernel, side, tlen, group),
        out_shape=out,
        in_specs=[VMEM] * (4 + len(before)),
        out_specs=[VMEM] * len(out),
        scratch_shapes=[
            pltpu.VMEM(((half + 1) * group // LANES, LANES, LANES), jnp.bfloat16),
            pltpu.VMEM((half + 1, DEPTH, width), jnp.bfloat16),
            pltpu.VMEM((half + 1, 8, LANES), jnp.int32),
            pltpu.VMEM((rows, width), jnp.float32),
        ],
        compiler_params=params(),
        cost_estimate=cost(3),
        name="correlate_" + ("second" if side else "first"),
    )(piece, left_a, inverse, expand, *before)


def add_kernel(*refs):
    parts, keep, send = refs[:-2], refs[-2], refs[-1]
    rows = keep.shape[0]
    core = lax.axis_index("tm") % 2
    for out, which in ((keep, core), (send, 1 - core)):
        place = pl.ds(pl.multiple_of(which * rows, rows), rows)
        value = parts[0][place, :].astype(jnp.float32)
        for part in parts[1:]:
            value = value + part[place, :].astype(jnp.float32)
        out[...] = value


def add(parts):
    rows, width = parts[0].shape
    out = jax.ShapeDtypeStruct((rows // 2, width), jnp.float32)
    return pl.pallas_call(
        add_kernel,
        out_shape=[out, out],
        in_specs=[VMEM] * len(parts),
        out_specs=[VMEM, VMEM],
        compiler_params=params(),
        cost_estimate=cost(0.5),
        name="add",
    )(*parts)


def finish_kernel(group, ours, received, place, out):
    samples = out.shape[1]
    value = ours[...] + received[...]
    high = value.astype(jnp.bfloat16).astype(jnp.float32)
    both = jnp.concatenate([high, value - high], axis=0).T.astype(jnp.bfloat16)
    wide = jnp.dot(both, place[...], preferred_element_type=jnp.float32)
    lane = lax.broadcasted_iota(jnp.int32, (group, samples), 1) // 8 % OFFSETS
    result = jnp.zeros((group, samples), jnp.float32)
    for offset in range(OFFSETS):
        result = jnp.where(lane == offset, wide[offset * group : (offset + 1) * group], result)
    out[...] = result


def finish(group, samples, ours, received, place):
    return pl.pallas_call(
        functools.partial(finish_kernel, group),
        out_shape=jax.ShapeDtypeStruct((group, samples), jnp.float32),
        in_specs=[VMEM] * 3,
        out_specs=VMEM,
        compiler_params=params(),
        cost_estimate=cost(1),
        name="finish",
    )(ours, received, place)


def shards(waveforms, templates, available, moveout, bank_blocks):
    channels, samples = waveforms.shape
    blocks, events, _, tlen = templates.shape
    count_tm = lax.axis_size("tm")
    count_sta = lax.axis_size("sta")
    chips = count_tm // 2
    near = chips // 2
    group = 2 * events // chips

    def swap(array):
        return lax.ppermute(array, "tm", [(i, i ^ 1) for i in range(count_tm)])

    def across(array, step):
        return lax.ppermute(array, "tm", [(i, i ^ (2 * step)) for i in range(count_tm)])

    partner = swap(waveforms)
    mine, theirs, owners = pack(
        chips,
        group,
        bank_blocks,
        jnp.transpose(templates, (0, 2, 1, 3)),
        jnp.transpose(available, (2, 0, 1)),
        jnp.transpose(moveout, (2, 0, 1)),
    )
    theirs, partner = lax.optimization_barrier((theirs, partner))
    other = swap(theirs)
    pair = pair_waves(waveforms, partner)
    far = []
    for number in range(near - 1):
        steps = (chips - 1 - 2 * number, chips - 2 - 2 * number)
        route = [(2 * z + c, 2 * (z ^ steps[c]) + c) for z in range(chips) for c in range(2)]
        far.append(lax.ppermute(pair, "tm", route))
    beside = across(waveforms, 1)
    merged = list(merge(owners, mine, other))
    def exchange(number):
        route = [
            (2 * z + c, 2 * (z ^ step_of(number, chips, c)) + c) for z in range(chips) for c in range(2)
        ]
        return lax.ppermute(merged[number], "tm", route)

    pieces = [exchange(number) for number in reversed(range(1, chips))]
    pieces = [merged[0]] + pieces[::-1]
    swapped = swap(choose_waves(pair, beside, far))
    left_a, inverse, expand, place = prepare_waves(tlen, group, swapped, pair, beside, far)

    order = sorted(range(chips), key=lambda step: (step < 2, step))
    placed = lax.optimization_barrier((left_a, inverse, *[pieces[step] for step in order]))
    left_a, inverse = placed[:2]
    pieces = [placed[2 + order.index(step)] for step in range(chips)]
    first = choose_piece(owners, pieces)
    second = swap(first)
    total = correlate(0, tlen, group, near, first, left_a, inverse, expand)
    parts = correlate(1, tlen, group, near, second, left_a, inverse, expand, *total)
    gathered = []
    for step in range(near):
        route = []
        for d in range(count_tm):
            for s in range(count_sta):
                dest = near * (d % 2) + (s // 2 ^ step)
                route.append((d * count_sta + s, (2 * dest + s % 2) * count_sta + d // 2))
        gathered.append(lax.ppermute(parts[step], ("tm", "sta"), route))
    ours, send = add(gathered)
    return finish(group, samples, ours, swap(send), place)


def solution(mesh):
    in_specs = (
        P("sta", "tm"),
        P("tm", None, "sta", None),
        P("tm", None, "sta"),
        P("tm", None, "sta"),
        P(),
    )
    out_specs = P("sta", "tm")
    return jax.shard_map(shards, mesh=mesh, in_specs=in_specs, out_specs=out_specs, check_vma=False)
```
